128 devices in a mesh: dp: 32 (over z, x, core), mp: 4 (over y).
Axes of the slice: x: 4, y: 4, z: 4, core: 2. Of those that a mesh axis runs over, the one named last changes fastest.
Arguments:
- pixels: bfloat16 [8192, 192], P('dp'), may hold values from -6 to 6
- targets: float32 [8192, 192], P('dp', 'mp'), may hold values from -6 to 6
- valid_mask: int32 [8192, 4], P('dp'), may hold values from 0 to 1, as said below
- segments: int32 [32, 256], P('dp'), may hold values from 0 to 3, never falling along the last dimension, each value on 1 to 128 neighbouring positions
- lead_index: int32 [32, 4], P('dp'), may hold values from 0 to 27
- latitude: int32 [8192], P('dp'), may hold values from 0 to 31
- var_ids: int32 [48], replicated, may hold values from 0 to 47, each once
- running_error: float32 [48], replicated, may hold values from 0.5 to 2
- agg_weight: float32 [4, 1024, 1024], P(None, 'dp', 'mp'), as said below
- attn_weight: float32 [4, 1024, 1024], P(None, 'dp', 'mp'), as said below
- mlp_weight: float32 [2, 1024, 4096], P(None, 'dp', 'mp'), as said below
- head_weight: float32 [1024, 192], P('dp', 'mp'), may hold values from -0.1875 to 0.1875
- embed_weight: float32 [48, 5, 1024], P(None, None, ('dp', 'mp')), may hold values from -3 to 3
- vectors: float32 [17, 1024], P(None, ('dp', 'mp')), as said below
- agg_first: float32 [4, 1024, 1024], P(None, 'dp', 'mp'), as said below
- attn_first: float32 [4, 1024, 1024], P(None, 'dp', 'mp'), as said below
- mlp_first: float32 [2, 1024, 4096], P(None, 'dp', 'mp'), as said below
- head_first: float32 [1024, 192], P('dp', 'mp'), as said below
- embed_first: float32 [48, 5, 1024], P(None, None, ('dp', 'mp')), as said below
- vector_first: float32 [17, 1024], P(None, ('dp', 'mp')), as said below
- agg_second: float32 [4, 1024, 1024], P(None, 'dp', 'mp'), as said below
- attn_second: float32 [4, 1024, 1024], P(None, 'dp', 'mp'), as said below
- mlp_second: float32 [2, 1024, 4096], P(None, 'dp', 'mp'), as said below
- head_second: float32 [1024, 192], P('dp', 'mp'), as said below
- embed_second: float32 [48, 5, 1024], P(None, None, ('dp', 'mp')), as said below
- vector_second: float32 [17, 1024], P(None, ('dp', 'mp')), as said below
Outputs:
- loss_sum: float32 [], replicated
- valid_count: float32 [], replicated
- running_out: float32 [48], replicated
- trust_ratios: float32 [29], replicated
- weight_norms: float32 [29], replicated
- agg_moment: float32 [4, 1024, 1024], P(None, 'dp', 'mp')
- attn_moment: float32 [4, 1024, 1024], P(None, 'dp', 'mp')
- mlp_moment: float32 [2, 1024, 4096], P(None, 'dp', 'mp')
- head_moment: float32 [1024, 192], P('dp', 'mp')
- embed_moment: float32 [48, 5, 1024], P(None, None, ('dp', 'mp'))
- vector_moment: float32 [17, 1024], P(None, ('dp', 'mp'))
- agg_square: float32 [4, 1024, 1024], P(None, 'dp', 'mp')
- attn_square: float32 [4, 1024, 1024], P(None, 'dp', 'mp')
- mlp_square: float32 [2, 1024, 4096], P(None, 'dp', 'mp')
- head_square: float32 [1024, 192], P('dp', 'mp')
- embed_square: float32 [48, 5, 1024], P(None, None, ('dp', 'mp'))
- vector_square: float32 [17, 1024], P(None, ('dp', 'mp'))
- agg_new: float32 [4, 1024, 1024], P(None, 'dp', 'mp')
- attn_new: float32 [4, 1024, 1024], P(None, 'dp', 'mp')
- mlp_new: float32 [2, 1024, 4096], P(None, 'dp', 'mp')
- head_new: float32 [1024, 192], P('dp', 'mp')
- embed_new: float32 [48, 5, 1024], P(None, None, ('dp', 'mp'))
- vector_new: float32 [17, 1024], P(None, ('dp', 'mp'))
The draws below stay inside these ranges and needn't reach their ends.
Inputs may be any that keep to these rules, and one draw needn't show every extreme that they name: `valid_mask`: 1 marks a valid pixel. `agg_weight`: projection weights. `attn_weight`: projection weights. `mlp_weight`: projection weights. `vectors`: gains near one, other rows of both signs. `agg_first`: first moments of both signs. `attn_first`: first moments of both signs. `mlp_first`: first moments of both signs. `head_first`: first moments of both signs. `embed_first`: first moments of both signs. `vector_first`: first moments of both signs. `agg_second`: positive second moments. `attn_second`: positive second moments. `mlp_second`: positive second moments. `head_second`: positive second moments. `embed_second`: positive second moments. `vector_second`: positive second moments.
All inputs are finite; a program needn't handle non-finite values.
Results may differ from the reference program's by a relative error of at most 0.019.
Values may be sent and summed in bfloat16 or wider, within the bound.
A program may use at most 192 MiB of HBM per device.

```python
import math
import jax
import jax.numpy as jnp
import numpy as np
from jax import lax

D = 1024
HEADS = 16
HEAD_DIM = 64
FF = 4096
NVAR = 48
P_SIZE = 4
TOK_DEV = 256
SEGS = 4
LEADS = 28
LATS = 32
STEP = 10
ROWS = 32
TOKENS = 8192
NVEC = 17


def first_moment(key, shape, level):
    typical = level * lax.rsqrt(jnp.float32(TOKENS))
    return 0.11 * typical * jax.random.normal(key, shape, jnp.float32)


def second_moment(key, shape, level):
    typical = level * lax.rsqrt(jnp.float32(TOKENS))
    factor = jnp.exp(jax.random.uniform(key, shape, jnp.float32, 0.6931472, 2.0794415))
    return 0.001 * factor * typical * typical


def projection_stack(key):
    base = jax.random.normal(key, (4, D, D), jnp.float32) * D ** (-0.5)
    scales = jnp.array([1.0, 1.0, 1.0, 4.0], jnp.float32)
    return base * scales[:, None, None]


def draw_valid_mask(key, part):
    key = jax.random.fold_in(key, 3)
    row_index = jnp.arange(TOKENS, dtype=jnp.int32) // TOK_DEV
    row_total = TOKENS // TOK_DEV
    level = 300 + 600 * row_index // max(row_total - 1, 1)
    picks = jax.random.randint(key, (TOKENS, P_SIZE), 0, 1000)
    return (picks < level[:, None]).astype(jnp.int32)


def draw_agg_weight(key, part):
    key = jax.random.fold_in(key, 5)
    return projection_stack(key)


def draw_attn_weight(key, part):
    key = jax.random.fold_in(key, 6)
    return projection_stack(key)


def draw_mlp_weight(key, part):
    key = jax.random.fold_in(key, 7)
    base = jax.random.normal(key, (2, D, FF), jnp.float32)
    scales = jnp.array([D ** (-0.5), 2.0 * FF ** (-0.5)], jnp.float32)
    return base * scales[:, None, None]


def draw_vectors(key, part):
    key = jax.random.fold_in(key, 8)
    noise = jax.random.normal(key, (NVEC, D), jnp.float32)
    ramp = 0.6 + 1.2 * jnp.arange(D, dtype=jnp.float32) / (D - 1)
    gains = ramp[None, :] * (1.0 + 0.1 * noise)
    row_index = jnp.arange(NVEC)[:, None]
    is_gain = (row_index == 3) | (row_index == 8) | (row_index == NVEC - 2)
    strong = (row_index == 0) | (row_index == 2)
    others = jnp.where(strong, 1.0, 0.3) * noise
    return jnp.where(is_gain, gains, others)


def draw_agg_first(key, part):
    key = jax.random.fold_in(key, 11)
    return first_moment(key, (4, D, D), 0.008)


def draw_attn_first(key, part):
    key = jax.random.fold_in(key, 12)
    return first_moment(key, (4, D, D), 0.07)


def draw_mlp_first(key, part):
    key = jax.random.fold_in(key, 13)
    return first_moment(key, (2, D, FF), 0.003)


def draw_head_first(key, part):
    key = jax.random.fold_in(key, 14)
    return first_moment(key, (D, NVAR * P_SIZE), 0.14)


def draw_embed_first(key, part):
    key = jax.random.fold_in(key, 15)
    return first_moment(key, (NVAR, P_SIZE + 1, D), 0.009)


def draw_vector_first(key, part):
    key = jax.random.fold_in(key, 16)
    return first_moment(key, (NVEC, D), 0.01)


def draw_agg_second(key, part):
    key = jax.random.fold_in(key, 21)
    return second_moment(key, (4, D, D), 0.008)


def draw_attn_second(key, part):
    key = jax.random.fold_in(key, 22)
    return second_moment(key, (4, D, D), 0.07)


def draw_mlp_second(key, part):
    key = jax.random.fold_in(key, 23)
    return second_moment(key, (2, D, FF), 0.003)


def draw_head_second(key, part):
    key = jax.random.fold_in(key, 24)
    return second_moment(key, (D, NVAR * P_SIZE), 0.14)


def draw_embed_second(key, part):
    key = jax.random.fold_in(key, 25)
    return second_moment(key, (NVAR, P_SIZE + 1, D), 0.009)


def draw_vector_second(key, part):
    key = jax.random.fold_in(key, 26)
    return second_moment(key, (NVEC, D), 0.01)


def with_ends(result, key, least, top_value):
    extent = result.shape
    place = [jax.random.randint(jax.random.fold_in(key, axis), (), 0, extent[axis]) for axis in range(len(extent))]
    result = result.at[tuple(place)].set(least)
    longest = extent.index(max(extent))
    place[longest] = (place[longest] + 1) % extent[longest]
    return result.at[tuple(place)].set(top_value)


def block_levels(rng, dims, split, smallest, largest):
    gain, own = 1.0, jax.random.fold_in(rng, 6)
    for axis_at, shards_of in split:
        heights = jnp.exp(jax.random.uniform(jax.random.fold_in(own, axis_at), (shards_of,), jnp.float32, smallest / len(split), largest / len(split)))
        gain = gain * jnp.repeat(heights, dims[axis_at] // shards_of).reshape([-1 if axis == axis_at else 1 for axis in range(len(dims))])
    return gain


def length_profile(number_of, total, limit, lean):
    portions = [(1 << 20) // math.isqrt(grade ** lean) + 1 for grade in range(2, number_of + 1)]
    spare, given = total - limit - (number_of - 1), [1] * (number_of - 1)
    while spare > 0:
        free = [i for i in range(number_of - 1) if given[i] < limit]
        mass, budget = sum([portions[i] for i in free]), spare
        for i in free:
            extra = min(limit - given[i], max(1, budget * portions[i] // mass), spare)
            given[i] = given[i] + extra
            spare = spare - extra
    return np.array([limit] + given)


def uneven(own_key, amount, total, reach, lean):
    if amount == 2:
        one = jax.random.randint(own_key, (), max(1, total - reach), min(reach, total - 1) + 1)
        return jnp.stack([one, total - one])
    lengths = jnp.asarray(length_profile(amount, total, reach, lean), jnp.int32)
    twos = (amount - 1) // 2
    source_of, taker = lengths[1:1 + 2 * twos:2], lengths[2:2 + 2 * twos:2]
    room = jnp.minimum(source_of - 1, reach - taker)
    passed = jax.random.randint(jax.random.fold_in(own_key, 1), (twos,), 0, 1 << 20) % (room + 1)
    lengths = lengths.at[1:1 + 2 * twos:2].set(source_of - passed).at[2:2 + 2 * twos:2].set(taker + passed)
    return lengths[jax.random.permutation(jax.random.fold_in(own_key, 2), amount)]


def gaussian(rng, shape, scale, most, cuts=(), kind=jnp.bfloat16):
    drawn = jax.random.normal(rng, shape, jnp.float32) * scale
    if len(cuts) > 0:
        drawn = block_levels(rng, shape, cuts, -0.22, 0.18) * drawn
    return jnp.clip(drawn, min=-most, max=most).astype(kind)


def setup_inputs(seed: int = 0) -> dict:
    key_of = jax.random.split(jax.random.key(seed), 27)
    return {
        "pixels": gaussian(key_of[0], (TOKENS, NVAR * P_SIZE), 1.0, 6.0, ((0, 32),)),
        "targets": gaussian(key_of[1], (TOKENS, NVAR * P_SIZE), 1.0, 6.0, ((0, 32), (1, 4)), jnp.float32),
        "valid_mask": draw_valid_mask(jax.random.fold_in(key_of[26], 71), 0),
        "segments": jax.vmap(lambda own: jnp.searchsorted(jnp.cumsum(uneven(own, SEGS, TOK_DEV, TOK_DEV // 2, 2)), jnp.arange(TOK_DEV), side="right"))(jax.random.split(key_of[3], ROWS)).reshape((ROWS, TOK_DEV)).astype(jnp.int32),
        "lead_index": with_ends(jax.random.randint(key_of[4], (ROWS, SEGS), 0, LEADS), jax.random.fold_in(key_of[4], 1), 0, LEADS - 1).astype(jnp.int32),
        "latitude": with_ends(jax.random.randint(key_of[5], (TOKENS,), 0, LATS), jax.random.fold_in(key_of[5], 1), 0, LATS - 1).astype(jnp.int32),
        "var_ids": jax.random.permutation(key_of[6], NVAR).astype(jnp.int32),
        "running_error": jnp.clip(jnp.exp(jax.random.uniform(key_of[7], (NVAR,), jnp.float32, math.log(0.5), math.log(2.0))), 0.5, 2.0),
        "agg_weight": draw_agg_weight(jax.random.fold_in(key_of[26], 71), 0),
        "attn_weight": draw_attn_weight(jax.random.fold_in(key_of[26], 71), 0),
        "mlp_weight": draw_mlp_weight(jax.random.fold_in(key_of[26], 71), 0),
        "head_weight": gaussian(key_of[11], (D, NVAR * P_SIZE), D ** -0.5, 0.1875, ((0, 32), (1, 4)), jnp.float32),
        "embed_weight": gaussian(key_of[12], (NVAR, P_SIZE + 1, D), 0.5, 3.0, ((2, 128),), jnp.float32),
        "vectors": draw_vectors(jax.random.fold_in(key_of[26], 71), 0),
        "agg_first": draw_agg_first(jax.random.fold_in(key_of[26], 71), 0),
        "attn_first": draw_attn_first(jax.random.fold_in(key_of[26], 71), 0),
        "mlp_first": draw_mlp_first(jax.random.fold_in(key_of[26], 71), 0),
        "head_first": draw_head_first(jax.random.fold_in(key_of[26], 71), 0),
        "embed_first": draw_embed_first(jax.random.fold_in(key_of[26], 71), 0),
        "vector_first": draw_vector_first(jax.random.fold_in(key_of[26], 71), 0),
        "agg_second": draw_agg_second(jax.random.fold_in(key_of[26], 71), 0),
        "attn_second": draw_attn_second(jax.random.fold_in(key_of[26], 71), 0),
        "mlp_second": draw_mlp_second(jax.random.fold_in(key_of[26], 71), 0),
        "head_second": draw_head_second(jax.random.fold_in(key_of[26], 71), 0),
        "embed_second": draw_embed_second(jax.random.fold_in(key_of[26], 71), 0),
        "vector_second": draw_vector_second(jax.random.fold_in(key_of[26], 71), 0),
    }


HIGH = lax.Precision.HIGHEST
NORM_EPS = 1e-06
BETA_ONE = 0.9
BETA_TWO = 0.999
LEARN_RATE = 0.3
WEIGHT_DECAY = 0.01
ADAM_EPS = 1e-08
STATS_DECAY = 0.9

@jax.custom_vjp
def low(v):
    return lax.optimization_barrier(v.astype(jnp.bfloat16)).astype(jnp.float32)

@jax.custom_vjp
def low_back(v):
    return v

def low_keep(v):
    return (low(v), None)

def low_pass(kept, grad):
    return (grad,)

def back_keep(v):
    return (v, None)

def back_low(kept, grad):
    return (low(grad),)
low.defvjp(low_keep, low_pass)
low_back.defvjp(back_keep, back_low)

def layer_norm(values, gain_row, bias_row):
    centre = lax.optimization_barrier(jnp.mean(values, -1, keepdims=True))
    shifted = values - centre
    spread = lax.optimization_barrier(jnp.mean(shifted * shifted, -1, keepdims=True))
    return shifted * lax.rsqrt(spread + NORM_EPS) * gain_row + bias_row

def latitude_weights():
    centres = (jnp.arange(LATS, dtype=jnp.float32) + 0.5) * (180.0 / LATS) - 90.0
    cosines = jnp.cos(centres * (math.pi / 180.0))
    return cosines / jnp.mean(cosines)

def adam_direction(weight, gradient, first, second):
    first_new = BETA_ONE * first + (1.0 - BETA_ONE) * gradient
    second_new = BETA_TWO * second + (1.0 - BETA_TWO) * gradient * gradient
    first_hat = first_new / (1.0 - BETA_ONE ** STEP)
    second_hat = second_new / (1.0 - BETA_TWO ** STEP)
    direction = first_hat / (jnp.sqrt(second_hat) + ADAM_EPS) + WEIGHT_DECAY * weight
    return (first_new, second_new, direction)

def tensor_squares(values, axes_set):
    if axes_set is None:
        return jnp.sum(values * values)[None]
    return lax.optimization_barrier(jnp.sum(values * values, axis=axes_set))

def apply_trust(weights, stepped, trust_ratios, axes_list):
    results = []
    offset = 0
    for weight, stepped_item, axes_set in zip(weights, stepped, axes_list):
        if axes_set is None:
            part_trust = trust_ratios[offset]
            offset += 1
        else:
            number = weight.shape[0]
            part_trust = trust_ratios[offset:offset + number].reshape((number,) + (1,) * len(axes_set))
            offset += number
        results.append(weight - LEARN_RATE * part_trust * stepped_item[2])
    return results

def matmul(left, right):
    return jnp.dot(left, right, precision=HIGH)

def reference(pixels, targets, valid_mask, segments, lead_index, latitude, var_ids, running_error, agg_weight, attn_weight, mlp_weight, head_weight, embed_weight, vectors, agg_first, attn_first, mlp_first, head_first, embed_first, vector_first, agg_second, attn_second, mlp_second, head_second, embed_second, vector_second):
    scale = 1.0 / math.sqrt(HEAD_DIM)
    ratio = FF // D
    pixel_rows = pixels.astype(jnp.float32).reshape(ROWS, TOK_DEV, NVAR, P_SIZE)
    target_rows = targets.reshape(ROWS, TOK_DEV, NVAR, P_SIZE)
    keep_rows = valid_mask.astype(jnp.float32).reshape(ROWS, TOK_DEV, 1, P_SIZE)
    lat_rows = latitude_weights()[latitude].reshape(ROWS, TOK_DEV)
    lead_rows = (jnp.take_along_axis(lead_index, segments, 1) + 1).astype(jnp.float32) / LEADS

    def loss_fn(params):
        agg_p, attn_p, mlp_p, head_p, embed_p, vector_p = params
        agg_w = low(agg_p)
        attn_w = low(attn_p)
        mlp_w = low(mlp_p)
        head_w = low(head_p)
        chosen = embed_p[var_ids]
        query_a = low(matmul(vector_p[0], agg_w[0])).reshape(HEADS, HEAD_DIM)

        def one_row(row_data):
            pixel_row, target_row, keep_row, lat_row, lead_row, segment_row = row_data
            tokens_v = low(jnp.einsum('tcp,cpd->tcd', pixel_row, chosen[:, :P_SIZE], precision=HIGH) + chosen[:, P_SIZE][None])
            flat_v = tokens_v.reshape(TOK_DEV * NVAR, D)
            keys_a = low_back(low(matmul(flat_v, agg_w[1]))).reshape(TOK_DEV, NVAR, HEADS, HEAD_DIM)
            vals_a = low_back(low(matmul(flat_v, agg_w[2]))).reshape(TOK_DEV, NVAR, HEADS, HEAD_DIM)
            scores_a = low_back(jnp.einsum('tchd,hd->thc', keys_a, query_a, precision=HIGH) * scale)
            weights_a = low(jax.nn.softmax(scores_a, -1))
            mixed_a = low_back(low(jnp.einsum('thc,tchd->thd', weights_a, vals_a, precision=HIGH))).reshape(TOK_DEV, D)
            stream = low_back(jnp.einsum('td,ed->te', mixed_a, agg_w[3], precision=HIGH)) + vector_p[1] + lead_row[:, None] * vector_p[2]
            normed = low(layer_norm(stream, vector_p[3], vector_p[4]))
            projected = jnp.einsum('td,kde->kte', normed, attn_w[:3], precision=HIGH)
            queries = low_back(low(projected[0] + vector_p[5])).reshape(TOK_DEV, HEADS, HEAD_DIM)
            key_rows = low_back(low(projected[1])).reshape(TOK_DEV, HEADS, HEAD_DIM)
            value_rows = low_back(low(projected[2] + vector_p[6])).reshape(TOK_DEV, HEADS, HEAD_DIM)
            raw_scores = low_back(jnp.einsum('thd,uhd->htu', queries, key_rows, precision=HIGH) * scale)
            same_crop = segment_row[:, None] == segment_row[None, :]
            masked = jnp.where(same_crop[None], raw_scores, -1e+30)
            weights_b = low(jax.nn.softmax(masked, -1))
            mixture = low_back(low(jnp.einsum('htu,uhd->thd', weights_b, value_rows, precision=HIGH))).reshape(TOK_DEV, D)
            stream = stream + low_back(jnp.einsum('td,ed->te', mixture, attn_w[3], precision=HIGH)) + vector_p[7]
            normed = low(layer_norm(stream, vector_p[8], vector_p[9]))
            inner = low_back(matmul(normed, mlp_w[0]) + vector_p[10:10 + ratio].reshape(FF))
            hidden = low(jax.nn.gelu(inner, approximate=False))
            stream = stream + low_back(jnp.einsum('tf,ef->te', hidden, mlp_w[1], precision=HIGH)) + vector_p[10 + ratio]
            normed = low(layer_norm(stream, vector_p[11 + ratio], vector_p[12 + ratio]))
            predicted = low_back(matmul(normed, head_w)).reshape(TOK_DEV, NVAR, P_SIZE)
            misfit = predicted - target_row
            return lax.optimization_barrier(jnp.sum(lat_row[:, None, None] * keep_row * misfit * misfit, axis=(0, 2)))
        per_row = lax.map(jax.checkpoint(one_row), (pixel_rows, target_rows, keep_rows, lat_rows, lead_rows, segments))
        totals = lax.optimization_barrier(jnp.sum(per_row, 0))
        return (jnp.sum(totals), totals)
    params = (agg_weight, attn_weight, mlp_weight, head_weight, embed_weight, vectors)
    loss_sum, pullback, totals = jax.vjp(loss_fn, params, has_aux=True)
    valid_count = NVAR * jnp.sum(valid_mask.astype(jnp.float32))
    grads = pullback(jnp.ones_like(loss_sum) / valid_count)[0]
    running_out = STATS_DECAY * running_error + (1.0 - STATS_DECAY) * totals * (NVAR / valid_count)
    firsts = (agg_first, attn_first, mlp_first, head_first, embed_first, vector_first)
    seconds = (agg_second, attn_second, mlp_second, head_second, embed_second, vector_second)
    axes_list = ((1, 2), (1, 2), (1, 2), None, None, (1,))
    stepped = [adam_direction(w, g, m, s) for w, g, m, s in zip(params, grads, firsts, seconds)]
    weight_sq = jnp.concatenate([tensor_squares(w, a) for w, a in zip(params, axes_list)])
    update_sq = jnp.concatenate([tensor_squares(item[2], a) for item, a in zip(stepped, axes_list)])
    weight_norms = jnp.sqrt(weight_sq)
    trust_ratios = weight_norms / jnp.sqrt(update_sq)
    news = apply_trust(params, stepped, trust_ratios, axes_list)
    return (loss_sum, valid_count, running_out, trust_ratios, weight_norms, stepped[0][0], stepped[1][0], stepped[2][0], stepped[3][0], stepped[4][0], stepped[5][0], stepped[0][1], stepped[1][1], stepped[2][1], stepped[3][1], stepped[4][1], stepped[5][1], news[0], news[1], news[2], news[3], news[4], news[5])
```

```python
import math

import jax
import jax.numpy as jnp
from jax import lax
from jax.experimental import pallas as pl
from jax.experimental.pallas import tpu as pltpu
from jax.sharding import PartitionSpec as P

D = 1024
HEAD_DIM = 64
FF = 4096
NVAR = 48
P_SIZE = 4
SEGS = 4
LEADS = 28
LATS = 32
STEP = 10
NVEC = 17
EROWS = NVAR * (P_SIZE + 1)

HIGH = lax.Precision.HIGHEST
NORM_EPS = 1e-06
BETA_ONE = 0.9
BETA_TWO = 0.999
LEARN_RATE = 0.3
WEIGHT_DECAY = 0.01
ADAM_EPS = 1e-08
STATS_DECAY = 0.9
MESH = pl.DeviceIdType.MESH
BF = jnp.bfloat16
F32 = jnp.float32

DPN, MPN, CHIPS, SH, TOK, COLS = 32, 4, 16, 64, 256, 256
SCALE = 1.0 / math.sqrt(HEAD_DIM)


def nn(a, b, precision=None):
    return lax.dot_general(
        a, b, (((1,), (0,)), ((), ())), preferred_element_type=F32, precision=precision
    )


def nt(a, b, precision=None):
    return lax.dot_general(
        a, b, (((1,), (1,)), ((), ())), preferred_element_type=F32, precision=precision
    )


def tn(a, b, precision=None):
    return lax.dot_general(
        a, b, (((0,), (0,)), ((), ())), preferred_element_type=F32, precision=precision
    )


def latitude_weights():
    centres = (jnp.arange(LATS, dtype=F32) + 0.5) * (180.0 / LATS) - 90.0
    cosines = jnp.cos(centres * (math.pi / 180.0))
    return cosines / jnp.mean(cosines)


def moments_new(gradient, first, second):
    first_new = BETA_ONE * first + (1.0 - BETA_ONE) * gradient
    second_new = BETA_TWO * second + (1.0 - BETA_TWO) * gradient * gradient
    return first_new, second_new


def adam_direction(weight, gradient, first, second):
    first_new, second_new = moments_new(gradient, first, second)
    first_hat = first_new * (1.0 / (1.0 - BETA_ONE**STEP))
    second_hat = second_new * (1.0 / (1.0 - BETA_TWO**STEP))
    direction = first_hat / (jnp.sqrt(second_hat) + ADAM_EPS) + WEIGHT_DECAY * weight
    return (first_new, second_new, direction)


def iota(shape, dim):
    return lax.broadcasted_iota(jnp.int32, shape, dim)


def ln_parts(x):
    centre = jnp.mean(x, -1, keepdims=True)
    shifted = x - centre
    r = lax.rsqrt(jnp.mean(shifted * shifted, -1, keepdims=True) + NORM_EPS)
    return shifted * r, r


def ln_back(n, r, gain, dh):
    e = dh * gain
    dx = r * (e - jnp.mean(e, -1, keepdims=True) - n * jnp.mean(e * n, -1, keepdims=True))
    dgain = jnp.sum(dh * n, 0, keepdims=True)
    dbias = jnp.sum(dh, 0, keepdims=True)
    return dx, dgain, dbias


def mega(
    tm,
    aggw,
    attnw,
    mlpw,
    headw,
    tfirst,
    tsecond,
    aggf,
    aggs,
    attnf,
    attns,
    mlpf,
    mlps,
    headf,
    heads,
    targ,
    lossw,
    cnt,
    lead,
    segc,
    segr,
    vidx,
    pix,
    o_t,
    o_agg,
    o_attn,
    o_mlp,
    o_head,
    o_stats,
    WA3,
    WB,
    W1,
    W2,
    HW,
    VEC,
    VR,
    VRN,
    TMPV,
    TA,
    TGT,
    PIXT,
    EWP,
    EWH,
    EWC,
    EWR,
    PRP,
    PRH,
    PRC,
    PRR,
    MT,
    PT,
    OAT,
    OA,
    RSS,
    RSR,
    AG,
    QKV,
    PB,
    OB,
    DOB,
    GEL,
    GELP,
    DU,
    LN,
    XS,
    RR,
    GA3,
    GB,
    G1,
    G2,
    GH,
    GVT,
    GVP,
    GVN,
    SA3,
    SB,
    S1,
    S2,
    SHH,
    SV,
    BA3,
    BB,
    B1,
    B2,
    BH,
    BV,
    TG,
    TGR,
    HG,
    HGR,
    NX,
    NXR,
    NY,
    NYR,
    ysend,
    yrecv,
    dsend,
    drecv,
    ssend,
    srecv,
):
    d = lax.axis_index("dp")
    m = lax.axis_index("mp")
    c = lax.rem(d, 2)
    k = d // 2
    sib = d + 1 - 2 * c
    rb = pl.multiple_of(c * 512 + k * 32, 32)
    half = pl.multiple_of(c * 512, 512)
    other = pl.multiple_of(512 - c * 512, 512)
    mine = pl.multiple_of(m * SH, SH)

    def rcopy(src, dst, ss, rs, dp, mp):
        return pltpu.make_async_remote_copy(
            src_ref=src,
            dst_ref=dst,
            send_sem=ss,
            recv_sem=rs,
            device_id={"dp": dp, "mp": mp},
            device_id_type=MESH,
        )

    def drain(ref, sem):
        pltpu.make_async_copy(ref, ref, sem).wait()

    def to_peers(fn):
        for i in (2, 1, 3):
            fn(i, lax.rem(m + i, MPN))

    def to_chips(fn):
        def step(i, carry):
            kk = lax.rem(k + i, CHIPS)
            fn(kk, kk * 2 + c)
            return carry

        lax.fori_loop(1, CHIPS, step, 0)

    def gather_start(buf, g):
        block = buf.at[pl.ds(rb, 32)]
        to_chips(lambda kk, t: rcopy(block, block, dsend.at[g], drecv.at[g], t, m).start())

    def gather_cross(buf, g):
        drain(buf.at[pl.ds(0, 480)], drecv.at[g])
        part = buf.at[pl.ds(half, 512)]
        rcopy(part, part, ssend.at[g], srecv.at[g], sib, m).start()

    def gather_wait(buf, g):
        drain(buf.at[pl.ds(0, 512)], srecv.at[g])

    def gather_end(buf, g):
        drain(buf.at[pl.ds(0, 480)], dsend.at[g])
        drain(buf.at[pl.ds(0, 512)], ssend.at[g])

    def reduce_cross(buf, sbuf, g):
        rcopy(buf.at[pl.ds(other, 512)], sbuf, ssend.at[g], srecv.at[g], sib, m).start()

    def reduce_spread(buf, sbuf, bbuf, g):
        drain(sbuf, srecv.at[g])

        def add(i, carry):
            at = pl.multiple_of(i * 128, 128)
            sbuf[pl.ds(at, 128), :] = (
                sbuf[pl.ds(at, 128), :].astype(F32)
                + buf[pl.ds(pl.multiple_of(half + at, 128), 128), :].astype(F32)
            ).astype(sbuf.dtype)
            return carry

        lax.fori_loop(0, 4, add, 0)
        land = bbuf.at[pl.ds(pl.multiple_of(k * 32, 32), 32)]

        def send(kk, t):
            src = sbuf.at[pl.ds(pl.multiple_of(kk * 32, 32), 32)]
            rcopy(src, land, dsend.at[g], drecv.at[g], t, m).start()

        to_chips(send)

    def reduce_end(buf, sbuf, bbuf, g):
        drain(bbuf.at[pl.ds(0, 480)], drecv.at[g])

        def add(i, acc):
            at = pl.multiple_of(lax.rem(k + i, CHIPS) * 32, 32)
            return acc + bbuf[pl.ds(at, 32), :].astype(F32)

        total = lax.fori_loop(
            1, CHIPS, add, sbuf[pl.ds(pl.multiple_of(k * 32, 32), 32), :].astype(F32)
        )
        drain(bbuf.at[pl.ds(0, 480)], dsend.at[g])
        drain(sbuf, ssend.at[g])
        return total

    def all_sum(src, hbuf, cbuf, res, g, between):
        mine_half = pl.multiple_of(c * 128, 128)
        rcopy(
            src.at[pl.ds(pl.multiple_of(128 - c * 128, 128), 128)],
            hbuf,
            ssend.at[g],
            srecv.at[g],
            sib,
            m,
        ).start()
        drain(hbuf, srecv.at[g])
        hbuf[...] = hbuf[...] + src[pl.ds(mine_half, 128), :]
        at_k = pl.multiple_of(k * 8, 8)

        def send(kk, t):
            rcopy(
                hbuf.at[pl.ds(pl.multiple_of(kk * 8, 8), 8)],
                cbuf.at[pl.ds(at_k, 8)],
                dsend.at[g],
                drecv.at[g],
                t,
                m,
            ).start()

        to_chips(send)
        drain(cbuf.at[pl.ds(0, 120)], drecv.at[g])

        def add(i, acc):
            at = pl.multiple_of(lax.rem(k + i, CHIPS) * 8, 8)
            return acc + cbuf[pl.ds(at, 8), :]

        total = lax.fori_loop(1, CHIPS, add, hbuf[pl.ds(at_k, 8), :])
        block = pl.ds(pl.multiple_of(mine_half + at_k, 8), 8)
        res[block, :] = total
        part = res.at[block]
        to_chips(lambda kk, t: rcopy(part, part, dsend.at[g + 1], drecv.at[g + 1], t, m).start())
        between()
        drain(res.at[pl.ds(0, 120)], drecv.at[g + 1])
        part2 = res.at[pl.ds(mine_half, 128)]
        rcopy(part2, part2, ssend.at[g + 1], srecv.at[g + 1], sib, m).start()
        drain(res.at[pl.ds(0, 128)], srecv.at[g + 1])
        drain(hbuf, ssend.at[g])
        drain(res.at[pl.ds(0, 128)], ssend.at[g + 1])
        drain(cbuf.at[pl.ds(0, 120)], dsend.at[g])
        drain(res.at[pl.ds(0, 120)], dsend.at[g + 1])

    def branch_start(ix, tile_fn):
        def step(n, carry):
            RSS[ix, n] = tile_fn(pl.multiple_of(n * 256, 256)).astype(BF)

            def send(i, t):
                rcopy(
                    RSS.at[ix, n, pl.ds(pl.multiple_of(t * SH, SH), SH)],
                    RSR.at[ix, i - 1, n],
                    ysend.at[3 + ix],
                    yrecv.at[3 + ix],
                    d,
                    t,
                ).start()

            to_peers(send)
            return carry

        lax.fori_loop(0, 4, step, 0)

    def branch_sum(ix):
        drain(RSR.at[ix], yrecv.at[3 + ix])
        parts = []
        for n in range(4):
            acc = RSS[ix, n, pl.ds(mine, SH), :].astype(F32)
            for i in range(3):
                acc = acc + RSR[ix, i, n].astype(F32)
            parts.append(acc)
        return jnp.concatenate(parts, 1)

    def share_start(ix, values):
        AG[ix, pl.ds(mine, SH), :] = values
        block = AG.at[ix, pl.ds(mine, SH)]
        to_peers(
            lambda i, t: rcopy(block, block, ysend.at[8 + ix], yrecv.at[8 + ix], d, t).start()
        )

    def share_wait(ix):
        drain(AG.at[ix, pl.ds(0, 192)], yrecv.at[8 + ix])

    aw = [aggw[j].astype(BF) for j in range(3)]
    WA3[pl.ds(rb, 32), :] = aggw[3].astype(BF)
    for j in range(4):
        WB[pl.ds(rb, 32), j * 256 : (j + 1) * 256] = attnw[j].astype(BF)
    W1[pl.ds(rb, 32), :] = mlpw[0].astype(BF)
    W2[pl.ds(rb, 32), :] = mlpw[1].astype(BF)
    my_slot = pl.ds(pl.multiple_of(m * 128, 128), 128)
    HW[pl.ds(rb, 32), my_slot] = headw[...].astype(BF)
    vhot = (iota((256, 256), 0) == vidx[...]).astype(F32)
    my_eight = pl.ds(pl.multiple_of(m * 8, 8), 8)
    TA[my_eight, 0:256] = nn(tm[:, 0:256], vhot, HIGH)
    TA[my_eight, 256:384] = tm[:, 256:384]
    TGT[m] = targ[pl.ds(mine, SH), :]
    GVP[...] = jnp.zeros_like(GVP)
    GVN[...] = jnp.zeros_like(GVN)

    bar = pltpu.get_barrier_semaphore()

    def greet(i, carry):
        pl.semaphore_signal(
            bar, inc=1, device_id={"dp": lax.rem(d + i, DPN), "mp": m}, device_id_type=MESH
        )
        return carry

    lax.fori_loop(1, DPN, greet, 0)
    for i in range(1, MPN):
        pl.semaphore_signal(
            bar, inc=1, device_id={"dp": d, "mp": lax.rem(m + i, MPN)}, device_id_type=MESH
        )
    pl.semaphore_wait(bar, DPN + MPN - 2)

    def first_sends(i, t):
        part = TA.at[my_eight]
        rcopy(part, part, ysend.at[0], yrecv.at[0], d, t).start()
        slot = HW.at[pl.ds(rb, 32), my_slot]
        rcopy(slot, slot, ysend.at[1], yrecv.at[1], d, t).start()
        rcopy(
            targ.at[pl.ds(pl.multiple_of(t * SH, SH), SH)],
            TGT.at[m],
            ysend.at[2],
            yrecv.at[2],
            d,
            t,
        ).start()

    to_peers(first_sends)
    gather_start(WA3, 0)

    rows = iota((256, 192), 0)
    cols = iota((256, 192), 1)
    pick = (rows < 192) & ((lax.rem(rows, NVAR) * P_SIZE + rows // NVAR) == cols)
    pixt = nt(pick.astype(BF), pix[...])
    row_at = iota((256, TOK), 0)
    PIXT[...] = jnp.where(row_at < 192, pixt, jnp.where(row_at < EROWS, 1.0, 0.0))

    drain(TA.at[pl.ds(0, 24)], yrecv.at[0])
    drain(HW.at[pl.ds(0, 32), pl.ds(0, 384)], yrecv.at[1])
    VEC[pl.ds(rb, 32), :] = TA[:, 256:384]
    emb = TA[:, 0:256]
    EWP[:, 0:256] = tn(emb, aw[1].astype(F32), HIGH)
    EWP[:, 256:512] = tn(emb, aw[2].astype(F32), HIGH)
    EWP[240:241, 0:256] = jnp.sum(TA[:, 256:257] * aw[0].astype(F32), 0, keepdims=True)
    EWP[241:242, 0:128] = cnt[...]

    def bulk():
        gather_start(VEC, 2)
        gather_start(WB, 1)
        gather_start(W1, 3)
        gather_start(W2, 4)
        gather_start(HW, 5)

    all_sum(EWP, EWH, EWC, EWR, 6, bulk)

    head_of = (iota((256, 128), 0) // HEAD_DIM == iota((256, 128), 1)).astype(F32)
    qa = EWR[240:241, 0:256].astype(BF).astype(F32)
    total_count = EWR[241:242, 0:1]
    qe = nn(EWR[:, 0:256] * (qa * SCALE), head_of, HIGH)
    ewv = EWR[:, 256:512].astype(BF)
    for h in range(4):
        scores = PIXT[0:48, :] * qe[0:48, h : h + 1]
        for p in range(1, 5):
            at = slice(p * 48, (p + 1) * 48)
            scores = scores + PIXT[at, :] * qe[at, h : h + 1]
        e = jnp.exp(scores - jnp.max(scores, 0, keepdims=True))
        probs = e / jnp.sum(e, 0, keepdims=True)
        PT[h] = probs
        probs = probs.astype(BF).astype(F32)
        for p in range(5):
            at = slice(p * 48, (p + 1) * 48)
            MT[h, at, :] = (probs * PIXT[at, :]).astype(BF)
        MT[h, 240:256, :] = jnp.zeros((16, TOK), BF)
        OAT[h * 64 : (h + 1) * 64, :] = tn(ewv[:, h * 64 : (h + 1) * 64], MT[h])
    OA[...] = OAT[...].T.astype(BF)

    gather_cross(WA3, 0)
    gather_wait(WA3, 0)
    branch_start(0, lambda at: nt(OA[...], WA3[pl.ds(at, 256), :]))
    gather_cross(VEC, 2)
    gather_wait(VEC, 2)
    VR[...] = VEC[...].T

    def natural(i, carry):
        at = pl.multiple_of(lax.rem(i, 2) * 512 + (i // 2) * 32, 32)
        TMPV[pl.ds(pl.multiple_of(i * 32, 32), 32), :] = VEC[pl.ds(at, 32), :]
        return carry

    lax.fori_loop(0, DPN, natural, 0)
    VRN[...] = TMPV[...].T

    def vrow(i):
        return VR[i : i + 1, :]

    leads = lead[...]
    x0 = branch_sum(0) + vrow(1) + leads * vrow(2)
    n1, r1 = ln_parts(x0)
    LN[0] = n1
    RR[0] = jnp.broadcast_to(r1, (SH, 128))
    XS[...] = x0
    share_start(0, (n1 * vrow(3) + vrow(4)).astype(BF))
    gather_cross(WB, 1)
    gather_wait(WB, 1)
    share_wait(0)

    my_cols = pl.ds(pl.multiple_of(m * COLS, COLS), COLS)
    h1 = AG[0]
    QKV[0] = (nn(h1, WB[:, 0:256]) + VRN[5:6, my_cols]).astype(BF)
    QKV[1] = nn(h1, WB[:, 256:512]).astype(BF)
    QKV[2] = (nn(h1, WB[:, 512:768]) + VRN[6:7, my_cols]).astype(BF)
    same = segc[...] == segr[...]
    for h in range(4):
        at = slice(h * 64, (h + 1) * 64)
        scores = nt(QKV[0, :, at], QKV[1, :, at]) * SCALE
        scores = jnp.where(same, scores, -1e30)
        e = jnp.exp(scores - jnp.max(scores, 1, keepdims=True))
        probs = e / jnp.sum(e, 1, keepdims=True)
        PB[h] = probs
        OB[:, at] = nn(probs.astype(BF), QKV[2, :, at]).astype(BF)
    branch_start(1, lambda at: nt(OB[...], WB[pl.ds(at, 256), 768:1024]))
    gather_cross(W1, 3)
    x1 = XS[...] + branch_sum(1) + vrow(7)
    n2, r2 = ln_parts(x1)
    LN[1] = n2
    RR[1] = jnp.broadcast_to(r2, (SH, 128))
    XS[...] = x1
    share_start(1, (n2 * vrow(8) + vrow(9)).astype(BF))
    gather_wait(W1, 3)
    share_wait(1)

    def inner(n, carry):
        at = pl.ds(pl.multiple_of(n * 256, 256), 256)
        u = nn(AG[1], W1[:, at]) + VRN[pl.ds(10 + m, 1), at]
        phi = 0.5 * (1.0 + lax.erf(u * (1.0 / math.sqrt(2.0))))
        GEL[:, at] = (u * phi).astype(BF)
        GELP[:, at] = phi + u * jnp.exp(-0.5 * u * u) * (1.0 / math.sqrt(2.0 * math.pi))
        return carry

    lax.fori_loop(0, 4, inner, 0)
    gather_cross(W2, 4)
    gather_wait(W2, 4)
    branch_start(2, lambda at: nt(GEL[...], W2[pl.ds(at, 256), :]))
    gather_cross(HW, 5)
    gather_wait(HW, 5)
    x2 = XS[...] + branch_sum(2) + vrow(14)
    n3, r3 = ln_parts(x2)
    h3 = (n3 * vrow(15) + vrow(16)).astype(BF)

    drain(TGT.at[pl.ds(0, 3)], yrecv.at[2])
    pred = nn(h3, HW[...])
    weight = lossw[...]
    dpreds = []
    NX[...] = jnp.zeros_like(NX)
    for j in range(4):
        misfit = pred[:, j * 128 : (j + 1) * 128] - TGT[j]
        weighted = weight * misfit
        NX[4 + j : 5 + j, :] = jnp.sum(weighted * misfit, 0, keepdims=True)
        dpreds.append((2.0 * weighted / total_count).astype(BF))
    dpred = jnp.concatenate(dpreds, 1)
    dh3 = nt(dpred, HW[...])
    dx2, dgain, dbias = ln_back(n3, r3, vrow(15), dh3)
    share_start(2, dx2.astype(BF))
    GVP[14:15, :] = jnp.sum(dx2, 0, keepdims=True)
    GVP[15:16, :] = dgain
    GVP[16:17, :] = dbias
    GH[...] = tn(h3, dpred).astype(BF)
    XS[...] = dx2
    reduce_cross(GH, SHH, 14)
    share_wait(2)

    def back_inner(n, carry):
        at = pl.ds(pl.multiple_of(n * 256, 256), 256)
        du = (nn(AG[2], W2[:, at]) * GELP[:, at]).astype(BF)
        DU[:, at] = du
        GVN[pl.ds(10 + m, 1), at] = jnp.sum(du.astype(F32), 0, keepdims=True)
        return carry

    lax.fori_loop(0, 4, back_inner, 0)
    branch_start(3, lambda at: nt(DU[...], W1[pl.ds(at, 256), :]))

    def weight_grad(dst, left_fn, right):
        def step(n, carry):
            at = pl.multiple_of(n * 256, 256)
            dst[pl.ds(at, 256), :] = tn(left_fn(pl.ds(at, 256)), right[...]).astype(BF)
            return carry

        lax.fori_loop(0, 4, step, 0)

    weight_grad(G2, lambda at: AG[2, :, at], GEL)
    reduce_cross(G2, S2, 13)
    reduce_spread(GH, SHH, BH, 14)
    dx1, dgain, dbias = ln_back(LN[1], RR[1, :, 0:1], vrow(8), branch_sum(3))
    dx1 = dx1 + XS[...]
    share_start(3, dx1.astype(BF))
    GVP[7:8, :] = jnp.sum(dx1, 0, keepdims=True)
    GVP[8:9, :] = dgain
    GVP[9:10, :] = dbias
    XS[...] = dx1
    reduce_spread(G2, S2, B2, 13)
    weight_grad(G1, lambda at: AG[1, :, at], DU)
    reduce_cross(G1, S1, 12)
    share_wait(3)

    DOB[...] = nn(AG[3], WB[:, 768:1024]).astype(BF)
    for h in range(4):
        at = slice(h * 64, (h + 1) * 64)
        probs = PB[h]
        dout = DOB[:, at]
        dv = tn(probs.astype(BF), dout).astype(BF)
        dprob = nt(dout, QKV[2, :, at])
        ds = (probs * (dprob - jnp.sum(probs * dprob, 1, keepdims=True))).astype(BF)
        dq = (nn(ds, QKV[1, :, at]) * SCALE).astype(BF)
        dk = (tn(ds, QKV[0, :, at]) * SCALE).astype(BF)
        DU[:, h * 64 : (h + 1) * 64] = dq
        DU[:, 256 + h * 64 : 256 + (h + 1) * 64] = dk
        DU[:, 512 + h * 64 : 512 + (h + 1) * 64] = dv
    branch_start(4, lambda at: nt(DU[:, 0:768], WB[pl.ds(at, 256), 0:768]))
    GVN[5:6, my_cols] = jnp.sum(DU[:, 0:256].astype(F32), 0, keepdims=True)
    GVN[6:7, my_cols] = jnp.sum(DU[:, 512:768].astype(F32), 0, keepdims=True)
    reduce_spread(G1, S1, B1, 12)

    def attn_grad(n, carry):
        at = pl.ds(pl.multiple_of(n * 256, 256), 256)
        GB[at, 0:768] = tn(AG[0, :, at], DU[:, 0:768]).astype(BF)
        GB[at, 768:1024] = tn(AG[3, :, at], OB[...]).astype(BF)
        return carry

    lax.fori_loop(0, 4, attn_grad, 0)
    reduce_cross(GB, SB, 11)
    dx0, dgain, dbias = ln_back(LN[0], RR[0, :, 0:1], vrow(3), branch_sum(4))
    dx0 = dx0 + XS[...]
    share_start(4, dx0.astype(BF))
    GVP[1:2, :] = jnp.sum(dx0, 0, keepdims=True)
    GVP[2:3, :] = jnp.sum(leads * dx0, 0, keepdims=True)
    GVP[3:4, :] = dgain
    GVP[4:5, :] = dbias
    TMPV[...] = GVN[...].T
    GVT[...] = GVP[...].T

    def permuted(i, carry):
        at = pl.ds(pl.multiple_of(lax.rem(i, 2) * 512 + (i // 2) * 32, 32), 32)
        GVT[at, :] = GVT[at, :] + TMPV[pl.ds(pl.multiple_of(i * 32, 32), 32), :]
        return carry

    lax.fori_loop(0, DPN, permuted, 0)
    reduce_cross(GVT, SV, 15)
    reduce_spread(GB, SB, BB, 11)
    reduce_spread(GVT, SV, BV, 15)
    share_wait(4)

    DOB[...] = nn(AG[4], WA3[...]).astype(BF)
    PRP[...] = jnp.zeros_like(PRP)
    for h in range(4):
        at = slice(h * 64, (h + 1) * 64)
        dout = DOB[:, at]
        through = nt(ewv[:, at], dout)
        dprob = PIXT[0:48, :] * through[0:48, :]
        for p in range(1, 5):
            row = slice(p * 48, (p + 1) * 48)
            dprob = dprob + PIXT[row, :] * through[row, :]
        probs = PT[h]
        ds = (probs * (dprob - jnp.sum(probs * dprob, 0, keepdims=True))).astype(BF).astype(F32)
        for p in range(5):
            row = slice(p * 48, (p + 1) * 48)
            PRP[row, 256 + h : 257 + h] = jnp.sum(ds * PIXT[row, :], 1, keepdims=True)
        PRP[:, at] = nn(MT[h], dout)

    def agg_grad():
        weight_grad(GA3, lambda at: AG[4, :, at], OA)
        reduce_cross(GA3, SA3, 10)
        reduce_spread(GA3, SA3, BA3, 10)

    all_sum(PRP, PRH, PRC, PRR, 8, agg_grad)

    spread = nt(PRR[:, 256:384], head_of, HIGH)
    dqa = jnp.sum(spread * EWR[:, 0:256], 0, keepdims=True) * SCALE
    pk = spread * (qa * SCALE)
    pv = PRR[:, 0:256]
    emb = TA[:, 0:256]
    wa = [aggw[j].astype(BF).astype(F32) for j in range(3)]
    TG[:, 0:256] = nt(wa[1], pk, HIGH) + nt(wa[2], pv, HIGH)
    TG[:, 256:384] = reduce_end(GVT, SV, BV, 15)
    TG[:, 256:257] = TG[:, 256:257] + jnp.sum(wa[0] * dqa, 1, keepdims=True)
    HG[...] = reduce_end(GH, SHH, BH, 14)

    def last_sends(i, t):
        rcopy(
            TG.at[pl.ds(pl.multiple_of(t * 8, 8), 8)],
            TGR.at[i - 1],
            ysend.at[13],
            yrecv.at[13],
            d,
            t,
        ).start()
        rcopy(
            HG.at[:, pl.ds(pl.multiple_of(t * 128, 128), 128)],
            HGR.at[i - 1],
            ysend.at[14],
            yrecv.at[14],
            d,
            t,
        ).start()

    to_peers(last_sends)

    lanes = iota((1, 128), 1)

    def square_sum(values):
        return jnp.sum(jnp.sum(values * values, 1, keepdims=True), 0, keepdims=True)

    wrow = jnp.zeros((1, 128), F32)
    urow = jnp.zeros((1, 128), F32)

    def tensor(index, weight, gradient, first, second):
        unused, unused2, direction = adam_direction(weight, gradient, first, second)
        here = lanes == index
        return (
            wrow + jnp.where(here, square_sum(weight), 0.0),
            urow + jnp.where(here, square_sum(direction), 0.0),
        )

    o_agg[0] = TA[:, 256:257] * dqa
    o_agg[1] = nn(emb, pk, HIGH)
    o_agg[2] = nn(emb, pv, HIGH)
    gsum = reduce_end(GB, SB, BB, 11)
    for j in range(4):
        o_attn[j] = gsum[:, j * 256 : (j + 1) * 256]
    o_mlp[0] = reduce_end(G1, S1, B1, 12)
    o_mlp[1] = reduce_end(G2, S2, B2, 13)
    o_agg[3] = reduce_end(GA3, SA3, BA3, 10)
    for j in range(4):
        wrow, urow = tensor(j, aggw[j], o_agg[j], aggf[j], aggs[j])
        wrow, urow = tensor(4 + j, attnw[j], o_attn[j], attnf[j], attns[j])
    for j in range(2):
        wrow, urow = tensor(8 + j, mlpw[j], o_mlp[j], mlpf[j], mlps[j])

    drain(HGR, yrecv.at[14])
    o_head[...] = HG[:, my_slot] + HGR[0] + HGR[1] + HGR[2]
    wrow, urow = tensor(10, headw[...], o_head[...], headf[...], heads[...])
    drain(TGR, yrecv.at[13])
    tgrad = TG[my_eight, :] + TGR[0] + TGR[1] + TGR[2]
    o_t[:, 0:256] = nt(tgrad[:, 0:256], vhot, HIGH)
    o_t[:, 256:384] = tgrad[:, 256:384]
    wrow, urow = tensor(
        11, tm[:, 0:256], o_t[:, 0:256], tfirst[:, 0:256], tsecond[:, 0:256]
    )
    vec_at = slice(256, 384)
    unused, unused2, direction = adam_direction(
        tm[:, vec_at], o_t[:, vec_at], tfirst[:, vec_at], tsecond[:, vec_at]
    )
    NX[0:1, :] = wrow
    NX[1:2, :] = urow
    NX[2:3, :] = jnp.sum(tm[:, vec_at] * tm[:, vec_at], 0, keepdims=True)
    NX[3:4, :] = jnp.sum(direction * direction, 0, keepdims=True)

    to_peers(lambda i, t: rcopy(NX, NXR.at[i - 1], ysend.at[15], yrecv.at[15], d, t).start())
    drain(NXR, yrecv.at[15])
    NY[...] = NX[...] + NXR[0] + NXR[1] + NXR[2]
    at_d = pl.ds(pl.multiple_of(d * 8, 8), 8)

    def norm_send(i, carry):
        t = lax.rem(d + i, DPN)
        rcopy(NY, NYR.at[at_d], dsend.at[16], drecv.at[16], t, m).start()
        return carry

    lax.fori_loop(1, DPN, norm_send, 0)
    drain(NYR.at[pl.ds(0, 248)], drecv.at[16])

    def norm_add(i, acc):
        at = pl.multiple_of(lax.rem(d + i, DPN) * 8, 8)
        return acc + NYR[pl.ds(at, 8), :]

    o_stats[...] = lax.fori_loop(1, DPN, norm_add, NY[...])
    o_stats[0:1, :] = jnp.where(lanes == 127, total_count, o_stats[0:1, :])

    for buf, g in ((WA3, 0), (WB, 1), (VEC, 2), (W1, 3), (W2, 4), (HW, 5)):
        gather_end(buf, g)
    drain(NYR.at[pl.ds(0, 248)], dsend.at[16])
    drain(TA.at[pl.ds(0, 24)], ysend.at[0])
    drain(HW.at[pl.ds(0, 32), pl.ds(0, 384)], ysend.at[1])
    drain(TGT.at[pl.ds(0, 3)], ysend.at[2])
    for ix in range(5):
        drain(RSR.at[ix], ysend.at[3 + ix])
        drain(AG.at[ix, pl.ds(0, 192)], ysend.at[8 + ix])
    drain(TGR, ysend.at[13])
    drain(HGR, ysend.at[14])
    drain(NXR, ysend.at[15])


def mega_call(inputs):
    vm = pltpu.VMEM
    dma = pltpu.SemaphoreType.DMA
    scratch = [
        vm((D, 256), BF),
        vm((D, 1024), BF),
        vm((D, 1024), BF),
        vm((D, 1024), BF),
        vm((D, 512), BF),
        vm((D, 128), F32),
        vm((128, D), F32),
        vm((128, D), F32),
        vm((D, 128), F32),
        vm((32, 384), F32),
        vm((4, SH, 128), F32),
        vm((256, TOK), F32),
        vm((256, 512), F32),
        vm((128, 512), F32),
        vm((128, 512), F32),
        vm((256, 512), F32),
        vm((256, 384), F32),
        vm((128, 384), F32),
        vm((128, 384), F32),
        vm((256, 384), F32),
        vm((4, 256, TOK), BF),
        vm((4, NVAR, TOK), F32),
        vm((256, TOK), F32),
        vm((TOK, 256), BF),
        vm((5, 4, TOK, 256), BF),
        vm((5, 3, 4, SH, 256), BF),
        vm((5, TOK, D), BF),
        vm((3, TOK, 256), BF),
        vm((4, TOK, TOK), F32),
        vm((TOK, 256), BF),
        vm((TOK, 256), BF),
        vm((TOK, 1024), BF),
        vm((TOK, 1024), F32),
        vm((TOK, 1024), BF),
        vm((2, SH, D), F32),
        vm((SH, D), F32),
        vm((2, SH, 128), F32),
        vm((D, 256), BF),
        vm((D, 1024), BF),
        vm((D, 1024), BF),
        vm((D, 1024), BF),
        vm((D, 512), BF),
        vm((D, 128), F32),
        vm((128, D), F32),
        vm((128, D), F32),
    ]
    for number in range(2):
        scratch += [
            vm((512, 256), BF),
            vm((512, 1024), BF),
            vm((512, 1024), BF),
            vm((512, 1024), BF),
            vm((512, 512), BF),
            vm((512, 128), F32),
        ]
    scratch += [
        vm((32, 384), F32),
        vm((3, 8, 384), F32),
        vm((32, 512), F32),
        vm((3, 32, 128), F32),
        vm((8, 128), F32),
        vm((3, 8, 128), F32),
        vm((8, 128), F32),
        vm((256, 128), F32),
        dma((16,)),
        dma((16,)),
        dma((17,)),
        dma((17,)),
        dma((16,)),
        dma((16,)),
    ]
    out_shape = (
        jax.ShapeDtypeStruct((8, 384), F32),
        jax.ShapeDtypeStruct((4, 32, 256), F32),
        jax.ShapeDtypeStruct((4, 32, 256), F32),
        jax.ShapeDtypeStruct((2, 32, 1024), F32),
        jax.ShapeDtypeStruct((32, 128), F32),
        jax.ShapeDtypeStruct((8, 128), F32),
    )
    return pl.pallas_call(
        mega,
        out_shape=out_shape,
        in_specs=[pl.BlockSpec(memory_space=pltpu.VMEM)] * len(inputs),
        out_specs=tuple(pl.BlockSpec(memory_space=pltpu.VMEM) for _ in out_shape),
        scratch_shapes=scratch,
        compiler_params=pltpu.CompilerParams(
            collective_id=0, has_side_effects=True, vmem_limit_bytes=60 * 2**20
        ),
        name="step",
    )(*inputs)


def to_table(embed, vecs):
    rows = embed.transpose(2, 1, 0).reshape(8, EROWS)
    return jnp.concatenate(
        [rows, jnp.zeros((8, 16), F32), vecs.T, jnp.zeros((8, 128 - NVEC), F32)], 1
    )


def wide(values):
    return jnp.pad(values, ((0, 0), (0, 128 - values.shape[1])))


def on_device(
    pixels,
    targets,
    valid_mask,
    segments,
    lead_index,
    latitude,
    var_ids,
    running_error,
    agg_weight,
    attn_weight,
    mlp_weight,
    head_weight,
    embed_weight,
    vectors,
    agg_first,
    attn_first,
    mlp_first,
    head_first,
    embed_first,
    vector_first,
    agg_second,
    attn_second,
    mlp_second,
    head_second,
    embed_second,
    vector_second,
):
    m = lax.axis_index("mp")
    keep = valid_mask.astype(F32)
    count = jnp.sum(keep) * NVAR
    keep_mine = lax.dynamic_slice_in_dim(keep, m * SH, SH, 0)
    lat_mine = lax.dynamic_slice_in_dim(latitude, m * SH, SH, 0)
    lat_hot = (lat_mine[:, None] == jnp.arange(LATS, dtype=jnp.int32)[None, :]).astype(F32)
    lat_w = jnp.sum(lat_hot * latitude_weights()[None, :], 1, keepdims=True)
    loss_weight = wide(jnp.tile(lat_w * keep_mine, (1, NVAR // 4)))
    seg = segments[0]
    seg_mine = lax.dynamic_slice_in_dim(seg, m * SH, SH, 0)
    crop_hot = (seg_mine[:, None] == jnp.arange(SEGS, dtype=jnp.int32)[None, :]).astype(F32)
    lead_values = (lead_index[0] + 1).astype(F32) / LEADS
    lead_mine = jnp.sum(crop_hot * lead_values[None, :], 1, keepdims=True)
    at = jnp.arange(256, dtype=jnp.int32)
    vidx = jnp.where(at < EROWS, at - at % NVAR + jnp.tile(var_ids, 6)[:256], at)[None, :]

    table = to_table(embed_weight, vectors)
    inputs = (
        table,
        agg_weight,
        attn_weight,
        mlp_weight,
        wide(head_weight),
        to_table(embed_first, vector_first),
        to_table(embed_second, vector_second),
        agg_first,
        agg_second,
        attn_first,
        attn_second,
        mlp_first,
        mlp_second,
        wide(head_first),
        wide(head_second),
        wide(targets),
        loss_weight,
        jnp.broadcast_to(count, (1, 128)),
        lead_mine,
        seg[:, None],
        seg[None, :],
        vidx,
        pixels,
    )
    g_table, g_agg, g_attn, g_mlp, g_head, stats = mega_call(inputs)

    g_embed = g_table[:, :EROWS].reshape(8, P_SIZE + 1, NVAR).transpose(2, 1, 0)
    g_vec = g_table[:, 256 : 256 + NVEC].T
    weight_norms = jnp.sqrt(jnp.concatenate([stats[0, :12], stats[2, :NVEC]]))
    trust = weight_norms / jnp.sqrt(jnp.concatenate([stats[1, :12], stats[3, :NVEC]]))
    error_all = jnp.sum(stats[4:8, : NVAR].reshape(4, 12, 4), -1).reshape(NVAR)
    total_count = stats[0, 127]

    def finish(weight, gradient, first, second, ratio):
        f, s, u = adam_direction(weight, gradient, first, second)
        return f, s, weight - LEARN_RATE * ratio * u

    done = [
        finish(agg_weight, g_agg, agg_first, agg_second, trust[0:4].reshape(4, 1, 1)),
        finish(attn_weight, g_attn, attn_first, attn_second, trust[4:8].reshape(4, 1, 1)),
        finish(mlp_weight, g_mlp, mlp_first, mlp_second, trust[8:10].reshape(2, 1, 1)),
        finish(head_weight, g_head[:, :48], head_first, head_second, trust[10]),
        finish(embed_weight, g_embed, embed_first, embed_second, trust[11]),
        finish(vectors, g_vec, vector_first, vector_second, trust[12:].reshape(NVEC, 1)),
    ]
    loss_sum = jnp.sum(error_all)
    running_out = STATS_DECAY * running_error + (1.0 - STATS_DECAY) * error_all * (
        NVAR / total_count
    )
    return (
        loss_sum,
        total_count,
        running_out,
        trust,
        weight_norms,
        *[item[0] for item in done],
        *[item[1] for item in done],
        *[item[2] for item in done],
    )


def solution(mesh):
    weights = (
        P(None, "dp", "mp"),
        P(None, "dp", "mp"),
        P(None, "dp", "mp"),
        P("dp", "mp"),
        P(None, None, ("dp", "mp")),
        P(None, ("dp", "mp")),
    )
    in_specs = (
        P("dp", None),
        P("dp", "mp"),
        P("dp", None),
        P("dp", None),
        P("dp", None),
        P("dp"),
        P(),
        P(),
        *weights,
        *weights,
        *weights,
    )
    out_specs = (P(), P(), P(), P(), P(), *weights, *weights, *weights)
    return jax.shard_map(
        on_device, mesh=mesh, in_specs=in_specs, out_specs=out_specs, check_vma=False
    )
```

```python
import math

import jax
import jax.numpy as jnp
from jax import lax
from jax.experimental import pallas as pl
from jax.experimental.pallas import tpu as pltpu
from jax.sharding import PartitionSpec as P

D = 1024
HEAD_DIM = 64
FF = 4096
NVAR = 48
P_SIZE = 4
SEGS = 4
LEADS = 28
LATS = 32
STEP = 10
NVEC = 17
EROWS = NVAR * (P_SIZE + 1)

HIGH = lax.Precision.HIGHEST
NORM_EPS = 1e-06
BETA_ONE = 0.9
BETA_TWO = 0.999
LEARN_RATE = 0.3
WEIGHT_DECAY = 0.01
ADAM_EPS = 1e-08
STATS_DECAY = 0.9
MESH = pl.DeviceIdType.MESH
BF = jnp.bfloat16
F32 = jnp.float32

DPN, MPN, CHIPS, SH, TOK, COLS = 32, 4, 16, 64, 256, 256
NQ = 4
RQ, CH = TOK // NQ, SH // NQ
SCALE = 1.0 / math.sqrt(HEAD_DIM)


def nn(a, b, precision=None):
    return lax.dot_general(
        a, b, (((1,), (0,)), ((), ())), preferred_element_type=F32, precision=precision
    )


def nt(a, b, precision=None):
    return lax.dot_general(
        a, b, (((1,), (1,)), ((), ())), preferred_element_type=F32, precision=precision
    )


def tn(a, b, precision=None):
    return lax.dot_general(
        a, b, (((0,), (0,)), ((), ())), preferred_element_type=F32, precision=precision
    )


def latitude_weights():
    cosines = [
        math.cos(((j + 0.5) * (180.0 / LATS) - 90.0) * (math.pi / 180.0)) for j in range(LATS)
    ]
    mean = sum(cosines) / LATS
    return [value / mean for value in cosines]


def moments_new(gradient, first, second):
    first_new = BETA_ONE * first + (1.0 - BETA_ONE) * gradient
    second_new = BETA_TWO * second + (1.0 - BETA_TWO) * gradient * gradient
    return first_new, second_new


def adam_direction(weight, gradient, first, second):
    first_new, second_new = moments_new(gradient, first, second)
    first_hat = first_new * (1.0 / (1.0 - BETA_ONE**STEP))
    second_hat = second_new * (1.0 / (1.0 - BETA_TWO**STEP))
    direction = first_hat / (jnp.sqrt(second_hat) + ADAM_EPS) + WEIGHT_DECAY * weight
    return (first_new, second_new, direction)


def iota(shape, dim):
    return lax.broadcasted_iota(jnp.int32, shape, dim)


def ln_parts(x):
    centre = jnp.mean(x, -1, keepdims=True)
    shifted = x - centre
    r = lax.rsqrt(jnp.mean(shifted * shifted, -1, keepdims=True) + NORM_EPS)
    return shifted * r, r


def ln_back(n, r, gain, dh):
    e = dh * gain
    dx = r * (e - jnp.mean(e, -1, keepdims=True) - n * jnp.mean(e * n, -1, keepdims=True))
    dgain = jnp.sum(dh * n, 0, keepdims=True)
    dbias = jnp.sum(dh, 0, keepdims=True)
    return dx, dgain, dbias


LARGE = ("pix", "targ", "aggw", "attnw", "mlpw", "headw", "emb", "vec")
MOMENTS = ("agg", "attn", "mlp", "head", "emb", "vec")
SMALL = ("mask", "seg", "leadi", "lat", "vid")
OUTS = ("o_emb", "o_vec", "o_agg", "o_attn", "o_mlp", "o_head", "o_stats")
SHAPES = {
    "pix": ((NVAR * P_SIZE, TOK), BF),
    "targ": ((NVAR, TOK), F32),
    "agg": ((4, 32, 256), F32),
    "attn": ((4, 32, 256), F32),
    "mlp": ((2, 32, 1024), F32),
    "head": ((32, NVAR), F32),
    "emb": ((40, NVAR), F32),
    "vec": ((8, NVEC), F32),
}
SHAPES.update({"aggw": SHAPES["agg"], "attnw": SHAPES["attn"], "mlpw": SHAPES["mlp"]})
SHAPES["headw"] = SHAPES["head"]
FETCH = LARGE + tuple(n + "_f" for n in MOMENTS) + tuple(n + "_s" for n in MOMENTS)


def fetch_shape(name):
    return SHAPES[name[:-2] if name[-2] == "_" else name]


def scratch_list():
    vm = pltpu.VMEM
    dma = pltpu.SemaphoreType.DMA
    items = [
        ("WA3", vm((D, 256), BF)),
        ("WB", vm((D, 1024), BF)),
        ("W1", vm((D, 1024), BF)),
        ("W2", vm((D, 1024), BF)),
        ("HW", vm((D, 512), BF)),
        ("VEC", vm((D, 128), F32)),
        ("VR", vm((128, D), F32)),
        ("VRN", vm((128, D), F32)),
        ("TMPV", vm((D, 128), F32)),
        ("TA", vm((32, 384), F32)),
        ("HWT", vm((32, 128), F32)),
        ("TT", vm((128, TOK), F32)),
        ("TS", vm((NQ, MPN, CH, 128), F32)),
        ("TGT", vm((MPN, NQ, CH, 128), F32)),
        ("ROWS", vm((128, TOK), F32)),
        ("TCOL", vm((TOK, 128), F32)),
        ("LW", vm((TOK, 128), F32)),
        ("PIXT", vm((256, TOK), F32)),
        ("EWP", vm((256, 512), F32)),
        ("EWH", vm((128, 512), F32)),
        ("EWC", vm((128, 512), F32)),
        ("EWR", vm((256, 512), F32)),
        ("PRP", vm((256, 384), F32)),
        ("PRH", vm((128, 384), F32)),
        ("PRC", vm((128, 384), F32)),
        ("PRR", vm((256, 384), F32)),
        ("MT", vm((4, 256, TOK), BF)),
        ("PT", vm((4, NVAR, TOK), F32)),
        ("OAT", vm((256, TOK), F32)),
        ("OA", vm((TOK, 256), BF)),
        ("RSS", vm((5, TOK, D), BF)),
        ("RSR", vm((5, 3, SH, D), BF)),
        ("AG", vm((5, TOK, D), BF)),
        ("QKV", vm((3, TOK, 256), BF)),
        ("PB", vm((4, TOK, TOK), F32)),
        ("OB", vm((TOK, 256), BF)),
        ("DOB", vm((TOK, 256), BF)),
        ("GEL", vm((TOK, 1024), BF)),
        ("GELP", vm((TOK, 1024), F32)),
        ("DU", vm((TOK, 1024), BF)),
        ("DQKV", vm((TOK, 768), BF)),
        ("LN", vm((2, SH, D), F32)),
        ("XS", vm((SH, D), F32)),
        ("RR", vm((2, SH, 128), F32)),
        ("H3", vm((SH, D), BF)),
        ("DP", vm((SH, 512), BF)),
        ("GVT", vm((D, 128), F32)),
        ("GVP", vm((128, D), F32)),
        ("GVN", vm((128, D), F32)),
        ("TG", vm((32, 256), F32)),
        ("TGR", vm((3, 8, 256), F32)),
        ("VG", vm((32, 128), F32)),
        ("VGR", vm((3, 8, 128), F32)),
        ("HG", vm((32, 512), F32)),
        ("HGR", vm((3, 32, 128), F32)),
        ("EG", vm((40, NVAR), F32)),
        ("NX", vm((8, 128), F32)),
        ("NXR", vm((3, 8, 128), F32)),
        ("NY", vm((8, 128), F32)),
        ("NYR", vm((256, 128), F32)),
    ]
    for name, width, kind in (
        ("A3", 256, BF),
        ("B", 1024, BF),
        ("1", 1024, BF),
        ("2", 1024, BF),
        ("H", 512, BF),
        ("V", 128, F32),
    ):
        if name != "V":
            items.append(("G" + name, vm((D, width), kind)))
        items.append(("S" + name, vm((512, width), kind)))
        items.append(("B" + name, vm((512, width), kind)))
    for name in FETCH:
        items.append(("in_" + name, vm(*fetch_shape(name))))
    items += [
        ("fsem", dma((len(FETCH),))),
        ("ysend", dma((20,))),
        ("yrecv", dma((8,))),
        ("rrecv", dma((5, NQ))),
        ("arecv", dma((5, NQ))),
        ("dsend", dma((19,))),
        ("drecv", dma((19,))),
        ("ssend", dma((16,))),
        ("srecv", dma((16,))),
    ]
    return items


SCRATCH = scratch_list()
NAMES = tuple(n + "_hbm" for n in FETCH) + SMALL + OUTS + tuple(n for n, unused in SCRATCH)


def mega(*refs):
    r = dict(zip(NAMES, refs))
    step_kernel(type("Refs", (), r))


def step_kernel(R):
    d = lax.axis_index("dp")
    m = lax.axis_index("mp")
    c = lax.rem(d, 2)
    k = d // 2
    z = k // 4
    x = lax.rem(k, 4)
    sib = d + 1 - 2 * c
    rb = pl.multiple_of(c * 512 + k * 32, 32)
    half = pl.multiple_of(c * 512, 512)
    other = pl.multiple_of(512 - c * 512, 512)
    my_slot = pl.ds(pl.multiple_of(m * 128, 128), 128)
    my_eight = pl.ds(pl.multiple_of(m * 8, 8), 8)
    my_cols = pl.ds(pl.multiple_of(m * COLS, COLS), COLS)

    def rcopy(src, dst, ss, rs, dp, mp):
        return pltpu.make_async_remote_copy(
            src_ref=src,
            dst_ref=dst,
            send_sem=ss,
            recv_sem=rs,
            device_id={"dp": dp, "mp": mp},
            device_id_type=MESH,
        )

    def drain(ref, sem):
        pltpu.make_async_copy(ref, ref, sem).wait()

    def loop(first, last, fn):
        def step(i, carry):
            fn(i)
            return carry

        lax.fori_loop(first, last, step, 0)

    def to_peers(fn):
        for i in (2, 1, 3):
            fn(i, lax.rem(m + i, MPN))

    def to_chips(fn):
        def step(i):
            kk = lax.rem(k + i, CHIPS)
            fn(kk, kk * 2 + c)

        loop(1, CHIPS, step)

    def fetch(name):
        i = FETCH.index(name)
        return pltpu.make_async_copy(
            getattr(R, name + "_hbm"), getattr(R, "in_" + name), R.fsem.at[i]
        )

    dsend, drecv, ssend, srecv = R.dsend, R.drecv, R.ssend, R.srecv
    ysend, yrecv = R.ysend, R.yrecv

    def gather_start(buf, g):
        block = buf.at[pl.ds(rb, 32)]
        to_chips(lambda kk, t: rcopy(block, block, dsend.at[g], drecv.at[g], t, m).start())

    def gather_cross(buf, g, rows=480):
        drain(buf.at[pl.ds(0, rows)], drecv.at[g])
        part = buf.at[pl.ds(half, 512)]
        rcopy(part, part, ssend.at[g], srecv.at[g], sib, m).start()

    def gather_wait(buf, g):
        drain(buf.at[pl.ds(0, 512)], srecv.at[g])

    def gather_end(buf, g, rows=480):
        drain(buf.at[pl.ds(0, rows)], dsend.at[g])
        drain(buf.at[pl.ds(0, 512)], ssend.at[g])

    def along(axis, i):
        if axis == "x":
            return (z * 4 + lax.rem(x + i, 4)) * 2 + c
        return (lax.rem(z + i, 4) * 4 + x) * 2 + c

    def two_first(buf, axis, g):
        block = buf.at[pl.ds(rb, 32)]
        for i in (2, 1, 3):
            rcopy(block, block, dsend.at[g], drecv.at[g], along(axis, i), m).start()

    def two_second(buf, axis, g, before):
        drain(buf.at[pl.ds(0, 96)], drecv.at[before])
        if axis == "z":
            block = buf.at[pl.ds(pl.multiple_of(half + z * 128, 128), 128)]
            for i in (2, 1, 3):
                rcopy(block, block, dsend.at[g], drecv.at[g], along("z", i), m).start()
        else:

            def send(zz):
                block = buf.at[pl.ds(pl.multiple_of(half + zz * 128 + x * 32, 32), 32)]
                for i in (2, 1, 3):
                    rcopy(block, block, dsend.at[g], drecv.at[g], along("x", i), m).start()

            loop(0, 4, send)

    def reduce_cross(name, g):
        buf, sbuf = (R.GVT if name == "V" else getattr(R, "G" + name)), getattr(R, "S" + name)
        rcopy(buf.at[pl.ds(other, 512)], sbuf, ssend.at[g], srecv.at[g], sib, m).start()

    def reduce_spread(name, g):
        buf, sbuf = (R.GVT if name == "V" else getattr(R, "G" + name)), getattr(R, "S" + name)
        bbuf = getattr(R, "B" + name)
        drain(sbuf, srecv.at[g])

        def add(i):
            at = pl.multiple_of(i * 128, 128)
            sbuf[pl.ds(at, 128), :] = (
                sbuf[pl.ds(at, 128), :].astype(F32)
                + buf[pl.ds(pl.multiple_of(half + at, 128), 128), :].astype(F32)
            ).astype(sbuf.dtype)

        loop(0, 4, add)
        land = bbuf.at[pl.ds(pl.multiple_of(k * 32, 32), 32)]

        def send(kk, t):
            src = sbuf.at[pl.ds(pl.multiple_of(kk * 32, 32), 32)]
            rcopy(src, land, dsend.at[g], drecv.at[g], t, m).start()

        to_chips(send)

    def reduce_end(name, g):
        sbuf, bbuf = getattr(R, "S" + name), getattr(R, "B" + name)
        drain(bbuf.at[pl.ds(0, 480)], drecv.at[g])

        def add(i, acc):
            at = pl.multiple_of(lax.rem(k + i, CHIPS) * 32, 32)
            return acc + bbuf[pl.ds(at, 32), :].astype(F32)

        total = lax.fori_loop(
            1, CHIPS, add, sbuf[pl.ds(pl.multiple_of(k * 32, 32), 32), :].astype(F32)
        )
        drain(bbuf.at[pl.ds(0, 480)], dsend.at[g])
        drain(sbuf, ssend.at[g])
        return total

    def all_sum(src, hbuf, cbuf, res, g, hooks):
        mine_half = pl.multiple_of(c * 128, 128)
        rcopy(
            src.at[pl.ds(pl.multiple_of(128 - c * 128, 128), 128)],
            hbuf,
            ssend.at[g],
            srecv.at[g],
            sib,
            m,
        ).start()
        hooks[0]()
        drain(hbuf, srecv.at[g])
        hbuf[...] = hbuf[...] + src[pl.ds(mine_half, 128), :]
        at_k = pl.multiple_of(k * 8, 8)

        def send(kk, t):
            rcopy(
                hbuf.at[pl.ds(pl.multiple_of(kk * 8, 8), 8)],
                cbuf.at[pl.ds(at_k, 8)],
                dsend.at[g],
                drecv.at[g],
                t,
                m,
            ).start()

        to_chips(send)
        hooks[1]()
        drain(cbuf.at[pl.ds(0, 120)], drecv.at[g])

        def add(i, acc):
            at = pl.multiple_of(lax.rem(k + i, CHIPS) * 8, 8)
            return acc + cbuf[pl.ds(at, 8), :]

        total = lax.fori_loop(1, CHIPS, add, hbuf[pl.ds(at_k, 8), :])
        block = pl.ds(pl.multiple_of(mine_half + at_k, 8), 8)
        res[block, :] = total
        part = res.at[block]
        to_chips(lambda kk, t: rcopy(part, part, dsend.at[g + 1], drecv.at[g + 1], t, m).start())
        hooks[2]()
        drain(res.at[pl.ds(0, 120)], drecv.at[g + 1])
        part2 = res.at[pl.ds(mine_half, 128)]
        rcopy(part2, part2, ssend.at[g + 1], srecv.at[g + 1], sib, m).start()
        hooks[3]()
        drain(res.at[pl.ds(0, 128)], srecv.at[g + 1])

    def all_sum_end(hbuf, cbuf, res, g):
        drain(hbuf, ssend.at[g])
        drain(res.at[pl.ds(0, 128)], ssend.at[g + 1])
        drain(cbuf.at[pl.ds(0, 120)], dsend.at[g])
        drain(res.at[pl.ds(0, 120)], dsend.at[g + 1])

    def rows_of(q):
        return pl.ds(pl.multiple_of(q * RQ, RQ), RQ)

    def own_of(q, t):
        return pl.ds(pl.multiple_of(q * RQ + t * CH, CH), CH)

    def local_of(q):
        return pl.ds(pl.multiple_of(q * CH, CH), CH)

    def branch_send(ix, q, left, weight, cols=None):
        for n in range(4):
            at = pl.ds(n * 256, 256)
            w = weight[at, :] if cols is None else weight[at, cols[0] : cols[1]]
            R.RSS[ix, rows_of(q), n * 256 : (n + 1) * 256] = nt(left, w).astype(BF)

        def send(i, t):
            rcopy(
                R.RSS.at[ix, own_of(q, t)],
                R.RSR.at[ix, i - 1, local_of(q)],
                ysend.at[ix],
                R.rrecv.at[ix, q],
                d,
                t,
            ).start()

        to_peers(send)

    def branch_sum(ix, q):
        drain(R.RSR.at[ix, :, pl.ds(0, CH)], R.rrecv.at[ix, q])
        acc = R.RSS[ix, own_of(q, m), :].astype(F32)
        for i in range(3):
            acc = acc + R.RSR[ix, i, local_of(q), :].astype(F32)
        return acc

    def share_send(ix, q, values):
        R.AG[ix, own_of(q, m), :] = values
        block = R.AG.at[ix, own_of(q, m)]
        to_peers(
            lambda i, t: rcopy(block, block, ysend.at[5 + ix], R.arecv.at[ix, q], d, t).start()
        )

    def share_wait(ix, q):
        drain(R.AG.at[ix, pl.ds(0, 3 * CH)], R.arecv.at[ix, q])

    for name in FETCH:
        fetch(name).start()
    bar = pltpu.get_barrier_semaphore()

    def greet(i):
        pl.semaphore_signal(
            bar, inc=1, device_id={"dp": lax.rem(d + i, DPN), "mp": m}, device_id_type=MESH
        )

    for i in range(1, MPN):
        pl.semaphore_signal(
            bar, inc=1, device_id={"dp": d, "mp": lax.rem(m + i, MPN)}, device_id_type=MESH
        )
    loop(1, DPN, greet)

    vhot = (iota((NVAR, NVAR), 0) == R.vid[...]).astype(F32)
    fetch("emb").wait()
    fetch("vec").wait()
    chosen = nn(R.in_emb[...], vhot, HIGH)
    R.TA[my_eight, :] = jnp.zeros((8, 384), F32)
    for p in range(5):
        R.TA[my_eight, p * 48 : (p + 1) * 48] = chosen[p * 8 : (p + 1) * 8, :]
    R.TA[my_eight, 256 : 256 + NVEC] = R.in_vec[...]
    fetch("aggw").wait()
    fetch("headw").wait()
    aw = [R.in_aggw[j].astype(BF) for j in range(3)]
    R.WA3[pl.ds(rb, 32), :] = R.in_aggw[3].astype(BF)
    R.HWT[...] = jnp.zeros_like(R.HWT)
    R.HWT[:, 0:NVAR] = R.in_headw[...]
    R.HW[pl.ds(rb, 32), my_slot] = R.HWT[...].astype(BF)
    fetch("mlpw").wait()
    R.W1[pl.ds(rb, 32), :] = R.in_mlpw[0].astype(BF)
    R.W2[pl.ds(rb, 32), :] = R.in_mlpw[1].astype(BF)
    fetch("attnw").wait()
    for j in range(4):
        R.WB[pl.ds(rb, 32), j * 256 : (j + 1) * 256] = R.in_attnw[j].astype(BF)
    fetch("targ").wait()
    R.TT[NVAR:, :] = jnp.zeros((128 - NVAR, TOK), F32)
    R.TT[0:NVAR, :] = R.in_targ[...]
    turned = R.TT[...].T
    for q in range(NQ):
        for t in range(MPN):
            at = q * RQ + t * CH
            R.TS[q, t] = turned[at : at + CH, :]
    R.TGT[m] = R.TS[:, m]
    R.GVP[...] = jnp.zeros_like(R.GVP)
    R.GVN[...] = jnp.zeros_like(R.GVN)
    R.NX[...] = jnp.zeros_like(R.NX)
    pl.semaphore_wait(bar, DPN + MPN - 2)

    def first_sends(i, t):
        part = R.TA.at[my_eight]
        rcopy(part, part, ysend.at[10], yrecv.at[0], d, t).start()

    def later_sends(i, t):
        slot = R.HW.at[pl.ds(rb, 32), my_slot]
        rcopy(slot, slot, ysend.at[11], yrecv.at[1], d, t).start()
        rcopy(R.TS.at[:, t], R.TGT.at[m], ysend.at[12], yrecv.at[2], d, t).start()

    to_peers(first_sends)
    gather_start(R.WA3, 0)
    two_first(R.W1, "x", 17)
    two_first(R.W2, "z", 18)
    to_peers(later_sends)

    fetch("pix").wait()
    rows = iota((256, 192), 0)
    cols = iota((256, 192), 1)
    pick = (rows < 192) & ((lax.rem(rows, NVAR) * P_SIZE + rows // NVAR) == cols)
    pixt = nn(pick.astype(BF), R.in_pix[...])
    row_at = iota((256, TOK), 0)
    R.PIXT[...] = jnp.where(row_at < 192, pixt, jnp.where(row_at < EROWS, 1.0, 0.0))

    drain(R.TA.at[pl.ds(0, 24)], yrecv.at[0])
    emb = R.TA[:, 0:256]
    R.EWP[:, 0:256] = tn(emb, aw[1].astype(F32), HIGH)
    R.EWP[:, 256:512] = tn(emb, aw[2].astype(F32), HIGH)
    R.EWP[240:241, 0:256] = jnp.sum(R.TA[:, 256:257] * aw[0].astype(F32), 0, keepdims=True)
    keep = R.mask[...].astype(F32)
    count = jnp.sum(jnp.sum(keep, 1, keepdims=True), 0, keepdims=True) * NVAR
    R.EWP[241:242, 0:128] = jnp.broadcast_to(count, (1, 128))

    def per_patch():
        seg = R.seg[...]
        lead_row = jnp.zeros((1, TOK), F32)
        for s in range(SEGS):
            value = (R.leadi[:, s : s + 1] + 1).astype(F32) / LEADS
            lead_row = jnp.where(seg == s, value, lead_row)
        lat = R.lat[...]
        lat_row = jnp.zeros((1, TOK), F32)
        for j, value in enumerate(latitude_weights()):
            lat_row = jnp.where(lat == j, value, lat_row)
        R.ROWS[...] = jnp.zeros_like(R.ROWS)
        R.ROWS[0:1, :] = seg.astype(F32)
        R.ROWS[1:2, :] = lead_row
        R.ROWS[8:12, :] = keep * lat_row
        R.TCOL[...] = R.ROWS[...].T
        lane = iota((128, 128), 1)
        pick = (lane < NVAR) & (iota((128, 128), 0) == 8 + lax.rem(lane, P_SIZE))
        R.LW[...] = nn(R.TCOL[...], pick.astype(F32), HIGH)

    def own_slot_done():
        drain(R.HW.at[pl.ds(0, 32), pl.ds(0, 384)], yrecv.at[1])
        R.VEC[pl.ds(rb, 32), :] = R.TA[:, 256:384]

    def bulk():
        gather_cross(R.WA3, 0)
        gather_start(R.VEC, 2)
        gather_start(R.WB, 1)
        gather_start(R.HW, 5)

    all_sum(R.EWP, R.EWH, R.EWC, R.EWR, 6, (own_slot_done, per_patch, bulk, lambda: None))

    head_of = (iota((256, 128), 0) // HEAD_DIM == iota((256, 128), 1)).astype(F32)
    qa = R.EWR[240:241, 0:256].astype(BF).astype(F32)
    total_count = R.EWR[241:242, 0:1]
    qe = nn(R.EWR[:, 0:256] * (qa * SCALE), head_of, HIGH)
    ewv = R.EWR[:, 256:512].astype(BF)
    for h in range(4):
        scores = R.PIXT[0:48, :] * qe[0:48, h : h + 1]
        for p in range(1, 5):
            at = slice(p * 48, (p + 1) * 48)
            scores = scores + R.PIXT[at, :] * qe[at, h : h + 1]
        e = jnp.exp(scores - jnp.max(scores, 0, keepdims=True))
        probs = e / jnp.sum(e, 0, keepdims=True)
        R.PT[h] = probs
        probs = probs.astype(BF).astype(F32)
        for p in range(5):
            at = slice(p * 48, (p + 1) * 48)
            R.MT[h, at, :] = (probs * R.PIXT[at, :]).astype(BF)
        R.MT[h, 240:256, :] = jnp.zeros((16, TOK), BF)
        R.OAT[h * 64 : (h + 1) * 64, :] = tn(ewv[:, h * 64 : (h + 1) * 64], R.MT[h])
    R.OA[...] = R.OAT[...].T.astype(BF)

    gather_wait(R.WA3, 0)
    loop(0, NQ, lambda q: branch_send(0, q, R.OA[rows_of(q), :], R.WA3))
    two_second(R.W1, "z", 3, 17)
    two_second(R.W2, "x", 4, 18)
    gather_cross(R.VEC, 2)
    gather_wait(R.VEC, 2)
    R.VR[...] = R.VEC[...].T

    def natural(i):
        at = pl.multiple_of(lax.rem(i, 2) * 512 + (i // 2) * 32, 32)
        R.TMPV[pl.ds(pl.multiple_of(i * 32, 32), 32), :] = R.VEC[pl.ds(at, 32), :]

    loop(0, DPN, natural)
    R.VRN[...] = R.TMPV[...].T

    def vrow(i):
        return R.VR[i : i + 1, :]

    def keep_norm(j, q, n, r):
        R.LN[j, local_of(q), :] = n
        R.RR[j, local_of(q), :] = jnp.broadcast_to(r, (CH, 128))

    def mixed_rows(q):
        lead = R.TCOL[own_of(q, m), 1:2]
        x0 = branch_sum(0, q) + vrow(1) + lead * vrow(2)
        n, r = ln_parts(x0)
        share_send(0, q, (n * vrow(3) + vrow(4)).astype(BF))
        R.XS[local_of(q), :] = x0
        keep_norm(0, q, n, r)

    loop(0, NQ, mixed_rows)
    gather_cross(R.WB, 1)
    gather_wait(R.WB, 1)

    def project(q):
        share_wait(0, q)
        at = rows_of(q)
        h1 = R.AG[0, at, :]
        R.QKV[0, at, :] = (nn(h1, R.WB[:, 0:256]) + R.VRN[5:6, my_cols]).astype(BF)
        R.QKV[1, at, :] = nn(h1, R.WB[:, 256:512]).astype(BF)
        R.QKV[2, at, :] = (nn(h1, R.WB[:, 512:768]) + R.VRN[6:7, my_cols]).astype(BF)

    loop(0, NQ, project)
    seg_row = R.seg[...].astype(F32)

    def attend(q):
        rows = rows_of(q)
        same = R.TCOL[rows, 0:1] == seg_row
        for h in range(4):
            at = slice(h * 64, (h + 1) * 64)
            scores = nt(R.QKV[0, rows, at], R.QKV[1, :, at]) * SCALE
            scores = jnp.where(same, scores, -1e30)
            e = jnp.exp(scores - jnp.max(scores, 1, keepdims=True))
            probs = e / jnp.sum(e, 1, keepdims=True)
            R.PB[h, rows, :] = probs
            R.OB[rows, at] = nn(probs.astype(BF), R.QKV[2, :, at]).astype(BF)
        branch_send(1, q, R.OB[rows, :], R.WB, (768, 1024))

    loop(0, NQ, attend)
    gather_cross(R.W1, 3, 384)
    gather_cross(R.W2, 4, 384)

    def second_rows(q):
        x1 = R.XS[local_of(q), :] + branch_sum(1, q) + vrow(7)
        n, r = ln_parts(x1)
        share_send(1, q, (n * vrow(8) + vrow(9)).astype(BF))
        R.XS[local_of(q), :] = x1
        keep_norm(1, q, n, r)

    loop(0, NQ, second_rows)
    gather_cross(R.HW, 5)
    gather_wait(R.W1, 3)
    gather_wait(R.W2, 4)

    def feed(q):
        share_wait(1, q)
        rows = rows_of(q)
        for n in range(4):
            at = slice(n * 256, (n + 1) * 256)
            u = nn(R.AG[1, rows, :], R.W1[:, at]) + R.VRN[pl.ds(10 + m, 1), at]
            phi = 0.5 * (1.0 + lax.erf(u * (1.0 / math.sqrt(2.0))))
            R.GEL[rows, at] = (u * phi).astype(BF)
            R.GELP[rows, at] = phi + u * jnp.exp(-0.5 * u * u) * (1.0 / math.sqrt(2.0 * math.pi))
        branch_send(2, q, R.GEL[rows, :], R.W2)

    loop(0, NQ, feed)
    gather_wait(R.HW, 5)
    drain(R.TGT.at[pl.ds(0, 3)], yrecv.at[2])

    def head_rows(q):
        here = local_of(q)
        x2 = R.XS[here, :] + branch_sum(2, q) + vrow(14)
        n, r = ln_parts(x2)
        h3 = (n * vrow(15) + vrow(16)).astype(BF)
        R.H3[here, :] = h3
        pred = nn(h3, R.HW[...])
        weight = R.LW[own_of(q, m), :]
        for j in range(4):
            misfit = pred[:, j * 128 : (j + 1) * 128] - R.TGT[j, q]
            weighted = weight * misfit
            R.NX[4 + j : 5 + j, :] = R.NX[4 + j : 5 + j, :] + jnp.sum(
                weighted * misfit, 0, keepdims=True
            )
            R.DP[here, j * 128 : (j + 1) * 128] = (2.0 * weighted / total_count).astype(BF)
        dh3 = nt(R.DP[here, :], R.HW[...])
        dx2, dgain, dbias = ln_back(n, r, vrow(15), dh3)
        share_send(2, q, dx2.astype(BF))
        R.XS[here, :] = dx2
        R.GVP[14:15, :] = R.GVP[14:15, :] + jnp.sum(dx2, 0, keepdims=True)
        R.GVP[15:16, :] = R.GVP[15:16, :] + dgain
        R.GVP[16:17, :] = R.GVP[16:17, :] + dbias

    loop(0, NQ, head_rows)

    def feed_back(q):
        share_wait(2, q)
        rows = rows_of(q)
        for n in range(4):
            at = slice(n * 256, (n + 1) * 256)
            du = (nn(R.AG[2, rows, :], R.W2[:, at]) * R.GELP[rows, at]).astype(BF)
            R.DU[rows, at] = du
            row = pl.ds(10 + m, 1)
            R.GVN[row, at] = R.GVN[row, at] + jnp.sum(du.astype(F32), 0, keepdims=True)
        branch_send(3, q, R.DU[rows, :], R.W1)

    loop(0, NQ, feed_back)

    def pieces(q, fn):
        for j in range(4 // NQ):
            fn(pl.ds(pl.multiple_of((q * (4 // NQ) + j) * 256, 256), 256))

    def grad_two(at):
        R.G2[at, :] = tn(R.AG[2, :, at], R.GEL[...]).astype(BF)

    def grad_one(at):
        R.G1[at, :] = tn(R.AG[1, :, at], R.DU[...]).astype(BF)

    def back_rows(q):
        here = local_of(q)
        n = R.LN[1, here, :]
        dx1, dgain, dbias = ln_back(n, R.RR[1, here, 0:1], vrow(8), branch_sum(3, q))
        dx1 = dx1 + R.XS[here, :]
        share_send(3, q, dx1.astype(BF))
        R.XS[here, :] = dx1
        R.GVP[7:8, :] = R.GVP[7:8, :] + jnp.sum(dx1, 0, keepdims=True)
        R.GVP[8:9, :] = R.GVP[8:9, :] + dgain
        R.GVP[9:10, :] = R.GVP[9:10, :] + dbias
        pieces(q, grad_two)

    R.GH[...] = tn(R.H3[...], R.DP[...]).astype(BF)
    reduce_cross("H", 14)
    loop(0, NQ, back_rows)
    reduce_cross("2", 13)

    def out_back(q):
        share_wait(3, q)
        rows = rows_of(q)
        R.DOB[rows, :] = nn(R.AG[3, rows, :], R.WB[:, 768:1024]).astype(BF)
        pieces(q, grad_one)

    loop(0, NQ, out_back)
    reduce_cross("1", 12)
    reduce_spread("H", 14)
    reduce_spread("2", 13)
    for h in range(4):
        at = slice(h * 64, (h + 1) * 64)
        probs = R.PB[h]
        dout = R.DOB[:, at]
        dv = tn(probs.astype(BF), dout).astype(BF)
        dprob = nt(dout, R.QKV[2, :, at])
        ds = (probs * (dprob - jnp.sum(probs * dprob, 1, keepdims=True))).astype(BF)
        dq = (nn(ds, R.QKV[1, :, at]) * SCALE).astype(BF)
        dk = (tn(ds, R.QKV[0, :, at]) * SCALE).astype(BF)
        R.DQKV[:, h * 64 : (h + 1) * 64] = dq
        R.DQKV[:, 256 + h * 64 : 256 + (h + 1) * 64] = dk
        R.DQKV[:, 512 + h * 64 : 512 + (h + 1) * 64] = dv
    loop(0, NQ, lambda q: branch_send(4, q, R.DQKV[rows_of(q), :], R.WB, (0, 768)))
    R.GVN[5:6, my_cols] = jnp.sum(R.DQKV[:, 0:256].astype(F32), 0, keepdims=True)
    R.GVN[6:7, my_cols] = jnp.sum(R.DQKV[:, 512:768].astype(F32), 0, keepdims=True)
    reduce_spread("1", 12)

    def grad_attn(at):
        R.GB[at, 0:768] = tn(R.AG[0, :, at], R.DQKV[...]).astype(BF)
        R.GB[at, 768:1024] = tn(R.AG[3, :, at], R.OB[...]).astype(BF)

    def first_rows(q):
        here = local_of(q)
        n = R.LN[0, here, :]
        dx0, dgain, dbias = ln_back(n, R.RR[0, here, 0:1], vrow(3), branch_sum(4, q))
        dx0 = dx0 + R.XS[here, :]
        share_send(4, q, dx0.astype(BF))
        lead = R.TCOL[own_of(q, m), 1:2]
        R.GVP[1:2, :] = R.GVP[1:2, :] + jnp.sum(dx0, 0, keepdims=True)
        R.GVP[2:3, :] = R.GVP[2:3, :] + jnp.sum(lead * dx0, 0, keepdims=True)
        R.GVP[3:4, :] = R.GVP[3:4, :] + dgain
        R.GVP[4:5, :] = R.GVP[4:5, :] + dbias
        pieces(q, grad_attn)

    loop(0, NQ, first_rows)
    reduce_cross("B", 11)
    R.TMPV[...] = R.GVN[...].T
    R.GVT[...] = R.GVP[...].T

    def permuted(i):
        at = pl.ds(pl.multiple_of(lax.rem(i, 2) * 512 + (i // 2) * 32, 32), 32)
        R.GVT[at, :] = R.GVT[at, :] + R.TMPV[pl.ds(pl.multiple_of(i * 32, 32), 32), :]

    loop(0, DPN, permuted)
    reduce_cross("V", 15)
    reduce_spread("B", 11)
    reduce_spread("V", 15)

    def mix_back(q):
        share_wait(4, q)
        rows = rows_of(q)
        R.DOB[rows, :] = nn(R.AG[4, rows, :], R.WA3[...]).astype(BF)

    loop(0, NQ, mix_back)
    R.PRP[...] = jnp.zeros_like(R.PRP)
    for h in range(4):
        at = slice(h * 64, (h + 1) * 64)
        dout = R.DOB[:, at]
        through = nt(ewv[:, at], dout)
        dprob = R.PIXT[0:48, :] * through[0:48, :]
        for p in range(1, 5):
            row = slice(p * 48, (p + 1) * 48)
            dprob = dprob + R.PIXT[row, :] * through[row, :]
        probs = R.PT[h]
        ds = (probs * (dprob - jnp.sum(probs * dprob, 0, keepdims=True))).astype(BF).astype(F32)
        for p in range(5):
            row = slice(p * 48, (p + 1) * 48)
            R.PRP[row, 256 + h : 257 + h] = jnp.sum(ds * R.PIXT[row, :], 1, keepdims=True)
        R.PRP[:, at] = nn(R.MT[h], dout)

    lanes = iota((1, 128), 1)
    sums = {"w": jnp.zeros((1, 128), F32), "u": jnp.zeros((1, 128), F32)}

    def square_sum(values):
        return jnp.sum(jnp.sum(values * values, 1, keepdims=True), 0, keepdims=True)

    def tensor(index, weight, gradient, first, second):
        unused, unused2, direction = adam_direction(weight, gradient, first, second)
        here = lanes == index
        sums["w"] = sums["w"] + jnp.where(here, square_sum(weight), 0.0)
        sums["u"] = sums["u"] + jnp.where(here, square_sum(direction), 0.0)

    def hook_first():
        def piece(n):
            at = pl.ds(pl.multiple_of(n * 256, 256), 256)
            R.GA3[at, :] = tn(R.AG[4, :, at], R.OA[...]).astype(BF)

        loop(0, 4, piece)
        reduce_cross("A3", 10)

    def hook_second():
        reduce_spread("A3", 10)
        for name in MOMENTS:
            fetch(name + "_f").wait()
            fetch(name + "_s").wait()
        R.o_mlp[1] = reduce_end("2", 13)
        R.o_mlp[0] = reduce_end("1", 12)
        for j in range(2):
            tensor(8 + j, R.in_mlpw[j], R.o_mlp[j], R.in_mlp_f[j], R.in_mlp_s[j])

    def hook_third():
        R.HG[...] = reduce_end("H", 14)
        R.VG[...] = reduce_end("V", 15)

        def sends(i, t):
            rcopy(
                R.HG.at[:, pl.ds(pl.multiple_of(t * 128, 128), 128)],
                R.HGR.at[i - 1],
                ysend.at[14],
                yrecv.at[4],
                d,
                t,
            ).start()
            rcopy(
                R.VG.at[pl.ds(pl.multiple_of(t * 8, 8), 8)],
                R.VGR.at[i - 1],
                ysend.at[15],
                yrecv.at[5],
                d,
                t,
            ).start()

        to_peers(sends)
        gsum = reduce_end("B", 11)
        for j in range(4):
            R.o_attn[j] = gsum[:, j * 256 : (j + 1) * 256]
        for j in range(4):
            tensor(4 + j, R.in_attnw[j], R.o_attn[j], R.in_attn_f[j], R.in_attn_s[j])

    all_sum(R.PRP, R.PRH, R.PRC, R.PRR, 8, (hook_first, hook_second, hook_third, lambda: None))

    spread = nt(R.PRR[:, 256:384], head_of, HIGH)
    dqa = jnp.sum(spread * R.EWR[:, 0:256], 0, keepdims=True) * SCALE
    pk = spread * (qa * SCALE)
    pv = R.PRR[:, 0:256]
    emb = R.TA[:, 0:256]
    wa = [R.in_aggw[j].astype(BF).astype(F32) for j in range(3)]
    R.TG[...] = nt(wa[1], pk, HIGH) + nt(wa[2], pv, HIGH)
    R.TG[:, 240:241] = jnp.sum(wa[0] * dqa, 1, keepdims=True)

    def last_sends(i, t):
        rcopy(
            R.TG.at[pl.ds(pl.multiple_of(t * 8, 8), 8)],
            R.TGR.at[i - 1],
            ysend.at[13],
            yrecv.at[3],
            d,
            t,
        ).start()

    to_peers(last_sends)
    R.o_agg[0] = R.TA[:, 256:257] * dqa
    R.o_agg[1] = nn(emb, pk, HIGH)
    R.o_agg[2] = nn(emb, pv, HIGH)
    R.o_agg[3] = reduce_end("A3", 10)
    for j in range(4):
        tensor(j, R.in_aggw[j], R.o_agg[j], R.in_agg_f[j], R.in_agg_s[j])
    drain(R.HGR, yrecv.at[4])
    hgrad = R.HG[:, my_slot] + R.HGR[0] + R.HGR[1] + R.HGR[2]
    R.o_head[...] = hgrad[:, 0:NVAR]
    tensor(10, R.in_headw[...], R.o_head[...], R.in_head_f[...], R.in_head_s[...])
    drain(R.VGR, yrecv.at[5])
    vgrad = R.VG[my_eight, :] + R.VGR[0] + R.VGR[1] + R.VGR[2]
    drain(R.TGR, yrecv.at[3])
    tgrad = R.TG[my_eight, :] + R.TGR[0] + R.TGR[1] + R.TGR[2]
    for p in range(5):
        R.EG[p * 8 : (p + 1) * 8, :] = tgrad[:, p * 48 : (p + 1) * 48]
    R.o_emb[...] = nt(R.EG[...], vhot, HIGH)
    tensor(11, R.in_emb[...], R.o_emb[...], R.in_emb_f[...], R.in_emb_s[...])
    R.o_vec[...] = vgrad[:, 0:NVEC]
    R.o_vec[:, 0:1] = tgrad[:, 240:241]
    unused, unused2, direction = adam_direction(
        R.in_vec[...], R.o_vec[...], R.in_vec_f[...], R.in_vec_s[...]
    )
    R.NX[0:1, :] = sums["w"]
    R.NX[1:2, :] = sums["u"]
    R.NX[0:1, 12 : 12 + NVEC] = jnp.sum(R.in_vec[...] * R.in_vec[...], 0, keepdims=True)
    R.NX[1:2, 12 : 12 + NVEC] = jnp.sum(direction * direction, 0, keepdims=True)

    to_peers(lambda i, t: rcopy(R.NX, R.NXR.at[i - 1], ysend.at[16], yrecv.at[6], d, t).start())
    drain(R.NXR, yrecv.at[6])
    R.NY[...] = R.NX[...] + R.NXR[0] + R.NXR[1] + R.NXR[2]
    at_d = pl.ds(pl.multiple_of(d * 8, 8), 8)

    def norm_send(i):
        t = lax.rem(d + i, DPN)
        rcopy(R.NY, R.NYR.at[at_d], dsend.at[16], drecv.at[16], t, m).start()

    loop(1, DPN, norm_send)

    gather_end(R.WA3, 0)
    gather_end(R.WB, 1)
    gather_end(R.VEC, 2)
    gather_end(R.HW, 5)
    for buf, g in ((R.W1, 3), (R.W2, 4)):
        gather_end(buf, g, 384)
        drain(buf.at[pl.ds(0, 96)], dsend.at[14 + g])
    all_sum_end(R.EWH, R.EWC, R.EWR, 6)
    all_sum_end(R.PRH, R.PRC, R.PRR, 8)
    for ix in range(5):
        drain(R.RSR.at[ix], ysend.at[ix])
        drain(R.AG.at[ix, pl.ds(0, 192)], ysend.at[5 + ix])
    drain(R.TA.at[pl.ds(0, 24)], ysend.at[10])
    drain(R.HW.at[pl.ds(0, 32), pl.ds(0, 384)], ysend.at[11])
    drain(R.TGT.at[pl.ds(0, 3)], ysend.at[12])
    drain(R.TGR, ysend.at[13])
    drain(R.HGR, ysend.at[14])
    drain(R.VGR, ysend.at[15])
    drain(R.NXR, ysend.at[16])

    drain(R.NYR.at[pl.ds(0, 248)], drecv.at[16])

    def norm_add(i, acc):
        at = pl.multiple_of(lax.rem(d + i, DPN) * 8, 8)
        return acc + R.NYR[pl.ds(at, 8), :]

    stats = lax.fori_loop(1, DPN, norm_add, R.NY[...])
    first_lane = (iota((8, 128), 0) == 0) & (iota((8, 128), 1) == 127)
    R.o_stats[...] = jnp.where(first_lane, total_count, stats)
    drain(R.NYR.at[pl.ds(0, 248)], dsend.at[16])


def mega_call(large, small):
    outs = [SHAPES[n] for n in ("emb", "vec", "agg", "attn", "mlp", "head")] + [((8, 128), F32)]
    out_shape = tuple(jax.ShapeDtypeStruct(*item) for item in outs)
    whole = pl.BlockSpec(memory_space=pltpu.VMEM)
    return pl.pallas_call(
        mega,
        out_shape=out_shape,
        in_specs=[pl.BlockSpec(memory_space=pl.ANY)] * len(large) + [whole] * len(small),
        out_specs=tuple(whole for unused in out_shape),
        scratch_shapes=[item for unused, item in SCRATCH],
        compiler_params=pltpu.CompilerParams(
            collective_id=0, has_side_effects=True, vmem_limit_bytes=60 * 2**20
        ),
        name="step",
    )(*large, *small)


def finish(*refs):
    weights, firsts, seconds, grads = (refs[6 * i : 6 * i + 6] for i in range(4))
    stats, running = refs[24:26]
    o_loss, o_count, o_running, o_trust, o_norms = refs[26:31]
    o_first, o_second, o_new = (refs[31 + 6 * i : 37 + 6 * i] for i in range(3))
    norms = jnp.sqrt(stats[0:1, :])
    trust = norms / jnp.sqrt(stats[1:2, :])
    o_norms[...] = norms[:, 0:29]
    o_trust[...] = trust[:, 0:29]
    count = stats[0:1, 127:128]
    o_count[...] = count
    errors = jnp.zeros((1, NVAR), F32)
    for j in range(4):
        lane = iota((128, NVAR), 0)
        pick = (lane < NVAR) & (iota((128, NVAR), 1) == 12 * j + lane // P_SIZE)
        errors = errors + nn(stats[4 + j : 5 + j, :], pick.astype(F32), HIGH)
    o_loss[...] = jnp.sum(errors, 1, keepdims=True)
    o_running[...] = STATS_DECAY * running[...] + (1.0 - STATS_DECAY) * errors * (NVAR / count)

    def update(i, at, ratio):
        first, second, direction = adam_direction(
            weights[i][at], grads[i][at], firsts[i][at], seconds[i][at]
        )
        o_first[i][at] = first
        o_second[i][at] = second
        o_new[i][at] = weights[i][at] - LEARN_RATE * ratio * direction

    for i, number, offset in ((0, 4, 0), (1, 4, 4), (2, 2, 8)):
        for j in range(number):
            update(i, j, trust[:, offset + j : offset + j + 1])
    update(3, Ellipsis, trust[:, 10:11])
    update(4, Ellipsis, trust[:, 11:12])
    update(5, Ellipsis, trust[:, 12 : 12 + NVEC])


def finish_call(weights, firsts, seconds, grads, stats, running):
    shapes = [(1, 1), (1, 1), (1, NVAR), (1, 29), (1, 29)] + 3 * [w.shape for w in weights]
    whole = pl.BlockSpec(memory_space=pltpu.VMEM)
    return pl.pallas_call(
        finish,
        out_shape=tuple(jax.ShapeDtypeStruct(s, F32) for s in shapes),
        in_specs=[whole] * 26,
        out_specs=tuple(whole for unused in shapes),
        compiler_params=pltpu.CompilerParams(vmem_limit_bytes=32 * 2**20),
        name="finish",
    )(*weights, *firsts, *seconds, *grads, stats, running)


def on_device(
    pixels,
    targets,
    valid_mask,
    segments,
    lead_index,
    latitude,
    var_ids,
    running_error,
    *tensors,
):
    def turned(group):
        agg, attn, mlp, head, embed, vecs = group
        return (agg, attn, mlp, head, embed.transpose(1, 2, 0).reshape(40, NVAR), vecs.T)

    weights, firsts, seconds = (turned(tensors[6 * i : 6 * i + 6]) for i in range(3))
    large = (pixels.T, targets.T, *weights, *firsts, *seconds)
    small = (
        valid_mask.T,
        segments,
        lead_index,
        latitude.reshape(1, TOK),
        var_ids.reshape(1, NVAR),
    )
    g_emb, g_vec, g_agg, g_attn, g_mlp, g_head, stats = mega_call(large, small)
    grads = (g_agg, g_attn, g_mlp, g_head, g_emb, g_vec)
    out = finish_call(weights, firsts, seconds, grads, stats, running_error.reshape(1, NVAR))

    def back(group):
        agg, attn, mlp, head, embed, vecs = group
        return (agg, attn, mlp, head, embed.reshape(5, 8, NVAR).transpose(2, 0, 1), vecs.T)

    return (
        out[0].reshape(()),
        out[1].reshape(()),
        out[2].reshape(NVAR),
        out[3].reshape(29),
        out[4].reshape(29),
        *back(out[5:11]),
        *back(out[11:17]),
        *back(out[17:23]),
    )


def solution(mesh):
    weights = (
        P(None, "dp", "mp"),
        P(None, "dp", "mp"),
        P(None, "dp", "mp"),
        P("dp", "mp"),
        P(None, None, ("dp", "mp")),
        P(None, ("dp", "mp")),
    )
    in_specs = (
        P("dp", None),
        P("dp", "mp"),
        P("dp", None),
        P("dp", None),
        P("dp", None),
        P("dp"),
        P(),
        P(),
        *weights,
        *weights,
        *weights,
    )
    out_specs = (P(), P(), P(), P(), P(), *weights, *weights, *weights)
    return jax.shard_map(
        on_device, mesh=mesh, in_specs=in_specs, out_specs=out_specs, check_vma=False
    )
```

```python
import math

import jax
import jax.numpy as jnp
from jax import lax
from jax.experimental import pallas as pl
from jax.experimental.pallas import tpu as pltpu
from jax.sharding import PartitionSpec as P

D = 1024
HEAD_DIM = 64
FF = 4096
NVAR = 48
P_SIZE = 4
SEGS = 4
LEADS = 28
LATS = 32
STEP = 10
NVEC = 17
EROWS = NVAR * (P_SIZE + 1)

HIGH = lax.Precision.HIGHEST
NORM_EPS = 1e-06
BETA_ONE = 0.9
BETA_TWO = 0.999
LEARN_RATE = 0.3
WEIGHT_DECAY = 0.01
ADAM_EPS = 1e-08
STATS_DECAY = 0.9
MESH = pl.DeviceIdType.MESH
BF = jnp.bfloat16
F32 = jnp.float32

DPN, MPN, CHIPS, SH, TOK, COLS = 32, 4, 16, 64, 256, 256
NQ = 4
RQ, CH = TOK // NQ, SH // NQ
SCALE = 1.0 / math.sqrt(HEAD_DIM)


def nn(a, b, precision=None):
    return lax.dot_general(
        a, b, (((1,), (0,)), ((), ())), preferred_element_type=F32, precision=precision
    )


def nt(a, b, precision=None):
    return lax.dot_general(
        a, b, (((1,), (1,)), ((), ())), preferred_element_type=F32, precision=precision
    )


def tn(a, b, precision=None):
    return lax.dot_general(
        a, b, (((0,), (0,)), ((), ())), preferred_element_type=F32, precision=precision
    )


def latitude_weights():
    cosines = [
        math.cos(((j + 0.5) * (180.0 / LATS) - 90.0) * (math.pi / 180.0)) for j in range(LATS)
    ]
    mean = sum(cosines) / LATS
    return [value / mean for value in cosines]


def moments_new(gradient, first, second):
    first_new = BETA_ONE * first + (1.0 - BETA_ONE) * gradient
    second_new = BETA_TWO * second + (1.0 - BETA_TWO) * gradient * gradient
    return first_new, second_new


def adam_direction(weight, gradient, first, second):
    first_new, second_new = moments_new(gradient, first, second)
    first_hat = first_new * (1.0 / (1.0 - BETA_ONE**STEP))
    second_hat = second_new * (1.0 / (1.0 - BETA_TWO**STEP))
    direction = first_hat / (jnp.sqrt(second_hat) + ADAM_EPS) + WEIGHT_DECAY * weight
    return (first_new, second_new, direction)


def iota(shape, dim):
    return lax.broadcasted_iota(jnp.int32, shape, dim)


def ln_parts(x):
    centre = jnp.mean(x, -1, keepdims=True)
    shifted = x - centre
    r = lax.rsqrt(jnp.mean(shifted * shifted, -1, keepdims=True) + NORM_EPS)
    return shifted * r, r


def ln_back(n, r, gain, dh):
    e = dh * gain
    dx = r * (e - jnp.mean(e, -1, keepdims=True) - n * jnp.mean(e * n, -1, keepdims=True))
    dgain = jnp.sum(dh * n, 0, keepdims=True)
    dbias = jnp.sum(dh, 0, keepdims=True)
    return dx, dgain, dbias


LARGE = ("pix", "targ", "aggw", "attnw", "mlpw", "headw", "emb", "vec")
MOMENTS = ("agg", "attn", "mlp", "head", "emb", "vec")
SMALL = ("mask", "seg", "leadi", "lat", "vid")
OUTS = ("o_emb", "o_vec", "o_agg", "o_attn", "o_mlp", "o_head", "o_stats")
SHAPES = {
    "pix": ((NVAR * P_SIZE, TOK), BF),
    "targ": ((NVAR, TOK), F32),
    "agg": ((4, 32, 256), F32),
    "attn": ((4, 32, 256), F32),
    "mlp": ((2, 32, 1024), F32),
    "head": ((32, NVAR), F32),
    "emb": ((40, NVAR), F32),
    "vec": ((8, NVEC), F32),
}
SHAPES.update({"aggw": SHAPES["agg"], "attnw": SHAPES["attn"], "mlpw": SHAPES["mlp"]})
SHAPES["headw"] = SHAPES["head"]
FETCH = LARGE + tuple(n + "_f" for n in MOMENTS) + tuple(n + "_s" for n in MOMENTS)


def fetch_shape(name):
    return SHAPES[name[:-2] if name[-2] == "_" else name]


def scratch_list():
    vm = pltpu.VMEM
    dma = pltpu.SemaphoreType.DMA
    items = [
        ("WA3", vm((D, 256), BF)),
        ("WB", vm((D, 1024), BF)),
        ("W1", vm((D, 1024), BF)),
        ("W2", vm((D, 1024), BF)),
        ("HW", vm((D, 512), BF)),
        ("VEC", vm((D, 128), F32)),
        ("VR", vm((128, D), F32)),
        ("VRN", vm((128, D), F32)),
        ("TMPV", vm((D, 128), F32)),
        ("TA", vm((32, 384), F32)),
        ("HWT", vm((32, 128), F32)),
        ("TT", vm((128, TOK), F32)),
        ("TS", vm((NQ, MPN, CH, 128), F32)),
        ("TGT", vm((MPN, NQ, CH, 128), F32)),
        ("ROWS", vm((128, TOK), F32)),
        ("TCOL", vm((TOK, 128), F32)),
        ("LW", vm((TOK, 128), F32)),
        ("PIXT", vm((256, TOK), F32)),
        ("EWP", vm((256, 512), F32)),
        ("EWH", vm((128, 512), F32)),
        ("EWC", vm((128, 512), F32)),
        ("EWR", vm((256, 512), F32)),
        ("PRP", vm((256, 384), F32)),
        ("PRH", vm((128, 384), F32)),
        ("PRC", vm((128, 384), F32)),
        ("PRR", vm((256, 384), F32)),
        ("MT", vm((4, 256, TOK), BF)),
        ("PT", vm((4, NVAR, TOK), F32)),
        ("OAT", vm((256, TOK), F32)),
        ("OA", vm((TOK, 256), BF)),
        ("RSS", vm((5, TOK, D), BF)),
        ("RSR", vm((5, 3, SH, D), BF)),
        ("AG", vm((5, TOK, D), BF)),
        ("QKV", vm((3, TOK, 256), BF)),
        ("PB", vm((4, TOK, TOK), F32)),
        ("OB", vm((TOK, 256), BF)),
        ("DOB", vm((TOK, 256), BF)),
        ("GEL", vm((TOK, 1024), BF)),
        ("GELP", vm((TOK, 1024), F32)),
        ("DU", vm((TOK, 1024), BF)),
        ("DQKV", vm((TOK, 768), BF)),
        ("LN", vm((2, SH, D), F32)),
        ("XS", vm((SH, D), F32)),
        ("RR", vm((2, SH, 128), F32)),
        ("H3", vm((SH, D), BF)),
        ("DP", vm((SH, 512), BF)),
        ("GVT", vm((D, 128), F32)),
        ("GVP", vm((128, D), F32)),
        ("GVN", vm((128, D), F32)),
        ("TG", vm((32, 256), F32)),
        ("TGR", vm((3, 8, 256), F32)),
        ("VG", vm((32, 128), F32)),
        ("VGR", vm((3, 8, 128), F32)),
        ("HG", vm((32, 512), F32)),
        ("HGR", vm((3, 32, 128), F32)),
        ("EG", vm((40, NVAR), F32)),
        ("NX", vm((8, 128), F32)),
        ("NXR", vm((3, 8, 128), F32)),
        ("NY", vm((8, 128), F32)),
        ("NYR", vm((256, 128), F32)),
    ]
    for name, width, kind in (
        ("A3", 256, BF),
        ("B", 1024, BF),
        ("1", 1024, BF),
        ("2", 1024, BF),
        ("H", 512, BF),
        ("V", 128, F32),
    ):
        if name != "V":
            items.append(("G" + name, vm((D, width), kind)))
        items.append(("S" + name, vm((512, width), kind)))
        if name in ("A3", "V"):
            items.append(("B" + name, vm((512, width), kind)))
        else:
            items.append(("FP" + name, vm((2, 3, 128, width // 2), kind)))
            items.append(("FQ" + name, vm((2, 3, 32, width // 2), kind)))
    for name in FETCH:
        items.append(("in_" + name, vm(*fetch_shape(name))))
    items += [
        ("fsem", dma((len(FETCH),))),
        ("ysend", dma((20,))),
        ("yrecv", dma((8,))),
        ("rrecv", dma((5, NQ))),
        ("arecv", dma((5, NQ))),
        ("dsend", dma((19,))),
        ("drecv", dma((19,))),
        ("tsend", dma((8, 4))),
        ("trecv", dma((8, 4))),
        ("ssend", dma((16,))),
        ("srecv", dma((16,))),
    ]
    return items


SCRATCH = scratch_list()
NAMES = tuple(n + "_hbm" for n in FETCH) + SMALL + OUTS + tuple(n for n, unused in SCRATCH)


def mega(*refs):
    r = dict(zip(NAMES, refs))
    step_kernel(type("Refs", (), r))


def step_kernel(R):
    d = lax.axis_index("dp")
    m = lax.axis_index("mp")
    c = lax.rem(d, 2)
    k = d // 2
    z = k // 4
    x = lax.rem(k, 4)
    sib = d + 1 - 2 * c
    rb = pl.multiple_of(c * 512 + k * 32, 32)
    half = pl.multiple_of(c * 512, 512)
    other = pl.multiple_of(512 - c * 512, 512)
    my_slot = pl.ds(pl.multiple_of(m * 128, 128), 128)
    my_eight = pl.ds(pl.multiple_of(m * 8, 8), 8)
    my_cols = pl.ds(pl.multiple_of(m * COLS, COLS), COLS)

    def rcopy(src, dst, ss, rs, dp, mp):
        return pltpu.make_async_remote_copy(
            src_ref=src,
            dst_ref=dst,
            send_sem=ss,
            recv_sem=rs,
            device_id={"dp": dp, "mp": mp},
            device_id_type=MESH,
        )

    def drain(ref, sem):
        pltpu.make_async_copy(ref, ref, sem).wait()

    def loop(first, last, fn):
        def step(i, carry):
            fn(i)
            return carry

        lax.fori_loop(first, last, step, 0)

    def to_peers(fn):
        for i in (2, 1, 3):
            fn(i, lax.rem(m + i, MPN))

    def to_chips(fn):
        def step(i):
            kk = lax.rem(k + i, CHIPS)
            fn(kk, kk * 2 + c)

        loop(1, CHIPS, step)

    def fetch(name):
        i = FETCH.index(name)
        return pltpu.make_async_copy(
            getattr(R, name + "_hbm"), getattr(R, "in_" + name), R.fsem.at[i]
        )

    dsend, drecv, ssend, srecv = R.dsend, R.drecv, R.ssend, R.srecv
    ysend, yrecv = R.ysend, R.yrecv

    def gather_start(buf, g):
        block = buf.at[pl.ds(rb, 32)]
        to_chips(lambda kk, t: rcopy(block, block, dsend.at[g], drecv.at[g], t, m).start())

    def gather_cross(buf, g):
        drain(buf.at[pl.ds(0, 480)], drecv.at[g])
        part = buf.at[pl.ds(half, 512)]
        rcopy(part, part, ssend.at[g], srecv.at[g], sib, m).start()

    def gather_wait(buf, g):
        drain(buf.at[pl.ds(0, 512)], srecv.at[g])

    def gather_end(buf, g):
        drain(buf.at[pl.ds(0, 480)], dsend.at[g])
        drain(buf.at[pl.ds(0, 512)], ssend.at[g])

    def along(axis, i):
        if axis == "x":
            return (z * 4 + lax.rem(x + i, 4)) * 2 + c
        return (lax.rem(z + i, 4) * 4 + x) * 2 + c

    def sides(buf):
        n = buf.shape[1] // 2
        return pl.ds(0, n), pl.ds(n, n)

    def tcopy(src, dst, g, j, t):
        rcopy(src, dst, R.tsend.at[g, j], R.trecv.at[g, j], t, m).start()

    def two_first(buf, g):
        left, right = sides(buf)
        for i in (2, 1, 3):
            block = buf.at[pl.ds(rb, 32), left]
            tcopy(block, block, g, 0, along("x", i))
            block = buf.at[pl.ds(rb, 32), right]
            tcopy(block, block, g, 1, along("z", i))

    def two_second(buf, g):
        left, right = sides(buf)
        drain(buf.at[pl.ds(0, 96), left], R.trecv.at[g, 0])
        block = buf.at[pl.ds(pl.multiple_of(half + z * 128, 128), 128), left]
        for i in (2, 1, 3):
            tcopy(block, block, g, 2, along("z", i))
        drain(buf.at[pl.ds(0, 96), right], R.trecv.at[g, 1])

        def send(zz):
            block = buf.at[pl.ds(pl.multiple_of(half + zz * 128 + x * 32, 32), 32), right]
            for i in (2, 1, 3):
                tcopy(block, block, g, 3, along("x", i))

        loop(0, 4, send)

    def two_cross(buf, g):
        for side, j in zip(sides(buf), (2, 3)):
            drain(buf.at[pl.ds(0, 384), side], R.trecv.at[g, j])
        part = buf.at[pl.ds(half, 512)]
        rcopy(part, part, ssend.at[g], srecv.at[g], sib, m).start()

    def two_end(buf, g):
        left, right = sides(buf)
        for j, rows in ((0, 96), (1, 96), (2, 384), (3, 384)):
            drain(buf.at[pl.ds(0, rows), left if j % 2 == 0 else right], R.tsend.at[g, j])
        drain(buf.at[pl.ds(0, 512)], ssend.at[g])

    def reduce_cross(name, g):
        buf, sbuf = (R.GVT if name == "V" else getattr(R, "G" + name)), getattr(R, "S" + name)
        rcopy(buf.at[pl.ds(other, 512)], sbuf, ssend.at[g], srecv.at[g], sib, m).start()

    def core_sum(name, g):
        buf, sbuf = (R.GVT if name == "V" else getattr(R, "G" + name)), getattr(R, "S" + name)
        drain(sbuf, srecv.at[g])

        def add(i):
            at = pl.multiple_of(i * 128, 128)
            sbuf[pl.ds(at, 128), :] = (
                sbuf[pl.ds(at, 128), :].astype(F32)
                + buf[pl.ds(pl.multiple_of(half + at, 128), 128), :].astype(F32)
            ).astype(sbuf.dtype)

        loop(0, 4, add)

    def reduce_spread(name, g):
        core_sum(name, g)
        sbuf, bbuf = getattr(R, "S" + name), getattr(R, "B" + name)
        land = bbuf.at[pl.ds(pl.multiple_of(k * 32, 32), 32)]

        def send(kk, t):
            src = sbuf.at[pl.ds(pl.multiple_of(kk * 32, 32), 32)]
            rcopy(src, land, dsend.at[g], drecv.at[g], t, m).start()

        to_chips(send)

    def row_block(zz, xx):
        return pl.ds(pl.multiple_of(zz * 128 + xx * 32, 32), 32)

    def fold_first(name, g):
        core_sum(name, g)
        sbuf, pbuf = getattr(R, "S" + name), getattr(R, "FP" + name)
        left, right = sides(sbuf)
        for i in (2, 1, 3):
            zz = lax.rem(z + i, 4)
            src = sbuf.at[pl.ds(pl.multiple_of(zz * 128, 128), 128), left]
            tcopy(src, pbuf.at[0, i - 1], g - 7, 0, along("z", i))

        def send(zz):
            for i in (2, 1, 3):
                src = sbuf.at[row_block(zz, lax.rem(x + i, 4)), right]
                land = pbuf.at[1, i - 1, pl.ds(pl.multiple_of(zz * 32, 32), 32)]
                tcopy(src, land, g - 7, 1, along("x", i))

        loop(0, 4, send)

    def fold_second(name, g):
        sbuf, pbuf, qbuf = getattr(R, "S" + name), getattr(R, "FP" + name), getattr(R, "FQ" + name)
        left, right = sides(sbuf)
        for side, j in ((left, 0), (right, 1)):
            drain(pbuf.at[j], R.trecv.at[g - 7, j])

            def add(i):
                at = row_block(z, i) if j == 0 else row_block(i, x)
                acc = sbuf[at, side].astype(F32)
                for n in range(3):
                    acc = acc + pbuf[j, n, pl.ds(pl.multiple_of(i * 32, 32), 32), :].astype(F32)
                sbuf[at, side] = acc.astype(sbuf.dtype)

            loop(0, 4, add)
            for i in (2, 1, 3):
                if j == 0:
                    src = sbuf.at[row_block(z, lax.rem(x + i, 4)), side]
                    tcopy(src, qbuf.at[0, i - 1], g - 7, 2, along("x", i))
                else:
                    src = sbuf.at[row_block(lax.rem(z + i, 4), x), side]
                    tcopy(src, qbuf.at[1, i - 1], g - 7, 3, along("z", i))

    def fold_end(name, g):
        sbuf, pbuf, qbuf = getattr(R, "S" + name), getattr(R, "FP" + name), getattr(R, "FQ" + name)
        parts = []
        for side, j in zip(sides(sbuf), (0, 1)):
            drain(qbuf.at[j], R.trecv.at[g - 7, 2 + j])
            acc = sbuf[row_block(z, x), side].astype(F32)
            for n in range(3):
                acc = acc + qbuf[j, n].astype(F32)
            parts.append(acc)
            drain(pbuf.at[j], R.tsend.at[g - 7, j])
            drain(qbuf.at[j], R.tsend.at[g - 7, 2 + j])
        drain(sbuf, ssend.at[g])
        return jnp.concatenate(parts, 1)

    def reduce_end(name, g):
        sbuf, bbuf = getattr(R, "S" + name), getattr(R, "B" + name)
        drain(bbuf.at[pl.ds(0, 480)], drecv.at[g])

        def add(i, acc):
            at = pl.multiple_of(lax.rem(k + i, CHIPS) * 32, 32)
            return acc + bbuf[pl.ds(at, 32), :].astype(F32)

        total = lax.fori_loop(
            1, CHIPS, add, sbuf[pl.ds(pl.multiple_of(k * 32, 32), 32), :].astype(F32)
        )
        drain(bbuf.at[pl.ds(0, 480)], dsend.at[g])
        drain(sbuf, ssend.at[g])
        return total

    def all_sum(src, hbuf, cbuf, res, g, hooks):
        mine_half = pl.multiple_of(c * 128, 128)
        rcopy(
            src.at[pl.ds(pl.multiple_of(128 - c * 128, 128), 128)],
            hbuf,
            ssend.at[g],
            srecv.at[g],
            sib,
            m,
        ).start()
        hooks[0]()
        drain(hbuf, srecv.at[g])
        hbuf[...] = hbuf[...] + src[pl.ds(mine_half, 128), :]
        at_k = pl.multiple_of(k * 8, 8)

        def send(kk, t):
            rcopy(
                hbuf.at[pl.ds(pl.multiple_of(kk * 8, 8), 8)],
                cbuf.at[pl.ds(at_k, 8)],
                dsend.at[g],
                drecv.at[g],
                t,
                m,
            ).start()

        to_chips(send)
        hooks[1]()
        drain(cbuf.at[pl.ds(0, 120)], drecv.at[g])

        def add(i, acc):
            at = pl.multiple_of(lax.rem(k + i, CHIPS) * 8, 8)
            return acc + cbuf[pl.ds(at, 8), :]

        total = lax.fori_loop(1, CHIPS, add, hbuf[pl.ds(at_k, 8), :])
        block = pl.ds(pl.multiple_of(mine_half + at_k, 8), 8)
        res[block, :] = total
        part = res.at[block]
        to_chips(lambda kk, t: rcopy(part, part, dsend.at[g + 1], drecv.at[g + 1], t, m).start())
        hooks[2]()
        drain(res.at[pl.ds(0, 120)], drecv.at[g + 1])
        part2 = res.at[pl.ds(mine_half, 128)]
        rcopy(part2, part2, ssend.at[g + 1], srecv.at[g + 1], sib, m).start()
        hooks[3]()
        drain(res.at[pl.ds(0, 128)], srecv.at[g + 1])

    def all_sum_end(hbuf, cbuf, res, g):
        drain(hbuf, ssend.at[g])
        drain(res.at[pl.ds(0, 128)], ssend.at[g + 1])
        drain(cbuf.at[pl.ds(0, 120)], dsend.at[g])
        drain(res.at[pl.ds(0, 120)], dsend.at[g + 1])

    def rows_of(q):
        return pl.ds(pl.multiple_of(q * RQ, RQ), RQ)

    def own_of(q, t):
        return pl.ds(pl.multiple_of(q * RQ + t * CH, CH), CH)

    def local_of(q):
        return pl.ds(pl.multiple_of(q * CH, CH), CH)

    def branch_send(ix, q, left, weight, cols=None):
        for n in range(4):
            at = pl.ds(n * 256, 256)
            w = weight[at, :] if cols is None else weight[at, cols[0] : cols[1]]
            R.RSS[ix, rows_of(q), n * 256 : (n + 1) * 256] = nt(left, w).astype(BF)

        def send(i, t):
            rcopy(
                R.RSS.at[ix, own_of(q, t)],
                R.RSR.at[ix, i - 1, local_of(q)],
                ysend.at[ix],
                R.rrecv.at[ix, q],
                d,
                t,
            ).start()

        to_peers(send)

    def branch_sum(ix, q):
        drain(R.RSR.at[ix, :, pl.ds(0, CH)], R.rrecv.at[ix, q])
        acc = R.RSS[ix, own_of(q, m), :].astype(F32)
        for i in range(3):
            acc = acc + R.RSR[ix, i, local_of(q), :].astype(F32)
        return acc

    def share_send(ix, q, values):
        R.AG[ix, own_of(q, m), :] = values
        block = R.AG.at[ix, own_of(q, m)]
        to_peers(
            lambda i, t: rcopy(block, block, ysend.at[5 + ix], R.arecv.at[ix, q], d, t).start()
        )

    def share_wait(ix, q):
        drain(R.AG.at[ix, pl.ds(0, 3 * CH)], R.arecv.at[ix, q])

    for name in FETCH:
        fetch(name).start()
    bar = pltpu.get_barrier_semaphore()

    def greet(i):
        pl.semaphore_signal(
            bar, inc=1, device_id={"dp": lax.rem(d + i, DPN), "mp": m}, device_id_type=MESH
        )

    for i in range(1, MPN):
        pl.semaphore_signal(
            bar, inc=1, device_id={"dp": d, "mp": lax.rem(m + i, MPN)}, device_id_type=MESH
        )
    loop(1, DPN, greet)

    vhot = (iota((NVAR, NVAR), 0) == R.vid[...]).astype(F32)
    fetch("emb").wait()
    fetch("vec").wait()
    chosen = nn(R.in_emb[...], vhot, HIGH)
    R.TA[my_eight, :] = jnp.zeros((8, 384), F32)
    for p in range(5):
        R.TA[my_eight, p * 48 : (p + 1) * 48] = chosen[p * 8 : (p + 1) * 8, :]
    R.TA[my_eight, 256 : 256 + NVEC] = R.in_vec[...]
    fetch("aggw").wait()
    fetch("headw").wait()
    aw = [R.in_aggw[j].astype(BF) for j in range(3)]
    R.WA3[pl.ds(rb, 32), :] = R.in_aggw[3].astype(BF)
    R.HWT[...] = jnp.zeros_like(R.HWT)
    R.HWT[:, 0:NVAR] = R.in_headw[...]
    R.HW[pl.ds(rb, 32), my_slot] = R.HWT[...].astype(BF)
    fetch("mlpw").wait()
    R.W1[pl.ds(rb, 32), :] = R.in_mlpw[0].astype(BF)
    R.W2[pl.ds(rb, 32), :] = R.in_mlpw[1].astype(BF)
    fetch("attnw").wait()
    for j in range(4):
        R.WB[pl.ds(rb, 32), j * 256 : (j + 1) * 256] = R.in_attnw[j].astype(BF)
    fetch("targ").wait()
    R.TT[NVAR:, :] = jnp.zeros((128 - NVAR, TOK), F32)
    R.TT[0:NVAR, :] = R.in_targ[...]
    turned = R.TT[...].T
    for q in range(NQ):
        for t in range(MPN):
            at = q * RQ + t * CH
            R.TS[q, t] = turned[at : at + CH, :]
    R.TGT[m] = R.TS[:, m]
    R.GVP[...] = jnp.zeros_like(R.GVP)
    R.GVN[...] = jnp.zeros_like(R.GVN)
    R.NX[...] = jnp.zeros_like(R.NX)
    pl.semaphore_wait(bar, DPN + MPN - 2)

    def first_sends(i, t):
        part = R.TA.at[my_eight]
        rcopy(part, part, ysend.at[10], yrecv.at[0], d, t).start()

    def later_sends(i, t):
        slot = R.HW.at[pl.ds(rb, 32), my_slot]
        rcopy(slot, slot, ysend.at[11], yrecv.at[1], d, t).start()
        rcopy(R.TS.at[:, t], R.TGT.at[m], ysend.at[12], yrecv.at[2], d, t).start()

    to_peers(first_sends)
    to_peers(later_sends)

    fetch("pix").wait()
    rows = iota((256, 192), 0)
    cols = iota((256, 192), 1)
    pick = (rows < 192) & ((lax.rem(rows, NVAR) * P_SIZE + rows // NVAR) == cols)
    pixt = nn(pick.astype(BF), R.in_pix[...])
    row_at = iota((256, TOK), 0)
    R.PIXT[...] = jnp.where(row_at < 192, pixt, jnp.where(row_at < EROWS, 1.0, 0.0))

    drain(R.TA.at[pl.ds(0, 24)], yrecv.at[0])
    emb = R.TA[:, 0:256]
    R.EWP[:, 0:256] = tn(emb, aw[1].astype(F32), HIGH)
    R.EWP[:, 256:512] = tn(emb, aw[2].astype(F32), HIGH)
    R.EWP[240:241, 0:256] = jnp.sum(R.TA[:, 256:257] * aw[0].astype(F32), 0, keepdims=True)
    keep = R.mask[...].astype(F32)
    count = jnp.sum(jnp.sum(keep, 1, keepdims=True), 0, keepdims=True) * NVAR
    R.EWP[241:242, 0:128] = jnp.broadcast_to(count, (1, 128))

    def per_patch():
        seg = R.seg[...]
        lead_row = jnp.zeros((1, TOK), F32)
        for s in range(SEGS):
            value = (R.leadi[:, s : s + 1] + 1).astype(F32) / LEADS
            lead_row = jnp.where(seg == s, value, lead_row)
        lat = R.lat[...]
        lat_row = jnp.zeros((1, TOK), F32)
        for j, value in enumerate(latitude_weights()):
            lat_row = jnp.where(lat == j, value, lat_row)
        R.ROWS[...] = jnp.zeros_like(R.ROWS)
        R.ROWS[0:1, :] = seg.astype(F32)
        R.ROWS[1:2, :] = lead_row
        R.ROWS[8:12, :] = keep * lat_row
        R.TCOL[...] = R.ROWS[...].T
        lane = iota((128, 128), 1)
        pick = (lane < NVAR) & (iota((128, 128), 0) == 8 + lax.rem(lane, P_SIZE))
        R.LW[...] = nn(R.TCOL[...], pick.astype(F32), HIGH)

    def own_slot_done():
        drain(R.HW.at[pl.ds(0, 32), pl.ds(0, 384)], yrecv.at[1])
        R.VEC[pl.ds(rb, 32), :] = R.TA[:, 256:384]

    def first_bulk():
        gather_start(R.WA3, 5)
        two_first(R.WB, 1)
        per_patch()

    def bulk():
        two_second(R.WB, 1)
        gather_start(R.VEC, 4)
        two_first(R.W1, 2)
        two_first(R.W2, 3)
        gather_cross(R.WA3, 5)

    all_sum(R.EWP, R.EWH, R.EWC, R.EWR, 6, (own_slot_done, first_bulk, bulk, lambda: None))

    head_of = (iota((256, 128), 0) // HEAD_DIM == iota((256, 128), 1)).astype(F32)
    qa = R.EWR[240:241, 0:256].astype(BF).astype(F32)
    total_count = R.EWR[241:242, 0:1]
    qe = nn(R.EWR[:, 0:256] * (qa * SCALE), head_of, HIGH)
    ewv = R.EWR[:, 256:512].astype(BF)
    for h in range(4):
        scores = R.PIXT[0:48, :] * qe[0:48, h : h + 1]
        for p in range(1, 5):
            at = slice(p * 48, (p + 1) * 48)
            scores = scores + R.PIXT[at, :] * qe[at, h : h + 1]
        e = jnp.exp(scores - jnp.max(scores, 0, keepdims=True))
        probs = e / jnp.sum(e, 0, keepdims=True)
        R.PT[h] = probs
        probs = probs.astype(BF).astype(F32)
        for p in range(5):
            at = slice(p * 48, (p + 1) * 48)
            R.MT[h, at, :] = (probs * R.PIXT[at, :]).astype(BF)
        R.MT[h, 240:256, :] = jnp.zeros((16, TOK), BF)
        R.OAT[h * 64 : (h + 1) * 64, :] = tn(ewv[:, h * 64 : (h + 1) * 64], R.MT[h])
    R.OA[...] = R.OAT[...].T.astype(BF)

    gather_wait(R.WA3, 5)
    loop(0, NQ, lambda q: branch_send(0, q, R.OA[rows_of(q), :], R.WA3))
    two_second(R.W1, 2)
    gather_cross(R.VEC, 4)
    two_cross(R.WB, 1)
    gather_wait(R.VEC, 4)
    R.VR[...] = R.VEC[...].T

    def natural(i):
        at = pl.multiple_of(lax.rem(i, 2) * 512 + (i // 2) * 32, 32)
        R.TMPV[pl.ds(pl.multiple_of(i * 32, 32), 32), :] = R.VEC[pl.ds(at, 32), :]

    loop(0, DPN, natural)
    R.VRN[...] = R.TMPV[...].T

    def vrow(i):
        return R.VR[i : i + 1, :]

    def keep_norm(j, q, n, r):
        R.LN[j, local_of(q), :] = n
        R.RR[j, local_of(q), :] = jnp.broadcast_to(r, (CH, 128))

    def mixed_rows(q):
        lead = R.TCOL[own_of(q, m), 1:2]
        x0 = branch_sum(0, q) + vrow(1) + lead * vrow(2)
        n, r = ln_parts(x0)
        share_send(0, q, (n * vrow(3) + vrow(4)).astype(BF))
        R.XS[local_of(q), :] = x0
        keep_norm(0, q, n, r)

    loop(0, NQ, mixed_rows)
    two_second(R.W2, 3)
    two_first(R.HW, 0)
    gather_wait(R.WB, 1)

    def project(q):
        share_wait(0, q)
        at = rows_of(q)
        h1 = R.AG[0, at, :]
        R.QKV[0, at, :] = (nn(h1, R.WB[:, 0:256]) + R.VRN[5:6, my_cols]).astype(BF)
        R.QKV[1, at, :] = nn(h1, R.WB[:, 256:512]).astype(BF)
        R.QKV[2, at, :] = (nn(h1, R.WB[:, 512:768]) + R.VRN[6:7, my_cols]).astype(BF)

    loop(0, NQ, project)
    seg_row = R.seg[...].astype(F32)

    same = R.TCOL[:, 0:1] == seg_row
    for h in range(4):
        at = slice(h * 64, (h + 1) * 64)
        scores = nt(R.QKV[0, :, at], R.QKV[1, :, at]) * SCALE
        scores = jnp.where(same, scores, -1e30)
        e = jnp.exp(scores - jnp.max(scores, 1, keepdims=True))
        probs = e / jnp.sum(e, 1, keepdims=True)
        R.PB[h] = probs
        R.OB[:, at] = nn(probs.astype(BF), R.QKV[2, :, at]).astype(BF)
    loop(0, NQ, lambda q: branch_send(1, q, R.OB[rows_of(q), :], R.WB, (768, 1024)))
    two_cross(R.W1, 2)
    two_second(R.HW, 0)

    def second_rows(q):
        x1 = R.XS[local_of(q), :] + branch_sum(1, q) + vrow(7)
        n, r = ln_parts(x1)
        share_send(1, q, (n * vrow(8) + vrow(9)).astype(BF))
        R.XS[local_of(q), :] = x1
        keep_norm(1, q, n, r)

    loop(0, NQ, second_rows)
    two_cross(R.W2, 3)
    two_cross(R.HW, 0)
    gather_wait(R.W1, 2)
    gather_wait(R.W2, 3)

    def feed(q):
        share_wait(1, q)
        rows = rows_of(q)
        for n in range(4):
            at = slice(n * 256, (n + 1) * 256)
            u = nn(R.AG[1, rows, :], R.W1[:, at]) + R.VRN[pl.ds(10 + m, 1), at]
            phi = 0.5 * (1.0 + lax.erf(u * (1.0 / math.sqrt(2.0))))
            R.GEL[rows, at] = (u * phi).astype(BF)
            R.GELP[rows, at] = phi + u * jnp.exp(-0.5 * u * u) * (1.0 / math.sqrt(2.0 * math.pi))
        branch_send(2, q, R.GEL[rows, :], R.W2)

    loop(0, NQ, feed)
    gather_wait(R.HW, 0)
    drain(R.TGT.at[pl.ds(0, 3)], yrecv.at[2])

    def head_rows(q):
        here = local_of(q)
        x2 = R.XS[here, :] + branch_sum(2, q) + vrow(14)
        n, r = ln_parts(x2)
        h3 = (n * vrow(15) + vrow(16)).astype(BF)
        R.H3[here, :] = h3
        pred = nn(h3, R.HW[...])
        weight = R.LW[own_of(q, m), :]
        for j in range(4):
            misfit = pred[:, j * 128 : (j + 1) * 128] - R.TGT[j, q]
            weighted = weight * misfit
            R.NX[4 + j : 5 + j, :] = R.NX[4 + j : 5 + j, :] + jnp.sum(
                weighted * misfit, 0, keepdims=True
            )
            R.DP[here, j * 128 : (j + 1) * 128] = (2.0 * weighted / total_count).astype(BF)
        dh3 = nt(R.DP[here, :], R.HW[...])
        dx2, dgain, dbias = ln_back(n, r, vrow(15), dh3)
        share_send(2, q, dx2.astype(BF))
        R.XS[here, :] = dx2
        R.GVP[14:15, :] = R.GVP[14:15, :] + jnp.sum(dx2, 0, keepdims=True)
        R.GVP[15:16, :] = R.GVP[15:16, :] + dgain
        R.GVP[16:17, :] = R.GVP[16:17, :] + dbias

    loop(0, NQ, head_rows)

    def feed_back(q):
        share_wait(2, q)
        rows = rows_of(q)
        for n in range(4):
            at = slice(n * 256, (n + 1) * 256)
            du = (nn(R.AG[2, rows, :], R.W2[:, at]) * R.GELP[rows, at]).astype(BF)
            R.DU[rows, at] = du
            row = pl.ds(10 + m, 1)
            R.GVN[row, at] = R.GVN[row, at] + jnp.sum(du.astype(F32), 0, keepdims=True)
        branch_send(3, q, R.DU[rows, :], R.W1)

    loop(0, NQ, feed_back)

    def pieces(q, fn):
        for j in range(4 // NQ):
            fn(pl.ds(pl.multiple_of((q * (4 // NQ) + j) * 256, 256), 256))

    def grad_two(at):
        R.G2[at, :] = tn(R.AG[2, :, at], R.GEL[...]).astype(BF)

    def grad_one(at):
        R.G1[at, :] = tn(R.AG[1, :, at], R.DU[...]).astype(BF)

    def back_rows(q):
        here = local_of(q)
        n = R.LN[1, here, :]
        dx1, dgain, dbias = ln_back(n, R.RR[1, here, 0:1], vrow(8), branch_sum(3, q))
        dx1 = dx1 + R.XS[here, :]
        share_send(3, q, dx1.astype(BF))
        R.XS[here, :] = dx1
        R.GVP[7:8, :] = R.GVP[7:8, :] + jnp.sum(dx1, 0, keepdims=True)
        R.GVP[8:9, :] = R.GVP[8:9, :] + dgain
        R.GVP[9:10, :] = R.GVP[9:10, :] + dbias
        pieces(q, grad_one)

    for n in range(4):
        grad_two(pl.ds(n * 256, 256))
    reduce_cross("2", 13)
    loop(0, NQ // 2, back_rows)
    fold_first("2", 13)
    loop(NQ // 2, NQ, back_rows)
    reduce_cross("1", 12)
    R.GH[...] = tn(R.H3[...], R.DP[...]).astype(BF)
    reduce_cross("H", 14)

    def out_back(q):
        share_wait(3, q)
        rows = rows_of(q)
        R.DOB[rows, :] = nn(R.AG[3, rows, :], R.WB[:, 768:1024]).astype(BF)

    loop(0, NQ // 2, out_back)
    fold_first("1", 12)
    fold_first("H", 14)
    loop(NQ // 2, NQ, out_back)
    fold_second("2", 13)
    for h in range(4):
        at = slice(h * 64, (h + 1) * 64)
        probs = R.PB[h]
        dout = R.DOB[:, at]
        dv = tn(probs.astype(BF), dout).astype(BF)
        dprob = nt(dout, R.QKV[2, :, at])
        ds = (probs * (dprob - jnp.sum(probs * dprob, 1, keepdims=True))).astype(BF)
        dq = (nn(ds, R.QKV[1, :, at]) * SCALE).astype(BF)
        dk = (tn(ds, R.QKV[0, :, at]) * SCALE).astype(BF)
        R.DQKV[:, h * 64 : (h + 1) * 64] = dq
        R.DQKV[:, 256 + h * 64 : 256 + (h + 1) * 64] = dk
        R.DQKV[:, 512 + h * 64 : 512 + (h + 1) * 64] = dv
    loop(0, NQ, lambda q: branch_send(4, q, R.DQKV[rows_of(q), :], R.WB, (0, 768)))
    R.GVN[5:6, my_cols] = jnp.sum(R.DQKV[:, 0:256].astype(F32), 0, keepdims=True)
    R.GVN[6:7, my_cols] = jnp.sum(R.DQKV[:, 512:768].astype(F32), 0, keepdims=True)

    def grad_attn(at):
        R.GB[at, 0:768] = tn(R.AG[0, :, at], R.DQKV[...]).astype(BF)
        R.GB[at, 768:1024] = tn(R.AG[3, :, at], R.OB[...]).astype(BF)

    def first_rows(q):
        here = local_of(q)
        n = R.LN[0, here, :]
        dx0, dgain, dbias = ln_back(n, R.RR[0, here, 0:1], vrow(3), branch_sum(4, q))
        dx0 = dx0 + R.XS[here, :]
        share_send(4, q, dx0.astype(BF))
        lead = R.TCOL[own_of(q, m), 1:2]
        R.GVP[1:2, :] = R.GVP[1:2, :] + jnp.sum(dx0, 0, keepdims=True)
        R.GVP[2:3, :] = R.GVP[2:3, :] + jnp.sum(lead * dx0, 0, keepdims=True)
        R.GVP[3:4, :] = R.GVP[3:4, :] + dgain
        R.GVP[4:5, :] = R.GVP[4:5, :] + dbias

    loop(0, 4, lambda n: grad_attn(pl.ds(pl.multiple_of(n * 256, 256), 256)))
    reduce_cross("B", 11)
    loop(0, NQ // 2, first_rows)
    fold_first("B", 11)
    loop(NQ // 2, NQ, first_rows)
    fold_second("1", 12)
    fold_second("H", 14)
    R.TMPV[...] = R.GVN[...].T
    R.GVT[...] = R.GVP[...].T

    def permuted(i):
        at = pl.ds(pl.multiple_of(lax.rem(i, 2) * 512 + (i // 2) * 32, 32), 32)
        R.GVT[at, :] = R.GVT[at, :] + R.TMPV[pl.ds(pl.multiple_of(i * 32, 32), 32), :]

    loop(0, DPN, permuted)
    reduce_cross("V", 15)
    reduce_spread("V", 15)

    def mix_back(q):
        share_wait(4, q)
        rows = rows_of(q)
        R.DOB[rows, :] = nn(R.AG[4, rows, :], R.WA3[...]).astype(BF)

    loop(0, NQ, mix_back)
    R.PRP[...] = jnp.zeros_like(R.PRP)
    for h in range(4):
        at = slice(h * 64, (h + 1) * 64)
        dout = R.DOB[:, at]
        through = nt(ewv[:, at], dout)
        dprob = R.PIXT[0:48, :] * through[0:48, :]
        for p in range(1, 5):
            row = slice(p * 48, (p + 1) * 48)
            dprob = dprob + R.PIXT[row, :] * through[row, :]
        probs = R.PT[h]
        ds = (probs * (dprob - jnp.sum(probs * dprob, 0, keepdims=True))).astype(BF).astype(F32)
        for p in range(5):
            row = slice(p * 48, (p + 1) * 48)
            R.PRP[row, 256 + h : 257 + h] = jnp.sum(ds * R.PIXT[row, :], 1, keepdims=True)
        R.PRP[:, at] = nn(R.MT[h], dout)

    lanes = iota((1, 128), 1)
    sums = {"w": jnp.zeros((1, 128), F32), "u": jnp.zeros((1, 128), F32)}

    def square_sum(values):
        return jnp.sum(jnp.sum(values * values, 1, keepdims=True), 0, keepdims=True)

    def tensor(index, weight, gradient, first, second):
        unused, unused2, direction = adam_direction(weight, gradient, first, second)
        here = lanes == index
        sums["w"] = sums["w"] + jnp.where(here, square_sum(weight), 0.0)
        sums["u"] = sums["u"] + jnp.where(here, square_sum(direction), 0.0)

    def hook_first():
        def piece(n):
            at = pl.ds(pl.multiple_of(n * 256, 256), 256)
            R.GA3[at, :] = tn(R.AG[4, :, at], R.OA[...]).astype(BF)

        loop(0, 4, piece)
        reduce_cross("A3", 10)

    def hook_second():
        reduce_spread("A3", 10)
        for name in MOMENTS:
            fetch(name + "_f").wait()
            fetch(name + "_s").wait()
        R.o_mlp[1] = fold_end("2", 13)
        R.o_mlp[0] = fold_end("1", 12)
        fold_second("B", 11)
        for j in range(2):
            tensor(8 + j, R.in_mlpw[j], R.o_mlp[j], R.in_mlp_f[j], R.in_mlp_s[j])

    def hook_third():
        R.HG[...] = fold_end("H", 14)
        R.VG[...] = reduce_end("V", 15)

        def sends(i, t):
            rcopy(
                R.HG.at[:, pl.ds(pl.multiple_of(t * 128, 128), 128)],
                R.HGR.at[i - 1],
                ysend.at[14],
                yrecv.at[4],
                d,
                t,
            ).start()
            rcopy(
                R.VG.at[pl.ds(pl.multiple_of(t * 8, 8), 8)],
                R.VGR.at[i - 1],
                ysend.at[15],
                yrecv.at[5],
                d,
                t,
            ).start()

        to_peers(sends)
        gsum = fold_end("B", 11)
        for j in range(4):
            R.o_attn[j] = gsum[:, j * 256 : (j + 1) * 256]
        for j in range(4):
            tensor(4 + j, R.in_attnw[j], R.o_attn[j], R.in_attn_f[j], R.in_attn_s[j])

    all_sum(R.PRP, R.PRH, R.PRC, R.PRR, 8, (hook_first, hook_second, hook_third, lambda: None))

    spread = nt(R.PRR[:, 256:384], head_of, HIGH)
    dqa = jnp.sum(spread * R.EWR[:, 0:256], 0, keepdims=True) * SCALE
    pk = spread * (qa * SCALE)
    pv = R.PRR[:, 0:256]
    emb = R.TA[:, 0:256]
    wa = [R.in_aggw[j].astype(BF).astype(F32) for j in range(3)]
    R.TG[...] = nt(wa[1], pk, HIGH) + nt(wa[2], pv, HIGH)
    R.TG[:, 240:241] = jnp.sum(wa[0] * dqa, 1, keepdims=True)

    def last_sends(i, t):
        rcopy(
            R.TG.at[pl.ds(pl.multiple_of(t * 8, 8), 8)],
            R.TGR.at[i - 1],
            ysend.at[13],
            yrecv.at[3],
            d,
            t,
        ).start()

    to_peers(last_sends)
    R.o_agg[0] = R.TA[:, 256:257] * dqa
    R.o_agg[1] = nn(emb, pk, HIGH)
    R.o_agg[2] = nn(emb, pv, HIGH)
    R.o_agg[3] = reduce_end("A3", 10)
    for j in range(4):
        tensor(j, R.in_aggw[j], R.o_agg[j], R.in_agg_f[j], R.in_agg_s[j])
    drain(R.HGR, yrecv.at[4])
    hgrad = R.HG[:, my_slot] + R.HGR[0] + R.HGR[1] + R.HGR[2]
    R.o_head[...] = hgrad[:, 0:NVAR]
    tensor(10, R.in_headw[...], R.o_head[...], R.in_head_f[...], R.in_head_s[...])
    drain(R.VGR, yrecv.at[5])
    vgrad = R.VG[my_eight, :] + R.VGR[0] + R.VGR[1] + R.VGR[2]
    drain(R.TGR, yrecv.at[3])
    tgrad = R.TG[my_eight, :] + R.TGR[0] + R.TGR[1] + R.TGR[2]
    for p in range(5):
        R.EG[p * 8 : (p + 1) * 8, :] = tgrad[:, p * 48 : (p + 1) * 48]
    R.o_emb[...] = nt(R.EG[...], vhot, HIGH)
    tensor(11, R.in_emb[...], R.o_emb[...], R.in_emb_f[...], R.in_emb_s[...])
    R.o_vec[...] = vgrad[:, 0:NVEC]
    R.o_vec[:, 0:1] = tgrad[:, 240:241]
    unused, unused2, direction = adam_direction(
        R.in_vec[...], R.o_vec[...], R.in_vec_f[...], R.in_vec_s[...]
    )
    R.NX[0:1, :] = sums["w"]
    R.NX[1:2, :] = sums["u"]
    R.NX[0:1, 12 : 12 + NVEC] = jnp.sum(R.in_vec[...] * R.in_vec[...], 0, keepdims=True)
    R.NX[1:2, 12 : 12 + NVEC] = jnp.sum(direction * direction, 0, keepdims=True)

    to_peers(lambda i, t: rcopy(R.NX, R.NXR.at[i - 1], ysend.at[16], yrecv.at[6], d, t).start())
    drain(R.NXR, yrecv.at[6])
    R.NY[...] = R.NX[...] + R.NXR[0] + R.NXR[1] + R.NXR[2]
    at_d = pl.ds(pl.multiple_of(d * 8, 8), 8)

    def norm_send(i):
        t = lax.rem(d + i, DPN)
        rcopy(R.NY, R.NYR.at[at_d], dsend.at[16], drecv.at[16], t, m).start()

    loop(1, DPN, norm_send)

    gather_end(R.WA3, 5)
    gather_end(R.VEC, 4)
    for buf, g in ((R.HW, 0), (R.WB, 1), (R.W1, 2), (R.W2, 3)):
        two_end(buf, g)
    all_sum_end(R.EWH, R.EWC, R.EWR, 6)
    all_sum_end(R.PRH, R.PRC, R.PRR, 8)
    for ix in range(5):
        drain(R.RSR.at[ix], ysend.at[ix])
        drain(R.AG.at[ix, pl.ds(0, 192)], ysend.at[5 + ix])
    drain(R.TA.at[pl.ds(0, 24)], ysend.at[10])
    drain(R.HW.at[pl.ds(0, 32), pl.ds(0, 384)], ysend.at[11])
    drain(R.TGT.at[pl.ds(0, 3)], ysend.at[12])
    drain(R.TGR, ysend.at[13])
    drain(R.HGR, ysend.at[14])
    drain(R.VGR, ysend.at[15])
    drain(R.NXR, ysend.at[16])

    drain(R.NYR.at[pl.ds(0, 248)], drecv.at[16])

    def norm_add(i, acc):
        at = pl.multiple_of(lax.rem(d + i, DPN) * 8, 8)
        return acc + R.NYR[pl.ds(at, 8), :]

    stats = lax.fori_loop(1, DPN, norm_add, R.NY[...])
    first_lane = (iota((8, 128), 0) == 0) & (iota((8, 128), 1) == 127)
    R.o_stats[...] = jnp.where(first_lane, total_count, stats)
    drain(R.NYR.at[pl.ds(0, 248)], dsend.at[16])


def mega_call(large, small):
    outs = [SHAPES[n] for n in ("emb", "vec", "agg", "attn", "mlp", "head")] + [((8, 128), F32)]
    out_shape = tuple(jax.ShapeDtypeStruct(*item) for item in outs)
    whole = pl.BlockSpec(memory_space=pltpu.VMEM)
    return pl.pallas_call(
        mega,
        out_shape=out_shape,
        in_specs=[pl.BlockSpec(memory_space=pl.ANY)] * len(large) + [whole] * len(small),
        out_specs=tuple(whole for unused in out_shape),
        scratch_shapes=[item for unused, item in SCRATCH],
        compiler_params=pltpu.CompilerParams(
            collective_id=0, has_side_effects=True, vmem_limit_bytes=60 * 2**20
        ),
        name="step",
    )(*large, *small)


def finish(*refs):
    held, sems = refs[49:75], refs[75]
    copies = [pltpu.make_async_copy(refs[i], held[i], sems.at[i]) for i in range(26)]
    for copy in copies[::-1]:
        copy.start()
    o_loss, o_count, o_running, o_trust, o_norms = refs[26:31]
    o_first, o_second, o_new = (refs[31 + 6 * i : 37 + 6 * i] for i in range(3))
    weights, firsts, seconds, grads = (held[6 * i : 6 * i + 6] for i in range(4))
    stats, running = held[24:26]
    for copy in copies[::-1]:
        copy.wait()
    norms = jnp.sqrt(stats[0:1, :])
    trust = norms / jnp.sqrt(stats[1:2, :])
    o_norms[...] = norms[:, 0:29]
    o_trust[...] = trust[:, 0:29]
    count = stats[0:1, 127:128]
    o_count[...] = count
    errors = jnp.zeros((1, NVAR), F32)
    for j in range(4):
        lane = iota((128, NVAR), 0)
        pick = (lane < NVAR) & (iota((128, NVAR), 1) == 12 * j + lane // P_SIZE)
        errors = errors + nn(stats[4 + j : 5 + j, :], pick.astype(F32), HIGH)
    o_loss[...] = jnp.sum(errors, 1, keepdims=True)
    o_running[...] = STATS_DECAY * running[...] + (1.0 - STATS_DECAY) * errors * (NVAR / count)

    def update(i, at, ratio):
        first, second, direction = adam_direction(
            weights[i][at], grads[i][at], firsts[i][at], seconds[i][at]
        )
        o_first[i][at] = first
        o_second[i][at] = second
        o_new[i][at] = weights[i][at] - LEARN_RATE * ratio * direction

    for i, number, offset in ((0, 4, 0), (1, 4, 4), (2, 2, 8)):
        for j in range(number):
            update(i, j, trust[:, offset + j : offset + j + 1])
    update(3, Ellipsis, trust[:, 10:11])
    update(4, Ellipsis, trust[:, 11:12])
    update(5, Ellipsis, trust[:, 12 : 12 + NVEC])


def finish_call(weights, firsts, seconds, grads, stats, running):
    shapes = [(1, 1), (1, 1), (1, NVAR), (1, 29), (1, 29)] + 3 * [w.shape for w in weights]
    whole = pl.BlockSpec(memory_space=pltpu.VMEM)
    values = (*weights, *firsts, *seconds, *grads, stats, running)
    return pl.pallas_call(
        finish,
        out_shape=tuple(jax.ShapeDtypeStruct(s, F32) for s in shapes),
        in_specs=[pl.BlockSpec(memory_space=pl.ANY)] * 26,
        out_specs=tuple(whole for unused in shapes),
        scratch_shapes=[pltpu.VMEM(v.shape, F32) for v in values]
        + [pltpu.SemaphoreType.DMA((26,))],
        compiler_params=pltpu.CompilerParams(vmem_limit_bytes=60 * 2**20),
        name="finish",
    )(*values)


def on_device(
    pixels,
    targets,
    valid_mask,
    segments,
    lead_index,
    latitude,
    var_ids,
    running_error,
    *tensors,
):
    def turned(group):
        agg, attn, mlp, head, embed, vecs = group
        return (agg, attn, mlp, head, embed.transpose(1, 2, 0).reshape(40, NVAR), vecs.T)

    weights, firsts, seconds = (turned(tensors[6 * i : 6 * i + 6]) for i in range(3))
    large = (pixels.T, targets.T, *weights, *firsts, *seconds)
    small = (
        valid_mask.T,
        segments,
        lead_index,
        latitude.reshape(1, TOK),
        var_ids.reshape(1, NVAR),
    )
    g_emb, g_vec, g_agg, g_attn, g_mlp, g_head, stats = mega_call(large, small)
    grads = (g_agg, g_attn, g_mlp, g_head, g_emb, g_vec)
    out = finish_call(weights, firsts, seconds, grads, stats, running_error.reshape(1, NVAR))

    def back(group):
        agg, attn, mlp, head, embed, vecs = group
        return (agg, attn, mlp, head, embed.reshape(5, 8, NVAR).transpose(2, 0, 1), vecs.T)

    return (
        out[0].reshape(()),
        out[1].reshape(()),
        out[2].reshape(NVAR),
        out[3].reshape(29),
        out[4].reshape(29),
        *back(out[5:11]),
        *back(out[11:17]),
        *back(out[17:23]),
    )


def solution(mesh):
    weights = (
        P(None, "dp", "mp"),
        P(None, "dp", "mp"),
        P(None, "dp", "mp"),
        P("dp", "mp"),
        P(None, None, ("dp", "mp")),
        P(None, ("dp", "mp")),
    )
    in_specs = (
        P("dp", None),
        P("dp", "mp"),
        P("dp", None),
        P("dp", None),
        P("dp", None),
        P("dp"),
        P(),
        P(),
        *weights,
        *weights,
        *weights,
    )
    out_specs = (P(), P(), P(), P(), P(), *weights, *weights, *weights)
    return jax.shard_map(
        on_device, mesh=mesh, in_specs=in_specs, out_specs=out_specs, check_vma=False
    )
```

```python
import math

import jax
import jax.numpy as jnp
from jax import lax
from jax.experimental import pallas as pl
from jax.experimental.pallas import tpu as pltpu
from jax.sharding import PartitionSpec as P

D = 1024
HEAD_DIM = 64
FF = 4096
NVAR = 48
P_SIZE = 4
SEGS = 4
LEADS = 28
LATS = 32
STEP = 10
NVEC = 17
EROWS = NVAR * (P_SIZE + 1)

HIGH = lax.Precision.HIGHEST
NORM_EPS = 1e-06
BETA_ONE = 0.9
BETA_TWO = 0.999
LEARN_RATE = 0.3
WEIGHT_DECAY = 0.01
ADAM_EPS = 1e-08
STATS_DECAY = 0.9
MESH = pl.DeviceIdType.MESH
BF = jnp.bfloat16
F32 = jnp.float32

DPN, MPN, CHIPS, SH, TOK, COLS = 32, 4, 16, 64, 256, 256
NQ = 4
RQ, CH = TOK // NQ, SH // NQ
SCALE = 1.0 / math.sqrt(HEAD_DIM)
FAR_FIRST = sorted(
    ((dz, dx) for dz in range(4) for dx in range(4) if dz or dx),
    key=lambda o: -(min(o[0], 4 - o[0]) + min(o[1], 4 - o[1])),
)


def nn(a, b, precision=None):
    return lax.dot_general(
        a, b, (((1,), (0,)), ((), ())), preferred_element_type=F32, precision=precision
    )


def nt(a, b, precision=None):
    return lax.dot_general(
        a, b, (((1,), (1,)), ((), ())), preferred_element_type=F32, precision=precision
    )


def tn(a, b, precision=None):
    return lax.dot_general(
        a, b, (((0,), (0,)), ((), ())), preferred_element_type=F32, precision=precision
    )


def latitude_weights():
    cosines = [
        math.cos(((j + 0.5) * (180.0 / LATS) - 90.0) * (math.pi / 180.0)) for j in range(LATS)
    ]
    mean = sum(cosines) / LATS
    return [value / mean for value in cosines]


def moments_new(gradient, first, second):
    first_new = BETA_ONE * first + (1.0 - BETA_ONE) * gradient
    second_new = BETA_TWO * second + (1.0 - BETA_TWO) * gradient * gradient
    return first_new, second_new


def adam_direction(weight, gradient, first, second):
    first_new, second_new = moments_new(gradient, first, second)
    first_hat = first_new * (1.0 / (1.0 - BETA_ONE**STEP))
    second_hat = second_new * (1.0 / (1.0 - BETA_TWO**STEP))
    direction = first_hat / (jnp.sqrt(second_hat) + ADAM_EPS) + WEIGHT_DECAY * weight
    return (first_new, second_new, direction)


def iota(shape, dim):
    return lax.broadcasted_iota(jnp.int32, shape, dim)


def ln_parts(x):
    centre = jnp.mean(x, -1, keepdims=True)
    shifted = x - centre
    r = lax.rsqrt(jnp.mean(shifted * shifted, -1, keepdims=True) + NORM_EPS)
    return shifted * r, r


def ln_back(n, r, gain, dh):
    e = dh * gain
    dx = r * (e - jnp.mean(e, -1, keepdims=True) - n * jnp.mean(e * n, -1, keepdims=True))
    dgain = jnp.sum(dh * n, 0, keepdims=True)
    dbias = jnp.sum(dh, 0, keepdims=True)
    return dx, dgain, dbias


LARGE = ("pix", "targ", "aggw", "attnw", "mlpw", "headw", "emb", "vec")
MOMENTS = ("agg", "attn", "mlp", "head", "emb", "vec")
SMALL = ("mask", "seg", "leadi", "lat", "vid")
OUTS = ("o_emb", "o_vec", "o_agg", "o_attn", "o_mlp", "o_head", "o_stats")
SHAPES = {
    "pix": ((NVAR * P_SIZE, TOK), BF),
    "targ": ((NVAR, TOK), F32),
    "agg": ((4, 32, 256), F32),
    "attn": ((4, 32, 256), F32),
    "mlp": ((2, 32, 1024), F32),
    "head": ((32, NVAR), F32),
    "emb": ((40, NVAR), F32),
    "vec": ((8, NVEC), F32),
}
SHAPES.update({"aggw": SHAPES["agg"], "attnw": SHAPES["attn"], "mlpw": SHAPES["mlp"]})
SHAPES["headw"] = SHAPES["head"]
FETCH = LARGE + tuple(n + "_f" for n in MOMENTS) + tuple(n + "_s" for n in MOMENTS)


def fetch_shape(name):
    return SHAPES[name[:-2] if name[-2] == "_" else name]


def scratch_list():
    vm = pltpu.VMEM
    dma = pltpu.SemaphoreType.DMA
    items = [
        ("WA3", vm((D, 256), BF)),
        ("WB", vm((D, 1024), BF)),
        ("W1", vm((D, 1024), BF)),
        ("W2", vm((D, 1024), BF)),
        ("HW", vm((D, 256), BF)),
        ("HWS", vm((MPN, 32, 128), BF)),
        ("VPK", vm((256, 128), F32)),
        ("VEC", vm((DPN, 4, 8, 128), F32)),
        ("VR", vm((128, D), F32)),
        ("VRN", vm((128, D), F32)),
        ("TMPV", vm((D, 128), F32)),
        ("TA", vm((32, 384), F32)),
        ("HWT", vm((32, 128), F32)),
        ("TT", vm((128, TOK), F32)),
        ("TS", vm((NQ, MPN, CH, 128), F32)),
        ("TGT", vm((MPN, NQ, CH, 128), F32)),
        ("ROWS", vm((128, TOK), F32)),
        ("TCOL", vm((TOK, 128), F32)),
        ("LW", vm((TOK, 128), F32)),
        ("PIXT", vm((256, TOK), F32)),
        ("EWP", vm((256, 512), F32)),
        ("EWH", vm((128, 512), F32)),
        ("EWC", vm((128, 512), F32)),
        ("EWR", vm((256, 512), F32)),
        ("PRP", vm((256, 384), F32)),
        ("PRH", vm((128, 384), F32)),
        ("PRC", vm((128, 384), F32)),
        ("PRR", vm((256, 384), F32)),
        ("MT", vm((4, 256, TOK), BF)),
        ("PT", vm((4, NVAR, TOK), F32)),
        ("OAT", vm((256, TOK), F32)),
        ("OA", vm((TOK, 256), BF)),
        ("RSS", vm((5, TOK, D), BF)),
        ("RSR", vm((5, 3, SH, D), BF)),
        ("AG", vm((5, TOK, D), BF)),
        ("QKV", vm((3, TOK, 256), BF)),
        ("PB", vm((4, TOK, TOK), F32)),
        ("OB", vm((TOK, 256), BF)),
        ("DOB", vm((TOK, 256), BF)),
        ("GEL", vm((TOK, 1024), BF)),
        ("GELP", vm((TOK, 1024), F32)),
        ("DU", vm((TOK, 1024), BF)),
        ("DQKV", vm((TOK, 768), BF)),
        ("LN", vm((2, SH, D), F32)),
        ("XS", vm((SH, D), F32)),
        ("RR", vm((2, SH, 128), F32)),
        ("H3", vm((SH, D), BF)),
        ("DP", vm((SH, 256), BF)),
        ("GVT", vm((D, 128), F32)),
        ("GVP", vm((128, D), F32)),
        ("GVN", vm((128, D), F32)),
        ("TG", vm((32, 256), F32)),
        ("TGR", vm((3, 8, 256), F32)),
        ("VG", vm((32, 128), F32)),
        ("VGR", vm((3, 8, 128), F32)),
        ("HG", vm((MPN, 32, 128), F32)),
        ("HGR", vm((3, 32, 128), F32)),
        ("EG", vm((40, NVAR), F32)),
        ("NX", vm((8, 128), F32)),
        ("NXR", vm((7, 8, 128), F32)),
        ("NY", vm((8, 128), F32)),
        ("NYR", vm((128, 128), F32)),
    ]
    for name, width, kind in (
        ("A3", 256, BF),
        ("B", 1024, BF),
        ("1", 1024, BF),
        ("2", 1024, BF),
        ("H", 256, BF),
        ("V", 128, F32),
    ):
        if name != "V":
            items.append(("G" + name, vm((D, width), kind)))
        items.append(("S" + name, vm((512, width), kind)))
        if name in ("A3", "V"):
            items.append(("B" + name, vm((512, width), kind)))
        else:
            items.append(("FP" + name, vm((2, 3, 128, width // 2), kind)))
            items.append(("FQ" + name, vm((2, 3, 32, width // 2), kind)))
    for name in FETCH:
        items.append(("in_" + name, vm(*fetch_shape(name))))
    items += [
        ("fsem", dma((len(FETCH),))),
        ("ysend", dma((20,))),
        ("yrecv", dma((8,))),
        ("rrecv", dma((5, NQ))),
        ("arecv", dma((5, NQ))),
        ("dsend", dma((19,))),
        ("drecv", dma((19,))),
        ("tsend", dma((9, 4))),
        ("trecv", dma((9, 4))),
        ("ssend", dma((16,))),
        ("srecv", dma((16,))),
    ]
    return items


SCRATCH = scratch_list()
NAMES = tuple(n + "_hbm" for n in FETCH) + SMALL + OUTS + tuple(n for n, unused in SCRATCH)


def mega(*refs):
    r = dict(zip(NAMES, refs))
    step_kernel(type("Refs", (), r))


def step_kernel(R):
    d = lax.axis_index("dp")
    m = lax.axis_index("mp")
    c = lax.rem(d, 2)
    k = d // 2
    z = k // 4
    x = lax.rem(k, 4)
    sib = d + 1 - 2 * c
    rb = pl.multiple_of(c * 512 + k * 32, 32)
    half = pl.multiple_of(c * 512, 512)
    other = pl.multiple_of(512 - c * 512, 512)
    my_slot = pl.ds(pl.multiple_of(m * 128, 128), 128)
    my_eight = pl.ds(pl.multiple_of(m * 8, 8), 8)
    my_cols = pl.ds(pl.multiple_of(m * COLS, COLS), COLS)

    def rcopy(src, dst, ss, rs, dp, mp):
        return pltpu.make_async_remote_copy(
            src_ref=src,
            dst_ref=dst,
            send_sem=ss,
            recv_sem=rs,
            device_id={"dp": dp, "mp": mp},
            device_id_type=MESH,
        )

    def drain(ref, sem):
        pltpu.make_async_copy(ref, ref, sem).wait()

    def loop(first, last, fn):
        def step(i, carry):
            fn(i)
            return carry

        lax.fori_loop(first, last, step, 0)

    def to_peers(fn):
        for i in (2, 1, 3):
            fn(i, lax.rem(m + i, MPN))

    def to_chips(fn):
        for dz, dx in FAR_FIRST:
            kk = lax.rem(z + dz, 4) * 4 + lax.rem(x + dx, 4)
            fn(kk, kk * 2 + c)

    def fetch(name):
        i = FETCH.index(name)
        return pltpu.make_async_copy(
            getattr(R, name + "_hbm"), getattr(R, "in_" + name), R.fsem.at[i]
        )

    dsend, drecv, ssend, srecv = R.dsend, R.drecv, R.ssend, R.srecv
    ysend, yrecv = R.ysend, R.yrecv

    def gather_start(buf, g):
        block = buf.at[pl.ds(pl.multiple_of(c * 128 + k * 8, 8), 8)]
        to_chips(lambda kk, t: rcopy(block, block, dsend.at[g], drecv.at[g], t, m).start())

    def gather_cross(buf, g):
        drain(buf.at[pl.ds(0, 120)], drecv.at[g])
        part = buf.at[pl.ds(pl.multiple_of(c * 128, 128), 128)]
        rcopy(part, part, ssend.at[g], srecv.at[g], sib, m).start()

    def gather_wait(buf, g):
        drain(buf.at[pl.ds(0, buf.shape[0] // 2)], srecv.at[g])

    def gather_end(buf, g):
        drain(buf.at[pl.ds(0, 120)], dsend.at[g])
        drain(buf.at[pl.ds(0, 128)], ssend.at[g])

    def along(axis, i):
        if axis == "x":
            return (z * 4 + lax.rem(x + i, 4)) * 2 + c
        return (lax.rem(z + i, 4) * 4 + x) * 2 + c

    def sides(buf):
        n = buf.shape[1] // 2
        return pl.ds(0, n), pl.ds(n, n)

    def tcopy(src, dst, g, j, t):
        rcopy(src, dst, R.tsend.at[g, j], R.trecv.at[g, j], t, m).start()

    def two_first(buf, g):
        left, right = sides(buf)
        for i in (2, 1, 3):
            block = buf.at[pl.ds(rb, 32), left]
            tcopy(block, block, g, 0, along("x", i))
            block = buf.at[pl.ds(rb, 32), right]
            tcopy(block, block, g, 1, along("z", i))

    def two_second(buf, g):
        left, right = sides(buf)
        drain(buf.at[pl.ds(0, 96), left], R.trecv.at[g, 0])
        block = buf.at[pl.ds(pl.multiple_of(half + z * 128, 128), 128), left]
        for i in (2, 1, 3):
            tcopy(block, block, g, 2, along("z", i))
        drain(buf.at[pl.ds(0, 96), right], R.trecv.at[g, 1])

        def send(zz):
            block = buf.at[pl.ds(pl.multiple_of(half + zz * 128 + x * 32, 32), 32), right]
            for i in (2, 1, 3):
                tcopy(block, block, g, 3, along("x", i))

        loop(0, 4, send)

    def two_cross(buf, g):
        for side, j in zip(sides(buf), (2, 3)):
            drain(buf.at[pl.ds(0, 384), side], R.trecv.at[g, j])
        part = buf.at[pl.ds(half, 512)]
        g = 5 if g == 8 else g
        rcopy(part, part, ssend.at[g], srecv.at[g], sib, m).start()

    def two_end(buf, g):
        left, right = sides(buf)
        for j, rows in ((0, 96), (1, 96), (2, 384), (3, 384)):
            drain(buf.at[pl.ds(0, rows), left if j % 2 == 0 else right], R.tsend.at[g, j])
        drain(buf.at[pl.ds(0, 512)], ssend.at[5 if g == 8 else g])

    def reduce_cross(name, g):
        buf, sbuf = (R.GVT if name == "V" else getattr(R, "G" + name)), getattr(R, "S" + name)
        rcopy(buf.at[pl.ds(other, 512)], sbuf, ssend.at[g], srecv.at[g], sib, m).start()

    def core_sum(name, g):
        buf, sbuf = (R.GVT if name == "V" else getattr(R, "G" + name)), getattr(R, "S" + name)
        drain(sbuf, srecv.at[g])

        def add(i):
            at = pl.multiple_of(i * 128, 128)
            sbuf[pl.ds(at, 128), :] = (
                sbuf[pl.ds(at, 128), :].astype(F32)
                + buf[pl.ds(pl.multiple_of(half + at, 128), 128), :].astype(F32)
            ).astype(sbuf.dtype)

        loop(0, 4, add)

    def reduce_spread(name, g):
        core_sum(name, g)
        sbuf, bbuf = getattr(R, "S" + name), getattr(R, "B" + name)
        land = bbuf.at[pl.ds(pl.multiple_of(k * 32, 32), 32)]

        def send(kk, t):
            src = sbuf.at[pl.ds(pl.multiple_of(kk * 32, 32), 32)]
            rcopy(src, land, dsend.at[g], drecv.at[g], t, m).start()

        to_chips(send)

    def row_block(zz, xx):
        return pl.ds(pl.multiple_of(zz * 128 + xx * 32, 32), 32)

    def fold_first(name, g):
        core_sum(name, g)
        sbuf, pbuf = getattr(R, "S" + name), getattr(R, "FP" + name)
        left, right = sides(sbuf)
        for i in (2, 1, 3):
            zz = lax.rem(z + i, 4)
            src = sbuf.at[pl.ds(pl.multiple_of(zz * 128, 128), 128), left]
            tcopy(src, pbuf.at[0, i - 1], g - 7, 0, along("z", i))

        def send(zz):
            for i in (2, 1, 3):
                src = sbuf.at[row_block(zz, lax.rem(x + i, 4)), right]
                land = pbuf.at[1, i - 1, pl.ds(pl.multiple_of(zz * 32, 32), 32)]
                tcopy(src, land, g - 7, 1, along("x", i))

        loop(0, 4, send)

    def fold_second(name, g):
        sbuf, pbuf, qbuf = getattr(R, "S" + name), getattr(R, "FP" + name), getattr(R, "FQ" + name)
        left, right = sides(sbuf)
        for side, j in ((left, 0), (right, 1)):
            drain(pbuf.at[j], R.trecv.at[g - 7, j])

            def add(i):
                at = row_block(z, i) if j == 0 else row_block(i, x)
                acc = sbuf[at, side].astype(F32)
                for n in range(3):
                    acc = acc + pbuf[j, n, pl.ds(pl.multiple_of(i * 32, 32), 32), :].astype(F32)
                sbuf[at, side] = acc.astype(sbuf.dtype)

            loop(0, 4, add)
            for i in (2, 1, 3):
                if j == 0:
                    src = sbuf.at[row_block(z, lax.rem(x + i, 4)), side]
                    tcopy(src, qbuf.at[0, i - 1], g - 7, 2, along("x", i))
                else:
                    src = sbuf.at[row_block(lax.rem(z + i, 4), x), side]
                    tcopy(src, qbuf.at[1, i - 1], g - 7, 3, along("z", i))

    def fold_end(name, g):
        sbuf, pbuf, qbuf = getattr(R, "S" + name), getattr(R, "FP" + name), getattr(R, "FQ" + name)
        parts = []
        for side, j in zip(sides(sbuf), (0, 1)):
            drain(qbuf.at[j], R.trecv.at[g - 7, 2 + j])
            acc = sbuf[row_block(z, x), side].astype(F32)
            for n in range(3):
                acc = acc + qbuf[j, n].astype(F32)
            parts.append(acc)
            drain(pbuf.at[j], R.tsend.at[g - 7, j])
            drain(qbuf.at[j], R.tsend.at[g - 7, 2 + j])
        drain(sbuf, ssend.at[g])
        return jnp.concatenate(parts, 1)

    def reduce_end(name, g):
        sbuf, bbuf = getattr(R, "S" + name), getattr(R, "B" + name)
        drain(bbuf.at[pl.ds(0, 480)], drecv.at[g])

        def add(i, acc):
            at = pl.multiple_of(lax.rem(k + i, CHIPS) * 32, 32)
            return acc + bbuf[pl.ds(at, 32), :].astype(F32)

        total = lax.fori_loop(
            1, CHIPS, add, sbuf[pl.ds(pl.multiple_of(k * 32, 32), 32), :].astype(F32)
        )
        drain(bbuf.at[pl.ds(0, 480)], dsend.at[g])
        drain(sbuf, ssend.at[g])
        return total

    def all_sum(src, hbuf, cbuf, res, g, hooks):
        mine_half = pl.multiple_of(c * 128, 128)
        rcopy(
            src.at[pl.ds(pl.multiple_of(128 - c * 128, 128), 128)],
            hbuf,
            ssend.at[g],
            srecv.at[g],
            sib,
            m,
        ).start()
        hooks[0]()
        drain(hbuf, srecv.at[g])
        hbuf[...] = hbuf[...] + src[pl.ds(mine_half, 128), :]
        at_k = pl.multiple_of(k * 8, 8)

        def send(kk, t):
            rcopy(
                hbuf.at[pl.ds(pl.multiple_of(kk * 8, 8), 8)],
                cbuf.at[pl.ds(at_k, 8)],
                dsend.at[g],
                drecv.at[g],
                t,
                m,
            ).start()

        to_chips(send)
        hooks[1]()
        drain(cbuf.at[pl.ds(0, 120)], drecv.at[g])

        def add(i, acc):
            at = pl.multiple_of(lax.rem(k + i, CHIPS) * 8, 8)
            return acc + cbuf[pl.ds(at, 8), :]

        total = lax.fori_loop(1, CHIPS, add, hbuf[pl.ds(at_k, 8), :])
        block = pl.ds(pl.multiple_of(mine_half + at_k, 8), 8)
        res[block, :] = total
        part = res.at[block]
        to_chips(lambda kk, t: rcopy(part, part, dsend.at[g + 1], drecv.at[g + 1], t, m).start())
        hooks[2]()
        drain(res.at[pl.ds(0, 120)], drecv.at[g + 1])
        part2 = res.at[pl.ds(mine_half, 128)]
        rcopy(part2, part2, ssend.at[g + 1], srecv.at[g + 1], sib, m).start()
        hooks[3]()
        drain(res.at[pl.ds(0, 128)], srecv.at[g + 1])

    def all_sum_end(hbuf, cbuf, res, g):
        drain(hbuf, ssend.at[g])
        drain(res.at[pl.ds(0, 128)], ssend.at[g + 1])
        drain(cbuf.at[pl.ds(0, 120)], dsend.at[g])
        drain(res.at[pl.ds(0, 120)], dsend.at[g + 1])

    def rows_of(q):
        return pl.ds(pl.multiple_of(q * RQ, RQ), RQ)

    def own_of(q, t):
        return pl.ds(pl.multiple_of(q * RQ + t * CH, CH), CH)

    def local_of(q):
        return pl.ds(pl.multiple_of(q * CH, CH), CH)

    def branch_send(ix, q, left, weight, cols=None):
        for n in range(4):
            at = pl.ds(n * 256, 256)
            w = weight[at, :] if cols is None else weight[at, cols[0] : cols[1]]
            R.RSS[ix, rows_of(q), n * 256 : (n + 1) * 256] = nt(left, w).astype(BF)

        def send(i, t):
            rcopy(
                R.RSS.at[ix, own_of(q, t)],
                R.RSR.at[ix, i - 1, local_of(q)],
                ysend.at[ix],
                R.rrecv.at[ix, q],
                d,
                t,
            ).start()

        to_peers(send)

    def branch_sum(ix, q):
        drain(R.RSR.at[ix, :, pl.ds(0, CH)], R.rrecv.at[ix, q])
        acc = R.RSS[ix, own_of(q, m), :].astype(F32)
        for i in range(3):
            acc = acc + R.RSR[ix, i, local_of(q), :].astype(F32)
        return acc

    def share_send(ix, q, values):
        R.AG[ix, own_of(q, m), :] = values
        block = R.AG.at[ix, own_of(q, m)]
        to_peers(
            lambda i, t: rcopy(block, block, ysend.at[5 + ix], R.arecv.at[ix, q], d, t).start()
        )

    def share_wait(ix, q):
        drain(R.AG.at[ix, pl.ds(0, 3 * CH)], R.arecv.at[ix, q])

    for name in FETCH:
        fetch(name).start()
    bar = pltpu.get_barrier_semaphore()

    def greet(i):
        pl.semaphore_signal(
            bar, inc=1, device_id={"dp": lax.rem(d + i, DPN), "mp": m}, device_id_type=MESH
        )

    for i in range(1, MPN):
        pl.semaphore_signal(
            bar, inc=1, device_id={"dp": d, "mp": lax.rem(m + i, MPN)}, device_id_type=MESH
        )
    loop(1, DPN, greet)
    for i in range(1, MPN):
        pl.semaphore_signal(
            bar, inc=1, device_id={"dp": sib, "mp": lax.rem(m + i, MPN)}, device_id_type=MESH
        )

    vhot = (iota((NVAR, NVAR), 0) == R.vid[...]).astype(F32)
    fetch("emb").wait()
    fetch("vec").wait()
    chosen = nn(R.in_emb[...], vhot, HIGH)
    R.TA[my_eight, :] = jnp.zeros((8, 384), F32)
    for p in range(5):
        R.TA[my_eight, p * 48 : (p + 1) * 48] = chosen[p * 8 : (p + 1) * 8, :]
    R.TA[my_eight, 256 : 256 + NVEC] = R.in_vec[...]
    fetch("aggw").wait()
    fetch("headw").wait()
    aw = [R.in_aggw[j].astype(BF) for j in range(3)]
    R.WA3[pl.ds(rb, 32), :] = R.in_aggw[3].astype(BF)
    R.HWT[...] = jnp.zeros_like(R.HWT)
    R.HWT[:, 0:NVAR] = R.in_headw[...]
    R.HWS[m] = R.HWT[...].astype(BF)
    fetch("mlpw").wait()
    R.W1[pl.ds(rb, 32), :] = R.in_mlpw[0].astype(BF)
    R.W2[pl.ds(rb, 32), :] = R.in_mlpw[1].astype(BF)
    fetch("attnw").wait()
    for j in range(4):
        R.WB[pl.ds(rb, 32), j * 256 : (j + 1) * 256] = R.in_attnw[j].astype(BF)
    fetch("targ").wait()
    R.TT[NVAR:, :] = jnp.zeros((128 - NVAR, TOK), F32)
    R.TT[0:NVAR, :] = R.in_targ[...]
    turned = R.TT[...].T
    for q in range(NQ):
        for t in range(MPN):
            at = q * RQ + t * CH
            R.TS[q, t] = turned[at : at + CH, :]
    R.TGT[m] = R.TS[:, m]
    R.GVP[...] = jnp.zeros_like(R.GVP)
    R.GVN[...] = jnp.zeros_like(R.GVN)
    R.NX[...] = jnp.zeros_like(R.NX)
    R.HG[...] = jnp.zeros_like(R.HG)
    pl.semaphore_wait(bar, DPN + 2 * MPN - 3)

    def first_sends(i, t):
        part = R.TA.at[my_eight]
        rcopy(part, part, ysend.at[10], yrecv.at[0], d, t).start()

    def later_sends(i, t):
        slot = R.HWS.at[m]
        rcopy(slot, slot, ysend.at[11], yrecv.at[1], d, t).start()
        rcopy(R.TS.at[:, t], R.TGT.at[m], ysend.at[12], yrecv.at[2], d, t).start()

    to_peers(first_sends)
    two_first(R.WA3, 8)
    two_first(R.WB, 1)
    two_first(R.W1, 2)
    two_first(R.W2, 3)
    to_peers(later_sends)

    fetch("pix").wait()
    rows = iota((256, 192), 0)
    cols = iota((256, 192), 1)
    pick = (rows < 192) & ((lax.rem(rows, NVAR) * P_SIZE + rows // NVAR) == cols)
    pixt = nn(pick.astype(BF), R.in_pix[...])
    row_at = iota((256, TOK), 0)
    R.PIXT[...] = jnp.where(row_at < 192, pixt, jnp.where(row_at < EROWS, 1.0, 0.0))

    drain(R.TA.at[pl.ds(0, 24)], yrecv.at[0])
    emb = R.TA[:, 0:256]
    R.EWP[:, 0:256] = tn(emb, aw[1].astype(F32), HIGH)
    R.EWP[:, 256:512] = tn(emb, aw[2].astype(F32), HIGH)
    R.EWP[240:241, 0:256] = jnp.sum(R.TA[:, 256:257] * aw[0].astype(F32), 0, keepdims=True)
    keep = R.mask[...].astype(F32)
    count = jnp.sum(jnp.sum(keep, 1, keepdims=True), 0, keepdims=True) * NVAR
    R.EWP[241:242, 0:128] = jnp.broadcast_to(count, (1, 128))

    def per_patch():
        seg = R.seg[...]
        lead_row = jnp.zeros((1, TOK), F32)
        for s in range(SEGS):
            value = (R.leadi[:, s : s + 1] + 1).astype(F32) / LEADS
            lead_row = jnp.where(seg == s, value, lead_row)
        lat = R.lat[...]
        lat_row = jnp.zeros((1, TOK), F32)
        for j, value in enumerate(latitude_weights()):
            lat_row = jnp.where(lat == j, value, lat_row)
        R.ROWS[...] = jnp.zeros_like(R.ROWS)
        R.ROWS[0:1, :] = seg.astype(F32)
        R.ROWS[1:2, :] = lead_row
        R.ROWS[8:12, :] = keep * lat_row
        R.TCOL[...] = R.ROWS[...].T
        lane = iota((128, 128), 1)
        pick = (lane < NVAR) & (iota((128, 128), 0) == 8 + lax.rem(lane, P_SIZE))
        R.LW[...] = nn(R.TCOL[...], pick.astype(F32), HIGH)

    def own_vectors():
        at = pl.ds(pl.multiple_of(c * 128 + k * 8, 8), 8)
        for g in range(4):
            R.VPK[at, 32 * g : 32 * (g + 1)] = R.TA[8 * g : 8 * (g + 1), 256:288]

    def first_bulk():
        two_second(R.WA3, 8)
        gather_start(R.VPK, 4)
        per_patch()

    def bulk():
        two_second(R.WB, 1)
        gather_cross(R.VPK, 4)
        two_cross(R.WA3, 8)

    all_sum(R.EWP, R.EWH, R.EWC, R.EWR, 6, (own_vectors, first_bulk, bulk, lambda: None))

    head_of = (iota((256, 128), 0) // HEAD_DIM == iota((256, 128), 1)).astype(F32)
    qa = R.EWR[240:241, 0:256].astype(BF).astype(F32)
    total_count = R.EWR[241:242, 0:1]
    qe = nn(R.EWR[:, 0:256] * (qa * SCALE), head_of, HIGH)
    ewv = R.EWR[:, 256:512].astype(BF)
    for h in range(4):
        scores = R.PIXT[0:48, :] * qe[0:48, h : h + 1]
        for p in range(1, 5):
            at = slice(p * 48, (p + 1) * 48)
            scores = scores + R.PIXT[at, :] * qe[at, h : h + 1]
        e = jnp.exp(scores - jnp.max(scores, 0, keepdims=True))
        probs = e / jnp.sum(e, 0, keepdims=True)
        R.PT[h] = probs
        probs = probs.astype(BF).astype(F32)
        for p in range(5):
            at = slice(p * 48, (p + 1) * 48)
            R.MT[h, at, :] = (probs * R.PIXT[at, :]).astype(BF)
        R.MT[h, 240:256, :] = jnp.zeros((16, TOK), BF)
        R.OAT[h * 64 : (h + 1) * 64, :] = tn(ewv[:, h * 64 : (h + 1) * 64], R.MT[h])
    R.OA[...] = R.OAT[...].T.astype(BF)

    gather_wait(R.WA3, 5)
    loop(0, NQ, lambda q: branch_send(0, q, R.OA[rows_of(q), :], R.WA3))
    two_second(R.W1, 2)
    gather_wait(R.VPK, 4)
    packed = R.VPK[...].reshape(DPN, 8, 128)
    for g in range(4):
        R.VEC[:, g, :, 0:32] = packed[:, :, 32 * g : 32 * (g + 1)]
    R.VR[...] = R.VEC[...].reshape(D, 128).T
    two_cross(R.WB, 1)

    def vrow(i):
        return R.VR[i : i + 1, :]

    def keep_norm(j, q, n, r):
        R.LN[j, local_of(q), :] = n
        R.RR[j, local_of(q), :] = jnp.broadcast_to(r, (CH, 128))

    def mixed_rows(q):
        lead = R.TCOL[own_of(q, m), 1:2]
        x0 = branch_sum(0, q) + vrow(1) + lead * vrow(2)
        n, r = ln_parts(x0)
        share_send(0, q, (n * vrow(3) + vrow(4)).astype(BF))
        R.XS[local_of(q), :] = x0
        keep_norm(0, q, n, r)

    loop(0, NQ, mixed_rows)
    two_second(R.W2, 3)

    def natural(i):
        block = R.VEC[lax.rem(i, 2) * 16 + i // 2]
        R.TMPV[pl.ds(pl.multiple_of(i * 32, 32), 32), :] = block.reshape(32, 128)

    loop(0, DPN, natural)
    R.VRN[...] = R.TMPV[...].T
    drain(R.HWS.at[pl.ds(0, 3)], yrecv.at[1])
    R.HW[pl.ds(rb, 32), :] = jnp.concatenate(
        [R.HWS[j].astype(F32)[:, 0:64] for j in range(MPN)], 1
    ).astype(BF)
    two_first(R.HW, 0)
    gather_wait(R.WB, 1)

    def project(q):
        share_wait(0, q)
        at = rows_of(q)
        h1 = R.AG[0, at, :]
        R.QKV[0, at, :] = (nn(h1, R.WB[:, 0:256]) + R.VRN[5:6, my_cols]).astype(BF)
        R.QKV[1, at, :] = nn(h1, R.WB[:, 256:512]).astype(BF)
        R.QKV[2, at, :] = (nn(h1, R.WB[:, 512:768]) + R.VRN[6:7, my_cols]).astype(BF)

    loop(0, NQ, project)
    seg_row = R.seg[...].astype(F32)

    same = R.TCOL[:, 0:1] == seg_row
    for h in range(4):
        at = slice(h * 64, (h + 1) * 64)
        scores = nt(R.QKV[0, :, at], R.QKV[1, :, at]) * SCALE
        scores = jnp.where(same, scores, -1e30)
        e = jnp.exp(scores - jnp.max(scores, 1, keepdims=True))
        probs = e / jnp.sum(e, 1, keepdims=True)
        R.PB[h] = probs
        R.OB[:, at] = nn(probs.astype(BF), R.QKV[2, :, at]).astype(BF)
    loop(0, NQ, lambda q: branch_send(1, q, R.OB[rows_of(q), :], R.WB, (768, 1024)))
    two_cross(R.W1, 2)

    def second_rows(q):
        x1 = R.XS[local_of(q), :] + branch_sum(1, q) + vrow(7)
        n, r = ln_parts(x1)
        share_send(1, q, (n * vrow(8) + vrow(9)).astype(BF))
        R.XS[local_of(q), :] = x1
        keep_norm(1, q, n, r)

    loop(0, NQ // 2, second_rows)
    two_cross(R.W2, 3)
    loop(NQ // 2, NQ, second_rows)
    two_second(R.HW, 0)
    gather_wait(R.W1, 2)
    gather_wait(R.W2, 3)

    def feed(q):
        share_wait(1, q)
        rows = rows_of(q)
        for n in range(4):
            at = slice(n * 256, (n + 1) * 256)
            u = nn(R.AG[1, rows, :], R.W1[:, at]) + R.VRN[pl.ds(10 + m, 1), at]
            phi = 0.5 * (1.0 + lax.erf(u * (1.0 / math.sqrt(2.0))))
            R.GEL[rows, at] = (u * phi).astype(BF)
            R.GELP[rows, at] = phi + u * jnp.exp(-0.5 * u * u) * (1.0 / math.sqrt(2.0 * math.pi))
        branch_send(2, q, R.GEL[rows, :], R.W2)

    loop(0, NQ - 1, feed)
    two_cross(R.HW, 0)
    loop(NQ - 1, NQ, feed)
    gather_wait(R.HW, 0)
    drain(R.TGT.at[pl.ds(0, 3)], yrecv.at[2])

    def head_rows(q):
        here = local_of(q)
        x2 = R.XS[here, :] + branch_sum(2, q) + vrow(14)
        n, r = ln_parts(x2)
        h3 = (n * vrow(15) + vrow(16)).astype(BF)
        R.H3[here, :] = h3
        pred = nn(h3, R.HW[...])
        weight = R.LW[own_of(q, m), 0:64]
        for j in range(4):
            misfit = pred[:, j * 64 : (j + 1) * 64] - R.TGT[j, q, :, 0:64]
            weighted = weight * misfit
            R.NX[4 + j : 5 + j, 0:64] = R.NX[4 + j : 5 + j, 0:64] + jnp.sum(
                weighted * misfit, 0, keepdims=True
            )
            R.DP[here, j * 64 : (j + 1) * 64] = (2.0 * weighted / total_count).astype(BF)
        dh3 = nt(R.DP[here, :], R.HW[...])
        dx2, dgain, dbias = ln_back(n, r, vrow(15), dh3)
        share_send(2, q, dx2.astype(BF))
        R.XS[here, :] = dx2
        R.GVP[14:15, :] = R.GVP[14:15, :] + jnp.sum(dx2, 0, keepdims=True)
        R.GVP[15:16, :] = R.GVP[15:16, :] + dgain
        R.GVP[16:17, :] = R.GVP[16:17, :] + dbias

    loop(0, NQ, head_rows)

    def feed_back(q):
        share_wait(2, q)
        rows = rows_of(q)
        for n in range(4):
            at = slice(n * 256, (n + 1) * 256)
            du = (nn(R.AG[2, rows, :], R.W2[:, at]) * R.GELP[rows, at]).astype(BF)
            R.DU[rows, at] = du
            row = pl.ds(10 + m, 1)
            R.GVN[row, at] = R.GVN[row, at] + jnp.sum(du.astype(F32), 0, keepdims=True)
        branch_send(3, q, R.DU[rows, :], R.W1)

    loop(0, NQ, feed_back)

    def pieces(q, fn):
        for j in range(4 // NQ):
            fn(pl.ds(pl.multiple_of((q * (4 // NQ) + j) * 256, 256), 256))

    def grad_two(at):
        R.G2[at, :] = tn(R.AG[2, :, at], R.GEL[...]).astype(BF)

    def grad_one(at):
        R.G1[at, :] = tn(R.AG[1, :, at], R.DU[...]).astype(BF)

    def back_rows(q):
        here = local_of(q)
        n = R.LN[1, here, :]
        dx1, dgain, dbias = ln_back(n, R.RR[1, here, 0:1], vrow(8), branch_sum(3, q))
        dx1 = dx1 + R.XS[here, :]
        share_send(3, q, dx1.astype(BF))
        R.XS[here, :] = dx1
        R.GVP[7:8, :] = R.GVP[7:8, :] + jnp.sum(dx1, 0, keepdims=True)
        R.GVP[8:9, :] = R.GVP[8:9, :] + dgain
        R.GVP[9:10, :] = R.GVP[9:10, :] + dbias
        pieces(q, grad_one)

    for n in range(4):
        grad_two(pl.ds(n * 256, 256))
    reduce_cross("2", 13)
    loop(0, NQ // 2, back_rows)
    fold_first("2", 13)
    loop(NQ // 2, NQ, back_rows)
    reduce_cross("1", 12)
    R.GH[...] = tn(R.H3[...], R.DP[...]).astype(BF)
    reduce_cross("H", 14)

    def out_back(q):
        share_wait(3, q)
        rows = rows_of(q)
        R.DOB[rows, :] = nn(R.AG[3, rows, :], R.WB[:, 768:1024]).astype(BF)

    loop(0, NQ // 2, out_back)
    fold_first("1", 12)
    fold_first("H", 14)
    loop(NQ // 2, NQ, out_back)
    for h in range(4):
        at = slice(h * 64, (h + 1) * 64)
        probs = R.PB[h]
        dout = R.DOB[:, at]
        dv = tn(probs.astype(BF), dout).astype(BF)
        dprob = nt(dout, R.QKV[2, :, at])
        ds = (probs * (dprob - jnp.sum(probs * dprob, 1, keepdims=True))).astype(BF)
        dq = (nn(ds, R.QKV[1, :, at]) * SCALE).astype(BF)
        dk = (tn(ds, R.QKV[0, :, at]) * SCALE).astype(BF)
        R.DQKV[:, h * 64 : (h + 1) * 64] = dq
        R.DQKV[:, 256 + h * 64 : 256 + (h + 1) * 64] = dk
        R.DQKV[:, 512 + h * 64 : 512 + (h + 1) * 64] = dv
    loop(0, NQ, lambda q: branch_send(4, q, R.DQKV[rows_of(q), :], R.WB, (0, 768)))
    fold_second("2", 13)
    R.GVN[5:6, my_cols] = jnp.sum(R.DQKV[:, 0:256].astype(F32), 0, keepdims=True)
    R.GVN[6:7, my_cols] = jnp.sum(R.DQKV[:, 512:768].astype(F32), 0, keepdims=True)

    def grad_attn(at):
        R.GB[at, 0:768] = tn(R.AG[0, :, at], R.DQKV[...]).astype(BF)
        R.GB[at, 768:1024] = tn(R.AG[3, :, at], R.OB[...]).astype(BF)

    def first_rows(q):
        here = local_of(q)
        n = R.LN[0, here, :]
        dx0, dgain, dbias = ln_back(n, R.RR[0, here, 0:1], vrow(3), branch_sum(4, q))
        dx0 = dx0 + R.XS[here, :]
        share_send(4, q, dx0.astype(BF))
        lead = R.TCOL[own_of(q, m), 1:2]
        R.GVP[1:2, :] = R.GVP[1:2, :] + jnp.sum(dx0, 0, keepdims=True)
        R.GVP[2:3, :] = R.GVP[2:3, :] + jnp.sum(lead * dx0, 0, keepdims=True)
        R.GVP[3:4, :] = R.GVP[3:4, :] + dgain
        R.GVP[4:5, :] = R.GVP[4:5, :] + dbias

    loop(0, 4, lambda n: grad_attn(pl.ds(pl.multiple_of(n * 256, 256), 256)))
    reduce_cross("B", 11)
    loop(0, NQ // 2, first_rows)
    fold_first("B", 11)
    loop(NQ // 2, NQ, first_rows)
    fold_second("1", 12)
    fold_second("H", 14)
    R.TMPV[...] = R.GVN[...].T
    R.GVT[...] = R.GVP[...].T

    def permuted(i):
        at = pl.ds(pl.multiple_of(lax.rem(i, 2) * 512 + (i // 2) * 32, 32), 32)
        R.GVT[at, :] = R.GVT[at, :] + R.TMPV[pl.ds(pl.multiple_of(i * 32, 32), 32), :]

    loop(0, DPN, permuted)
    reduce_cross("V", 15)

    def mix_back(q):
        share_wait(4, q)
        rows = rows_of(q)
        R.DOB[rows, :] = nn(R.AG[4, rows, :], R.WA3[...]).astype(BF)

    loop(0, NQ, mix_back)
    reduce_spread("V", 15)
    fold_second("B", 11)
    R.PRP[...] = jnp.zeros_like(R.PRP)
    for h in range(4):
        at = slice(h * 64, (h + 1) * 64)
        dout = R.DOB[:, at]
        through = nt(ewv[:, at], dout)
        dprob = R.PIXT[0:48, :] * through[0:48, :]
        for p in range(1, 5):
            row = slice(p * 48, (p + 1) * 48)
            dprob = dprob + R.PIXT[row, :] * through[row, :]
        probs = R.PT[h]
        ds = (probs * (dprob - jnp.sum(probs * dprob, 0, keepdims=True))).astype(BF).astype(F32)
        for p in range(5):
            row = slice(p * 48, (p + 1) * 48)
            R.PRP[row, 256 + h : 257 + h] = jnp.sum(ds * R.PIXT[row, :], 1, keepdims=True)
        R.PRP[:, at] = nn(R.MT[h], dout)

    lanes = iota((1, 128), 1)
    sums = {"w": jnp.zeros((1, 128), F32), "u": jnp.zeros((1, 128), F32)}

    def square_sum(values):
        return jnp.sum(jnp.sum(values * values, 1, keepdims=True), 0, keepdims=True)

    def tensor(index, weight, gradient, first, second):
        unused, unused2, direction = adam_direction(weight, gradient, first, second)
        here = lanes == index
        sums["w"] = sums["w"] + jnp.where(here, square_sum(weight), 0.0)
        sums["u"] = sums["u"] + jnp.where(here, square_sum(direction), 0.0)

    def hook_first():
        def piece(n):
            at = pl.ds(pl.multiple_of(n * 256, 256), 256)
            R.GA3[at, :] = tn(R.AG[4, :, at], R.OA[...]).astype(BF)

        loop(0, 4, piece)
        reduce_cross("A3", 10)

    def hook_second():
        for name in MOMENTS:
            fetch(name + "_f").wait()
            fetch(name + "_s").wait()
        R.o_mlp[1] = fold_end("2", 13)
        R.o_mlp[0] = fold_end("1", 12)
        for j in range(2):
            tensor(8 + j, R.in_mlpw[j], R.o_mlp[j], R.in_mlp_f[j], R.in_mlp_s[j])

    def hook_third():
        reduce_spread("A3", 10)
        total = fold_end("H", 14)
        for j in range(MPN):
            R.HG[j, :, 0:64] = total[:, 64 * j : 64 * (j + 1)]
        R.VG[...] = reduce_end("V", 15)

        def sends(i, t):
            rcopy(
                R.HG.at[t],
                R.HGR.at[i - 1],
                ysend.at[14],
                yrecv.at[4],
                d,
                t,
            ).start()
            rcopy(
                R.VG.at[pl.ds(pl.multiple_of(t * 8, 8), 8)],
                R.VGR.at[i - 1],
                ysend.at[15],
                yrecv.at[5],
                d,
                t,
            ).start()

        to_peers(sends)
        gsum = fold_end("B", 11)
        for j in range(4):
            R.o_attn[j] = gsum[:, j * 256 : (j + 1) * 256]
        for j in range(4):
            tensor(4 + j, R.in_attnw[j], R.o_attn[j], R.in_attn_f[j], R.in_attn_s[j])

    all_sum(R.PRP, R.PRH, R.PRC, R.PRR, 8, (hook_first, hook_second, hook_third, lambda: None))

    spread = nt(R.PRR[:, 256:384], head_of, HIGH)
    dqa = jnp.sum(spread * R.EWR[:, 0:256], 0, keepdims=True) * SCALE
    pk = spread * (qa * SCALE)
    pv = R.PRR[:, 0:256]
    emb = R.TA[:, 0:256]
    wa = [R.in_aggw[j].astype(BF).astype(F32) for j in range(3)]
    pk, pv = pk.astype(BF), pv.astype(BF)
    R.TG[...] = nt(wa[1].astype(BF), pk) + nt(wa[2].astype(BF), pv)
    R.TG[:, 240:241] = jnp.sum(wa[0] * dqa, 1, keepdims=True)

    def last_sends(i, t):
        rcopy(
            R.TG.at[pl.ds(pl.multiple_of(t * 8, 8), 8)],
            R.TGR.at[i - 1],
            ysend.at[13],
            yrecv.at[3],
            d,
            t,
        ).start()

    to_peers(last_sends)
    R.o_agg[0] = R.TA[:, 256:257] * dqa
    emb = emb.astype(BF)
    R.o_agg[1] = nn(emb, pk)
    R.o_agg[2] = nn(emb, pv)
    R.o_agg[3] = reduce_end("A3", 10)
    for j in range(4):
        tensor(j, R.in_aggw[j], R.o_agg[j], R.in_agg_f[j], R.in_agg_s[j])
    drain(R.HGR, yrecv.at[4])
    hgrad = R.HG[m] + R.HGR[0] + R.HGR[1] + R.HGR[2]
    R.o_head[...] = hgrad[:, 0:NVAR]
    tensor(10, R.in_headw[...], R.o_head[...], R.in_head_f[...], R.in_head_s[...])
    drain(R.VGR, yrecv.at[5])
    vgrad = R.VG[my_eight, :] + R.VGR[0] + R.VGR[1] + R.VGR[2]
    drain(R.TGR, yrecv.at[3])
    tgrad = R.TG[my_eight, :] + R.TGR[0] + R.TGR[1] + R.TGR[2]
    for p in range(5):
        R.EG[p * 8 : (p + 1) * 8, :] = tgrad[:, p * 48 : (p + 1) * 48]
    R.o_emb[...] = nt(R.EG[...], vhot, HIGH)
    tensor(11, R.in_emb[...], R.o_emb[...], R.in_emb_f[...], R.in_emb_s[...])
    R.o_vec[...] = vgrad[:, 0:NVEC]
    R.o_vec[:, 0:1] = tgrad[:, 240:241]
    unused, unused2, direction = adam_direction(
        R.in_vec[...], R.o_vec[...], R.in_vec_f[...], R.in_vec_s[...]
    )
    R.NX[0:1, :] = sums["w"]
    R.NX[1:2, :] = sums["u"]
    R.NX[0:1, 12 : 12 + NVEC] = jnp.sum(R.in_vec[...] * R.in_vec[...], 0, keepdims=True)
    R.NX[1:2, 12 : 12 + NVEC] = jnp.sum(direction * direction, 0, keepdims=True)

    for j in range(1, 2 * MPN):
        t = lax.rem(m + j, MPN)
        rcopy(
            R.NX, R.NXR.at[j - 1], ysend.at[16], yrecv.at[6], sib if j >= MPN else d, t
        ).start()
    drain(R.NXR, yrecv.at[6])
    norm = R.NX[...]
    for j in range(7):
        norm = norm + R.NXR[j]
    R.NY[...] = norm
    at_k = pl.ds(pl.multiple_of(k * 8, 8), 8)
    to_chips(lambda kk, t: rcopy(R.NY, R.NYR.at[at_k], dsend.at[16], drecv.at[16], t, m).start())

    gather_end(R.VPK, 4)
    for buf, g in ((R.HW, 0), (R.WB, 1), (R.W1, 2), (R.W2, 3), (R.WA3, 8)):
        two_end(buf, g)
    all_sum_end(R.EWH, R.EWC, R.EWR, 6)
    all_sum_end(R.PRH, R.PRC, R.PRR, 8)
    for ix in range(5):
        drain(R.RSR.at[ix], ysend.at[ix])
        drain(R.AG.at[ix, pl.ds(0, 192)], ysend.at[5 + ix])
    drain(R.TA.at[pl.ds(0, 24)], ysend.at[10])
    drain(R.HWS.at[pl.ds(0, 3)], ysend.at[11])
    drain(R.TGT.at[pl.ds(0, 3)], ysend.at[12])
    drain(R.TGR, ysend.at[13])
    drain(R.HGR, ysend.at[14])
    drain(R.VGR, ysend.at[15])
    drain(R.NXR, ysend.at[16])

    drain(R.NYR.at[pl.ds(0, 120)], drecv.at[16])
    stats = R.NY[...]
    for dz, dx in FAR_FIRST:
        kk = lax.rem(z + dz, 4) * 4 + lax.rem(x + dx, 4)
        stats = stats + R.NYR[pl.ds(pl.multiple_of(kk * 8, 8), 8), :]
    first_lane = (iota((8, 128), 0) == 0) & (iota((8, 128), 1) == 127)
    R.o_stats[...] = jnp.where(first_lane, total_count, stats)
    drain(R.NYR.at[pl.ds(0, 120)], dsend.at[16])


def mega_call(large, small):
    outs = [SHAPES[n] for n in ("emb", "vec", "agg", "attn", "mlp", "head")] + [((8, 128), F32)]
    out_shape = tuple(pltpu.VMEM(*item) for item in outs)
    whole = pl.BlockSpec(memory_space=pltpu.VMEM)
    return pl.pallas_call(
        mega,
        out_shape=out_shape,
        in_specs=[pl.BlockSpec(memory_space=pl.ANY)] * len(large) + [whole] * len(small),
        out_specs=tuple(whole for unused in out_shape),
        scratch_shapes=[item for unused, item in SCRATCH],
        compiler_params=pltpu.CompilerParams(
            collective_id=0, has_side_effects=True, vmem_limit_bytes=54 * 2**20
        ),
        name="step",
    )(*large, *small)


def finish(*refs):
    weights, firsts, seconds, grads = (refs[6 * i : 6 * i + 6] for i in range(4))
    stats, running = refs[24:26]
    o_loss, o_count, o_running, o_trust, o_norms = refs[26:31]
    outs = refs[31:49]
    norms = jnp.sqrt(stats[0:1, :])
    trust = norms / jnp.sqrt(stats[1:2, :])
    o_norms[...] = norms[:, 0:29]
    o_trust[...] = trust[:, 0:29]
    count = stats[0:1, 127:128]
    o_count[...] = count
    errors = jnp.zeros((1, NVAR), F32)
    for j in range(4):
        lane = iota((128, NVAR), 0)
        pick = (lane < NVAR) & (iota((128, NVAR), 1) == 12 * j + lane // P_SIZE)
        errors = errors + nn(stats[4 + j : 5 + j, :], pick.astype(F32), HIGH)
    o_loss[...] = jnp.sum(errors, 1, keepdims=True)
    o_running[...] = STATS_DECAY * running[...] + (1.0 - STATS_DECAY) * errors * (NVAR / count)

    def update(i, at, ratio):
        first, second, direction = adam_direction(
            weights[i][at], grads[i][at], firsts[i][at], seconds[i][at]
        )
        outs[i][at] = first
        outs[6 + i][at] = second
        outs[12 + i][at] = weights[i][at] - LEARN_RATE * ratio * direction

    for i, number, offset in ((0, 4, 0), (1, 4, 4), (2, 2, 8)):
        for j in range(number):
            update(i, j, trust[:, offset + j : offset + j + 1])
    update(3, Ellipsis, trust[:, 10:11])
    update(4, Ellipsis, trust[:, 11:12])
    update(5, Ellipsis, trust[:, 12 : 12 + NVEC])


def finish_call(weights, firsts, seconds, grads, stats, running):
    shapes = [(1, 1), (1, 1), (1, NVAR), (1, 29), (1, 29)] + 3 * [w.shape for w in weights]
    whole = pl.BlockSpec(memory_space=pltpu.VMEM)
    values = (*weights, *firsts, *seconds, *grads, stats, running)
    return pl.pallas_call(
        finish,
        out_shape=tuple(jax.ShapeDtypeStruct(s, F32) for s in shapes),
        in_specs=[whole] * 26,
        out_specs=(whole,) * 23,
        compiler_params=pltpu.CompilerParams(vmem_limit_bytes=32 * 2**20),
        name="finish",
    )(*values)


def on_device(
    pixels,
    targets,
    valid_mask,
    segments,
    lead_index,
    latitude,
    var_ids,
    running_error,
    *tensors,
):
    def turned(group):
        agg, attn, mlp, head, embed, vecs = group
        return (agg, attn, mlp, head, embed.transpose(1, 2, 0).reshape(40, NVAR), vecs.T)

    weights, firsts, seconds = (turned(tensors[6 * i : 6 * i + 6]) for i in range(3))
    large = (pixels.T, targets.T, *weights, *firsts, *seconds)
    small = (
        valid_mask.T,
        segments,
        lead_index,
        latitude.reshape(1, TOK),
        var_ids.reshape(1, NVAR),
    )
    g_emb, g_vec, g_agg, g_attn, g_mlp, g_head, stats = mega_call(large, small)
    grads = (g_agg, g_attn, g_mlp, g_head, g_emb, g_vec)
    out = finish_call(weights, firsts, seconds, grads, stats, running_error.reshape(1, NVAR))

    def back(group):
        agg, attn, mlp, head, embed, vecs = group
        return (agg, attn, mlp, head, embed.reshape(5, 8, NVAR).transpose(2, 0, 1), vecs.T)

    return (
        out[0].reshape(()),
        out[1].reshape(()),
        out[2].reshape(NVAR),
        out[3].reshape(29),
        out[4].reshape(29),
        *back(out[5:11]),
        *back(out[11:17]),
        *back(out[17:23]),
    )


def solution(mesh):
    weights = (
        P(None, "dp", "mp"),
        P(None, "dp", "mp"),
        P(None, "dp", "mp"),
        P("dp", "mp"),
        P(None, None, ("dp", "mp")),
        P(None, ("dp", "mp")),
    )
    in_specs = (
        P("dp", None),
        P("dp", "mp"),
        P("dp", None),
        P("dp", None),
        P("dp", None),
        P("dp"),
        P(),
        P(),
        *weights,
        *weights,
        *weights,
    )
    out_specs = (P(), P(), P(), P(), P(), *weights, *weights, *weights)
    return jax.shard_map(
        on_device, mesh=mesh, in_specs=in_specs, out_specs=out_specs, check_vma=False
    )
```

```python
import math

import jax
import jax.numpy as jnp
from jax import lax
from jax.experimental import pallas as pl
from jax.experimental.pallas import tpu as pltpu
from jax.sharding import PartitionSpec as P

D = 1024
HEAD_DIM = 64
FF = 4096
NVAR = 48
P_SIZE = 4
SEGS = 4
LEADS = 28
LATS = 32
STEP = 10
NVEC = 17
EROWS = NVAR * (P_SIZE + 1)

HIGH = lax.Precision.HIGHEST
NORM_EPS = 1e-06
BETA_ONE = 0.9
BETA_TWO = 0.999
LEARN_RATE = 0.3
WEIGHT_DECAY = 0.01
ADAM_EPS = 1e-08
STATS_DECAY = 0.9
MESH = pl.DeviceIdType.MESH
BF = jnp.bfloat16
F32 = jnp.float32

DPN, MPN, CHIPS, SH, TOK, COLS = 32, 4, 16, 64, 256, 256
NQ = 4
RQ, CH = TOK // NQ, SH // NQ
SCALE = 1.0 / math.sqrt(HEAD_DIM)
FAR_FIRST = sorted(
    ((dz, dx) for dz in range(4) for dx in range(4) if dz or dx),
    key=lambda o: -(min(o[0], 4 - o[0]) + min(o[1], 4 - o[1])),
)


def nn(a, b, precision=None):
    return lax.dot_general(
        a, b, (((1,), (0,)), ((), ())), preferred_element_type=F32, precision=precision
    )


def nt(a, b, precision=None):
    return lax.dot_general(
        a, b, (((1,), (1,)), ((), ())), preferred_element_type=F32, precision=precision
    )


def tn(a, b, precision=None):
    return lax.dot_general(
        a, b, (((0,), (0,)), ((), ())), preferred_element_type=F32, precision=precision
    )


def latitude_weights():
    cosines = [
        math.cos(((j + 0.5) * (180.0 / LATS) - 90.0) * (math.pi / 180.0)) for j in range(LATS)
    ]
    mean = sum(cosines) / LATS
    return [value / mean for value in cosines]


def moments_new(gradient, first, second):
    first_new = BETA_ONE * first + (1.0 - BETA_ONE) * gradient
    second_new = BETA_TWO * second + (1.0 - BETA_TWO) * gradient * gradient
    return first_new, second_new


def adam_direction(weight, gradient, first, second):
    first_new, second_new = moments_new(gradient, first, second)
    first_hat = first_new * (1.0 / (1.0 - BETA_ONE**STEP))
    second_hat = second_new * (1.0 / (1.0 - BETA_TWO**STEP))
    direction = first_hat / (jnp.sqrt(second_hat) + ADAM_EPS) + WEIGHT_DECAY * weight
    return (first_new, second_new, direction)


def iota(shape, dim):
    return lax.broadcasted_iota(jnp.int32, shape, dim)


def ln_parts(x):
    centre = jnp.mean(x, -1, keepdims=True)
    shifted = x - centre
    r = lax.rsqrt(jnp.mean(shifted * shifted, -1, keepdims=True) + NORM_EPS)
    return shifted * r, r


def ln_back(n, r, gain, dh):
    e = dh * gain
    dx = r * (e - jnp.mean(e, -1, keepdims=True) - n * jnp.mean(e * n, -1, keepdims=True))
    dgain = jnp.sum(dh * n, 0, keepdims=True)
    dbias = jnp.sum(dh, 0, keepdims=True)
    return dx, dgain, dbias


LARGE = ("emb", "vid", "vec", "aggw", "headw", "mlpw", "attnw", "targ", "pix")
MOMENTS = ("agg", "attn", "mlp", "head", "emb", "vec")
SMALL = ("mask", "seg", "leadi", "lat", "run")
OUTS = ("o_emb", "o_vec", "o_agg", "o_attn", "o_mlp", "o_head", "o_stats")
OUTS = OUTS + ("o_vw", "o_vf", "o_vs", "o_run")
SHAPES = {
    "pix": ((NVAR * P_SIZE, TOK), BF),
    "targ": ((NVAR, TOK), F32),
    "agg": ((4, 32, 256), F32),
    "attn": ((4, 32, 256), F32),
    "mlp": ((2, 32, 1024), F32),
    "head": ((32, NVAR), F32),
    "emb": ((40, NVAR), F32),
    "vec": ((8, NVEC), F32),
    "mask": ((P_SIZE, TOK), jnp.int32),
    "seg": ((1, TOK), jnp.int32),
    "leadi": ((1, SEGS), jnp.int32),
    "lat": ((1, TOK), jnp.int32),
    "vid": ((1, NVAR), jnp.int32),
    "run": ((1, NVAR), F32),
}
SHAPES.update({"aggw": SHAPES["agg"], "attnw": SHAPES["attn"], "mlpw": SHAPES["mlp"]})
SHAPES["headw"] = SHAPES["head"]
FETCH = LARGE + SMALL + tuple(n + "_f" for n in MOMENTS) + tuple(n + "_s" for n in MOMENTS)


def fetch_shape(name):
    return SHAPES[name[:-2] if name[-2] == "_" else name]


def scratch_list():
    vm = pltpu.VMEM
    dma = pltpu.SemaphoreType.DMA
    items = [
        ("WA3", vm((D, 256), BF)),
        ("WB", vm((D, 768), BF)),
        ("WA3F", vm((D, 1024), BF)),
        ("WB3F", vm((D, 1024), BF)),
        ("W1", vm((D, 1024), BF)),
        ("W2", vm((D, 1024), BF)),
        ("HW", vm((D, 256), BF)),
        ("HWS", vm((MPN, 32, 128), BF)),
        ("VPK", vm((256, 128), F32)),
        ("VEC", vm((DPN, 4, 8, 128), F32)),
        ("VR", vm((128, D), F32)),
        ("VRN", vm((128, D), F32)),
        ("TMPV", vm((D, 128), F32)),
        ("TA", vm((32, 384), F32)),
        ("HWT", vm((32, 128), F32)),
        ("TT", vm((128, TOK), F32)),
        ("TS", vm((NQ, MPN, CH, 128), F32)),
        ("TGT", vm((MPN, NQ, CH, 128), F32)),
        ("ROWS", vm((128, TOK), F32)),
        ("TCOL", vm((TOK, 128), F32)),
        ("LW", vm((TOK, 128), F32)),
        ("PIXT", vm((256, TOK), F32)),
        ("EWP", vm((256, 512), F32)),
        ("EWB", vm((256, 512), BF)),
        ("EWC", vm((256, 512), BF)),
        ("EWH", vm((2, 16, 512), F32)),
        ("EWR", vm((256, 512), BF)),
        ("PRP", vm((256, 384), F32)),
        ("PRB", vm((256, 384), BF)),
        ("PRC", vm((256, 384), BF)),
        ("PRH", vm((2, 16, 384), F32)),
        ("PRR", vm((256, 384), BF)),
        ("MT", vm((4, 256, TOK), BF)),
        ("PT", vm((4, NVAR, TOK), F32)),
        ("OAT", vm((256, TOK), F32)),
        ("OA", vm((TOK, 256), BF)),
        ("RSS", vm((5, TOK, D), BF)),
        ("RSR", vm((5, 3, SH, D), BF)),
        ("AG", vm((5, TOK, D), BF)),
        ("QKV", vm((3, TOK, 256), BF)),
        ("PB", vm((4, TOK, TOK), F32)),
        ("OB", vm((TOK, 256), BF)),
        ("OF", vm((SH, D), BF)),
        ("DOB", vm((TOK, 256), BF)),
        ("DOF", vm((SH, D), BF)),
        ("DMB", vm((TOK, 256), BF)),
        ("DMF", vm((SH, D), BF)),
        ("GEL", vm((TOK, 1024), BF)),
        ("GELP", vm((TOK, 1024), F32)),
        ("DU", vm((TOK, 1024), BF)),
        ("DQKV", vm((TOK, 768), BF)),
        ("LN", vm((2, SH, D), F32)),
        ("XS", vm((SH, D), F32)),
        ("RR", vm((2, SH, 128), F32)),
        ("H3", vm((SH, D), BF)),
        ("DP", vm((SH, 256), BF)),
        ("GVT", vm((DPN, 4, 8, 128), F32)),
        ("GVK", vm((256, 128), F32)),
        ("GVS", vm((128, 128), F32)),
        ("GVB", vm((128, 128), F32)),
        ("GVP", vm((128, D), F32)),
        ("GVN", vm((128, D), F32)),
        ("TG", vm((32, 256), F32)),
        ("TGR", vm((3, 8, 256), F32)),
        ("VG", vm((32, 128), F32)),
        ("VGR", vm((3, 8, 128), F32)),
        ("HG", vm((MPN, 32, 128), F32)),
        ("HGR", vm((3, 32, 128), F32)),
        ("EG", vm((40, NVAR), F32)),
        ("NX", vm((8, 128), F32)),
        ("NXR", vm((7, 8, 128), F32)),
        ("NY", vm((8, 128), F32)),
        ("NYR", vm((128, 128), F32)),
    ]
    for name, width, kind in (
        ("A3", 256, BF),
        ("B", 1024, BF),
        ("1", 1024, BF),
        ("2", 1024, BF),
        ("H", 256, BF),
    ):
        items.append(("G" + name, vm((D, width), kind)))
        items.append(("S" + name, vm((512, width), kind)))
        if name == "A3":
            items.append(("B" + name, vm((512, width), kind)))
        else:
            items.append(("FP" + name, vm((2, 3, 128, width // 2), kind)))
            items.append(("FQ" + name, vm((2, 3, 32, width // 2), kind)))
    for name in FETCH:
        items.append(("in_" + name, vm(*fetch_shape(name))))
    items += [
        ("fsem", dma((len(FETCH),))),
        ("ysend", dma((22,))),
        ("yrecv", dma((10,))),
        ("nrecv", dma((2, NQ))),
        ("rrecv", dma((5, NQ))),
        ("arecv", dma((5, NQ))),
        ("dsend", dma((19,))),
        ("drecv", dma((19,))),
        ("tsend", dma((12, 4))),
        ("trecv", dma((12, 4))),
        ("ssend", dma((19,))),
        ("srecv", dma((19,))),
    ]
    return items


SCRATCH = scratch_list()
NAMES = tuple(n + "_hbm" for n in FETCH) + OUTS + tuple(n for n, unused in SCRATCH)


def mega(*refs):
    r = dict(zip(NAMES, refs))
    step_kernel(type("Refs", (), r))


def step_kernel(R):
    d = lax.axis_index("dp")
    m = lax.axis_index("mp")
    c = lax.rem(d, 2)
    k = d // 2
    z = k // 4
    x = lax.rem(k, 4)
    sib = d + 1 - 2 * c
    rb = pl.multiple_of(c * 512 + k * 32, 32)
    half = pl.multiple_of(c * 512, 512)
    other = pl.multiple_of(512 - c * 512, 512)
    my_slot = pl.ds(pl.multiple_of(m * 128, 128), 128)
    my_eight = pl.ds(pl.multiple_of(m * 8, 8), 8)
    my_cols = pl.ds(pl.multiple_of(m * COLS, COLS), COLS)

    def rcopy(src, dst, ss, rs, dp, mp):
        return pltpu.make_async_remote_copy(
            src_ref=src,
            dst_ref=dst,
            send_sem=ss,
            recv_sem=rs,
            device_id={"dp": dp, "mp": mp},
            device_id_type=MESH,
        )

    def drain(ref, sem):
        pltpu.make_async_copy(ref, ref, sem).wait()

    def loop(first, last, fn):
        def step(i, carry):
            fn(i)
            return carry

        lax.fori_loop(first, last, step, 0)

    def to_peers(fn):
        for i in (2, 1, 3):
            fn(i, lax.rem(m + i, MPN))

    def to_chips(fn):
        for dz, dx in FAR_FIRST:
            kk = lax.rem(z + dz, 4) * 4 + lax.rem(x + dx, 4)
            fn(kk, kk * 2 + c)

    def fetch(name):
        i = FETCH.index(name)
        return pltpu.make_async_copy(
            getattr(R, name + "_hbm"), getattr(R, "in_" + name), R.fsem.at[i]
        )

    dsend, drecv, ssend, srecv = R.dsend, R.drecv, R.ssend, R.srecv
    ysend, yrecv = R.ysend, R.yrecv

    def gather_start(buf, g):
        block = buf.at[pl.ds(pl.multiple_of(c * 128 + k * 8, 8), 8)]
        to_chips(lambda kk, t: rcopy(block, block, dsend.at[g], drecv.at[g], t, m).start())

    def gather_cross(buf, g):
        drain(buf.at[pl.ds(0, 120)], drecv.at[g])
        part = buf.at[pl.ds(pl.multiple_of(c * 128, 128), 128)]
        rcopy(part, part, ssend.at[g], srecv.at[g], sib, m).start()

    def gather_wait(buf, g):
        drain(buf.at[pl.ds(0, buf.shape[0] // 2)], srecv.at[g])

    def gather_end(buf, g):
        drain(buf.at[pl.ds(0, 120)], dsend.at[g])
        drain(buf.at[pl.ds(0, 128)], ssend.at[g])

    def along(axis, i):
        if axis == "x":
            return (z * 4 + lax.rem(x + i, 4)) * 2 + c
        return (lax.rem(z + i, 4) * 4 + x) * 2 + c

    def sides(buf):
        n = buf.shape[1] // 2
        return pl.ds(0, n), pl.ds(n, n)

    def tcopy(src, dst, g, j, t):
        rcopy(src, dst, R.tsend.at[g, j], R.trecv.at[g, j], t, m).start()

    def two_first(buf, g):
        left, right = sides(buf)
        for i in (2, 1, 3):
            block = buf.at[pl.ds(rb, 32), left]
            tcopy(block, block, g, 0, along("x", i))
            block = buf.at[pl.ds(rb, 32), right]
            tcopy(block, block, g, 1, along("z", i))

    def two_second(buf, g):
        left, right = sides(buf)
        drain(buf.at[pl.ds(0, 96), left], R.trecv.at[g, 0])
        block = buf.at[pl.ds(pl.multiple_of(half + z * 128, 128), 128), left]
        for i in (2, 1, 3):
            tcopy(block, block, g, 2, along("z", i))
        drain(buf.at[pl.ds(0, 96), right], R.trecv.at[g, 1])

        def send(zz):
            block = buf.at[pl.ds(pl.multiple_of(half + zz * 128 + x * 32, 32), 32), right]
            for i in (2, 1, 3):
                tcopy(block, block, g, 3, along("x", i))

        loop(0, 4, send)

    def two_cross(buf, g):
        for side, j in zip(sides(buf), (2, 3)):
            drain(buf.at[pl.ds(0, 384), side], R.trecv.at[g, j])
        part = buf.at[pl.ds(half, 512)]
        g = {8: 5, 9: 16, 10: 17}.get(g, g)
        rcopy(part, part, ssend.at[g], srecv.at[g], sib, m).start()

    def two_end(buf, g):
        left, right = sides(buf)
        for j, rows in ((0, 96), (1, 96), (2, 384), (3, 384)):
            drain(buf.at[pl.ds(0, rows), left if j % 2 == 0 else right], R.tsend.at[g, j])
        drain(buf.at[pl.ds(0, 512)], ssend.at[{8: 5, 9: 16, 10: 17}.get(g, g)])

    def reduce_cross(name, g):
        buf, sbuf = getattr(R, "G" + name), getattr(R, "S" + name)
        rcopy(buf.at[pl.ds(other, 512)], sbuf, ssend.at[g], srecv.at[g], sib, m).start()

    def core_sum(name, g):
        buf, sbuf = getattr(R, "G" + name), getattr(R, "S" + name)
        drain(sbuf, srecv.at[g])

        def add(i):
            at = pl.multiple_of(i * 128, 128)
            sbuf[pl.ds(at, 128), :] = (
                sbuf[pl.ds(at, 128), :].astype(F32)
                + buf[pl.ds(pl.multiple_of(half + at, 128), 128), :].astype(F32)
            ).astype(sbuf.dtype)

        loop(0, 4, add)

    def reduce_spread(name, g):
        core_sum(name, g)
        sbuf, bbuf = getattr(R, "S" + name), getattr(R, "B" + name)
        land = bbuf.at[pl.ds(pl.multiple_of(k * 32, 32), 32)]

        def send(kk, t):
            src = sbuf.at[pl.ds(pl.multiple_of(kk * 32, 32), 32)]
            rcopy(src, land, dsend.at[g], drecv.at[g], t, m).start()

        to_chips(send)

    def row_block(zz, xx):
        return pl.ds(pl.multiple_of(zz * 128 + xx * 32, 32), 32)

    def fold_first(name, g):
        core_sum(name, g)
        sbuf, pbuf = getattr(R, "S" + name), getattr(R, "FP" + name)
        left, right = sides(sbuf)
        for i in (2, 1, 3):
            zz = lax.rem(z + i, 4)
            src = sbuf.at[pl.ds(pl.multiple_of(zz * 128, 128), 128), left]
            tcopy(src, pbuf.at[0, i - 1], g - 7, 0, along("z", i))

        def send(zz):
            for i in (2, 1, 3):
                src = sbuf.at[row_block(zz, lax.rem(x + i, 4)), right]
                land = pbuf.at[1, i - 1, pl.ds(pl.multiple_of(zz * 32, 32), 32)]
                tcopy(src, land, g - 7, 1, along("x", i))

        loop(0, 4, send)

    def fold_second(name, g):
        sbuf, pbuf, qbuf = getattr(R, "S" + name), getattr(R, "FP" + name), getattr(R, "FQ" + name)
        left, right = sides(sbuf)
        for side, j in ((left, 0), (right, 1)):
            drain(pbuf.at[j], R.trecv.at[g - 7, j])

            def add(i):
                at = row_block(z, i) if j == 0 else row_block(i, x)
                acc = sbuf[at, side].astype(F32)
                for n in range(3):
                    acc = acc + pbuf[j, n, pl.ds(pl.multiple_of(i * 32, 32), 32), :].astype(F32)
                sbuf[at, side] = acc.astype(sbuf.dtype)

            loop(0, 4, add)
            for i in (2, 1, 3):
                if j == 0:
                    src = sbuf.at[row_block(z, lax.rem(x + i, 4)), side]
                    tcopy(src, qbuf.at[0, i - 1], g - 7, 2, along("x", i))
                else:
                    src = sbuf.at[row_block(lax.rem(z + i, 4), x), side]
                    tcopy(src, qbuf.at[1, i - 1], g - 7, 3, along("z", i))

    def fold_end(name, g):
        sbuf, pbuf, qbuf = getattr(R, "S" + name), getattr(R, "FP" + name), getattr(R, "FQ" + name)
        parts = []
        for side, j in zip(sides(sbuf), (0, 1)):
            drain(qbuf.at[j], R.trecv.at[g - 7, 2 + j])
            acc = sbuf[row_block(z, x), side].astype(F32)
            for n in range(3):
                acc = acc + qbuf[j, n].astype(F32)
            parts.append(acc)
            drain(pbuf.at[j], R.tsend.at[g - 7, j])
            drain(qbuf.at[j], R.tsend.at[g - 7, 2 + j])
        drain(sbuf, ssend.at[g])
        return jnp.concatenate(parts, 1)

    def reduce_end(name, g):
        sbuf, bbuf = getattr(R, "S" + name), getattr(R, "B" + name)
        drain(bbuf.at[pl.ds(0, 480)], drecv.at[g])

        def add(i, acc):
            at = pl.multiple_of(lax.rem(k + i, CHIPS) * 32, 32)
            return acc + bbuf[pl.ds(at, 32), :].astype(F32)

        total = lax.fori_loop(
            1, CHIPS, add, sbuf[pl.ds(pl.multiple_of(k * 32, 32), 32), :].astype(F32)
        )
        drain(bbuf.at[pl.ds(0, 480)], dsend.at[g])
        drain(sbuf, ssend.at[g])
        return total

    def all_sum(src, cbuf, hbuf, res, g, hooks):
        at_k = pl.ds(pl.multiple_of(k * 16, 16), 16)

        def send(kk, t):
            block = src.at[pl.ds(pl.multiple_of(kk * 16, 16), 16)]
            rcopy(block, cbuf.at[at_k], dsend.at[g], drecv.at[g], t, m).start()

        to_chips(send)
        hooks[0]()
        drain(cbuf.at[pl.ds(0, 240)], drecv.at[g])
        total = src[at_k, :].astype(F32)
        for dz, dx in FAR_FIRST:
            kk = lax.rem(z + dz, 4) * 4 + lax.rem(x + dx, 4)
            total = total + cbuf[pl.ds(pl.multiple_of(kk * 16, 16), 16), :].astype(F32)
        hbuf[0] = total
        rcopy(hbuf.at[0], hbuf.at[1], ssend.at[g], srecv.at[g], sib, m).start()
        hooks[1]()
        drain(hbuf.at[1], srecv.at[g])
        res[at_k, :] = (hbuf[0] + hbuf[1]).astype(BF)
        part = res.at[at_k]
        to_chips(lambda kk, t: rcopy(part, part, dsend.at[g + 1], drecv.at[g + 1], t, m).start())
        hooks[2]()
        drain(res.at[pl.ds(0, 240)], drecv.at[g + 1])

    def all_sum_end(cbuf, hbuf, res, g):
        drain(hbuf.at[0], ssend.at[g])
        drain(cbuf.at[pl.ds(0, 240)], dsend.at[g])
        drain(res.at[pl.ds(0, 240)], dsend.at[g + 1])

    def rows_of(q):
        return pl.ds(pl.multiple_of(q * RQ, RQ), RQ)

    def own_of(q, t):
        return pl.ds(pl.multiple_of(q * RQ + t * CH, CH), CH)

    def local_of(q):
        return pl.ds(pl.multiple_of(q * CH, CH), CH)

    def branch_send(ix, q, left, weight, cols=None):
        for n in range(4):
            at = pl.ds(n * 256, 256)
            w = weight[at, :] if cols is None else weight[at, cols[0] : cols[1]]
            R.RSS[ix, rows_of(q), n * 256 : (n + 1) * 256] = nt(left, w).astype(BF)

        def send(i, t):
            rcopy(
                R.RSS.at[ix, own_of(q, t)],
                R.RSR.at[ix, i - 1, local_of(q)],
                ysend.at[ix],
                R.rrecv.at[ix, q],
                d,
                t,
            ).start()

        to_peers(send)

    def branch_sum(ix, q):
        drain(R.RSR.at[ix, :, pl.ds(0, CH)], R.rrecv.at[ix, q])
        acc = R.RSS[ix, own_of(q, m), :].astype(F32)
        for i in range(3):
            acc = acc + R.RSR[ix, i, local_of(q), :].astype(F32)
        return acc

    def share_send(ix, q, values):
        R.AG[ix, own_of(q, m), :] = values
        share_start(ix, q)

    def heads_out(src, dst, q, ss, rs):
        land = dst.at[local_of(q), my_cols]
        to_peers(lambda i, t: rcopy(src.at[own_of(q, t)], land, ss, rs, d, t).start())
        dst[local_of(q), my_cols] = src[own_of(q, m), :]

    def heads_back(src, dst, q, ss, rs):
        def send(i, t):
            block = src.at[local_of(q), pl.ds(pl.multiple_of(t * COLS, COLS), COLS)]
            rcopy(block, dst.at[own_of(q, m)], ss, rs, d, t).start()

        to_peers(send)
        dst[own_of(q, m), :] = src[local_of(q), my_cols]

    def share_start(ix, q):
        block = R.AG.at[ix, own_of(q, m)]
        to_peers(
            lambda i, t: rcopy(block, block, ysend.at[5 + ix], R.arecv.at[ix, q], d, t).start()
        )

    def share_wait(ix, q):
        drain(R.AG.at[ix, pl.ds(0, 3 * CH)], R.arecv.at[ix, q])

    bar = pltpu.get_barrier_semaphore()

    def greet(i):
        pl.semaphore_signal(
            bar, inc=1, device_id={"dp": lax.rem(d + i, DPN), "mp": m}, device_id_type=MESH
        )

    for i in range(1, MPN):
        pl.semaphore_signal(
            bar, inc=1, device_id={"dp": d, "mp": lax.rem(m + i, MPN)}, device_id_type=MESH
        )
    loop(1, DPN, greet)
    for i in range(1, MPN):
        pl.semaphore_signal(
            bar, inc=1, device_id={"dp": sib, "mp": lax.rem(m + i, MPN)}, device_id_type=MESH
        )

    for name in FETCH:
        fetch(name).start()

    fetch("vid").wait()
    vhot = (iota((NVAR, NVAR), 0) == R.in_vid[...]).astype(F32)
    fetch("emb").wait()
    fetch("vec").wait()
    chosen = nn(R.in_emb[...], vhot, HIGH)
    R.TA[my_eight, :] = jnp.zeros((8, 384), F32)
    for p in range(5):
        R.TA[my_eight, p * 48 : (p + 1) * 48] = chosen[p * 8 : (p + 1) * 8, :]
    R.TA[my_eight, 256 : 256 + NVEC] = R.in_vec[...]
    fetch("aggw").wait()
    fetch("headw").wait()
    aw = [R.in_aggw[j].astype(BF) for j in range(3)]
    R.WA3[pl.ds(rb, 32), :] = R.in_aggw[3].astype(BF)
    R.HWT[...] = jnp.zeros_like(R.HWT)
    R.HWT[:, 0:NVAR] = R.in_headw[...]
    R.HWS[m] = R.HWT[...].astype(BF)
    fetch("mlpw").wait()
    R.W1[pl.ds(rb, 32), :] = R.in_mlpw[0].astype(BF)
    R.W2[pl.ds(rb, 32), :] = R.in_mlpw[1].astype(BF)
    fetch("attnw").wait()
    for j in range(3):
        R.WB[pl.ds(rb, 32), j * 256 : (j + 1) * 256] = R.in_attnw[j].astype(BF)
    R.WB3F[pl.ds(rb, 32), my_cols] = R.in_attnw[3].astype(BF)
    R.WA3F[pl.ds(rb, 32), my_cols] = R.in_aggw[3].astype(BF)
    fetch("targ").wait()
    R.TT[NVAR:, :] = jnp.zeros((128 - NVAR, TOK), F32)
    R.TT[0:NVAR, :] = R.in_targ[...]
    turned = R.TT[...].T
    for q in range(NQ):
        for t in range(MPN):
            at = q * RQ + t * CH
            R.TS[q, t] = turned[at : at + CH, :]
    R.TGT[m] = R.TS[:, m]
    R.GVP[...] = jnp.zeros_like(R.GVP)
    R.GVN[...] = jnp.zeros_like(R.GVN)
    R.NX[...] = jnp.zeros_like(R.NX)
    R.HG[...] = jnp.zeros_like(R.HG)
    R.VG[...] = jnp.zeros_like(R.VG)
    pl.semaphore_wait(bar, DPN + 2 * MPN - 3)

    def first_sends(i, t):
        part = R.TA.at[my_eight]
        rcopy(part, part, ysend.at[10], yrecv.at[0], d, t).start()
        block = R.WB3F.at[pl.ds(rb, 32), my_cols]
        rcopy(block, block, ysend.at[17], yrecv.at[7], d, t).start()

    def later_sends(i, t):
        slot = R.HWS.at[m]
        rcopy(slot, slot, ysend.at[11], yrecv.at[1], d, t).start()
        block = R.WA3F.at[pl.ds(rb, 32), my_cols]
        rcopy(block, block, ysend.at[18], yrecv.at[8], d, t).start()
        rcopy(R.TS.at[:, t], R.TGT.at[m], ysend.at[12], yrecv.at[2], d, t).start()

    to_peers(first_sends)
    two_first(R.WA3, 8)
    two_first(R.WB, 1)
    two_first(R.W1, 2)
    two_first(R.W2, 3)
    to_peers(later_sends)

    fetch("pix").wait()
    for name in SMALL:
        fetch(name).wait()
    rows = iota((256, 192), 0)
    cols = iota((256, 192), 1)
    pick = (rows < 192) & ((lax.rem(rows, NVAR) * P_SIZE + rows // NVAR) == cols)
    pixt = nn(pick.astype(BF), R.in_pix[...])
    row_at = iota((256, TOK), 0)
    R.PIXT[...] = jnp.where(row_at < 192, pixt, jnp.where(row_at < EROWS, 1.0, 0.0))

    drain(R.TA.at[pl.ds(0, 24)], yrecv.at[0])
    emb = R.TA[:, 0:256]
    R.EWP[:, 0:256] = tn(emb, aw[1].astype(F32), HIGH)
    R.EWP[:, 256:512] = tn(emb, aw[2].astype(F32), HIGH)
    R.EWP[240:241, 0:256] = jnp.sum(R.TA[:, 256:257] * aw[0].astype(F32), 0, keepdims=True)
    R.EWB[...] = R.EWP[...].astype(BF)
    keep = R.in_mask[...].astype(F32)
    count = jnp.sum(jnp.sum(keep, 1, keepdims=True), 0, keepdims=True) * NVAR

    def per_patch():
        seg = R.in_seg[...]
        lead_row = jnp.zeros((1, TOK), F32)
        for s in range(SEGS):
            value = (R.in_leadi[:, s : s + 1] + 1).astype(F32) / LEADS
            lead_row = jnp.where(seg == s, value, lead_row)
        lat = R.in_lat[...]
        lat_row = jnp.zeros((1, TOK), F32)
        for j, value in enumerate(latitude_weights()):
            lat_row = jnp.where(lat == j, value, lat_row)
        R.ROWS[...] = jnp.zeros_like(R.ROWS)
        R.ROWS[0:1, :] = seg.astype(F32)
        R.ROWS[1:2, :] = lead_row
        R.ROWS[8:12, :] = keep * lat_row
        R.TCOL[...] = R.ROWS[...].T
        lane = iota((128, 128), 1)
        pick = (lane < NVAR) & (iota((128, 128), 0) == 8 + lax.rem(lane, P_SIZE))
        R.LW[...] = nn(R.TCOL[...], pick.astype(F32), HIGH)

    def own_vectors():
        at = pl.ds(pl.multiple_of(c * 128 + k * 8, 8), 8)
        for g in range(4):
            R.VPK[at, 32 * g : 32 * (g + 1)] = R.TA[8 * g : 8 * (g + 1), 256:288]
        R.VPK[at, 31:32] = jnp.broadcast_to(count, (8, 1))

    def first_bulk():
        own_vectors()
        two_second(R.WA3, 8)
        gather_start(R.VPK, 4)
        drain(R.WB3F.at[pl.ds(0, 32), pl.ds(0, 768)], yrecv.at[7])
        two_first(R.WB3F, 10)
        per_patch()

    def bulk():
        two_second(R.WB, 1)
        gather_cross(R.VPK, 4)
        two_cross(R.WA3, 8)

    all_sum(R.EWB, R.EWC, R.EWH, R.EWR, 6, (first_bulk, lambda: None, bulk))

    two_second(R.WB3F, 10)

    head_of = (iota((256, 128), 0) // HEAD_DIM == iota((256, 128), 1)).astype(F32)
    ewk = R.EWR[:, 0:256].astype(F32)
    qa = ewk[240:241, :]
    qe = nn(ewk * (qa * SCALE), head_of, HIGH)
    ewv = R.EWR[:, 256:512]
    for h in range(4):
        scores = R.PIXT[0:48, :] * qe[0:48, h : h + 1]
        for p in range(1, 5):
            at = slice(p * 48, (p + 1) * 48)
            scores = scores + R.PIXT[at, :] * qe[at, h : h + 1]
        e = jnp.exp(scores - jnp.max(scores, 0, keepdims=True))
        probs = e / jnp.sum(e, 0, keepdims=True)
        R.PT[h] = probs
        probs = probs.astype(BF).astype(F32)
        for p in range(5):
            at = slice(p * 48, (p + 1) * 48)
            R.MT[h, at, :] = (probs * R.PIXT[at, :]).astype(BF)
        R.MT[h, 240:256, :] = jnp.zeros((16, TOK), BF)
        R.OAT[h * 64 : (h + 1) * 64, :] = tn(ewv[:, h * 64 : (h + 1) * 64], R.MT[h])
    R.OA[...] = R.OAT[...].T.astype(BF)

    gather_wait(R.WA3, 5)
    loop(0, NQ, lambda q: branch_send(0, q, R.OA[rows_of(q), :], R.WA3))
    two_second(R.W1, 2)
    gather_wait(R.VPK, 4)
    packed = R.VPK[...].reshape(DPN, 8, 128)
    total_count = jnp.sum(packed, 0)[0:1, 31:32]
    for g in range(4):
        R.VEC[:, g, :, 0:32] = packed[:, :, 32 * g : 32 * (g + 1)]
    R.VR[...] = R.VEC[...].reshape(D, 128).T
    two_cross(R.WB, 1)

    def vrow(i):
        return R.VR[i : i + 1, :]

    def keep_norm(j, q, n, r):
        R.LN[j, local_of(q), :] = n
        R.RR[j, local_of(q), :] = jnp.broadcast_to(r, (CH, 128))

    def mixed_rows(q):
        lead = R.TCOL[own_of(q, m), 1:2]
        x0 = branch_sum(0, q) + vrow(1) + lead * vrow(2)
        n, r = ln_parts(x0)
        share_send(0, q, (n * vrow(3) + vrow(4)).astype(BF))
        R.XS[local_of(q), :] = x0
        keep_norm(0, q, n, r)

    loop(0, NQ // 2, mixed_rows)
    two_second(R.W2, 3)
    loop(NQ // 2, NQ, mixed_rows)

    def natural(i):
        block = R.VEC[lax.rem(i, 2) * 16 + i // 2]
        R.TMPV[pl.ds(pl.multiple_of(i * 32, 32), 32), :] = block.reshape(32, 128)

    loop(0, DPN, natural)
    R.VRN[...] = R.TMPV[...].T
    drain(R.HWS.at[pl.ds(0, 3)], yrecv.at[1])
    R.HW[pl.ds(rb, 32), :] = jnp.concatenate(
        [R.HWS[j].astype(F32)[:, 0:64] for j in range(MPN)], 1
    ).astype(BF)
    two_first(R.HW, 0)
    drain(R.WA3F.at[pl.ds(0, 32), pl.ds(0, 768)], yrecv.at[8])
    gather_wait(R.WB, 1)

    def project(q):
        share_wait(0, q)
        at = rows_of(q)
        h1 = R.AG[0, at, :]
        R.QKV[0, at, :] = (nn(h1, R.WB[:, 0:256]) + R.VRN[5:6, my_cols]).astype(BF)
        R.QKV[1, at, :] = nn(h1, R.WB[:, 256:512]).astype(BF)
        R.QKV[2, at, :] = (nn(h1, R.WB[:, 512:768]) + R.VRN[6:7, my_cols]).astype(BF)

    loop(0, NQ // 2, project)
    two_cross(R.WB3F, 10)
    loop(NQ // 2, NQ, project)
    seg_row = R.in_seg[...].astype(F32)

    same = R.TCOL[:, 0:1] == seg_row
    for h in range(4):
        at = slice(h * 64, (h + 1) * 64)
        scores = nt(R.QKV[0, :, at], R.QKV[1, :, at]) * SCALE
        scores = jnp.where(same, scores, -1e30)
        e = jnp.exp(scores - jnp.max(scores, 1, keepdims=True))
        probs = e / jnp.sum(e, 1, keepdims=True)
        R.PB[h] = probs
        R.OB[:, at] = nn(probs.astype(BF), R.QKV[2, :, at]).astype(BF)
    loop(0, NQ, lambda q: heads_out(R.OB, R.OF, q, ysend.at[1], R.rrecv.at[1, q]))
    two_cross(R.W1, 2)
    gather_wait(R.WB3F, 17)

    def second_rows(q):
        drain(R.OF.at[pl.ds(0, CH), pl.ds(0, 768)], R.rrecv.at[1, q])
        x1 = R.XS[local_of(q), :] + nt(R.OF[local_of(q), :], R.WB3F[...]) + vrow(7)
        n, r = ln_parts(x1)
        share_send(1, q, (n * vrow(8) + vrow(9)).astype(BF))
        R.XS[local_of(q), :] = x1
        keep_norm(1, q, n, r)

    loop(0, NQ // 2, second_rows)
    two_cross(R.W2, 3)
    loop(NQ // 2, NQ, second_rows)
    two_second(R.HW, 0)
    two_first(R.WA3F, 9)
    gather_wait(R.W1, 2)
    gather_wait(R.W2, 3)

    def feed(q):
        share_wait(1, q)
        rows = rows_of(q)
        for n in range(4):
            at = slice(n * 256, (n + 1) * 256)
            u = nn(R.AG[1, rows, :], R.W1[:, at]) + R.VRN[pl.ds(10 + m, 1), at]
            phi = 0.5 * (1.0 + lax.erf(u * (1.0 / math.sqrt(2.0))))
            R.GEL[rows, at] = (u * phi).astype(BF)
            R.GELP[rows, at] = phi + u * jnp.exp(-0.5 * u * u) * (1.0 / math.sqrt(2.0 * math.pi))
        branch_send(2, q, R.GEL[rows, :], R.W2)

    loop(0, NQ - 1, feed)
    two_cross(R.HW, 0)
    loop(NQ - 1, NQ, feed)
    two_second(R.WA3F, 9)
    gather_wait(R.HW, 0)
    drain(R.TGT.at[pl.ds(0, 3)], yrecv.at[2])

    def head_rows(q):
        here = local_of(q)
        x2 = R.XS[here, :] + branch_sum(2, q) + vrow(14)
        n, r = ln_parts(x2)
        h3 = (n * vrow(15) + vrow(16)).astype(BF)
        R.H3[here, :] = h3
        pred = nn(h3, R.HW[...])
        weight = R.LW[own_of(q, m), 0:64]
        for j in range(4):
            misfit = pred[:, j * 64 : (j + 1) * 64] - R.TGT[j, q, :, 0:64]
            weighted = weight * misfit
            R.NX[4 + j : 5 + j, 0:64] = R.NX[4 + j : 5 + j, 0:64] + jnp.sum(
                weighted * misfit, 0, keepdims=True
            )
            R.DP[here, j * 64 : (j + 1) * 64] = (2.0 * weighted / total_count).astype(BF)
        dh3 = nt(R.DP[here, :], R.HW[...])
        dx2, dgain, dbias = ln_back(n, r, vrow(15), dh3)
        share_send(2, q, dx2.astype(BF))
        R.XS[here, :] = dx2
        R.GVP[14:15, :] = R.GVP[14:15, :] + jnp.sum(dx2, 0, keepdims=True)
        R.GVP[15:16, :] = R.GVP[15:16, :] + dgain
        R.GVP[16:17, :] = R.GVP[16:17, :] + dbias

    loop(0, NQ, head_rows)

    def feed_back(q):
        share_wait(2, q)
        rows = rows_of(q)
        for n in range(4):
            at = slice(n * 256, (n + 1) * 256)
            du = (nn(R.AG[2, rows, :], R.W2[:, at]) * R.GELP[rows, at]).astype(BF)
            R.DU[rows, at] = du
            row = pl.ds(10 + m, 1)
            R.GVN[row, at] = R.GVN[row, at] + jnp.sum(du.astype(F32), 0, keepdims=True)
        branch_send(3, q, R.DU[rows, :], R.W1)

    loop(0, NQ, feed_back)
    two_cross(R.WA3F, 9)

    def pieces(q, fn):
        for j in range(4 // NQ):
            fn(pl.ds(pl.multiple_of((q * (4 // NQ) + j) * 256, 256), 256))

    def grad_two(at):
        R.G2[at, :] = tn(R.AG[2, :, at], R.GEL[...]).astype(BF)

    def grad_one(at):
        R.G1[at, :] = tn(R.AG[1, :, at], R.DU[...]).astype(BF)

    def back_rows(q):
        here = local_of(q)
        n = R.LN[1, here, :]
        dx1, dgain, dbias = ln_back(n, R.RR[1, here, 0:1], vrow(8), branch_sum(3, q))
        dx1 = dx1 + R.XS[here, :]
        dy = dx1.astype(BF)
        R.DOF[here, :] = nn(dy, R.WB3F[...]).astype(BF)
        heads_back(R.DOF, R.DOB, q, ysend.at[19], R.nrecv.at[0, q])
        R.AG[3, own_of(q, m), :] = dy
        R.XS[here, :] = dx1
        R.GVP[7:8, :] = R.GVP[7:8, :] + jnp.sum(dx1, 0, keepdims=True)
        R.GVP[8:9, :] = R.GVP[8:9, :] + dgain
        R.GVP[9:10, :] = R.GVP[9:10, :] + dbias
        pieces(q, grad_one)

    for n in range(4):
        grad_two(pl.ds(n * 256, 256))
    reduce_cross("2", 13)
    loop(0, NQ // 2, back_rows)
    fold_first("2", 13)
    loop(NQ // 2, NQ, back_rows)
    loop(0, NQ, lambda q: share_start(3, q))
    reduce_cross("1", 12)
    R.GH[...] = tn(R.H3[...], R.DP[...]).astype(BF)
    reduce_cross("H", 14)
    gather_wait(R.WA3F, 16)
    fold_first("1", 12)
    fold_first("H", 14)

    loop(0, NQ, lambda q: drain(R.DOB.at[pl.ds(0, 3 * CH)], R.nrecv.at[0, q]))
    for h in range(4):
        at = slice(h * 64, (h + 1) * 64)
        probs = R.PB[h]
        dout = R.DOB[:, at]
        dv = tn(probs.astype(BF), dout).astype(BF)
        dprob = nt(dout, R.QKV[2, :, at])
        ds = (probs * (dprob - jnp.sum(probs * dprob, 1, keepdims=True))).astype(BF)
        dq = (nn(ds, R.QKV[1, :, at]) * SCALE).astype(BF)
        dk = (tn(ds, R.QKV[0, :, at]) * SCALE).astype(BF)
        R.DQKV[:, h * 64 : (h + 1) * 64] = dq
        R.DQKV[:, 256 + h * 64 : 256 + (h + 1) * 64] = dk
        R.DQKV[:, 512 + h * 64 : 512 + (h + 1) * 64] = dv
    loop(0, NQ, lambda q: branch_send(4, q, R.DQKV[rows_of(q), :], R.WB, (0, 768)))
    fold_second("2", 13)
    R.GVN[5:6, my_cols] = jnp.sum(R.DQKV[:, 0:256].astype(F32), 0, keepdims=True)
    R.GVN[6:7, my_cols] = jnp.sum(R.DQKV[:, 512:768].astype(F32), 0, keepdims=True)

    def grad_attn(at):
        R.GB[at, 0:768] = tn(R.AG[0, :, at], R.DQKV[...]).astype(BF)

    def grad_out(n):
        at = pl.ds(pl.multiple_of(n * 256, 256), 256)
        R.GB[at, 768:1024] = tn(R.AG[3, :, at], R.OB[...]).astype(BF)

    def first_rows(q):
        here = local_of(q)
        n = R.LN[0, here, :]
        dx0, dgain, dbias = ln_back(n, R.RR[0, here, 0:1], vrow(3), branch_sum(4, q))
        dx0 = dx0 + R.XS[here, :]
        dya = dx0.astype(BF)
        R.DMF[here, :] = nn(dya, R.WA3F[...]).astype(BF)
        heads_back(R.DMF, R.DMB, q, ysend.at[20], R.nrecv.at[1, q])
        R.AG[4, own_of(q, m), :] = dya
        lead = R.TCOL[own_of(q, m), 1:2]
        R.GVP[1:2, :] = R.GVP[1:2, :] + jnp.sum(dx0, 0, keepdims=True)
        R.GVP[2:3, :] = R.GVP[2:3, :] + jnp.sum(lead * dx0, 0, keepdims=True)
        R.GVP[3:4, :] = R.GVP[3:4, :] + dgain
        R.GVP[4:5, :] = R.GVP[4:5, :] + dbias

    loop(0, 4, lambda n: grad_attn(pl.ds(pl.multiple_of(n * 256, 256), 256)))
    loop(0, NQ, lambda q: share_wait(3, q))
    loop(0, 4, grad_out)
    reduce_cross("B", 11)
    loop(0, NQ // 2, first_rows)
    fold_first("B", 11)
    loop(NQ // 2, NQ, first_rows)
    loop(0, NQ, lambda q: share_start(4, q))
    fold_second("1", 12)
    fold_second("H", 14)
    R.TMPV[...] = R.GVN[...].T
    R.GVT[...] = R.GVP[...].T.reshape(DPN, 4, 8, 128)

    def permuted(i):
        block = lax.rem(i, 2) * 16 + i // 2
        own = R.TMPV[pl.ds(pl.multiple_of(i * 32, 32), 32), :]
        R.GVT[block] = R.GVT[block] + own.reshape(4, 8, 128)

    loop(0, DPN, permuted)
    for g in range(4):
        R.GVK[:, 32 * g : 32 * (g + 1)] = R.GVT[:, g, :, 0:32].reshape(256, 32)
    core_rows = pl.ds(pl.multiple_of(c * 128, 128), 128)
    rcopy(
        R.GVK.at[pl.ds(pl.multiple_of(128 - c * 128, 128), 128)],
        R.GVS,
        ssend.at[15],
        srecv.at[15],
        sib,
        m,
    ).start()
    at_eight = pl.ds(pl.multiple_of(k * 8, 8), 8)

    def vectors_spread():
        drain(R.GVS, srecv.at[15])
        R.GVS[...] = R.GVS[...] + R.GVK[core_rows, :]

        def send(kk, t):
            src = R.GVS.at[pl.ds(pl.multiple_of(kk * 8, 8), 8)]
            rcopy(src, R.GVB.at[at_eight], dsend.at[15], drecv.at[15], t, m).start()

        to_chips(send)

    def vectors_end():
        drain(R.GVB.at[pl.ds(0, 120)], drecv.at[15])
        total = R.GVS[at_eight, :]
        for dz, dx in FAR_FIRST:
            kk = lax.rem(z + dz, 4) * 4 + lax.rem(x + dx, 4)
            total = total + R.GVB[pl.ds(pl.multiple_of(kk * 8, 8), 8), :]
        for g in range(4):
            R.VG[8 * g : 8 * (g + 1), 0:32] = total[:, 32 * g : 32 * (g + 1)]
        drain(R.GVB.at[pl.ds(0, 120)], dsend.at[15])
        drain(R.GVS, ssend.at[15])

    loop(0, NQ, lambda q: drain(R.DMB.at[pl.ds(0, 3 * CH)], R.nrecv.at[1, q]))
    vectors_spread()
    R.PRP[...] = jnp.zeros_like(R.PRP)
    for h in range(4):
        at = slice(h * 64, (h + 1) * 64)
        dout = R.DMB[:, at]
        through = nt(ewv[:, at], dout)
        dprob = R.PIXT[0:48, :] * through[0:48, :]
        for p in range(1, 5):
            row = slice(p * 48, (p + 1) * 48)
            dprob = dprob + R.PIXT[row, :] * through[row, :]
        probs = R.PT[h]
        ds = (probs * (dprob - jnp.sum(probs * dprob, 0, keepdims=True))).astype(BF).astype(F32)
        for p in range(5):
            row = slice(p * 48, (p + 1) * 48)
            R.PRP[row, 256 + h : 257 + h] = jnp.sum(ds * R.PIXT[row, :], 1, keepdims=True)
        R.PRP[:, at] = nn(R.MT[h], dout)
    R.PRB[...] = R.PRP[...].astype(BF)

    lanes = iota((1, 128), 1)
    sums = {"w": jnp.zeros((1, 128), F32), "u": jnp.zeros((1, 128), F32)}

    def square_sum(values):
        return jnp.sum(jnp.sum(values * values, 1, keepdims=True), 0, keepdims=True)

    def tensor(index, weight, gradient, first, second):
        unused, unused2, direction = adam_direction(weight, gradient, first, second)
        here = lanes == index
        sums["w"] = sums["w"] + jnp.where(here, square_sum(weight), 0.0)
        sums["u"] = sums["u"] + jnp.where(here, square_sum(direction), 0.0)

    def hook_second():
        loop(0, NQ, lambda q: share_wait(4, q))

        def piece(n):
            at = pl.ds(pl.multiple_of(n * 256, 256), 256)
            R.GA3[at, :] = tn(R.AG[4, :, at], R.OA[...]).astype(BF)

        loop(0, 4, piece)
        reduce_cross("A3", 10)

    def hook_first():
        for name in MOMENTS:
            fetch(name + "_f").wait()
            fetch(name + "_s").wait()
        R.o_mlp[1] = fold_end("2", 13)
        R.o_mlp[0] = fold_end("1", 12)
        for j in range(2):
            tensor(8 + j, R.in_mlpw[j], R.o_mlp[j], R.in_mlp_f[j], R.in_mlp_s[j])
        fold_second("B", 11)
    def hook_third():
        total = fold_end("H", 14)
        for j in range(MPN):
            R.HG[j, :, 0:64] = total[:, 64 * j : 64 * (j + 1)]
        vectors_end()

        def sends(i, t):
            rcopy(
                R.HG.at[t],
                R.HGR.at[i - 1],
                ysend.at[14],
                yrecv.at[4],
                d,
                t,
            ).start()
            rcopy(
                R.VG.at[pl.ds(pl.multiple_of(t * 8, 8), 8)],
                R.VGR.at[i - 1],
                ysend.at[15],
                yrecv.at[5],
                d,
                t,
            ).start()

        to_peers(sends)
        gsum = fold_end("B", 11)
        for j in range(4):
            R.o_attn[j] = gsum[:, j * 256 : (j + 1) * 256]
        for j in range(4):
            tensor(4 + j, R.in_attnw[j], R.o_attn[j], R.in_attn_f[j], R.in_attn_s[j])
        reduce_spread("A3", 10)

    all_sum(R.PRB, R.PRC, R.PRH, R.PRR, 8, (hook_first, hook_second, hook_third))

    spread = nt(R.PRR[:, 256:384], head_of.astype(BF))
    dqa = jnp.sum(spread * ewk, 0, keepdims=True) * SCALE
    pk = spread * (qa * SCALE)
    pv = R.PRR[:, 0:256]
    emb = R.TA[:, 0:256]
    wa = [R.in_aggw[j].astype(BF).astype(F32) for j in range(3)]
    pk = pk.astype(BF)
    R.TG[...] = nt(wa[1].astype(BF), pk) + nt(wa[2].astype(BF), pv)
    R.TG[:, 240:241] = jnp.sum(wa[0] * dqa, 1, keepdims=True)

    def last_sends(i, t):
        rcopy(
            R.TG.at[pl.ds(pl.multiple_of(t * 8, 8), 8)],
            R.TGR.at[i - 1],
            ysend.at[13],
            yrecv.at[3],
            d,
            t,
        ).start()

    to_peers(last_sends)
    R.o_agg[0] = R.TA[:, 256:257] * dqa
    emb = emb.astype(BF)
    R.o_agg[1] = nn(emb, pk)
    R.o_agg[2] = nn(emb, pv)
    for j in range(3):
        tensor(j, R.in_aggw[j], R.o_agg[j], R.in_agg_f[j], R.in_agg_s[j])
    drain(R.HGR, yrecv.at[4])
    hgrad = R.HG[m] + R.HGR[0] + R.HGR[1] + R.HGR[2]
    R.o_head[...] = hgrad[:, 0:NVAR]
    tensor(10, R.in_headw[...], R.o_head[...], R.in_head_f[...], R.in_head_s[...])
    drain(R.VGR, yrecv.at[5])
    vgrad = R.VG[my_eight, :] + R.VGR[0] + R.VGR[1] + R.VGR[2]
    drain(R.TGR, yrecv.at[3])
    tgrad = R.TG[my_eight, :] + R.TGR[0] + R.TGR[1] + R.TGR[2]
    for p in range(5):
        R.EG[p * 8 : (p + 1) * 8, :] = tgrad[:, p * 48 : (p + 1) * 48]
    R.o_emb[...] = nt(R.EG[...], vhot, HIGH)
    tensor(11, R.in_emb[...], R.o_emb[...], R.in_emb_f[...], R.in_emb_s[...])
    R.o_vec[...] = vgrad[:, 0:NVEC]
    R.o_vec[:, 0:1] = tgrad[:, 240:241]
    unused, unused2, direction = adam_direction(
        R.in_vec[...], R.o_vec[...], R.in_vec_f[...], R.in_vec_s[...]
    )
    R.o_agg[3] = reduce_end("A3", 10)
    tensor(3, R.in_aggw[3], R.o_agg[3], R.in_agg_f[3], R.in_agg_s[3])
    R.o_vw[...] = R.in_vec[...]
    R.o_vf[...] = R.in_vec_f[...]
    R.o_vs[...] = R.in_vec_s[...]
    R.o_run[...] = R.in_run[...]
    R.NX[0:1, :] = sums["w"]
    R.NX[1:2, :] = sums["u"]
    R.NX[0:1, 12 : 12 + NVEC] = jnp.sum(R.in_vec[...] * R.in_vec[...], 0, keepdims=True)
    R.NX[1:2, 12 : 12 + NVEC] = jnp.sum(direction * direction, 0, keepdims=True)

    for j in range(1, 2 * MPN):
        t = lax.rem(m + j, MPN)
        rcopy(
            R.NX, R.NXR.at[j - 1], ysend.at[16], yrecv.at[6], sib if j >= MPN else d, t
        ).start()
    drain(R.NXR, yrecv.at[6])
    norm = R.NX[...]
    for j in range(7):
        norm = norm + R.NXR[j]
    R.NY[...] = norm
    at_k = pl.ds(pl.multiple_of(k * 8, 8), 8)
    to_chips(lambda kk, t: rcopy(R.NY, R.NYR.at[at_k], dsend.at[16], drecv.at[16], t, m).start())

    gather_end(R.VPK, 4)
    for buf, g in ((R.HW, 0), (R.WB, 1), (R.W1, 2), (R.W2, 3), (R.WA3, 8), (R.WA3F, 9), (R.WB3F, 10)):
        two_end(buf, g)
    all_sum_end(R.EWC, R.EWH, R.EWR, 6)
    all_sum_end(R.PRC, R.PRH, R.PRR, 8)
    for ix in range(5):
        if ix == 1:
            drain(R.OF.at[:, pl.ds(0, 768)], ysend.at[1])
        else:
            drain(R.RSR.at[ix], ysend.at[ix])
        drain(R.AG.at[ix, pl.ds(0, 192)], ysend.at[5 + ix])
    drain(R.TA.at[pl.ds(0, 24)], ysend.at[10])
    drain(R.HWS.at[pl.ds(0, 3)], ysend.at[11])
    drain(R.TGT.at[pl.ds(0, 3)], ysend.at[12])
    drain(R.TGR, ysend.at[13])
    drain(R.HGR, ysend.at[14])
    drain(R.VGR, ysend.at[15])
    drain(R.NXR, ysend.at[16])
    drain(R.WB3F.at[pl.ds(0, 32), pl.ds(0, 768)], ysend.at[17])
    drain(R.WA3F.at[pl.ds(0, 32), pl.ds(0, 768)], ysend.at[18])
    drain(R.OF.at[:, pl.ds(0, 768)], ysend.at[19])
    drain(R.OF.at[:, pl.ds(0, 768)], ysend.at[20])

    drain(R.NYR.at[pl.ds(0, 120)], drecv.at[16])
    stats = R.NY[...]
    for dz, dx in FAR_FIRST:
        kk = lax.rem(z + dz, 4) * 4 + lax.rem(x + dx, 4)
        stats = stats + R.NYR[pl.ds(pl.multiple_of(kk * 8, 8), 8), :]
    first_lane = (iota((8, 128), 0) == 0) & (iota((8, 128), 1) == 127)
    R.o_stats[...] = jnp.where(first_lane, total_count, stats)
    drain(R.NYR.at[pl.ds(0, 120)], dsend.at[16])


def mega_call(inputs):
    outs = [SHAPES[n] for n in ("emb", "vec", "agg", "attn", "mlp", "head")] + [((8, 128), F32)]
    outs += [SHAPES["vec"]] * 3 + [SHAPES["run"]]
    whole = pl.BlockSpec(memory_space=pltpu.VMEM)
    return pl.pallas_call(
        mega,
        out_shape=tuple(pltpu.VMEM(*item) for item in outs),
        in_specs=[pl.BlockSpec(memory_space=pl.ANY)] * len(inputs),
        out_specs=(whole,) * len(outs),
        scratch_shapes=[item for unused, item in SCRATCH],
        compiler_params=pltpu.CompilerParams(
            collective_id=0, has_side_effects=True, vmem_limit_bytes=54 * 2**20
        ),
        name="step",
    )(*inputs)


def finish(*refs):
    weights, firsts, seconds, grads = (refs[6 * i : 6 * i + 6] for i in range(4))
    stats, running = refs[24:26]
    o_loss, o_count, o_running, o_trust, o_norms = refs[26:31]
    outs = refs[31:49]
    norms = jnp.sqrt(stats[0:1, :])
    trust = norms / jnp.sqrt(stats[1:2, :])
    o_norms[...] = norms[:, 0:29]
    o_trust[...] = trust[:, 0:29]
    count = stats[0:1, 127:128]
    o_count[...] = count
    errors = jnp.zeros((1, NVAR), F32)
    for j in range(4):
        lane = iota((128, NVAR), 0)
        pick = (lane < NVAR) & (iota((128, NVAR), 1) == 12 * j + lane // P_SIZE)
        errors = errors + nn(stats[4 + j : 5 + j, :], pick.astype(F32), HIGH)
    o_loss[...] = jnp.sum(errors, 1, keepdims=True)
    o_running[...] = STATS_DECAY * running[...] + (1.0 - STATS_DECAY) * errors * (NVAR / count)

    def update(i, at, ratio):
        first, second, direction = adam_direction(
            weights[i][at], grads[i][at], firsts[i][at], seconds[i][at]
        )
        outs[i][at] = first
        outs[6 + i][at] = second
        outs[12 + i][at] = weights[i][at] - LEARN_RATE * ratio * direction

    for i, number, offset in ((0, 4, 0), (1, 4, 4), (2, 2, 8)):
        for j in range(number):
            update(i, j, trust[:, offset + j : offset + j + 1])
    update(3, Ellipsis, trust[:, 10:11])
    update(4, Ellipsis, trust[:, 11:12])
    update(5, Ellipsis, trust[:, 12 : 12 + NVEC])


def finish_call(weights, firsts, seconds, grads, stats, running):
    shapes = [(1, 1), (1, 1), (1, NVAR), (1, 29), (1, 29)] + 3 * [w.shape for w in weights]
    whole = pl.BlockSpec(memory_space=pltpu.VMEM)
    values = (*weights, *firsts, *seconds, *grads, stats, running)
    return pl.pallas_call(
        finish,
        out_shape=tuple(jax.ShapeDtypeStruct(s, F32) for s in shapes),
        in_specs=[whole] * 26,
        out_specs=(whole,) * 23,
        compiler_params=pltpu.CompilerParams(vmem_limit_bytes=32 * 2**20),
        name="finish",
    )(*values)


def on_device(
    pixels,
    targets,
    valid_mask,
    segments,
    lead_index,
    latitude,
    var_ids,
    running_error,
    *tensors,
):
    def turned(group):
        agg, attn, mlp, head, embed, vecs = group
        return (agg, attn, mlp, head, embed.transpose(1, 2, 0).reshape(40, NVAR), vecs.T)

    weights, firsts, seconds = (turned(tensors[6 * i : 6 * i + 6]) for i in range(3))
    agg, attn, mlp, head, embed, vecs = weights
    first = (embed, var_ids.reshape(1, NVAR), vecs, agg, head, mlp, attn, targets.T, pixels.T)
    second = (
        valid_mask.T,
        segments,
        lead_index,
        latitude.reshape(1, TOK),
        running_error.reshape(1, NVAR),
    )
    g_emb, g_vec, g_agg, g_attn, g_mlp, g_head, stats, *rest = mega_call(
        (*first, *second, *firsts, *seconds)
    )
    grads = (g_agg, g_attn, g_mlp, g_head, g_emb, g_vec)
    weights, firsts, seconds = (
        (*group[:5], own) for group, own in zip((weights, firsts, seconds), rest)
    )
    out = finish_call(weights, firsts, seconds, grads, stats, rest[3])

    def back(group):
        agg, attn, mlp, head, embed, vecs = group
        return (agg, attn, mlp, head, embed.reshape(5, 8, NVAR).transpose(2, 0, 1), vecs.T)

    return (
        out[0].reshape(()),
        out[1].reshape(()),
        out[2].reshape(NVAR),
        out[3].reshape(29),
        out[4].reshape(29),
        *back(out[5:11]),
        *back(out[11:17]),
        *back(out[17:23]),
    )


def solution(mesh):
    weights = (
        P(None, "dp", "mp"),
        P(None, "dp", "mp"),
        P(None, "dp", "mp"),
        P("dp", "mp"),
        P(None, None, ("dp", "mp")),
        P(None, ("dp", "mp")),
    )
    in_specs = (
        P("dp", None),
        P("dp", "mp"),
        P("dp", None),
        P("dp", None),
        P("dp", None),
        P("dp"),
        P(),
        P(),
        *weights,
        *weights,
        *weights,
    )
    out_specs = (P(), P(), P(), P(), P(), *weights, *weights, *weights)
    return jax.shard_map(
        on_device, mesh=mesh, in_specs=in_specs, out_specs=out_specs, check_vma=False
    )
```

```python
import math

import jax
import jax.numpy as jnp
from jax import lax
from jax.experimental import pallas as pl
from jax.experimental.pallas import tpu as pltpu
from jax.sharding import PartitionSpec as P

D = 1024
HEAD_DIM = 64
FF = 4096
NVAR = 48
P_SIZE = 4
SEGS = 4
LEADS = 28
LATS = 32
STEP = 10
NVEC = 17
EROWS = NVAR * (P_SIZE + 1)

HIGH = lax.Precision.HIGHEST
NORM_EPS = 1e-06
BETA_ONE = 0.9
BETA_TWO = 0.999
LEARN_RATE = 0.3
WEIGHT_DECAY = 0.01
ADAM_EPS = 1e-08
STATS_DECAY = 0.9
MESH = pl.DeviceIdType.MESH
BF = jnp.bfloat16
F32 = jnp.float32

DPN, MPN, CHIPS, SH, TOK, COLS = 32, 4, 16, 64, 256, 256
NQ = 4
RQ, CH = TOK // NQ, SH // NQ
SCALE = 1.0 / math.sqrt(HEAD_DIM)
FAR_FIRST = sorted(
    ((dz, dx) for dz in range(4) for dx in range(4) if dz or dx),
    key=lambda o: -(min(o[0], 4 - o[0]) + min(o[1], 4 - o[1])),
)


def nn(a, b, precision=None):
    return lax.dot_general(
        a, b, (((1,), (0,)), ((), ())), preferred_element_type=F32, precision=precision
    )


def nt(a, b, precision=None):
    return lax.dot_general(
        a, b, (((1,), (1,)), ((), ())), preferred_element_type=F32, precision=precision
    )


def tn(a, b, precision=None):
    return lax.dot_general(
        a, b, (((0,), (0,)), ((), ())), preferred_element_type=F32, precision=precision
    )


def latitude_weights():
    cosines = [
        math.cos(((j + 0.5) * (180.0 / LATS) - 90.0) * (math.pi / 180.0)) for j in range(LATS)
    ]
    mean = sum(cosines) / LATS
    return [value / mean for value in cosines]


def moments_new(gradient, first, second):
    first_new = BETA_ONE * first + (1.0 - BETA_ONE) * gradient
    second_new = BETA_TWO * second + (1.0 - BETA_TWO) * gradient * gradient
    return first_new, second_new


def adam_direction(weight, gradient, first, second):
    first_new, second_new = moments_new(gradient, first, second)
    first_hat = first_new * (1.0 / (1.0 - BETA_ONE**STEP))
    second_hat = second_new * (1.0 / (1.0 - BETA_TWO**STEP))
    direction = first_hat / (jnp.sqrt(second_hat) + ADAM_EPS) + WEIGHT_DECAY * weight
    return (first_new, second_new, direction)


def iota(shape, dim):
    return lax.broadcasted_iota(jnp.int32, shape, dim)


def ln_parts(x):
    centre = jnp.mean(x, -1, keepdims=True)
    shifted = x - centre
    r = lax.rsqrt(jnp.mean(shifted * shifted, -1, keepdims=True) + NORM_EPS)
    return shifted * r, r


def ln_back(n, r, gain, dh):
    e = dh * gain
    dx = r * (e - jnp.mean(e, -1, keepdims=True) - n * jnp.mean(e * n, -1, keepdims=True))
    dgain = jnp.sum(dh * n, 0, keepdims=True)
    dbias = jnp.sum(dh, 0, keepdims=True)
    return dx, dgain, dbias


LARGE = ("emb", "vid", "vec", "aggw", "headw", "mlpw", "attnw", "targ", "pix")
MOMENTS = ("agg", "attn", "mlp", "head", "emb", "vec")
SMALL = ("mask", "seg", "leadi", "lat", "run")
OUTS = ("o_emb", "o_vec", "o_agg", "o_attn", "o_mlp", "o_head", "o_stats")
OUTS = OUTS + ("o_vw", "o_vf", "o_vs", "o_run")
SHAPES = {
    "pix": ((NVAR * P_SIZE, TOK), BF),
    "targ": ((NVAR, TOK), F32),
    "agg": ((4, 32, 256), F32),
    "attn": ((4, 32, 256), F32),
    "mlp": ((2, 32, 1024), F32),
    "head": ((32, NVAR), F32),
    "emb": ((40, NVAR), F32),
    "vec": ((8, NVEC), F32),
    "mask": ((P_SIZE, TOK), jnp.int32),
    "seg": ((1, TOK), jnp.int32),
    "leadi": ((1, SEGS), jnp.int32),
    "lat": ((1, TOK), jnp.int32),
    "vid": ((1, NVAR), jnp.int32),
    "run": ((1, NVAR), F32),
}
SHAPES.update({"aggw": SHAPES["agg"], "attnw": SHAPES["attn"], "mlpw": SHAPES["mlp"]})
SHAPES["headw"] = SHAPES["head"]
FETCH = LARGE + SMALL + tuple(n + "_f" for n in MOMENTS) + tuple(n + "_s" for n in MOMENTS)


def fetch_shape(name):
    return SHAPES[name[:-2] if name[-2] == "_" else name]


def scratch_list():
    vm = pltpu.VMEM
    dma = pltpu.SemaphoreType.DMA
    items = [
        ("WA3", vm((D, 256), BF)),
        ("WB", vm((D, 768), BF)),
        ("WA3F", vm((D, 1024), BF)),
        ("WB3F", vm((D, 1024), BF)),
        ("W1", vm((D, 1024), BF)),
        ("W2", vm((D, 1024), BF)),
        ("HW", vm((D, 256), BF)),
        ("HWS", vm((MPN, 32, 128), BF)),
        ("VPK", vm((256, 128), F32)),
        ("VEC", vm((DPN, 4, 8, 128), F32)),
        ("VR", vm((128, D), F32)),
        ("VRN", vm((128, D), F32)),
        ("TMPV", vm((D, 128), F32)),
        ("TA", vm((32, 384), F32)),
        ("HWT", vm((32, 128), F32)),
        ("TT", vm((128, TOK), F32)),
        ("TS", vm((NQ, MPN, CH, 128), F32)),
        ("TGT", vm((MPN, NQ, CH, 128), F32)),
        ("ROWS", vm((128, TOK), F32)),
        ("TCOL", vm((TOK, 128), F32)),
        ("LW", vm((TOK, 128), F32)),
        ("PIXT", vm((256, TOK), F32)),
        ("EWP", vm((256, 512), F32)),
        ("EWB", vm((256, 512), BF)),
        ("EWC", vm((256, 512), BF)),
        ("EWH", vm((2, 16, 512), F32)),
        ("EWR", vm((256, 512), BF)),
        ("PRP", vm((256, 384), F32)),
        ("PRB", vm((256, 384), BF)),
        ("PRC", vm((256, 384), BF)),
        ("PRH", vm((2, 16, 384), F32)),
        ("PRR", vm((256, 384), BF)),
        ("MT", vm((4, 256, TOK), BF)),
        ("PT", vm((4, NVAR, TOK), F32)),
        ("OAT", vm((256, TOK), F32)),
        ("OA", vm((TOK, 256), BF)),
        ("RSS", vm((5, TOK, D), BF)),
        ("RSR", vm((5, 3, SH, D), BF)),
        ("AG", vm((5, TOK, D), BF)),
        ("QKV", vm((3, TOK, 256), BF)),
        ("PB", vm((4, TOK, TOK), F32)),
        ("OB", vm((TOK, 256), BF)),
        ("OF", vm((SH, D), BF)),
        ("DOB", vm((TOK, 256), BF)),
        ("DOF", vm((SH, D), BF)),
        ("DMB", vm((TOK, 256), BF)),
        ("DMF", vm((SH, D), BF)),
        ("GEL", vm((TOK, 1024), BF)),
        ("GELP", vm((TOK, 1024), F32)),
        ("DU", vm((TOK, 1024), BF)),
        ("DQKV", vm((TOK, 768), BF)),
        ("LN", vm((2, SH, D), F32)),
        ("XS", vm((SH, D), F32)),
        ("RR", vm((2, SH, 128), F32)),
        ("H3", vm((SH, D), BF)),
        ("DP", vm((SH, 256), BF)),
        ("GVT", vm((DPN, 4, 8, 128), F32)),
        ("GVK", vm((256, 128), F32)),
        ("GVS", vm((128, 128), F32)),
        ("GVB", vm((128, 128), F32)),
        ("GVP", vm((128, D), F32)),
        ("GVN", vm((128, D), F32)),
        ("TG", vm((32, 256), F32)),
        ("TGR", vm((3, 32, 256), F32)),
        ("TGF", vm((32, 256), F32)),
        ("TMO", vm((32, 512), F32)),
        ("WT", vm((32, 256), F32)),
        ("VG", vm((32, 128), F32)),
        ("VGR", vm((3, 8, 128), F32)),
        ("HG", vm((MPN, 32, 128), F32)),
        ("HGR", vm((3, 32, 128), F32)),
        ("EG", vm((40, NVAR), F32)),
        ("NX", vm((8, 128), F32)),
        ("NXR", vm((3, 8, 128), F32)),
        ("NY", vm((8, 128), F32)),
        ("NYR", vm((256, 128), F32)),
    ]
    for name, width, kind in (
        ("A3", 256, BF),
        ("B", 768, BF),
        ("3", 256, BF),
        ("1", 1024, BF),
        ("2", 1024, BF),
        ("H", 256, BF),
    ):
        items.append(("G" + name, vm((D, width), kind)))
        items.append(("S" + name, vm((512, width), kind)))
        if name == "A3":
            items.append(("B" + name, vm((512, width), kind)))
        else:
            items.append(("FP" + name, vm((2, 3, 128, width // 2), kind)))
            items.append(("FQ" + name, vm((2, 3, 32, width // 2), kind)))
    for name in FETCH:
        items.append(("in_" + name, vm(*fetch_shape(name))))
    items += [
        ("fsem", dma((len(FETCH),))),
        ("ysend", dma((22,))),
        ("yrecv", dma((10,))),
        ("nrecv", dma((2, NQ))),
        ("rrecv", dma((5, NQ))),
        ("arecv", dma((5, NQ))),
        ("dsend", dma((19,))),
        ("drecv", dma((19,))),
        ("tsend", dma((12, 4))),
        ("trecv", dma((12, 4))),
        ("ssend", dma((19,))),
        ("srecv", dma((19,))),
    ]
    return items


SCRATCH = scratch_list()
NAMES = tuple(n + "_hbm" for n in FETCH) + OUTS + tuple(n for n, unused in SCRATCH)


def mega(*refs):
    r = dict(zip(NAMES, refs))
    step_kernel(type("Refs", (), r))


def step_kernel(R):
    d = lax.axis_index("dp")
    m = lax.axis_index("mp")
    c = lax.rem(d, 2)
    k = d // 2
    z = k // 4
    x = lax.rem(k, 4)
    sib = d + 1 - 2 * c
    rb = pl.multiple_of(c * 512 + k * 32, 32)
    half = pl.multiple_of(c * 512, 512)
    other = pl.multiple_of(512 - c * 512, 512)
    my_slot = pl.ds(pl.multiple_of(m * 128, 128), 128)
    my_eight = pl.ds(pl.multiple_of(m * 8, 8), 8)
    my_cols = pl.ds(pl.multiple_of(m * COLS, COLS), COLS)

    def rcopy(src, dst, ss, rs, dp, mp):
        return pltpu.make_async_remote_copy(
            src_ref=src,
            dst_ref=dst,
            send_sem=ss,
            recv_sem=rs,
            device_id={"dp": dp, "mp": mp},
            device_id_type=MESH,
        )

    def drain(ref, sem):
        pltpu.make_async_copy(ref, ref, sem).wait()

    def loop(first, last, fn):
        def step(i, carry):
            fn(i)
            return carry

        lax.fori_loop(first, last, step, 0)

    def to_peers(fn):
        for i in (2, 1, 3):
            fn(i, lax.rem(m + i, MPN))

    def to_chips(fn):
        for dz, dx in FAR_FIRST:
            kk = lax.rem(z + dz, 4) * 4 + lax.rem(x + dx, 4)
            fn(kk, kk * 2 + c)

    def fetch(name):
        i = FETCH.index(name)
        return pltpu.make_async_copy(
            getattr(R, name + "_hbm"), getattr(R, "in_" + name), R.fsem.at[i]
        )

    dsend, drecv, ssend, srecv = R.dsend, R.drecv, R.ssend, R.srecv
    ysend, yrecv = R.ysend, R.yrecv

    def gather_start(buf, g):
        block = buf.at[pl.ds(pl.multiple_of(c * 128 + k * 8, 8), 8)]
        to_chips(lambda kk, t: rcopy(block, block, dsend.at[g], drecv.at[g], t, m).start())

    def gather_cross(buf, g):
        drain(buf.at[pl.ds(0, 120)], drecv.at[g])
        part = buf.at[pl.ds(pl.multiple_of(c * 128, 128), 128)]
        rcopy(part, part, ssend.at[g], srecv.at[g], sib, m).start()

    def gather_wait(buf, g):
        drain(buf.at[pl.ds(0, buf.shape[0] // 2)], srecv.at[g])

    def gather_end(buf, g):
        drain(buf.at[pl.ds(0, 120)], dsend.at[g])
        drain(buf.at[pl.ds(0, 128)], ssend.at[g])

    def along(axis, i):
        if axis == "x":
            return (z * 4 + lax.rem(x + i, 4)) * 2 + c
        return (lax.rem(z + i, 4) * 4 + x) * 2 + c

    def sides(buf):
        n = buf.shape[1] // 2
        return pl.ds(0, n), pl.ds(n, n)

    def tcopy(src, dst, g, j, t):
        rcopy(src, dst, R.tsend.at[g, j], R.trecv.at[g, j], t, m).start()

    def two_first(buf, g):
        left, right = sides(buf)
        for i in (2, 1, 3):
            block = buf.at[pl.ds(rb, 32), left]
            tcopy(block, block, g, 0, along("x", i))
            block = buf.at[pl.ds(rb, 32), right]
            tcopy(block, block, g, 1, along("z", i))

    def two_second(buf, g):
        left, right = sides(buf)
        drain(buf.at[pl.ds(0, 96), left], R.trecv.at[g, 0])
        block = buf.at[pl.ds(pl.multiple_of(half + z * 128, 128), 128), left]
        for i in (2, 1, 3):
            tcopy(block, block, g, 2, along("z", i))
        drain(buf.at[pl.ds(0, 96), right], R.trecv.at[g, 1])

        def send(zz):
            block = buf.at[pl.ds(pl.multiple_of(half + zz * 128 + x * 32, 32), 32), right]
            for i in (2, 1, 3):
                tcopy(block, block, g, 3, along("x", i))

        loop(0, 4, send)

    def two_cross(buf, g):
        for side, j in zip(sides(buf), (2, 3)):
            drain(buf.at[pl.ds(0, 384), side], R.trecv.at[g, j])
        part = buf.at[pl.ds(half, 512)]
        g = {8: 5, 9: 16, 10: 17}.get(g, g)
        rcopy(part, part, ssend.at[g], srecv.at[g], sib, m).start()

    def two_end(buf, g):
        left, right = sides(buf)
        for j, rows in ((0, 96), (1, 96), (2, 384), (3, 384)):
            drain(buf.at[pl.ds(0, rows), left if j % 2 == 0 else right], R.tsend.at[g, j])
        drain(buf.at[pl.ds(0, 512)], ssend.at[{8: 5, 9: 16, 10: 17}.get(g, g)])

    def reduce_cross(name, g):
        buf, sbuf = getattr(R, "G" + name), getattr(R, "S" + name)
        rcopy(buf.at[pl.ds(other, 512)], sbuf, ssend.at[g], srecv.at[g], sib, m).start()

    def core_sum(name, g):
        buf, sbuf = getattr(R, "G" + name), getattr(R, "S" + name)
        drain(sbuf, srecv.at[g])

        def add(i):
            at = pl.multiple_of(i * 128, 128)
            sbuf[pl.ds(at, 128), :] = (
                sbuf[pl.ds(at, 128), :].astype(F32)
                + buf[pl.ds(pl.multiple_of(half + at, 128), 128), :].astype(F32)
            ).astype(sbuf.dtype)

        loop(0, 4, add)

    def reduce_spread(name, g):
        core_sum(name, g)
        sbuf, bbuf = getattr(R, "S" + name), getattr(R, "B" + name)
        land = bbuf.at[pl.ds(pl.multiple_of(k * 32, 32), 32)]

        def send(kk, t):
            src = sbuf.at[pl.ds(pl.multiple_of(kk * 32, 32), 32)]
            rcopy(src, land, dsend.at[g], drecv.at[g], t, m).start()

        to_chips(send)

    def row_block(zz, xx):
        return pl.ds(pl.multiple_of(zz * 128 + xx * 32, 32), 32)

    def fold_first(name, g):
        core_sum(name, g)
        sbuf, pbuf = getattr(R, "S" + name), getattr(R, "FP" + name)
        left, right = sides(sbuf)
        for i in (2, 1, 3):
            zz = lax.rem(z + i, 4)
            src = sbuf.at[pl.ds(pl.multiple_of(zz * 128, 128), 128), left]
            tcopy(src, pbuf.at[0, i - 1], g - 7, 0, along("z", i))

        def send(zz):
            for i in (2, 1, 3):
                src = sbuf.at[row_block(zz, lax.rem(x + i, 4)), right]
                land = pbuf.at[1, i - 1, pl.ds(pl.multiple_of(zz * 32, 32), 32)]
                tcopy(src, land, g - 7, 1, along("x", i))

        loop(0, 4, send)

    def fold_second(name, g):
        sbuf, pbuf, qbuf = getattr(R, "S" + name), getattr(R, "FP" + name), getattr(R, "FQ" + name)
        left, right = sides(sbuf)
        for side, j in ((left, 0), (right, 1)):
            drain(pbuf.at[j], R.trecv.at[g - 7, j])

            def add(i):
                at = row_block(z, i) if j == 0 else row_block(i, x)
                acc = sbuf[at, side].astype(F32)
                for n in range(3):
                    acc = acc + pbuf[j, n, pl.ds(pl.multiple_of(i * 32, 32), 32), :].astype(F32)
                sbuf[at, side] = acc.astype(sbuf.dtype)

            loop(0, 4, add)
            for i in (2, 1, 3):
                if j == 0:
                    src = sbuf.at[row_block(z, lax.rem(x + i, 4)), side]
                    tcopy(src, qbuf.at[0, i - 1], g - 7, 2, along("x", i))
                else:
                    src = sbuf.at[row_block(lax.rem(z + i, 4), x), side]
                    tcopy(src, qbuf.at[1, i - 1], g - 7, 3, along("z", i))

    def fold_end(name, g):
        sbuf, pbuf, qbuf = getattr(R, "S" + name), getattr(R, "FP" + name), getattr(R, "FQ" + name)
        parts = []
        for side, j in zip(sides(sbuf), (0, 1)):
            drain(qbuf.at[j], R.trecv.at[g - 7, 2 + j])
            acc = sbuf[row_block(z, x), side].astype(F32)
            for n in range(3):
                acc = acc + qbuf[j, n].astype(F32)
            parts.append(acc)
            drain(pbuf.at[j], R.tsend.at[g - 7, j])
            drain(qbuf.at[j], R.tsend.at[g - 7, 2 + j])
        drain(sbuf, ssend.at[g])
        return jnp.concatenate(parts, 1)

    def reduce_end(name, g):
        sbuf, bbuf = getattr(R, "S" + name), getattr(R, "B" + name)
        drain(bbuf.at[pl.ds(0, 480)], drecv.at[g])

        def add(i, acc):
            at = pl.multiple_of(lax.rem(k + i, CHIPS) * 32, 32)
            return acc + bbuf[pl.ds(at, 32), :].astype(F32)

        total = lax.fori_loop(
            1, CHIPS, add, sbuf[pl.ds(pl.multiple_of(k * 32, 32), 32), :].astype(F32)
        )
        drain(bbuf.at[pl.ds(0, 480)], dsend.at[g])
        drain(sbuf, ssend.at[g])
        return total

    def all_sum(src, cbuf, hbuf, res, g, hooks):
        at_k = pl.ds(pl.multiple_of(k * 16, 16), 16)

        def send(kk, t):
            block = src.at[pl.ds(pl.multiple_of(kk * 16, 16), 16)]
            rcopy(block, cbuf.at[at_k], dsend.at[g], drecv.at[g], t, m).start()

        to_chips(send)
        hooks[0]()
        drain(cbuf.at[pl.ds(0, 240)], drecv.at[g])
        total = src[at_k, :].astype(F32)
        for dz, dx in FAR_FIRST:
            kk = lax.rem(z + dz, 4) * 4 + lax.rem(x + dx, 4)
            total = total + cbuf[pl.ds(pl.multiple_of(kk * 16, 16), 16), :].astype(F32)
        hbuf[0] = total
        rcopy(hbuf.at[0], hbuf.at[1], ssend.at[g], srecv.at[g], sib, m).start()
        hooks[1]()
        drain(hbuf.at[1], srecv.at[g])
        res[at_k, :] = (hbuf[0] + hbuf[1]).astype(BF)
        part = res.at[at_k]
        to_chips(lambda kk, t: rcopy(part, part, dsend.at[g + 1], drecv.at[g + 1], t, m).start())
        hooks[2]()
        drain(res.at[pl.ds(0, 240)], drecv.at[g + 1])

    def all_sum_end(cbuf, hbuf, res, g):
        drain(hbuf.at[0], ssend.at[g])
        drain(cbuf.at[pl.ds(0, 240)], dsend.at[g])
        drain(res.at[pl.ds(0, 240)], dsend.at[g + 1])

    def rows_of(q):
        return pl.ds(pl.multiple_of(q * RQ, RQ), RQ)

    def own_of(q, t):
        return pl.ds(pl.multiple_of(q * RQ + t * CH, CH), CH)

    def local_of(q):
        return pl.ds(pl.multiple_of(q * CH, CH), CH)

    def branch_send(ix, q, left, weight, cols=None):
        for n in range(4):
            at = pl.ds(n * 256, 256)
            w = weight[at, :] if cols is None else weight[at, cols[0] : cols[1]]
            R.RSS[ix, rows_of(q), n * 256 : (n + 1) * 256] = nt(left, w).astype(BF)

        def send(i, t):
            rcopy(
                R.RSS.at[ix, own_of(q, t)],
                R.RSR.at[ix, i - 1, local_of(q)],
                ysend.at[ix],
                R.rrecv.at[ix, q],
                d,
                t,
            ).start()

        to_peers(send)

    def branch_sum(ix, q):
        drain(R.RSR.at[ix, :, pl.ds(0, CH)], R.rrecv.at[ix, q])
        acc = R.RSS[ix, own_of(q, m), :].astype(F32)
        for i in range(3):
            acc = acc + R.RSR[ix, i, local_of(q), :].astype(F32)
        return acc

    def share_send(ix, q, values):
        R.AG[ix, own_of(q, m), :] = values
        share_start(ix, q)

    def heads_out(src, dst, q, ss, rs):
        land = dst.at[local_of(q), my_cols]
        to_peers(lambda i, t: rcopy(src.at[own_of(q, t)], land, ss, rs, d, t).start())
        dst[local_of(q), my_cols] = src[own_of(q, m), :]

    def heads_back(src, dst, q, ss, rs):
        def send(i, t):
            block = src.at[local_of(q), pl.ds(pl.multiple_of(t * COLS, COLS), COLS)]
            rcopy(block, dst.at[own_of(q, m)], ss, rs, d, t).start()

        to_peers(send)
        dst[own_of(q, m), :] = src[local_of(q), my_cols]

    def share_start(ix, q):
        block = R.AG.at[ix, own_of(q, m)]
        to_peers(
            lambda i, t: rcopy(block, block, ysend.at[5 + ix], R.arecv.at[ix, q], d, t).start()
        )

    def share_wait(ix, q):
        drain(R.AG.at[ix, pl.ds(0, 3 * CH)], R.arecv.at[ix, q])

    bar = pltpu.get_barrier_semaphore()

    def greet(i):
        pl.semaphore_signal(
            bar, inc=1, device_id={"dp": lax.rem(d + i, DPN), "mp": m}, device_id_type=MESH
        )

    for i in range(1, MPN):
        pl.semaphore_signal(
            bar, inc=1, device_id={"dp": d, "mp": lax.rem(m + i, MPN)}, device_id_type=MESH
        )
    loop(1, DPN, greet)

    for name in FETCH:
        fetch(name).start()

    fetch("vid").wait()
    vhot = (iota((NVAR, NVAR), 0) == R.in_vid[...]).astype(F32)
    fetch("emb").wait()
    fetch("vec").wait()
    chosen = nn(R.in_emb[...], vhot, HIGH)
    R.TA[my_eight, :] = jnp.zeros((8, 384), F32)
    for p in range(5):
        R.TA[my_eight, p * 48 : (p + 1) * 48] = chosen[p * 8 : (p + 1) * 8, :]
    R.TA[my_eight, 256 : 256 + NVEC] = R.in_vec[...]
    fetch("aggw").wait()
    fetch("headw").wait()
    aw = [R.in_aggw[j].astype(BF) for j in range(3)]
    R.WA3[pl.ds(rb, 32), :] = R.in_aggw[3].astype(BF)
    R.HWT[...] = jnp.zeros_like(R.HWT)
    R.HWT[:, 0:NVAR] = R.in_headw[...]
    R.HWS[m] = R.HWT[...].astype(BF)
    fetch("mlpw").wait()
    R.W1[pl.ds(rb, 32), :] = R.in_mlpw[0].astype(BF)
    R.W2[pl.ds(rb, 32), :] = R.in_mlpw[1].astype(BF)
    fetch("attnw").wait()
    for j in range(3):
        R.WB[pl.ds(rb, 32), j * 256 : (j + 1) * 256] = R.in_attnw[j].astype(BF)
    R.WB3F[pl.ds(rb, 32), my_cols] = R.in_attnw[3].astype(BF)
    R.WA3F[pl.ds(rb, 32), my_cols] = R.in_aggw[3].astype(BF)
    fetch("targ").wait()
    R.TT[NVAR:, :] = jnp.zeros((128 - NVAR, TOK), F32)
    R.TT[0:NVAR, :] = R.in_targ[...]
    turned = R.TT[...].T
    for q in range(NQ):
        for t in range(MPN):
            at = q * RQ + t * CH
            R.TS[q, t] = turned[at : at + CH, :]
    R.TGT[m] = R.TS[:, m]
    R.GVP[...] = jnp.zeros_like(R.GVP)
    R.GVN[...] = jnp.zeros_like(R.GVN)
    R.NX[...] = jnp.zeros_like(R.NX)
    R.HG[...] = jnp.zeros_like(R.HG)
    R.VG[...] = jnp.zeros_like(R.VG)
    pl.semaphore_wait(bar, DPN + MPN - 2)

    def first_sends(i, t):
        part = R.TA.at[my_eight]
        rcopy(part, part, ysend.at[10], yrecv.at[0], d, t).start()
        block = R.WB3F.at[pl.ds(rb, 32), my_cols]
        rcopy(block, block, ysend.at[17], yrecv.at[7], d, t).start()

    def later_sends(i, t):
        slot = R.HWS.at[m]
        rcopy(slot, slot, ysend.at[11], yrecv.at[1], d, t).start()
        block = R.WA3F.at[pl.ds(rb, 32), my_cols]
        rcopy(block, block, ysend.at[18], yrecv.at[8], d, t).start()
        rcopy(R.TS.at[:, t], R.TGT.at[m], ysend.at[12], yrecv.at[2], d, t).start()

    to_peers(first_sends)
    two_first(R.WA3, 8)
    two_first(R.WB, 1)
    two_first(R.W1, 2)
    two_first(R.W2, 3)
    to_peers(later_sends)

    fetch("pix").wait()
    for name in SMALL:
        fetch(name).wait()
    rows = iota((256, 192), 0)
    cols = iota((256, 192), 1)
    pick = (rows < 192) & ((lax.rem(rows, NVAR) * P_SIZE + rows // NVAR) == cols)
    pixt = nn(pick.astype(BF), R.in_pix[...])
    row_at = iota((256, TOK), 0)
    R.PIXT[...] = jnp.where(row_at < 192, pixt, jnp.where(row_at < EROWS, 1.0, 0.0))

    drain(R.TA.at[pl.ds(0, 24)], yrecv.at[0])
    emb = R.TA[:, 0:256]
    R.EWP[:, 0:256] = tn(emb, aw[1].astype(F32), HIGH)
    R.EWP[:, 256:512] = tn(emb, aw[2].astype(F32), HIGH)
    R.EWP[240:241, 0:256] = jnp.sum(R.TA[:, 256:257] * aw[0].astype(F32), 0, keepdims=True)
    R.EWB[...] = R.EWP[...].astype(BF)
    keep = R.in_mask[...].astype(F32)
    count = jnp.sum(jnp.sum(keep, 1, keepdims=True), 0, keepdims=True) * NVAR

    def per_patch():
        seg = R.in_seg[...]
        lead_row = jnp.zeros((1, TOK), F32)
        for s in range(SEGS):
            value = (R.in_leadi[:, s : s + 1] + 1).astype(F32) / LEADS
            lead_row = jnp.where(seg == s, value, lead_row)
        lat = R.in_lat[...]
        lat_row = jnp.zeros((1, TOK), F32)
        for j, value in enumerate(latitude_weights()):
            lat_row = jnp.where(lat == j, value, lat_row)
        R.ROWS[...] = jnp.zeros_like(R.ROWS)
        R.ROWS[0:1, :] = seg.astype(F32)
        R.ROWS[1:2, :] = lead_row
        R.ROWS[8:12, :] = keep * lat_row
        R.TCOL[...] = R.ROWS[...].T
        lane = iota((128, 128), 1)
        pick = (lane < NVAR) & (iota((128, 128), 0) == 8 + lax.rem(lane, P_SIZE))
        R.LW[...] = nn(R.TCOL[...], pick.astype(F32), HIGH)

    def own_vectors():
        at = pl.ds(pl.multiple_of(c * 128 + k * 8, 8), 8)
        for g in range(4):
            R.VPK[at, 32 * g : 32 * (g + 1)] = R.TA[8 * g : 8 * (g + 1), 256:288]
        R.VPK[at, 31:32] = jnp.broadcast_to(count, (8, 1))

    def embed_moments():
        for name in ("emb_f", "vec_f", "emb_s", "vec_s"):
            fetch(name).wait()
        R.TMO[my_eight, :] = jnp.zeros((8, 512), F32)
        for start, held, vecs in ((0, R.in_emb_f, R.in_vec_f), (256, R.in_emb_s, R.in_vec_s)):
            picked = nn(held[...], vhot, HIGH)
            for p in range(5):
                lane = start + p * 48
                R.TMO[my_eight, lane : lane + 48] = picked[p * 8 : (p + 1) * 8, :]
            R.TMO[my_eight, start + 240 : start + 241] = vecs[:, 0:1]
        part = R.TMO.at[my_eight]
        to_peers(lambda i, t: rcopy(part, part, ysend.at[21], yrecv.at[9], d, t).start())

    def first_bulk():
        own_vectors()
        two_second(R.WA3, 8)
        gather_start(R.VPK, 4)
        drain(R.WB3F.at[pl.ds(0, 32), pl.ds(0, 768)], yrecv.at[7])
        two_first(R.WB3F, 10)
        per_patch()
        embed_moments()

    def bulk():
        two_second(R.WB, 1)
        gather_cross(R.VPK, 4)
        two_cross(R.WA3, 8)

    all_sum(R.EWB, R.EWC, R.EWH, R.EWR, 6, (first_bulk, lambda: None, bulk))

    two_second(R.WB3F, 10)

    head_of = (iota((256, 128), 0) // HEAD_DIM == iota((256, 128), 1)).astype(F32)
    ewk = R.EWR[:, 0:256].astype(F32)
    qa = ewk[240:241, :]
    qe = nn(ewk * (qa * SCALE), head_of, HIGH)
    ewv = R.EWR[:, 256:512]
    for h in range(4):
        scores = R.PIXT[0:48, :] * qe[0:48, h : h + 1]
        for p in range(1, 5):
            at = slice(p * 48, (p + 1) * 48)
            scores = scores + R.PIXT[at, :] * qe[at, h : h + 1]
        e = jnp.exp(scores - jnp.max(scores, 0, keepdims=True))
        probs = e / jnp.sum(e, 0, keepdims=True)
        R.PT[h] = probs
        probs = probs.astype(BF).astype(F32)
        for p in range(5):
            at = slice(p * 48, (p + 1) * 48)
            R.MT[h, at, :] = (probs * R.PIXT[at, :]).astype(BF)
        R.MT[h, 240:256, :] = jnp.zeros((16, TOK), BF)
        R.OAT[h * 64 : (h + 1) * 64, :] = tn(ewv[:, h * 64 : (h + 1) * 64], R.MT[h])
    R.OA[...] = R.OAT[...].T.astype(BF)

    gather_wait(R.WA3, 5)
    loop(0, NQ, lambda q: branch_send(0, q, R.OA[rows_of(q), :], R.WA3))
    two_second(R.W1, 2)
    gather_wait(R.VPK, 4)
    packed = R.VPK[...].reshape(DPN, 8, 128)
    total_count = jnp.sum(packed, 0)[0:1, 31:32]
    for g in range(4):
        R.VEC[:, g, :, 0:32] = packed[:, :, 32 * g : 32 * (g + 1)]
    R.VR[...] = R.VEC[...].reshape(D, 128).T
    two_cross(R.WB, 1)

    def vrow(i):
        return R.VR[i : i + 1, :]

    def keep_norm(j, q, n, r):
        R.LN[j, local_of(q), :] = n
        R.RR[j, local_of(q), :] = jnp.broadcast_to(r, (CH, 128))

    def mixed_rows(q):
        lead = R.TCOL[own_of(q, m), 1:2]
        x0 = branch_sum(0, q) + vrow(1) + lead * vrow(2)
        n, r = ln_parts(x0)
        share_send(0, q, (n * vrow(3) + vrow(4)).astype(BF))
        R.XS[local_of(q), :] = x0
        keep_norm(0, q, n, r)

    loop(0, NQ // 2, mixed_rows)
    two_second(R.W2, 3)
    loop(NQ // 2, NQ, mixed_rows)

    def natural(i):
        block = R.VEC[lax.rem(i, 2) * 16 + i // 2]
        R.TMPV[pl.ds(pl.multiple_of(i * 32, 32), 32), :] = block.reshape(32, 128)

    loop(0, DPN, natural)
    R.VRN[...] = R.TMPV[...].T
    drain(R.HWS.at[pl.ds(0, 3)], yrecv.at[1])
    R.HW[pl.ds(rb, 32), :] = jnp.concatenate(
        [R.HWS[j].astype(F32)[:, 0:64] for j in range(MPN)], 1
    ).astype(BF)
    two_first(R.HW, 0)
    drain(R.WA3F.at[pl.ds(0, 32), pl.ds(0, 768)], yrecv.at[8])
    gather_wait(R.WB, 1)

    def project(q):
        share_wait(0, q)
        at = rows_of(q)
        h1 = R.AG[0, at, :]
        R.QKV[0, at, :] = (nn(h1, R.WB[:, 0:256]) + R.VRN[5:6, my_cols]).astype(BF)
        R.QKV[1, at, :] = nn(h1, R.WB[:, 256:512]).astype(BF)
        R.QKV[2, at, :] = (nn(h1, R.WB[:, 512:768]) + R.VRN[6:7, my_cols]).astype(BF)

    loop(0, NQ // 2, project)
    two_cross(R.WB3F, 10)
    loop(NQ // 2, NQ, project)
    seg_row = R.in_seg[...].astype(F32)

    same = R.TCOL[:, 0:1] == seg_row
    for h in range(4):
        at = slice(h * 64, (h + 1) * 64)
        scores = nt(R.QKV[0, :, at], R.QKV[1, :, at]) * SCALE
        scores = jnp.where(same, scores, -1e30)
        e = jnp.exp(scores - jnp.max(scores, 1, keepdims=True))
        probs = e / jnp.sum(e, 1, keepdims=True)
        R.PB[h] = probs
        R.OB[:, at] = nn(probs.astype(BF), R.QKV[2, :, at]).astype(BF)
    loop(0, NQ, lambda q: heads_out(R.OB, R.OF, q, ysend.at[1], R.rrecv.at[1, q]))
    two_cross(R.W1, 2)
    gather_wait(R.WB3F, 17)

    def second_rows(q):
        drain(R.OF.at[pl.ds(0, CH), pl.ds(0, 768)], R.rrecv.at[1, q])
        x1 = R.XS[local_of(q), :] + nt(R.OF[local_of(q), :], R.WB3F[...]) + vrow(7)
        n, r = ln_parts(x1)
        share_send(1, q, (n * vrow(8) + vrow(9)).astype(BF))
        R.XS[local_of(q), :] = x1
        keep_norm(1, q, n, r)

    loop(0, NQ // 2, second_rows)
    two_cross(R.W2, 3)
    loop(NQ // 2, NQ, second_rows)
    two_second(R.HW, 0)
    two_first(R.WA3F, 9)
    gather_wait(R.W1, 2)
    gather_wait(R.W2, 3)

    def feed(q):
        share_wait(1, q)
        rows = rows_of(q)
        for n in range(4):
            at = slice(n * 256, (n + 1) * 256)
            u = nn(R.AG[1, rows, :], R.W1[:, at]) + R.VRN[pl.ds(10 + m, 1), at]
            phi = 0.5 * (1.0 + lax.erf(u * (1.0 / math.sqrt(2.0))))
            R.GEL[rows, at] = (u * phi).astype(BF)
            R.GELP[rows, at] = phi + u * jnp.exp(-0.5 * u * u) * (1.0 / math.sqrt(2.0 * math.pi))
        branch_send(2, q, R.GEL[rows, :], R.W2)

    loop(0, NQ - 1, feed)
    two_cross(R.HW, 0)
    loop(NQ - 1, NQ, feed)
    two_second(R.WA3F, 9)
    gather_wait(R.HW, 0)
    drain(R.TGT.at[pl.ds(0, 3)], yrecv.at[2])

    def head_rows(q):
        here = local_of(q)
        x2 = R.XS[here, :] + branch_sum(2, q) + vrow(14)
        n, r = ln_parts(x2)
        h3 = (n * vrow(15) + vrow(16)).astype(BF)
        R.H3[here, :] = h3
        pred = nn(h3, R.HW[...])
        weight = R.LW[own_of(q, m), 0:64]
        for j in range(4):
            misfit = pred[:, j * 64 : (j + 1) * 64] - R.TGT[j, q, :, 0:64]
            weighted = weight * misfit
            R.NX[4 + j : 5 + j, 0:64] = R.NX[4 + j : 5 + j, 0:64] + jnp.sum(
                weighted * misfit, 0, keepdims=True
            )
            R.DP[here, j * 64 : (j + 1) * 64] = (2.0 * weighted / total_count).astype(BF)
        dh3 = nt(R.DP[here, :], R.HW[...])
        dx2, dgain, dbias = ln_back(n, r, vrow(15), dh3)
        share_send(2, q, dx2.astype(BF))
        R.XS[here, :] = dx2
        R.GVP[14:15, :] = R.GVP[14:15, :] + jnp.sum(dx2, 0, keepdims=True)
        R.GVP[15:16, :] = R.GVP[15:16, :] + dgain
        R.GVP[16:17, :] = R.GVP[16:17, :] + dbias

    loop(0, NQ, head_rows)

    def feed_back(q):
        share_wait(2, q)
        rows = rows_of(q)
        for n in range(4):
            at = slice(n * 256, (n + 1) * 256)
            du = (nn(R.AG[2, rows, :], R.W2[:, at]) * R.GELP[rows, at]).astype(BF)
            R.DU[rows, at] = du
            row = pl.ds(10 + m, 1)
            R.GVN[row, at] = R.GVN[row, at] + jnp.sum(du.astype(F32), 0, keepdims=True)
        branch_send(3, q, R.DU[rows, :], R.W1)

    loop(0, NQ, feed_back)
    two_cross(R.WA3F, 9)

    def pieces(q, fn):
        for j in range(4 // NQ):
            fn(pl.ds(pl.multiple_of((q * (4 // NQ) + j) * 256, 256), 256))

    def grad_two(at):
        R.G2[at, :] = tn(R.AG[2, :, at], R.GEL[...]).astype(BF)

    def grad_one(at):
        R.G1[at, :] = tn(R.AG[1, :, at], R.DU[...]).astype(BF)

    def back_rows(q):
        here = local_of(q)
        n = R.LN[1, here, :]
        dx1, dgain, dbias = ln_back(n, R.RR[1, here, 0:1], vrow(8), branch_sum(3, q))
        dx1 = dx1 + R.XS[here, :]
        dy = dx1.astype(BF)
        R.DOF[here, :] = nn(dy, R.WB3F[...]).astype(BF)
        heads_back(R.DOF, R.DOB, q, ysend.at[19], R.nrecv.at[0, q])
        R.AG[3, own_of(q, m), :] = dy
        R.XS[here, :] = dx1
        R.GVP[7:8, :] = R.GVP[7:8, :] + jnp.sum(dx1, 0, keepdims=True)
        R.GVP[8:9, :] = R.GVP[8:9, :] + dgain
        R.GVP[9:10, :] = R.GVP[9:10, :] + dbias
        pieces(q, grad_one)

    for n in range(4):
        grad_two(pl.ds(n * 256, 256))
    reduce_cross("2", 13)
    loop(0, NQ // 2, back_rows)
    fold_first("2", 13)
    loop(NQ // 2, NQ, back_rows)
    loop(0, NQ, lambda q: share_start(3, q))
    reduce_cross("1", 12)
    R.GH[...] = tn(R.H3[...], R.DP[...]).astype(BF)
    reduce_cross("H", 14)
    gather_wait(R.WA3F, 16)
    fold_first("1", 12)
    fold_first("H", 14)

    loop(0, NQ, lambda q: drain(R.DOB.at[pl.ds(0, 3 * CH)], R.nrecv.at[0, q]))
    for h in range(4):
        at = slice(h * 64, (h + 1) * 64)
        probs = R.PB[h]
        dout = R.DOB[:, at]
        dv = tn(probs.astype(BF), dout).astype(BF)
        dprob = nt(dout, R.QKV[2, :, at])
        ds = (probs * (dprob - jnp.sum(probs * dprob, 1, keepdims=True))).astype(BF)
        dq = (nn(ds, R.QKV[1, :, at]) * SCALE).astype(BF)
        dk = (tn(ds, R.QKV[0, :, at]) * SCALE).astype(BF)
        R.DQKV[:, h * 64 : (h + 1) * 64] = dq
        R.DQKV[:, 256 + h * 64 : 256 + (h + 1) * 64] = dk
        R.DQKV[:, 512 + h * 64 : 512 + (h + 1) * 64] = dv
    loop(0, NQ, lambda q: branch_send(4, q, R.DQKV[rows_of(q), :], R.WB, (0, 768)))
    fold_second("2", 13)
    R.GVN[5:6, my_cols] = jnp.sum(R.DQKV[:, 0:256].astype(F32), 0, keepdims=True)
    R.GVN[6:7, my_cols] = jnp.sum(R.DQKV[:, 512:768].astype(F32), 0, keepdims=True)

    def grad_attn(at):
        R.GB[at, :] = tn(R.AG[0, :, at], R.DQKV[...]).astype(BF)

    def grad_out(n):
        at = pl.ds(pl.multiple_of(n * 256, 256), 256)
        R.G3[at, :] = tn(R.AG[3, :, at], R.OB[...]).astype(BF)

    def first_rows(q):
        here = local_of(q)
        n = R.LN[0, here, :]
        dx0, dgain, dbias = ln_back(n, R.RR[0, here, 0:1], vrow(3), branch_sum(4, q))
        dx0 = dx0 + R.XS[here, :]
        dya = dx0.astype(BF)
        R.DMF[here, :] = nn(dya, R.WA3F[...]).astype(BF)
        heads_back(R.DMF, R.DMB, q, ysend.at[20], R.nrecv.at[1, q])
        R.AG[4, own_of(q, m), :] = dya
        lead = R.TCOL[own_of(q, m), 1:2]
        R.GVP[1:2, :] = R.GVP[1:2, :] + jnp.sum(dx0, 0, keepdims=True)
        R.GVP[2:3, :] = R.GVP[2:3, :] + jnp.sum(lead * dx0, 0, keepdims=True)
        R.GVP[3:4, :] = R.GVP[3:4, :] + dgain
        R.GVP[4:5, :] = R.GVP[4:5, :] + dbias

    loop(0, NQ, lambda q: share_wait(3, q))
    loop(0, 4, grad_out)
    reduce_cross("3", 18)
    loop(0, 4, lambda n: grad_attn(pl.ds(pl.multiple_of(n * 256, 256), 256)))
    reduce_cross("B", 11)
    fold_first("3", 18)
    loop(0, NQ // 2, first_rows)
    fold_second("1", 12)
    fold_first("B", 11)
    loop(0, NQ // 2, lambda q: share_start(4, q))
    loop(NQ // 2, NQ, first_rows)
    loop(NQ // 2, NQ, lambda q: share_start(4, q))
    R.TMPV[...] = R.GVN[...].T
    R.GVT[...] = R.GVP[...].T.reshape(DPN, 4, 8, 128)

    def permuted(i):
        block = lax.rem(i, 2) * 16 + i // 2
        own = R.TMPV[pl.ds(pl.multiple_of(i * 32, 32), 32), :]
        R.GVT[block] = R.GVT[block] + own.reshape(4, 8, 128)

    loop(0, DPN, permuted)
    for g in range(4):
        R.GVK[:, 32 * g : 32 * (g + 1)] = R.GVT[:, g, :, 0:32].reshape(256, 32)
    core_rows = pl.ds(pl.multiple_of(c * 128, 128), 128)
    rcopy(
        R.GVK.at[pl.ds(pl.multiple_of(128 - c * 128, 128), 128)],
        R.GVS,
        ssend.at[15],
        srecv.at[15],
        sib,
        m,
    ).start()
    at_eight = pl.ds(pl.multiple_of(k * 8, 8), 8)

    def vectors_spread():
        drain(R.GVS, srecv.at[15])
        R.GVS[...] = R.GVS[...] + R.GVK[core_rows, :]

        def send(kk, t):
            src = R.GVS.at[pl.ds(pl.multiple_of(kk * 8, 8), 8)]
            rcopy(src, R.GVB.at[at_eight], dsend.at[15], drecv.at[15], t, m).start()

        to_chips(send)

    def vectors_end():
        drain(R.GVB.at[pl.ds(0, 120)], drecv.at[15])
        total = R.GVS[at_eight, :]
        for dz, dx in FAR_FIRST:
            kk = lax.rem(z + dz, 4) * 4 + lax.rem(x + dx, 4)
            total = total + R.GVB[pl.ds(pl.multiple_of(kk * 8, 8), 8), :]
        for g in range(4):
            R.VG[8 * g : 8 * (g + 1), 0:32] = total[:, 32 * g : 32 * (g + 1)]
        drain(R.GVB.at[pl.ds(0, 120)], dsend.at[15])
        drain(R.GVS, ssend.at[15])

    loop(0, NQ, lambda q: drain(R.DMB.at[pl.ds(0, 3 * CH)], R.nrecv.at[1, q]))
    vectors_spread()
    R.PRP[...] = jnp.zeros_like(R.PRP)
    for h in range(4):
        at = slice(h * 64, (h + 1) * 64)
        dout = R.DMB[:, at]
        through = nt(ewv[:, at], dout)
        dprob = R.PIXT[0:48, :] * through[0:48, :]
        for p in range(1, 5):
            row = slice(p * 48, (p + 1) * 48)
            dprob = dprob + R.PIXT[row, :] * through[row, :]
        probs = R.PT[h]
        ds = (probs * (dprob - jnp.sum(probs * dprob, 0, keepdims=True))).astype(BF).astype(F32)
        for p in range(5):
            row = slice(p * 48, (p + 1) * 48)
            R.PRP[row, 256 + h : 257 + h] = jnp.sum(ds * R.PIXT[row, :], 1, keepdims=True)
        R.PRP[:, at] = nn(R.MT[h], dout)
    R.PRB[...] = R.PRP[...].astype(BF)

    lanes = iota((1, 128), 1)
    sums = {"w": jnp.zeros((1, 128), F32), "u": jnp.zeros((1, 128), F32)}

    def square_sum(values):
        return jnp.sum(jnp.sum(values * values, 1, keepdims=True), 0, keepdims=True)

    def tensor(index, weight, gradient, first, second):
        unused, unused2, direction = adam_direction(weight, gradient, first, second)
        here = lanes == index
        sums["w"] = sums["w"] + jnp.where(here, square_sum(weight), 0.0)
        sums["u"] = sums["u"] + jnp.where(here, square_sum(direction), 0.0)

    def hook_first():
        loop(0, NQ, lambda q: share_wait(4, q))

        def piece(n):
            at = pl.ds(pl.multiple_of(n * 256, 256), 256)
            R.GA3[at, :] = tn(R.AG[4, :, at], R.OA[...]).astype(BF)

        loop(0, 4, piece)
        reduce_cross("A3", 10)
        fold_second("H", 14)
        fold_second("3", 18)
        reduce_spread("A3", 10)

    def hook_second():
        fold_second("B", 11)

    def hook_third():
        total = fold_end("H", 14)
        for j in range(MPN):
            R.HG[j, :, 0:64] = total[:, 64 * j : 64 * (j + 1)]
        vectors_end()

        def sends(i, t):
            rcopy(
                R.HG.at[t],
                R.HGR.at[i - 1],
                ysend.at[14],
                yrecv.at[4],
                d,
                t,
            ).start()
            rcopy(
                R.VG.at[pl.ds(pl.multiple_of(t * 8, 8), 8)],
                R.VGR.at[i - 1],
                ysend.at[15],
                yrecv.at[5],
                d,
                t,
            ).start()

        to_peers(sends)
        for name in ("agg", "attn", "mlp", "head"):
            fetch(name + "_f").wait()
            fetch(name + "_s").wait()
        R.o_mlp[1] = fold_end("2", 13)
        R.o_mlp[0] = fold_end("1", 12)
        for j in range(2):
            tensor(8 + j, R.in_mlpw[j], R.o_mlp[j], R.in_mlp_f[j], R.in_mlp_s[j])

    all_sum(R.PRB, R.PRC, R.PRH, R.PRR, 8, (hook_first, hook_second, hook_third))

    spread = nt(R.PRR[:, 256:384], head_of.astype(BF))
    dqa = jnp.sum(spread * ewk, 0, keepdims=True) * SCALE
    pk = spread * (qa * SCALE)
    pv = R.PRR[:, 0:256]
    emb = R.TA[:, 0:256]
    wa = [R.in_aggw[j].astype(BF).astype(F32) for j in range(3)]
    pk = pk.astype(BF)
    R.TG[...] = nt(wa[1].astype(BF), pk) + nt(wa[2].astype(BF), pv)
    R.TG[:, 240:241] = jnp.sum(wa[0] * dqa, 1, keepdims=True)

    to_peers(
        lambda i, t: rcopy(R.TG, R.TGR.at[i - 1], ysend.at[13], yrecv.at[3], d, t).start()
    )
    R.o_agg[0] = R.TA[:, 256:257] * dqa
    emb = emb.astype(BF)
    R.o_agg[1] = nn(emb, pk)
    R.o_agg[2] = nn(emb, pv)
    for j in range(3):
        tensor(j, R.in_aggw[j], R.o_agg[j], R.in_agg_f[j], R.in_agg_s[j])
    gsum = fold_end("B", 11)
    for j in range(3):
        R.o_attn[j] = gsum[:, j * 256 : (j + 1) * 256]
    R.o_attn[3] = fold_end("3", 18)
    for j in range(4):
        tensor(4 + j, R.in_attnw[j], R.o_attn[j], R.in_attn_f[j], R.in_attn_s[j])
    drain(R.HGR, yrecv.at[4])
    hgrad = R.HG[m] + R.HGR[0] + R.HGR[1] + R.HGR[2]
    R.o_head[...] = hgrad[:, 0:NVAR]
    tensor(10, R.in_headw[...], R.o_head[...], R.in_head_f[...], R.in_head_s[...])
    drain(R.VGR, yrecv.at[5])
    vgrad = R.VG[my_eight, :] + R.VGR[0] + R.VGR[1] + R.VGR[2]
    R.o_vec[...] = vgrad[:, 0:NVEC]
    unused, unused2, direction = adam_direction(
        R.in_vec[...], R.o_vec[...], R.in_vec_f[...], R.in_vec_s[...]
    )
    R.o_agg[3] = reduce_end("A3", 10)
    tensor(3, R.in_aggw[3], R.o_agg[3], R.in_agg_f[3], R.in_agg_s[3])
    R.NX[0:1, :] = sums["w"]
    R.NX[1:2, :] = sums["u"]
    vector_w = jnp.sum(R.in_vec[...] * R.in_vec[...], 0, keepdims=True)
    vector_u = jnp.sum(direction * direction, 0, keepdims=True)
    R.NX[0:1, 13 : 12 + NVEC] = vector_w[:, 1:]
    R.NX[1:2, 13 : 12 + NVEC] = vector_u[:, 1:]
    to_peers(lambda i, t: rcopy(R.NX, R.NXR.at[i - 1], ysend.at[16], yrecv.at[6], d, t).start())

    drain(R.TMO.at[pl.ds(0, 24)], yrecv.at[9])
    R.WT[...] = R.TA[:, 0:256]
    R.WT[:, 240:241] = R.TA[:, 256:257]
    R.o_vw[...] = R.in_vec[...]
    R.o_vf[...] = R.in_vec_f[...]
    R.o_vs[...] = R.in_vec_s[...]
    R.o_run[...] = R.in_run[...]
    drain(R.TGR, yrecv.at[3])
    whole = R.TG[...] + R.TGR[0] + R.TGR[1] + R.TGR[2]
    R.TGF[...] = whole
    unused, unused2, direction = adam_direction(
        R.WT[...], whole, R.TMO[:, 0:256], R.TMO[:, 256:512]
    )
    lane = iota((1, 256), 1)

    def two_sums(values):
        columns = jnp.sum(values * values, 0, keepdims=True)
        embed = jnp.sum(jnp.where(lane < 240, columns, 0.0), 1, keepdims=True)
        first = jnp.sum(jnp.where(lane == 240, columns, 0.0), 1, keepdims=True)
        return jnp.where(lanes == 11, embed, 0.0) + jnp.where(lanes == 12, first, 0.0)

    embed_w, embed_u = two_sums(R.WT[...]), two_sums(direction)
    drain(R.NXR, yrecv.at[6])
    R.NY[...] = R.NX[...] + R.NXR[0] + R.NXR[1] + R.NXR[2]
    R.NY[0:1, :] = R.NY[0:1, :] + embed_w
    R.NY[1:2, :] = R.NY[1:2, :] + embed_u
    at_d = pl.ds(pl.multiple_of(d * 8, 8), 8)

    def norm_send(t):
        rcopy(R.NY, R.NYR.at[at_d], dsend.at[16], drecv.at[16], t, m).start()

    for dz, dx in FAR_FIRST:
        chip = lax.rem(z + dz, 4) * 4 + lax.rem(x + dx, 4)
        norm_send(chip * 2)
        norm_send(chip * 2 + 1)
    norm_send(sib)

    tgrad = R.TGF[my_eight, :]
    for p in range(5):
        R.EG[p * 8 : (p + 1) * 8, :] = tgrad[:, p * 48 : (p + 1) * 48]
    R.o_emb[...] = nt(R.EG[...], vhot, HIGH)
    R.o_vec[:, 0:1] = tgrad[:, 240:241]

    gather_end(R.VPK, 4)
    for buf, g in ((R.HW, 0), (R.WB, 1), (R.W1, 2), (R.W2, 3), (R.WA3, 8), (R.WA3F, 9), (R.WB3F, 10)):
        two_end(buf, g)
    all_sum_end(R.EWC, R.EWH, R.EWR, 6)
    all_sum_end(R.PRC, R.PRH, R.PRR, 8)
    for ix in range(5):
        if ix == 1:
            drain(R.OF.at[:, pl.ds(0, 768)], ysend.at[1])
        else:
            drain(R.RSR.at[ix], ysend.at[ix])
        drain(R.AG.at[ix, pl.ds(0, 192)], ysend.at[5 + ix])
    drain(R.TA.at[pl.ds(0, 24)], ysend.at[10])
    drain(R.HWS.at[pl.ds(0, 3)], ysend.at[11])
    drain(R.TGT.at[pl.ds(0, 3)], ysend.at[12])
    drain(R.TGR, ysend.at[13])
    drain(R.HGR, ysend.at[14])
    drain(R.VGR, ysend.at[15])
    drain(R.NXR, ysend.at[16])
    drain(R.TMO.at[pl.ds(0, 24)], ysend.at[21])
    drain(R.WB3F.at[pl.ds(0, 32), pl.ds(0, 768)], ysend.at[17])
    drain(R.WA3F.at[pl.ds(0, 32), pl.ds(0, 768)], ysend.at[18])
    drain(R.OF.at[:, pl.ds(0, 768)], ysend.at[19])
    drain(R.OF.at[:, pl.ds(0, 768)], ysend.at[20])

    drain(R.NYR.at[pl.ds(0, 248)], drecv.at[16])
    stats = R.NY[...]
    for i in range(1, DPN):
        at = pl.multiple_of(lax.rem(d + i, DPN) * 8, 8)
        stats = stats + R.NYR[pl.ds(at, 8), :]
    first_lane = (iota((8, 128), 0) == 0) & (iota((8, 128), 1) == 127)
    R.o_stats[...] = jnp.where(first_lane, total_count, stats)
    drain(R.NYR.at[pl.ds(0, 248)], dsend.at[16])


def mega_call(inputs):
    outs = [SHAPES[n] for n in ("emb", "vec", "agg", "attn", "mlp", "head")] + [((8, 128), F32)]
    outs += [SHAPES["vec"]] * 3 + [SHAPES["run"]]
    whole = pl.BlockSpec(memory_space=pltpu.VMEM)
    return pl.pallas_call(
        mega,
        out_shape=tuple(pltpu.VMEM(*item) for item in outs),
        in_specs=[pl.BlockSpec(memory_space=pl.ANY)] * len(inputs),
        out_specs=(whole,) * len(outs),
        scratch_shapes=[item for unused, item in SCRATCH],
        compiler_params=pltpu.CompilerParams(
            collective_id=0, has_side_effects=True, vmem_limit_bytes=56 * 2**20
        ),
        name="step",
    )(*inputs)


def finish(*refs):
    weights, firsts, seconds, grads = (refs[6 * i : 6 * i + 6] for i in range(4))
    stats, running = refs[24:26]
    o_loss, o_count, o_running, o_trust, o_norms = refs[26:31]
    outs = refs[31:49]
    norms = jnp.sqrt(stats[0:1, :])
    trust = norms / jnp.sqrt(stats[1:2, :])
    o_norms[...] = norms[:, 0:29]
    o_trust[...] = trust[:, 0:29]
    count = stats[0:1, 127:128]
    o_count[...] = count
    errors = jnp.zeros((1, NVAR), F32)
    for j in range(4):
        lane = iota((128, NVAR), 0)
        pick = (lane < NVAR) & (iota((128, NVAR), 1) == 12 * j + lane // P_SIZE)
        errors = errors + nn(stats[4 + j : 5 + j, :], pick.astype(F32), HIGH)
    o_loss[...] = jnp.sum(errors, 1, keepdims=True)
    o_running[...] = STATS_DECAY * running[...] + (1.0 - STATS_DECAY) * errors * (NVAR / count)

    def update(i, at, ratio):
        first, second, direction = adam_direction(
            weights[i][at], grads[i][at], firsts[i][at], seconds[i][at]
        )
        outs[i][at] = first
        outs[6 + i][at] = second
        outs[12 + i][at] = weights[i][at] - LEARN_RATE * ratio * direction

    for i, number, offset in ((0, 4, 0), (1, 4, 4), (2, 2, 8)):
        for j in range(number):
            update(i, j, trust[:, offset + j : offset + j + 1])
    update(3, Ellipsis, trust[:, 10:11])
    update(4, Ellipsis, trust[:, 11:12])
    update(5, Ellipsis, trust[:, 12 : 12 + NVEC])


def finish_call(weights, firsts, seconds, grads, stats, running):
    shapes = [(1, 1), (1, 1), (1, NVAR), (1, 29), (1, 29)] + 3 * [w.shape for w in weights]
    whole = pl.BlockSpec(memory_space=pltpu.VMEM)
    values = (*weights, *firsts, *seconds, *grads, stats, running)
    return pl.pallas_call(
        finish,
        out_shape=tuple(jax.ShapeDtypeStruct(s, F32) for s in shapes),
        in_specs=[whole] * 26,
        out_specs=(whole,) * 23,
        compiler_params=pltpu.CompilerParams(vmem_limit_bytes=32 * 2**20),
        name="finish",
    )(*values)


def on_device(
    pixels,
    targets,
    valid_mask,
    segments,
    lead_index,
    latitude,
    var_ids,
    running_error,
    *tensors,
):
    def turned(group):
        agg, attn, mlp, head, embed, vecs = group
        return (agg, attn, mlp, head, embed.transpose(1, 2, 0).reshape(40, NVAR), vecs.T)

    weights, firsts, seconds = (turned(tensors[6 * i : 6 * i + 6]) for i in range(3))
    agg, attn, mlp, head, embed, vecs = weights
    first = (embed, var_ids.reshape(1, NVAR), vecs, agg, head, mlp, attn, targets.T, pixels.T)
    second = (
        valid_mask.T,
        segments,
        lead_index,
        latitude.reshape(1, TOK),
        running_error.reshape(1, NVAR),
    )
    g_emb, g_vec, g_agg, g_attn, g_mlp, g_head, stats, *rest = mega_call(
        (*first, *second, *firsts, *seconds)
    )
    grads = (g_agg, g_attn, g_mlp, g_head, g_emb, g_vec)
    weights, firsts, seconds = (
        (*group[:5], own) for group, own in zip((weights, firsts, seconds), rest)
    )
    out = finish_call(weights, firsts, seconds, grads, stats, rest[3])

    def back(group):
        agg, attn, mlp, head, embed, vecs = group
        return (agg, attn, mlp, head, embed.reshape(5, 8, NVAR).transpose(2, 0, 1), vecs.T)

    return (
        out[0].reshape(()),
        out[1].reshape(()),
        out[2].reshape(NVAR),
        out[3].reshape(29),
        out[4].reshape(29),
        *back(out[5:11]),
        *back(out[11:17]),
        *back(out[17:23]),
    )


def solution(mesh):
    weights = (
        P(None, "dp", "mp"),
        P(None, "dp", "mp"),
        P(None, "dp", "mp"),
        P("dp", "mp"),
        P(None, None, ("dp", "mp")),
        P(None, ("dp", "mp")),
    )
    in_specs = (
        P("dp", None),
        P("dp", "mp"),
        P("dp", None),
        P("dp", None),
        P("dp", None),
        P("dp"),
        P(),
        P(),
        *weights,
        *weights,
        *weights,
    )
    out_specs = (P(), P(), P(), P(), P(), *weights, *weights, *weights)
    return jax.shard_map(
        on_device, mesh=mesh, in_specs=in_specs, out_specs=out_specs, check_vma=False
    )
```

```python
import math

import jax
import jax.numpy as jnp
from jax import lax
from jax.experimental import pallas as pl
from jax.experimental.pallas import tpu as pltpu
from jax.sharding import PartitionSpec as P

D = 1024
HEAD_DIM = 64
FF = 4096
NVAR = 48
P_SIZE = 4
SEGS = 4
LEADS = 28
LATS = 32
STEP = 10
NVEC = 17
EROWS = NVAR * (P_SIZE + 1)

HIGH = lax.Precision.HIGHEST
NORM_EPS = 1e-06
BETA_ONE = 0.9
BETA_TWO = 0.999
LEARN_RATE = 0.3
WEIGHT_DECAY = 0.01
ADAM_EPS = 1e-08
STATS_DECAY = 0.9
MESH = pl.DeviceIdType.MESH
BF = jnp.bfloat16
F32 = jnp.float32

DPN, MPN, CHIPS, SH, TOK, COLS = 32, 4, 16, 64, 256, 256
NQ = 4
RQ, CH = TOK // NQ, SH // NQ
SCALE = 1.0 / math.sqrt(HEAD_DIM)
FAR_FIRST = sorted(
    ((dz, dx) for dz in range(4) for dx in range(4) if dz or dx),
    key=lambda o: -(min(o[0], 4 - o[0]) + min(o[1], 4 - o[1])),
)


def nn(a, b, precision=None):
    return lax.dot_general(
        a, b, (((1,), (0,)), ((), ())), preferred_element_type=F32, precision=precision
    )


def nt(a, b, precision=None):
    return lax.dot_general(
        a, b, (((1,), (1,)), ((), ())), preferred_element_type=F32, precision=precision
    )


def tn(a, b, precision=None):
    return lax.dot_general(
        a, b, (((0,), (0,)), ((), ())), preferred_element_type=F32, precision=precision
    )


def latitude_weights():
    cosines = [
        math.cos(((j + 0.5) * (180.0 / LATS) - 90.0) * (math.pi / 180.0)) for j in range(LATS)
    ]
    mean = sum(cosines) / LATS
    return [value / mean for value in cosines]


def moments_new(gradient, first, second):
    first_new = BETA_ONE * first + (1.0 - BETA_ONE) * gradient
    second_new = BETA_TWO * second + (1.0 - BETA_TWO) * gradient * gradient
    return first_new, second_new


def adam_direction(weight, gradient, first, second):
    first_new, second_new = moments_new(gradient, first, second)
    first_hat = first_new * (1.0 / (1.0 - BETA_ONE**STEP))
    second_hat = second_new * (1.0 / (1.0 - BETA_TWO**STEP))
    direction = first_hat / (jnp.sqrt(second_hat) + ADAM_EPS) + WEIGHT_DECAY * weight
    return (first_new, second_new, direction)


def iota(shape, dim):
    return lax.broadcasted_iota(jnp.int32, shape, dim)


def ln_parts(x):
    centre = jnp.mean(x, -1, keepdims=True)
    shifted = x - centre
    r = lax.rsqrt(jnp.mean(shifted * shifted, -1, keepdims=True) + NORM_EPS)
    return shifted * r, r


def ln_back(n, r, gain, dh):
    e = dh * gain
    dx = r * (e - jnp.mean(e, -1, keepdims=True) - n * jnp.mean(e * n, -1, keepdims=True))
    dgain = jnp.sum(dh * n, 0, keepdims=True)
    dbias = jnp.sum(dh, 0, keepdims=True)
    return dx, dgain, dbias


LARGE = ("emb", "vid", "vec", "aggw", "headw", "mlpw", "attnw", "targ", "pix")
MOMENTS = ("agg", "attn", "mlp", "head", "emb", "vec")
SMALL = ("mask", "seg", "leadi", "lat", "run")
OUTS = ("o_emb", "o_vec", "o_agg", "o_attn", "o_mlp", "o_head", "o_stats")
OUTS = OUTS + ("o_vw", "o_vf", "o_vs", "o_run", "o_ew", "o_ef", "o_es")
OUTS = OUTS + ("o_hw", "o_hf", "o_hs")
SHAPES = {
    "pix": ((NVAR * P_SIZE, TOK), BF),
    "targ": ((NVAR, TOK), F32),
    "agg": ((4, 32, 256), F32),
    "attn": ((4, 32, 256), F32),
    "mlp": ((2, 32, 1024), F32),
    "head": ((32, NVAR), F32),
    "emb": ((40, NVAR), F32),
    "vec": ((8, NVEC), F32),
    "mask": ((P_SIZE, TOK), jnp.int32),
    "seg": ((1, TOK), jnp.int32),
    "leadi": ((1, SEGS), jnp.int32),
    "lat": ((1, TOK), jnp.int32),
    "vid": ((1, NVAR), jnp.int32),
    "run": ((1, NVAR), F32),
}
SHAPES.update({"aggw": SHAPES["agg"], "attnw": SHAPES["attn"], "mlpw": SHAPES["mlp"]})
SHAPES["headw"] = SHAPES["head"]
FETCH = LARGE + SMALL + tuple(n + "_f" for n in MOMENTS) + tuple(n + "_s" for n in MOMENTS)


def fetch_shape(name):
    return SHAPES[name[:-2] if name[-2] == "_" else name]


def scratch_list():
    vm = pltpu.VMEM
    dma = pltpu.SemaphoreType.DMA
    items = [
        ("WA3", vm((D, 256), BF)),
        ("WB", vm((D, 768), BF)),
        ("WA3F", vm((D, 1024), BF)),
        ("WB3F", vm((D, 1024), BF)),
        ("W1", vm((D, 1024), BF)),
        ("W2", vm((D, 1024), BF)),
        ("HW", vm((D, 256), BF)),
        ("HWS", vm((MPN, 32, 128), BF)),
        ("VPK", vm((256, 128), F32)),
        ("VEC", vm((DPN, 4, 8, 128), F32)),
        ("VR", vm((128, D), F32)),
        ("VRN", vm((128, D), F32)),
        ("TMPV", vm((D, 128), F32)),
        ("TA", vm((32, 384), F32)),
        ("HWT", vm((32, 128), F32)),
        ("TT", vm((128, TOK), F32)),
        ("TS", vm((NQ, MPN, CH, 128), F32)),
        ("TGT", vm((MPN, NQ, CH, 128), F32)),
        ("ROWS", vm((128, TOK), F32)),
        ("TCOL", vm((TOK, 128), F32)),
        ("LW", vm((TOK, 128), F32)),
        ("PIXT", vm((256, TOK), F32)),
        ("EWP", vm((256, 512), F32)),
        ("EWB", vm((256, 512), BF)),
        ("EWC", vm((256, 512), BF)),
        ("EWH", vm((2, 16, 512), F32)),
        ("EWR", vm((256, 512), BF)),
        ("PRP", vm((256, 384), F32)),
        ("PRB", vm((256, 384), BF)),
        ("PRC", vm((256, 384), BF)),
        ("PRH", vm((2, 16, 384), F32)),
        ("PRR", vm((256, 384), BF)),
        ("MT", vm((4, 256, TOK), BF)),
        ("PT", vm((4, NVAR, TOK), F32)),
        ("OAT", vm((256, TOK), F32)),
        ("OA", vm((TOK, 256), BF)),
        ("RSS", vm((5, TOK, D), BF)),
        ("RSR", vm((5, 3, SH, D), BF)),
        ("AG", vm((5, TOK, D), BF)),
        ("QKV", vm((3, TOK, 256), BF)),
        ("PB", vm((4, TOK, TOK), F32)),
        ("OB", vm((TOK, 256), BF)),
        ("OF", vm((SH, D), BF)),
        ("DOB", vm((TOK, 256), BF)),
        ("DOF", vm((SH, D), BF)),
        ("DMB", vm((TOK, 256), BF)),
        ("DMF", vm((SH, D), BF)),
        ("GEL", vm((TOK, 1024), BF)),
        ("GELP", vm((TOK, 1024), F32)),
        ("DU", vm((TOK, 1024), BF)),
        ("DQKV", vm((TOK, 768), BF)),
        ("LN", vm((2, SH, D), F32)),
        ("XS", vm((SH, D), F32)),
        ("RR", vm((2, SH, 128), F32)),
        ("H3", vm((SH, D), BF)),
        ("DP", vm((SH, 256), BF)),
        ("GVT", vm((DPN, 4, 8, 128), F32)),
        ("GVK", vm((256, 128), F32)),
        ("GVS", vm((128, 128), F32)),
        ("GVB", vm((128, 128), F32)),
        ("GVP", vm((128, D), F32)),
        ("GVN", vm((128, D), F32)),
        ("TG", vm((32, 256), F32)),
        ("TGR", vm((3, 32, 256), F32)),
        ("TGF", vm((32, 256), F32)),
        ("TMO", vm((32, 512), F32)),
        ("WT", vm((32, 256), F32)),
        ("VG", vm((32, 128), F32)),
        ("VGR", vm((3, 8, 128), F32)),
        ("HG", vm((MPN, 32, 128), F32)),
        ("HGR", vm((3, 32, 128), F32)),
        ("EG", vm((40, NVAR), F32)),
        ("NX", vm((8, 128), F32)),
        ("NXR", vm((3, 8, 128), F32)),
        ("NY", vm((8, 128), F32)),
        ("NYR", vm((256, 128), F32)),
    ]
    for name, width, kind in (
        ("A3", 256, BF),
        ("B", 768, BF),
        ("3", 256, BF),
        ("1", 1024, BF),
        ("2", 1024, BF),
        ("H", 256, BF),
    ):
        items.append(("G" + name, vm((D, width), kind)))
        items.append(("S" + name, vm((512, width), kind)))
        if name == "A3":
            items.append(("B" + name, vm((512, width), kind)))
        else:
            items.append(("FP" + name, vm((2, 3, 128, width // 2), kind)))
            items.append(("FQ" + name, vm((2, 3, 32, width // 2), kind)))
    for name in FETCH:
        items.append(("in_" + name, vm(*fetch_shape(name))))
    items += [
        ("fsem", dma((len(FETCH),))),
        ("ysend", dma((22,))),
        ("yrecv", dma((10,))),
        ("nrecv", dma((2, NQ))),
        ("rrecv", dma((5, NQ))),
        ("arecv", dma((5, NQ))),
        ("dsend", dma((19,))),
        ("drecv", dma((19,))),
        ("tsend", dma((12, 4))),
        ("trecv", dma((12, 4))),
        ("ssend", dma((19,))),
        ("srecv", dma((19,))),
    ]
    return items


SCRATCH = scratch_list()
NAMES = tuple(n + "_hbm" for n in FETCH) + OUTS + tuple(n for n, unused in SCRATCH)


def mega(*refs):
    r = dict(zip(NAMES, refs))
    step_kernel(type("Refs", (), r))


def step_kernel(R):
    d = lax.axis_index("dp")
    m = lax.axis_index("mp")
    c = lax.rem(d, 2)
    k = d // 2
    z = k // 4
    x = lax.rem(k, 4)
    sib = d + 1 - 2 * c
    rb = pl.multiple_of(c * 512 + k * 32, 32)
    half = pl.multiple_of(c * 512, 512)
    other = pl.multiple_of(512 - c * 512, 512)
    my_slot = pl.ds(pl.multiple_of(m * 128, 128), 128)
    my_eight = pl.ds(pl.multiple_of(m * 8, 8), 8)
    my_cols = pl.ds(pl.multiple_of(m * COLS, COLS), COLS)

    def rcopy(src, dst, ss, rs, dp, mp):
        return pltpu.make_async_remote_copy(
            src_ref=src,
            dst_ref=dst,
            send_sem=ss,
            recv_sem=rs,
            device_id={"dp": dp, "mp": mp},
            device_id_type=MESH,
        )

    def drain(ref, sem):
        pltpu.make_async_copy(ref, ref, sem).wait()

    def loop(first, last, fn):
        def step(i, carry):
            fn(i)
            return carry

        lax.fori_loop(first, last, step, 0)

    def to_peers(fn):
        for i in (2, 1, 3):
            fn(i, lax.rem(m + i, MPN))

    def to_chips(fn):
        for dz, dx in FAR_FIRST:
            kk = lax.rem(z + dz, 4) * 4 + lax.rem(x + dx, 4)
            fn(kk, kk * 2 + c)

    def fetch(name):
        i = FETCH.index(name)
        return pltpu.make_async_copy(
            getattr(R, name + "_hbm"), getattr(R, "in_" + name), R.fsem.at[i]
        )

    dsend, drecv, ssend, srecv = R.dsend, R.drecv, R.ssend, R.srecv
    ysend, yrecv = R.ysend, R.yrecv

    def gather_start(buf, g):
        block = buf.at[pl.ds(pl.multiple_of(c * 128 + k * 8, 8), 8)]
        to_chips(lambda kk, t: rcopy(block, block, dsend.at[g], drecv.at[g], t, m).start())

    def gather_cross(buf, g):
        drain(buf.at[pl.ds(0, 120)], drecv.at[g])
        part = buf.at[pl.ds(pl.multiple_of(c * 128, 128), 128)]
        rcopy(part, part, ssend.at[g], srecv.at[g], sib, m).start()

    def gather_wait(buf, g):
        drain(buf.at[pl.ds(0, buf.shape[0] // 2)], srecv.at[g])

    def gather_end(buf, g):
        drain(buf.at[pl.ds(0, 120)], dsend.at[g])
        drain(buf.at[pl.ds(0, 128)], ssend.at[g])

    def along(axis, i):
        if axis == "x":
            return (z * 4 + lax.rem(x + i, 4)) * 2 + c
        return (lax.rem(z + i, 4) * 4 + x) * 2 + c

    def sides(buf):
        n = buf.shape[1] // 2
        return pl.ds(0, n), pl.ds(n, n)

    def tcopy(src, dst, g, j, t):
        rcopy(src, dst, R.tsend.at[g, j], R.trecv.at[g, j], t, m).start()

    def two_first(buf, g):
        left, right = sides(buf)
        for i in (2, 1, 3):
            block = buf.at[pl.ds(rb, 32), left]
            tcopy(block, block, g, 0, along("x", i))
            block = buf.at[pl.ds(rb, 32), right]
            tcopy(block, block, g, 1, along("z", i))

    def two_second(buf, g):
        left, right = sides(buf)
        drain(buf.at[pl.ds(0, 96), left], R.trecv.at[g, 0])
        block = buf.at[pl.ds(pl.multiple_of(half + z * 128, 128), 128), left]
        for i in (2, 1, 3):
            tcopy(block, block, g, 2, along("z", i))
        drain(buf.at[pl.ds(0, 96), right], R.trecv.at[g, 1])

        def send(zz):
            block = buf.at[pl.ds(pl.multiple_of(half + zz * 128 + x * 32, 32), 32), right]
            for i in (2, 1, 3):
                tcopy(block, block, g, 3, along("x", i))

        loop(0, 4, send)

    def two_cross(buf, g):
        for side, j in zip(sides(buf), (2, 3)):
            drain(buf.at[pl.ds(0, 384), side], R.trecv.at[g, j])
        part = buf.at[pl.ds(half, 512)]
        g = {8: 5, 9: 16, 10: 17}.get(g, g)
        rcopy(part, part, ssend.at[g], srecv.at[g], sib, m).start()

    def two_end(buf, g):
        left, right = sides(buf)
        for j, rows in ((0, 96), (1, 96), (2, 384), (3, 384)):
            drain(buf.at[pl.ds(0, rows), left if j % 2 == 0 else right], R.tsend.at[g, j])
        drain(buf.at[pl.ds(0, 512)], ssend.at[{8: 5, 9: 16, 10: 17}.get(g, g)])

    def reduce_cross(name, g):
        buf, sbuf = getattr(R, "G" + name), getattr(R, "S" + name)
        rcopy(buf.at[pl.ds(other, 512)], sbuf, ssend.at[g], srecv.at[g], sib, m).start()

    def core_sum(name, g):
        buf, sbuf = getattr(R, "G" + name), getattr(R, "S" + name)
        drain(sbuf, srecv.at[g])

        def add(i):
            at = pl.multiple_of(i * 128, 128)
            sbuf[pl.ds(at, 128), :] = (
                sbuf[pl.ds(at, 128), :].astype(F32)
                + buf[pl.ds(pl.multiple_of(half + at, 128), 128), :].astype(F32)
            ).astype(sbuf.dtype)

        loop(0, 4, add)

    def reduce_spread(name, g):
        core_sum(name, g)
        sbuf, bbuf = getattr(R, "S" + name), getattr(R, "B" + name)
        land = bbuf.at[pl.ds(pl.multiple_of(k * 32, 32), 32)]

        def send(kk, t):
            src = sbuf.at[pl.ds(pl.multiple_of(kk * 32, 32), 32)]
            rcopy(src, land, dsend.at[g], drecv.at[g], t, m).start()

        to_chips(send)

    def row_block(zz, xx):
        return pl.ds(pl.multiple_of(zz * 128 + xx * 32, 32), 32)

    def fold_first(name, g):
        core_sum(name, g)
        sbuf, pbuf = getattr(R, "S" + name), getattr(R, "FP" + name)
        left, right = sides(sbuf)
        for i in (2, 1, 3):
            zz = lax.rem(z + i, 4)
            src = sbuf.at[pl.ds(pl.multiple_of(zz * 128, 128), 128), left]
            tcopy(src, pbuf.at[0, i - 1], g - 7, 0, along("z", i))

        def send(zz):
            for i in (2, 1, 3):
                src = sbuf.at[row_block(zz, lax.rem(x + i, 4)), right]
                land = pbuf.at[1, i - 1, pl.ds(pl.multiple_of(zz * 32, 32), 32)]
                tcopy(src, land, g - 7, 1, along("x", i))

        loop(0, 4, send)

    def fold_second(name, g):
        sbuf, pbuf, qbuf = getattr(R, "S" + name), getattr(R, "FP" + name), getattr(R, "FQ" + name)
        left, right = sides(sbuf)
        for side, j in ((left, 0), (right, 1)):
            drain(pbuf.at[j], R.trecv.at[g - 7, j])

            def add(i):
                at = row_block(z, i) if j == 0 else row_block(i, x)
                acc = sbuf[at, side].astype(F32)
                for n in range(3):
                    acc = acc + pbuf[j, n, pl.ds(pl.multiple_of(i * 32, 32), 32), :].astype(F32)
                sbuf[at, side] = acc.astype(sbuf.dtype)

            loop(0, 4, add)
            for i in (2, 1, 3):
                if j == 0:
                    src = sbuf.at[row_block(z, lax.rem(x + i, 4)), side]
                    tcopy(src, qbuf.at[0, i - 1], g - 7, 2, along("x", i))
                else:
                    src = sbuf.at[row_block(lax.rem(z + i, 4), x), side]
                    tcopy(src, qbuf.at[1, i - 1], g - 7, 3, along("z", i))

    def fold_end(name, g):
        sbuf, pbuf, qbuf = getattr(R, "S" + name), getattr(R, "FP" + name), getattr(R, "FQ" + name)
        parts = []
        for side, j in zip(sides(sbuf), (0, 1)):
            drain(qbuf.at[j], R.trecv.at[g - 7, 2 + j])
            acc = sbuf[row_block(z, x), side].astype(F32)
            for n in range(3):
                acc = acc + qbuf[j, n].astype(F32)
            parts.append(acc)
            drain(pbuf.at[j], R.tsend.at[g - 7, j])
            drain(qbuf.at[j], R.tsend.at[g - 7, 2 + j])
        drain(sbuf, ssend.at[g])
        return jnp.concatenate(parts, 1)

    def reduce_end(name, g):
        sbuf, bbuf = getattr(R, "S" + name), getattr(R, "B" + name)
        drain(bbuf.at[pl.ds(0, 480)], drecv.at[g])

        def add(i, acc):
            at = pl.multiple_of(lax.rem(k + i, CHIPS) * 32, 32)
            return acc + bbuf[pl.ds(at, 32), :].astype(F32)

        total = lax.fori_loop(
            1, CHIPS, add, sbuf[pl.ds(pl.multiple_of(k * 32, 32), 32), :].astype(F32)
        )
        drain(bbuf.at[pl.ds(0, 480)], dsend.at[g])
        drain(sbuf, ssend.at[g])
        return total

    def all_sum(src, cbuf, hbuf, res, g, hooks):
        at_k = pl.ds(pl.multiple_of(k * 16, 16), 16)

        def send(kk, t):
            block = src.at[pl.ds(pl.multiple_of(kk * 16, 16), 16)]
            rcopy(block, cbuf.at[at_k], dsend.at[g], drecv.at[g], t, m).start()

        to_chips(send)
        hooks[0]()
        drain(cbuf.at[pl.ds(0, 240)], drecv.at[g])
        total = src[at_k, :].astype(F32)
        for dz, dx in FAR_FIRST:
            kk = lax.rem(z + dz, 4) * 4 + lax.rem(x + dx, 4)
            total = total + cbuf[pl.ds(pl.multiple_of(kk * 16, 16), 16), :].astype(F32)
        hbuf[0] = total
        rcopy(hbuf.at[0], hbuf.at[1], ssend.at[g], srecv.at[g], sib, m).start()
        hooks[1]()
        drain(hbuf.at[1], srecv.at[g])
        res[at_k, :] = (hbuf[0] + hbuf[1]).astype(BF)
        part = res.at[at_k]
        to_chips(lambda kk, t: rcopy(part, part, dsend.at[g + 1], drecv.at[g + 1], t, m).start())
        hooks[2]()
        drain(res.at[pl.ds(0, 240)], drecv.at[g + 1])

    def all_sum_end(cbuf, hbuf, res, g):
        drain(hbuf.at[0], ssend.at[g])
        drain(cbuf.at[pl.ds(0, 240)], dsend.at[g])
        drain(res.at[pl.ds(0, 240)], dsend.at[g + 1])

    def rows_of(q):
        return pl.ds(pl.multiple_of(q * RQ, RQ), RQ)

    def own_of(q, t):
        return pl.ds(pl.multiple_of(q * RQ + t * CH, CH), CH)

    def local_of(q):
        return pl.ds(pl.multiple_of(q * CH, CH), CH)

    def branch_send(ix, q, left, weight, cols=None):
        for n in range(4):
            at = pl.ds(n * 256, 256)
            w = weight[at, :] if cols is None else weight[at, cols[0] : cols[1]]
            R.RSS[ix, rows_of(q), n * 256 : (n + 1) * 256] = nt(left, w).astype(BF)

        def send(i, t):
            rcopy(
                R.RSS.at[ix, own_of(q, t)],
                R.RSR.at[ix, i - 1, local_of(q)],
                ysend.at[ix],
                R.rrecv.at[ix, q],
                d,
                t,
            ).start()

        to_peers(send)

    def branch_sum(ix, q):
        drain(R.RSR.at[ix, :, pl.ds(0, CH)], R.rrecv.at[ix, q])
        acc = R.RSS[ix, own_of(q, m), :].astype(F32)
        for i in range(3):
            acc = acc + R.RSR[ix, i, local_of(q), :].astype(F32)
        return acc

    def share_send(ix, q, values):
        R.AG[ix, own_of(q, m), :] = values
        share_start(ix, q)

    def heads_out(src, dst, q, ss, rs):
        land = dst.at[local_of(q), my_cols]
        to_peers(lambda i, t: rcopy(src.at[own_of(q, t)], land, ss, rs, d, t).start())
        dst[local_of(q), my_cols] = src[own_of(q, m), :]

    def heads_back(src, dst, q, ss, rs):
        def send(i, t):
            block = src.at[local_of(q), pl.ds(pl.multiple_of(t * COLS, COLS), COLS)]
            rcopy(block, dst.at[own_of(q, m)], ss, rs, d, t).start()

        to_peers(send)
        dst[own_of(q, m), :] = src[local_of(q), my_cols]

    def share_start(ix, q):
        block = R.AG.at[ix, own_of(q, m)]
        to_peers(
            lambda i, t: rcopy(block, block, ysend.at[5 + ix], R.arecv.at[ix, q], d, t).start()
        )

    def share_wait(ix, q):
        drain(R.AG.at[ix, pl.ds(0, 3 * CH)], R.arecv.at[ix, q])

    bar = pltpu.get_barrier_semaphore()

    def greet(i):
        pl.semaphore_signal(
            bar, inc=1, device_id={"dp": lax.rem(d + i, DPN), "mp": m}, device_id_type=MESH
        )

    for i in range(1, MPN):
        pl.semaphore_signal(
            bar, inc=1, device_id={"dp": d, "mp": lax.rem(m + i, MPN)}, device_id_type=MESH
        )
    loop(1, DPN, greet)

    for name in FETCH:
        fetch(name).start()

    fetch("vid").wait()
    vhot = (iota((NVAR, NVAR), 0) == R.in_vid[...]).astype(F32)
    fetch("emb").wait()
    fetch("vec").wait()
    chosen = nn(R.in_emb[...], vhot, HIGH)
    R.TA[my_eight, :] = jnp.zeros((8, 384), F32)
    for p in range(5):
        R.TA[my_eight, p * 48 : (p + 1) * 48] = chosen[p * 8 : (p + 1) * 8, :]
    R.TA[my_eight, 256 : 256 + NVEC] = R.in_vec[...]
    fetch("aggw").wait()
    fetch("headw").wait()
    aw = [R.in_aggw[j].astype(BF) for j in range(3)]
    R.WA3[pl.ds(rb, 32), :] = R.in_aggw[3].astype(BF)
    R.HWT[...] = jnp.zeros_like(R.HWT)
    R.HWT[:, 0:NVAR] = R.in_headw[...]
    R.HWS[m] = R.HWT[...].astype(BF)
    fetch("mlpw").wait()
    R.W1[pl.ds(rb, 32), :] = R.in_mlpw[0].astype(BF)
    R.W2[pl.ds(rb, 32), :] = R.in_mlpw[1].astype(BF)
    fetch("attnw").wait()
    for j in range(3):
        R.WB[pl.ds(rb, 32), j * 256 : (j + 1) * 256] = R.in_attnw[j].astype(BF)
    R.WB3F[pl.ds(rb, 32), my_cols] = R.in_attnw[3].astype(BF)
    R.WA3F[pl.ds(rb, 32), my_cols] = R.in_aggw[3].astype(BF)
    fetch("targ").wait()
    R.TT[NVAR:, :] = jnp.zeros((128 - NVAR, TOK), F32)
    R.TT[0:NVAR, :] = R.in_targ[...]
    turned = R.TT[...].T
    for q in range(NQ):
        for t in range(MPN):
            at = q * RQ + t * CH
            R.TS[q, t] = turned[at : at + CH, :]
    R.TGT[m] = R.TS[:, m]
    R.GVP[...] = jnp.zeros_like(R.GVP)
    R.GVN[...] = jnp.zeros_like(R.GVN)
    R.NX[...] = jnp.zeros_like(R.NX)
    R.HG[...] = jnp.zeros_like(R.HG)
    R.VG[...] = jnp.zeros_like(R.VG)
    pl.semaphore_wait(bar, DPN + MPN - 2)

    def first_sends(i, t):
        part = R.TA.at[my_eight]
        rcopy(part, part, ysend.at[10], yrecv.at[0], d, t).start()
        block = R.WB3F.at[pl.ds(rb, 32), my_cols]
        rcopy(block, block, ysend.at[17], yrecv.at[7], d, t).start()

    def later_sends(i, t):
        slot = R.HWS.at[m]
        rcopy(slot, slot, ysend.at[11], yrecv.at[1], d, t).start()
        block = R.WA3F.at[pl.ds(rb, 32), my_cols]
        rcopy(block, block, ysend.at[18], yrecv.at[8], d, t).start()
        rcopy(R.TS.at[:, t], R.TGT.at[m], ysend.at[12], yrecv.at[2], d, t).start()

    to_peers(first_sends)
    two_first(R.WA3, 8)
    two_first(R.WB, 1)
    two_first(R.W1, 2)
    two_first(R.W2, 3)
    to_peers(later_sends)

    fetch("pix").wait()
    for name in SMALL:
        fetch(name).wait()
    rows = iota((256, 192), 0)
    cols = iota((256, 192), 1)
    pick = (rows < 192) & ((lax.rem(rows, NVAR) * P_SIZE + rows // NVAR) == cols)
    pixt = nn(pick.astype(BF), R.in_pix[...])
    row_at = iota((256, TOK), 0)
    R.PIXT[...] = jnp.where(row_at < 192, pixt, jnp.where(row_at < EROWS, 1.0, 0.0))

    drain(R.TA.at[pl.ds(0, 24)], yrecv.at[0])
    emb = R.TA[:, 0:256]
    R.EWP[:, 0:256] = tn(emb, aw[1].astype(F32), HIGH)
    R.EWP[:, 256:512] = tn(emb, aw[2].astype(F32), HIGH)
    R.EWP[240:241, 0:256] = jnp.sum(R.TA[:, 256:257] * aw[0].astype(F32), 0, keepdims=True)
    R.EWB[...] = R.EWP[...].astype(BF)
    keep = R.in_mask[...].astype(F32)
    count = jnp.sum(jnp.sum(keep, 1, keepdims=True), 0, keepdims=True) * NVAR

    def per_patch():
        seg = R.in_seg[...]
        lead_row = jnp.zeros((1, TOK), F32)
        for s in range(SEGS):
            value = (R.in_leadi[:, s : s + 1] + 1).astype(F32) / LEADS
            lead_row = jnp.where(seg == s, value, lead_row)
        lat = R.in_lat[...]
        lat_row = jnp.zeros((1, TOK), F32)
        for j, value in enumerate(latitude_weights()):
            lat_row = jnp.where(lat == j, value, lat_row)
        R.ROWS[...] = jnp.zeros_like(R.ROWS)
        R.ROWS[0:1, :] = seg.astype(F32)
        R.ROWS[1:2, :] = lead_row
        R.ROWS[8:12, :] = keep * lat_row
        R.TCOL[...] = R.ROWS[...].T
        lane = iota((128, 128), 1)
        pick = (lane < NVAR) & (iota((128, 128), 0) == 8 + lax.rem(lane, P_SIZE))
        R.LW[...] = nn(R.TCOL[...], pick.astype(F32), HIGH)

    def own_vectors():
        at = pl.ds(pl.multiple_of(c * 128 + k * 8, 8), 8)
        for g in range(4):
            R.VPK[at, 32 * g : 32 * (g + 1)] = R.TA[8 * g : 8 * (g + 1), 256:288]
        R.VPK[at, 31:32] = jnp.broadcast_to(count, (8, 1))

    def embed_moments():
        for name in ("emb_f", "vec_f", "emb_s", "vec_s"):
            fetch(name).wait()
        R.TMO[my_eight, :] = jnp.zeros((8, 512), F32)
        for start, held, vecs in ((0, R.in_emb_f, R.in_vec_f), (256, R.in_emb_s, R.in_vec_s)):
            picked = nn(held[...], vhot, HIGH)
            for p in range(5):
                lane = start + p * 48
                R.TMO[my_eight, lane : lane + 48] = picked[p * 8 : (p + 1) * 8, :]
            R.TMO[my_eight, start + 240 : start + 241] = vecs[:, 0:1]
        part = R.TMO.at[my_eight]
        to_peers(lambda i, t: rcopy(part, part, ysend.at[21], yrecv.at[9], d, t).start())

    def first_bulk():
        own_vectors()
        two_second(R.WA3, 8)
        gather_start(R.VPK, 4)
        drain(R.WB3F.at[pl.ds(0, 32), pl.ds(0, 768)], yrecv.at[7])
        two_first(R.WB3F, 10)
        per_patch()
        embed_moments()

    def bulk():
        two_second(R.WB, 1)
        gather_cross(R.VPK, 4)
        two_cross(R.WA3, 8)

    all_sum(R.EWB, R.EWC, R.EWH, R.EWR, 6, (first_bulk, lambda: None, bulk))

    two_second(R.WB3F, 10)

    head_of = (iota((256, 128), 0) // HEAD_DIM == iota((256, 128), 1)).astype(F32)
    ewk = R.EWR[:, 0:256].astype(F32)
    qa = ewk[240:241, :]
    qe = nn(ewk * (qa * SCALE), head_of, HIGH)
    ewv = R.EWR[:, 256:512]
    for h in range(4):
        scores = R.PIXT[0:48, :] * qe[0:48, h : h + 1]
        for p in range(1, 5):
            at = slice(p * 48, (p + 1) * 48)
            scores = scores + R.PIXT[at, :] * qe[at, h : h + 1]
        e = jnp.exp(scores - jnp.max(scores, 0, keepdims=True))
        probs = e / jnp.sum(e, 0, keepdims=True)
        R.PT[h] = probs
        probs = probs.astype(BF).astype(F32)
        for p in range(5):
            at = slice(p * 48, (p + 1) * 48)
            R.MT[h, at, :] = (probs * R.PIXT[at, :]).astype(BF)
        R.MT[h, 240:256, :] = jnp.zeros((16, TOK), BF)
        R.OAT[h * 64 : (h + 1) * 64, :] = tn(ewv[:, h * 64 : (h + 1) * 64], R.MT[h])
    R.OA[...] = R.OAT[...].T.astype(BF)

    gather_wait(R.WA3, 5)
    loop(0, NQ, lambda q: branch_send(0, q, R.OA[rows_of(q), :], R.WA3))
    two_second(R.W1, 2)
    gather_wait(R.VPK, 4)
    packed = R.VPK[...].reshape(DPN, 8, 128)
    total_count = jnp.sum(packed, 0)[0:1, 31:32]
    for g in range(4):
        R.VEC[:, g, :, 0:32] = packed[:, :, 32 * g : 32 * (g + 1)]
    R.VR[...] = R.VEC[...].reshape(D, 128).T
    two_cross(R.WB, 1)

    def vrow(i):
        return R.VR[i : i + 1, :]

    def keep_norm(j, q, n, r):
        R.LN[j, local_of(q), :] = n
        R.RR[j, local_of(q), :] = jnp.broadcast_to(r, (CH, 128))

    def mixed_rows(q):
        lead = R.TCOL[own_of(q, m), 1:2]
        x0 = branch_sum(0, q) + vrow(1) + lead * vrow(2)
        n, r = ln_parts(x0)
        share_send(0, q, (n * vrow(3) + vrow(4)).astype(BF))
        R.XS[local_of(q), :] = x0
        keep_norm(0, q, n, r)

    loop(0, NQ // 2, mixed_rows)
    two_second(R.W2, 3)
    loop(NQ // 2, NQ, mixed_rows)

    def natural(i):
        block = R.VEC[lax.rem(i, 2) * 16 + i // 2]
        R.TMPV[pl.ds(pl.multiple_of(i * 32, 32), 32), :] = block.reshape(32, 128)

    loop(0, DPN, natural)
    R.VRN[...] = R.TMPV[...].T
    drain(R.HWS.at[pl.ds(0, 3)], yrecv.at[1])
    R.HW[pl.ds(rb, 32), :] = jnp.concatenate(
        [R.HWS[j].astype(F32)[:, 0:64] for j in range(MPN)], 1
    ).astype(BF)
    two_first(R.HW, 0)
    drain(R.WA3F.at[pl.ds(0, 32), pl.ds(0, 768)], yrecv.at[8])
    gather_wait(R.WB, 1)

    def project(q):
        share_wait(0, q)
        at = rows_of(q)
        h1 = R.AG[0, at, :]
        R.QKV[0, at, :] = (nn(h1, R.WB[:, 0:256]) + R.VRN[5:6, my_cols]).astype(BF)
        R.QKV[1, at, :] = nn(h1, R.WB[:, 256:512]).astype(BF)
        R.QKV[2, at, :] = (nn(h1, R.WB[:, 512:768]) + R.VRN[6:7, my_cols]).astype(BF)

    loop(0, NQ // 2, project)
    two_cross(R.WB3F, 10)
    loop(NQ // 2, NQ, project)
    seg_row = R.in_seg[...].astype(F32)

    same = R.TCOL[:, 0:1] == seg_row
    for h in range(4):
        at = slice(h * 64, (h + 1) * 64)
        scores = nt(R.QKV[0, :, at], R.QKV[1, :, at]) * SCALE
        scores = jnp.where(same, scores, -1e30)
        e = jnp.exp(scores - jnp.max(scores, 1, keepdims=True))
        probs = e / jnp.sum(e, 1, keepdims=True)
        R.PB[h] = probs
        R.OB[:, at] = nn(probs.astype(BF), R.QKV[2, :, at]).astype(BF)
    loop(0, NQ, lambda q: heads_out(R.OB, R.OF, q, ysend.at[1], R.rrecv.at[1, q]))
    two_cross(R.W1, 2)
    gather_wait(R.WB3F, 17)

    def second_rows(q):
        drain(R.OF.at[pl.ds(0, CH), pl.ds(0, 768)], R.rrecv.at[1, q])
        x1 = R.XS[local_of(q), :] + nt(R.OF[local_of(q), :], R.WB3F[...]) + vrow(7)
        n, r = ln_parts(x1)
        share_send(1, q, (n * vrow(8) + vrow(9)).astype(BF))
        R.XS[local_of(q), :] = x1
        keep_norm(1, q, n, r)

    loop(0, NQ // 2, second_rows)
    two_cross(R.W2, 3)
    loop(NQ // 2, NQ, second_rows)
    two_second(R.HW, 0)
    two_first(R.WA3F, 9)
    gather_wait(R.W1, 2)
    gather_wait(R.W2, 3)

    def feed(q):
        share_wait(1, q)
        rows = rows_of(q)
        for n in range(4):
            at = slice(n * 256, (n + 1) * 256)
            u = nn(R.AG[1, rows, :], R.W1[:, at]) + R.VRN[pl.ds(10 + m, 1), at]
            phi = 0.5 * (1.0 + lax.erf(u * (1.0 / math.sqrt(2.0))))
            R.GEL[rows, at] = (u * phi).astype(BF)
            R.GELP[rows, at] = phi + u * jnp.exp(-0.5 * u * u) * (1.0 / math.sqrt(2.0 * math.pi))
        branch_send(2, q, R.GEL[rows, :], R.W2)

    loop(0, NQ - 1, feed)
    two_cross(R.HW, 0)
    loop(NQ - 1, NQ, feed)
    two_second(R.WA3F, 9)
    gather_wait(R.HW, 0)
    drain(R.TGT.at[pl.ds(0, 3)], yrecv.at[2])

    def head_rows(q):
        here = local_of(q)
        x2 = R.XS[here, :] + branch_sum(2, q) + vrow(14)
        n, r = ln_parts(x2)
        h3 = (n * vrow(15) + vrow(16)).astype(BF)
        R.H3[here, :] = h3
        pred = nn(h3, R.HW[...])
        weight = R.LW[own_of(q, m), 0:64]
        for j in range(4):
            misfit = pred[:, j * 64 : (j + 1) * 64] - R.TGT[j, q, :, 0:64]
            weighted = weight * misfit
            R.NX[4 + j : 5 + j, 0:64] = R.NX[4 + j : 5 + j, 0:64] + jnp.sum(
                weighted * misfit, 0, keepdims=True
            )
            R.DP[here, j * 64 : (j + 1) * 64] = (2.0 * weighted / total_count).astype(BF)
        dh3 = nt(R.DP[here, :], R.HW[...])
        dx2, dgain, dbias = ln_back(n, r, vrow(15), dh3)
        share_send(2, q, dx2.astype(BF))
        R.XS[here, :] = dx2
        R.GVP[14:15, :] = R.GVP[14:15, :] + jnp.sum(dx2, 0, keepdims=True)
        R.GVP[15:16, :] = R.GVP[15:16, :] + dgain
        R.GVP[16:17, :] = R.GVP[16:17, :] + dbias

    loop(0, NQ, head_rows)

    def feed_back(q):
        share_wait(2, q)
        rows = rows_of(q)
        for n in range(4):
            at = slice(n * 256, (n + 1) * 256)
            du = (nn(R.AG[2, rows, :], R.W2[:, at]) * R.GELP[rows, at]).astype(BF)
            R.DU[rows, at] = du
            row = pl.ds(10 + m, 1)
            R.GVN[row, at] = R.GVN[row, at] + jnp.sum(du.astype(F32), 0, keepdims=True)
        branch_send(3, q, R.DU[rows, :], R.W1)

    loop(0, NQ, feed_back)
    two_cross(R.WA3F, 9)

    def pieces(q, fn):
        for j in range(4 // NQ):
            fn(pl.ds(pl.multiple_of((q * (4 // NQ) + j) * 256, 256), 256))

    def grad_two(at):
        R.G2[at, :] = tn(R.AG[2, :, at], R.GEL[...]).astype(BF)

    def grad_one(at):
        R.G1[at, :] = tn(R.AG[1, :, at], R.DU[...]).astype(BF)

    def back_rows(q):
        here = local_of(q)
        n = R.LN[1, here, :]
        dx1, dgain, dbias = ln_back(n, R.RR[1, here, 0:1], vrow(8), branch_sum(3, q))
        dx1 = dx1 + R.XS[here, :]
        dy = dx1.astype(BF)
        R.DOF[here, :] = nn(dy, R.WB3F[...]).astype(BF)
        heads_back(R.DOF, R.DOB, q, ysend.at[19], R.nrecv.at[0, q])
        R.AG[3, own_of(q, m), :] = dy
        R.XS[here, :] = dx1
        R.GVP[7:8, :] = R.GVP[7:8, :] + jnp.sum(dx1, 0, keepdims=True)
        R.GVP[8:9, :] = R.GVP[8:9, :] + dgain
        R.GVP[9:10, :] = R.GVP[9:10, :] + dbias

    for n in range(4):
        grad_two(pl.ds(n * 256, 256))
    reduce_cross("2", 13)
    for n in range(4):
        grad_one(pl.ds(n * 256, 256))
    reduce_cross("1", 12)
    loop(0, NQ // 2, back_rows)
    fold_first("2", 13)
    loop(NQ // 2, NQ, back_rows)
    loop(0, NQ, lambda q: share_start(3, q))
    fold_first("1", 12)
    R.GH[...] = tn(R.H3[...], R.DP[...]).astype(BF)
    reduce_cross("H", 14)
    gather_wait(R.WA3F, 16)
    fold_first("H", 14)

    loop(0, NQ, lambda q: drain(R.DOB.at[pl.ds(0, 3 * CH)], R.nrecv.at[0, q]))
    for h in range(4):
        at = slice(h * 64, (h + 1) * 64)
        probs = R.PB[h]
        dout = R.DOB[:, at]
        dv = tn(probs.astype(BF), dout).astype(BF)
        dprob = nt(dout, R.QKV[2, :, at])
        ds = (probs * (dprob - jnp.sum(probs * dprob, 1, keepdims=True))).astype(BF)
        dq = (nn(ds, R.QKV[1, :, at]) * SCALE).astype(BF)
        dk = (tn(ds, R.QKV[0, :, at]) * SCALE).astype(BF)
        R.DQKV[:, h * 64 : (h + 1) * 64] = dq
        R.DQKV[:, 256 + h * 64 : 256 + (h + 1) * 64] = dk
        R.DQKV[:, 512 + h * 64 : 512 + (h + 1) * 64] = dv
    loop(0, NQ, lambda q: branch_send(4, q, R.DQKV[rows_of(q), :], R.WB, (0, 768)))
    fold_second("2", 13)
    R.GVN[5:6, my_cols] = jnp.sum(R.DQKV[:, 0:256].astype(F32), 0, keepdims=True)
    R.GVN[6:7, my_cols] = jnp.sum(R.DQKV[:, 512:768].astype(F32), 0, keepdims=True)

    def grad_attn(at):
        R.GB[at, :] = tn(R.AG[0, :, at], R.DQKV[...]).astype(BF)

    def grad_out(n):
        at = pl.ds(pl.multiple_of(n * 256, 256), 256)
        R.G3[at, :] = tn(R.AG[3, :, at], R.OB[...]).astype(BF)

    def first_rows(q):
        here = local_of(q)
        n = R.LN[0, here, :]
        dx0, dgain, dbias = ln_back(n, R.RR[0, here, 0:1], vrow(3), branch_sum(4, q))
        dx0 = dx0 + R.XS[here, :]
        dya = dx0.astype(BF)
        R.DMF[here, :] = nn(dya, R.WA3F[...]).astype(BF)
        heads_back(R.DMF, R.DMB, q, ysend.at[20], R.nrecv.at[1, q])
        R.AG[4, own_of(q, m), :] = dya
        lead = R.TCOL[own_of(q, m), 1:2]
        R.GVP[1:2, :] = R.GVP[1:2, :] + jnp.sum(dx0, 0, keepdims=True)
        R.GVP[2:3, :] = R.GVP[2:3, :] + jnp.sum(lead * dx0, 0, keepdims=True)
        R.GVP[3:4, :] = R.GVP[3:4, :] + dgain
        R.GVP[4:5, :] = R.GVP[4:5, :] + dbias

    loop(0, NQ, lambda q: share_wait(3, q))
    loop(0, 4, grad_out)
    reduce_cross("3", 18)
    loop(0, 4, lambda n: grad_attn(pl.ds(pl.multiple_of(n * 256, 256), 256)))
    reduce_cross("B", 11)
    fold_first("3", 18)
    loop(0, NQ // 2, first_rows)
    fold_second("1", 12)
    fold_first("B", 11)
    loop(0, NQ // 2, lambda q: share_start(4, q))
    loop(NQ // 2, NQ, first_rows)
    loop(NQ // 2, NQ, lambda q: share_start(4, q))
    R.TMPV[...] = R.GVN[...].T
    R.GVT[...] = R.GVP[...].T.reshape(DPN, 4, 8, 128)

    def permuted(i):
        block = lax.rem(i, 2) * 16 + i // 2
        own = R.TMPV[pl.ds(pl.multiple_of(i * 32, 32), 32), :]
        R.GVT[block] = R.GVT[block] + own.reshape(4, 8, 128)

    loop(0, DPN, permuted)
    for g in range(4):
        R.GVK[:, 32 * g : 32 * (g + 1)] = R.GVT[:, g, :, 0:32].reshape(256, 32)
    core_rows = pl.ds(pl.multiple_of(c * 128, 128), 128)
    rcopy(
        R.GVK.at[pl.ds(pl.multiple_of(128 - c * 128, 128), 128)],
        R.GVS,
        ssend.at[15],
        srecv.at[15],
        sib,
        m,
    ).start()
    at_eight = pl.ds(pl.multiple_of(k * 8, 8), 8)

    def vectors_spread():
        drain(R.GVS, srecv.at[15])
        R.GVS[...] = R.GVS[...] + R.GVK[core_rows, :]

        def send(kk, t):
            src = R.GVS.at[pl.ds(pl.multiple_of(kk * 8, 8), 8)]
            rcopy(src, R.GVB.at[at_eight], dsend.at[15], drecv.at[15], t, m).start()

        to_chips(send)

    def vectors_end():
        drain(R.GVB.at[pl.ds(0, 120)], drecv.at[15])
        total = R.GVS[at_eight, :]
        for dz, dx in FAR_FIRST:
            kk = lax.rem(z + dz, 4) * 4 + lax.rem(x + dx, 4)
            total = total + R.GVB[pl.ds(pl.multiple_of(kk * 8, 8), 8), :]
        for g in range(4):
            R.VG[8 * g : 8 * (g + 1), 0:32] = total[:, 32 * g : 32 * (g + 1)]
        drain(R.GVB.at[pl.ds(0, 120)], dsend.at[15])
        drain(R.GVS, ssend.at[15])

    loop(0, NQ, lambda q: drain(R.DMB.at[pl.ds(0, 3 * CH)], R.nrecv.at[1, q]))
    vectors_spread()
    R.PRP[...] = jnp.zeros_like(R.PRP)
    for h in range(4):
        at = slice(h * 64, (h + 1) * 64)
        dout = R.DMB[:, at]
        through = nt(ewv[:, at], dout)
        dprob = R.PIXT[0:48, :] * through[0:48, :]
        for p in range(1, 5):
            row = slice(p * 48, (p + 1) * 48)
            dprob = dprob + R.PIXT[row, :] * through[row, :]
        probs = R.PT[h]
        ds = (probs * (dprob - jnp.sum(probs * dprob, 0, keepdims=True))).astype(BF).astype(F32)
        for p in range(5):
            row = slice(p * 48, (p + 1) * 48)
            R.PRP[row, 256 + h : 257 + h] = jnp.sum(ds * R.PIXT[row, :], 1, keepdims=True)
        R.PRP[:, at] = nn(R.MT[h], dout)
    R.PRB[...] = R.PRP[...].astype(BF)

    lanes = iota((1, 128), 1)
    sums = {"w": jnp.zeros((1, 128), F32), "u": jnp.zeros((1, 128), F32)}

    def square_sum(values):
        return jnp.sum(jnp.sum(values * values, 1, keepdims=True), 0, keepdims=True)

    def tensor(index, weight, gradient, first, second):
        unused, unused2, direction = adam_direction(weight, gradient, first, second)
        here = lanes == index
        sums["w"] = sums["w"] + jnp.where(here, square_sum(weight), 0.0)
        sums["u"] = sums["u"] + jnp.where(here, square_sum(direction), 0.0)

    def hook_first():
        fold_second("H", 14)
        fold_second("3", 18)
        loop(0, NQ, lambda q: share_wait(4, q))

        def piece(n):
            at = pl.ds(pl.multiple_of(n * 256, 256), 256)
            R.GA3[at, :] = tn(R.AG[4, :, at], R.OA[...]).astype(BF)

        loop(0, 4, piece)
        reduce_cross("A3", 10)
        for name in ("agg", "attn", "mlp", "head"):
            fetch(name + "_f").wait()
            fetch(name + "_s").wait()
        R.o_mlp[1] = fold_end("2", 13)
        R.o_mlp[0] = fold_end("1", 12)
        for j in range(2):
            tensor(8 + j, R.in_mlpw[j], R.o_mlp[j], R.in_mlp_f[j], R.in_mlp_s[j])
        reduce_spread("A3", 10)

    def hook_second():
        fold_second("B", 11)

    def hook_third():
        total = fold_end("H", 14)
        for j in range(MPN):
            R.HG[j, :, 0:64] = total[:, 64 * j : 64 * (j + 1)]
        vectors_end()

        def sends(i, t):
            rcopy(
                R.HG.at[t],
                R.HGR.at[i - 1],
                ysend.at[14],
                yrecv.at[4],
                d,
                t,
            ).start()
            rcopy(
                R.VG.at[pl.ds(pl.multiple_of(t * 8, 8), 8)],
                R.VGR.at[i - 1],
                ysend.at[15],
                yrecv.at[5],
                d,
                t,
            ).start()

        to_peers(sends)

    all_sum(R.PRB, R.PRC, R.PRH, R.PRR, 8, (hook_first, hook_second, hook_third))

    spread = nt(R.PRR[:, 256:384], head_of.astype(BF))
    dqa = jnp.sum(spread * ewk, 0, keepdims=True) * SCALE
    pk = spread * (qa * SCALE)
    pv = R.PRR[:, 0:256]
    emb = R.TA[:, 0:256]
    wa = [R.in_aggw[j].astype(BF).astype(F32) for j in range(3)]
    pk = pk.astype(BF)
    R.TG[...] = nt(wa[1].astype(BF), pk) + nt(wa[2].astype(BF), pv)
    R.TG[:, 240:241] = jnp.sum(wa[0] * dqa, 1, keepdims=True)

    to_peers(
        lambda i, t: rcopy(R.TG, R.TGR.at[i - 1], ysend.at[13], yrecv.at[3], d, t).start()
    )
    R.o_agg[0] = R.TA[:, 256:257] * dqa
    emb = emb.astype(BF)
    R.o_agg[1] = nn(emb, pk)
    R.o_agg[2] = nn(emb, pv)
    for j in range(3):
        tensor(j, R.in_aggw[j], R.o_agg[j], R.in_agg_f[j], R.in_agg_s[j])
    gsum = fold_end("B", 11)
    for j in range(3):
        R.o_attn[j] = gsum[:, j * 256 : (j + 1) * 256]
    R.o_attn[3] = fold_end("3", 18)
    for j in range(4):
        tensor(4 + j, R.in_attnw[j], R.o_attn[j], R.in_attn_f[j], R.in_attn_s[j])
    drain(R.HGR, yrecv.at[4])
    hgrad = R.HG[m] + R.HGR[0] + R.HGR[1] + R.HGR[2]
    R.o_head[...] = hgrad[:, 0:NVAR]
    tensor(10, R.in_headw[...], R.o_head[...], R.in_head_f[...], R.in_head_s[...])
    drain(R.VGR, yrecv.at[5])
    vgrad = R.VG[my_eight, :] + R.VGR[0] + R.VGR[1] + R.VGR[2]
    R.o_vec[...] = vgrad[:, 0:NVEC]
    unused, unused2, direction = adam_direction(
        R.in_vec[...], R.o_vec[...], R.in_vec_f[...], R.in_vec_s[...]
    )
    R.o_agg[3] = reduce_end("A3", 10)
    tensor(3, R.in_aggw[3], R.o_agg[3], R.in_agg_f[3], R.in_agg_s[3])
    R.NX[0:1, :] = sums["w"]
    R.NX[1:2, :] = sums["u"]
    vector_w = jnp.sum(R.in_vec[...] * R.in_vec[...], 0, keepdims=True)
    vector_u = jnp.sum(direction * direction, 0, keepdims=True)
    R.NX[0:1, 13 : 12 + NVEC] = vector_w[:, 1:]
    R.NX[1:2, 13 : 12 + NVEC] = vector_u[:, 1:]
    to_peers(lambda i, t: rcopy(R.NX, R.NXR.at[i - 1], ysend.at[16], yrecv.at[6], d, t).start())

    drain(R.TMO.at[pl.ds(0, 24)], yrecv.at[9])
    R.WT[...] = R.TA[:, 0:256]
    R.WT[:, 240:241] = R.TA[:, 256:257]
    R.o_vw[...] = R.in_vec[...]
    R.o_vf[...] = R.in_vec_f[...]
    R.o_vs[...] = R.in_vec_s[...]
    R.o_run[...] = R.in_run[...]
    R.o_ew[...] = R.in_emb[...]
    R.o_ef[...] = R.in_emb_f[...]
    R.o_es[...] = R.in_emb_s[...]
    R.o_hw[...] = R.in_headw[...]
    R.o_hf[...] = R.in_head_f[...]
    R.o_hs[...] = R.in_head_s[...]
    drain(R.TGR, yrecv.at[3])
    whole = R.TG[...] + R.TGR[0] + R.TGR[1] + R.TGR[2]
    R.TGF[...] = whole
    unused, unused2, direction = adam_direction(
        R.WT[...], whole, R.TMO[:, 0:256], R.TMO[:, 256:512]
    )
    lane = iota((1, 256), 1)

    def two_sums(values):
        columns = jnp.sum(values * values, 0, keepdims=True)
        embed = jnp.sum(jnp.where(lane < 240, columns, 0.0), 1, keepdims=True)
        first = jnp.sum(jnp.where(lane == 240, columns, 0.0), 1, keepdims=True)
        return jnp.where(lanes == 11, embed, 0.0) + jnp.where(lanes == 12, first, 0.0)

    embed_w, embed_u = two_sums(R.WT[...]), two_sums(direction)
    drain(R.NXR, yrecv.at[6])
    R.NY[...] = R.NX[...] + R.NXR[0] + R.NXR[1] + R.NXR[2]
    R.NY[0:1, :] = R.NY[0:1, :] + embed_w
    R.NY[1:2, :] = R.NY[1:2, :] + embed_u
    at_d = pl.ds(pl.multiple_of(d * 8, 8), 8)

    def norm_send(t):
        rcopy(R.NY, R.NYR.at[at_d], dsend.at[16], drecv.at[16], t, m).start()

    for dz, dx in FAR_FIRST:
        chip = lax.rem(z + dz, 4) * 4 + lax.rem(x + dx, 4)
        norm_send(chip * 2)
        norm_send(chip * 2 + 1)
    norm_send(sib)

    tgrad = R.TGF[my_eight, :]
    for p in range(5):
        R.EG[p * 8 : (p + 1) * 8, :] = tgrad[:, p * 48 : (p + 1) * 48]
    R.o_emb[...] = nt(R.EG[...], vhot, HIGH)
    R.o_vec[:, 0:1] = tgrad[:, 240:241]

    gather_end(R.VPK, 4)
    for buf, g in ((R.HW, 0), (R.WB, 1), (R.W1, 2), (R.W2, 3), (R.WA3, 8), (R.WA3F, 9), (R.WB3F, 10)):
        two_end(buf, g)
    all_sum_end(R.EWC, R.EWH, R.EWR, 6)
    all_sum_end(R.PRC, R.PRH, R.PRR, 8)
    for ix in range(5):
        if ix == 1:
            drain(R.OF.at[:, pl.ds(0, 768)], ysend.at[1])
        else:
            drain(R.RSR.at[ix], ysend.at[ix])
        drain(R.AG.at[ix, pl.ds(0, 192)], ysend.at[5 + ix])
    drain(R.TA.at[pl.ds(0, 24)], ysend.at[10])
    drain(R.HWS.at[pl.ds(0, 3)], ysend.at[11])
    drain(R.TGT.at[pl.ds(0, 3)], ysend.at[12])
    drain(R.TGR, ysend.at[13])
    drain(R.HGR, ysend.at[14])
    drain(R.VGR, ysend.at[15])
    drain(R.NXR, ysend.at[16])
    drain(R.TMO.at[pl.ds(0, 24)], ysend.at[21])
    drain(R.WB3F.at[pl.ds(0, 32), pl.ds(0, 768)], ysend.at[17])
    drain(R.WA3F.at[pl.ds(0, 32), pl.ds(0, 768)], ysend.at[18])
    drain(R.OF.at[:, pl.ds(0, 768)], ysend.at[19])
    drain(R.OF.at[:, pl.ds(0, 768)], ysend.at[20])

    drain(R.NYR.at[pl.ds(0, 248)], drecv.at[16])
    stats = R.NY[...]
    for i in range(1, DPN):
        at = pl.multiple_of(lax.rem(d + i, DPN) * 8, 8)
        stats = stats + R.NYR[pl.ds(at, 8), :]
    first_lane = (iota((8, 128), 0) == 0) & (iota((8, 128), 1) == 127)
    R.o_stats[...] = jnp.where(first_lane, total_count, stats)
    drain(R.NYR.at[pl.ds(0, 248)], dsend.at[16])


def mega_call(inputs):
    outs = [SHAPES[n] for n in ("emb", "vec", "agg", "attn", "mlp", "head")] + [((8, 128), F32)]
    outs += [SHAPES["vec"]] * 3 + [SHAPES["run"]] + [SHAPES["emb"]] * 3 + [SHAPES["head"]] * 3
    whole = pl.BlockSpec(memory_space=pltpu.VMEM)
    return pl.pallas_call(
        mega,
        out_shape=tuple(pltpu.VMEM(*item) for item in outs),
        in_specs=[pl.BlockSpec(memory_space=pl.ANY)] * len(inputs),
        out_specs=(whole,) * len(outs),
        scratch_shapes=[item for unused, item in SCRATCH],
        compiler_params=pltpu.CompilerParams(
            collective_id=0, has_side_effects=True, vmem_limit_bytes=56 * 2**20
        ),
        name="step",
    )(*inputs)


def finish(*refs):
    weights, firsts, seconds, grads = (refs[6 * i : 6 * i + 6] for i in range(4))
    stats, running = refs[24:26]
    o_loss, o_count, o_running, o_trust, o_norms = refs[26:31]
    outs = refs[31:49]
    norms = jnp.sqrt(stats[0:1, :])
    trust = norms / jnp.sqrt(stats[1:2, :])
    o_norms[...] = norms[:, 0:29]
    o_trust[...] = trust[:, 0:29]
    count = stats[0:1, 127:128]
    o_count[...] = count
    errors = jnp.zeros((1, NVAR), F32)
    for j in range(4):
        lane = iota((128, NVAR), 0)
        pick = (lane < NVAR) & (iota((128, NVAR), 1) == 12 * j + lane // P_SIZE)
        errors = errors + nn(stats[4 + j : 5 + j, :], pick.astype(F32), HIGH)
    o_loss[...] = jnp.sum(errors, 1, keepdims=True)
    o_running[...] = STATS_DECAY * running[...] + (1.0 - STATS_DECAY) * errors * (NVAR / count)

    def update(i, at, ratio):
        first, second, direction = adam_direction(
            weights[i][at], grads[i][at], firsts[i][at], seconds[i][at]
        )
        outs[i][at] = first
        outs[6 + i][at] = second
        outs[12 + i][at] = weights[i][at] - LEARN_RATE * ratio * direction

    for i, number, offset in ((0, 4, 0), (1, 4, 4), (2, 2, 8)):
        for j in range(number):
            update(i, j, trust[:, offset + j : offset + j + 1])
    update(3, Ellipsis, trust[:, 10:11])
    update(4, Ellipsis, trust[:, 11:12])
    update(5, Ellipsis, trust[:, 12 : 12 + NVEC])


def finish_call(weights, firsts, seconds, grads, stats, running):
    shapes = [(1, 1), (1, 1), (1, NVAR), (1, 29), (1, 29)] + 3 * [w.shape for w in weights]
    whole = pl.BlockSpec(memory_space=pltpu.VMEM)
    values = (*weights, *firsts, *seconds, *grads, stats, running)
    return pl.pallas_call(
        finish,
        out_shape=tuple(jax.ShapeDtypeStruct(s, F32) for s in shapes),
        in_specs=[whole] * 26,
        out_specs=(whole,) * 23,
        compiler_params=pltpu.CompilerParams(vmem_limit_bytes=32 * 2**20),
        name="finish",
    )(*values)


def on_device(
    pixels,
    targets,
    valid_mask,
    segments,
    lead_index,
    latitude,
    var_ids,
    running_error,
    *tensors,
):
    def turned(group):
        agg, attn, mlp, head, embed, vecs = group
        return (agg, attn, mlp, head, embed.transpose(1, 2, 0).reshape(40, NVAR), vecs.T)

    weights, firsts, seconds = (turned(tensors[6 * i : 6 * i + 6]) for i in range(3))
    agg, attn, mlp, head, embed, vecs = weights
    first = (embed, var_ids.reshape(1, NVAR), vecs, agg, head, mlp, attn, targets.T, pixels.T)
    second = (
        valid_mask.T,
        segments,
        lead_index,
        latitude.reshape(1, TOK),
        running_error.reshape(1, NVAR),
    )
    g_emb, g_vec, g_agg, g_attn, g_mlp, g_head, stats, *rest = mega_call(
        (*first, *second, *firsts, *seconds)
    )
    grads = (g_agg, g_attn, g_mlp, g_head, g_emb, g_vec)
    weights, firsts, seconds = (
        (*group[:3], head, embed, own)
        for group, own, embed, head in zip((weights, firsts, seconds), rest, rest[4:], rest[7:])
    )
    out = finish_call(weights, firsts, seconds, grads, stats, rest[3])

    def back(group):
        agg, attn, mlp, head, embed, vecs = group
        return (agg, attn, mlp, head, embed.reshape(5, 8, NVAR).transpose(2, 0, 1), vecs.T)

    return (
        out[0].reshape(()),
        out[1].reshape(()),
        out[2].reshape(NVAR),
        out[3].reshape(29),
        out[4].reshape(29),
        *back(out[5:11]),
        *back(out[11:17]),
        *back(out[17:23]),
    )


def solution(mesh):
    weights = (
        P(None, "dp", "mp"),
        P(None, "dp", "mp"),
        P(None, "dp", "mp"),
        P("dp", "mp"),
        P(None, None, ("dp", "mp")),
        P(None, ("dp", "mp")),
    )
    in_specs = (
        P("dp", None),
        P("dp", "mp"),
        P("dp", None),
        P("dp", None),
        P("dp", None),
        P("dp"),
        P(),
        P(),
        *weights,
        *weights,
        *weights,
    )
    out_specs = (P(), P(), P(), P(), P(), *weights, *weights, *weights)
    return jax.shard_map(
        on_device, mesh=mesh, in_specs=in_specs, out_specs=out_specs, check_vma=False
    )
```

```python
import math

import jax
import jax.numpy as jnp
from jax import lax
from jax.experimental import pallas as pl
from jax.experimental.pallas import tpu as pltpu
from jax.sharding import PartitionSpec as P

D = 1024
HEAD_DIM = 64
FF = 4096
NVAR = 48
P_SIZE = 4
SEGS = 4
LEADS = 28
LATS = 32
STEP = 10
NVEC = 17
EROWS = NVAR * (P_SIZE + 1)

HIGH = lax.Precision.HIGHEST
NORM_EPS = 1e-06
BETA_ONE = 0.9
BETA_TWO = 0.999
LEARN_RATE = 0.3
WEIGHT_DECAY = 0.01
ADAM_EPS = 1e-08
STATS_DECAY = 0.9
MESH = pl.DeviceIdType.MESH
BF = jnp.bfloat16
F32 = jnp.float32

DPN, MPN, CHIPS, SH, TOK, COLS = 32, 4, 16, 64, 256, 256
NQ = 4
RQ, CH = TOK // NQ, SH // NQ
SCALE = 1.0 / math.sqrt(HEAD_DIM)
FAR_FIRST = sorted(
    ((dz, dx) for dz in range(4) for dx in range(4) if dz or dx),
    key=lambda o: -(min(o[0], 4 - o[0]) + min(o[1], 4 - o[1])),
)


def nn(a, b, precision=None):
    return lax.dot_general(
        a, b, (((1,), (0,)), ((), ())), preferred_element_type=F32, precision=precision
    )


def nt(a, b, precision=None):
    return lax.dot_general(
        a, b, (((1,), (1,)), ((), ())), preferred_element_type=F32, precision=precision
    )


def tn(a, b, precision=None):
    return lax.dot_general(
        a, b, (((0,), (0,)), ((), ())), preferred_element_type=F32, precision=precision
    )


def latitude_weights():
    cosines = [
        math.cos(((j + 0.5) * (180.0 / LATS) - 90.0) * (math.pi / 180.0)) for j in range(LATS)
    ]
    mean = sum(cosines) / LATS
    return [value / mean for value in cosines]


def moments_new(gradient, first, second):
    first_new = BETA_ONE * first + (1.0 - BETA_ONE) * gradient
    second_new = BETA_TWO * second + (1.0 - BETA_TWO) * gradient * gradient
    return first_new, second_new


def adam_direction(weight, gradient, first, second):
    first_new, second_new = moments_new(gradient, first, second)
    first_hat = first_new * (1.0 / (1.0 - BETA_ONE**STEP))
    second_hat = second_new * (1.0 / (1.0 - BETA_TWO**STEP))
    direction = first_hat / (jnp.sqrt(second_hat) + ADAM_EPS) + WEIGHT_DECAY * weight
    return (first_new, second_new, direction)


def iota(shape, dim):
    return lax.broadcasted_iota(jnp.int32, shape, dim)


def ln_parts(x):
    centre = jnp.mean(x, -1, keepdims=True)
    shifted = x - centre
    r = lax.rsqrt(jnp.mean(shifted * shifted, -1, keepdims=True) + NORM_EPS)
    return shifted * r, r


def ln_back(n, r, gain, dh):
    e = dh * gain
    dx = r * (e - jnp.mean(e, -1, keepdims=True) - n * jnp.mean(e * n, -1, keepdims=True))
    dgain = jnp.sum(dh * n, 0, keepdims=True)
    dbias = jnp.sum(dh, 0, keepdims=True)
    return dx, dgain, dbias


LARGE = ("emb", "vid", "vec", "aggw", "headw", "mlpw", "attnw", "targ", "pix")
MOMENTS = ("agg", "attn", "mlp", "head", "emb", "vec")
SMALL = ("mask", "seg", "leadi", "lat", "run")
OUTS = ("o_emb", "o_vec", "o_agg", "o_attn", "o_mlp", "o_head", "o_stats")
OUTS = OUTS + ("o_vw", "o_vf", "o_vs", "o_run", "o_ew", "o_ef", "o_es")
OUTS = OUTS + ("o_hw", "o_hf", "o_hs")
SHAPES = {
    "pix": ((NVAR * P_SIZE, TOK), BF),
    "targ": ((NVAR, TOK), F32),
    "agg": ((4, 32, 256), F32),
    "attn": ((4, 32, 256), F32),
    "mlp": ((2, 32, 1024), F32),
    "head": ((32, NVAR), F32),
    "emb": ((40, NVAR), F32),
    "vec": ((8, NVEC), F32),
    "mask": ((P_SIZE, TOK), jnp.int32),
    "seg": ((1, TOK), jnp.int32),
    "leadi": ((1, SEGS), jnp.int32),
    "lat": ((1, TOK), jnp.int32),
    "vid": ((1, NVAR), jnp.int32),
    "run": ((1, NVAR), F32),
}
SHAPES.update({"aggw": SHAPES["agg"], "attnw": SHAPES["attn"], "mlpw": SHAPES["mlp"]})
SHAPES["headw"] = SHAPES["head"]
FETCH = LARGE + SMALL + tuple(n + "_f" for n in MOMENTS) + tuple(n + "_s" for n in MOMENTS)


def fetch_shape(name):
    return SHAPES[name[:-2] if name[-2] == "_" else name]


def scratch_list():
    vm = pltpu.VMEM
    dma = pltpu.SemaphoreType.DMA
    items = [
        ("WA3", vm((D, 256), BF)),
        ("WB", vm((D, 768), BF)),
        ("WA3F", vm((D, 1024), BF)),
        ("WB3F", vm((D, 1024), BF)),
        ("W1", vm((D, 1024), BF)),
        ("W2", vm((D, 1024), BF)),
        ("HW", vm((D, 256), BF)),
        ("HWS", vm((MPN, 32, 128), BF)),
        ("VPK", vm((256, 128), F32)),
        ("VEC", vm((DPN, 4, 8, 128), F32)),
        ("VR", vm((128, D), F32)),
        ("VRN", vm((128, D), F32)),
        ("TMPV", vm((D, 128), F32)),
        ("TA", vm((32, 384), F32)),
        ("HWT", vm((32, 128), F32)),
        ("TT", vm((128, TOK), F32)),
        ("TS", vm((NQ, MPN, CH, 128), F32)),
        ("TGT", vm((MPN, NQ, CH, 128), F32)),
        ("ROWS", vm((128, TOK), F32)),
        ("TCOL", vm((TOK, 128), F32)),
        ("LW", vm((TOK, 128), F32)),
        ("PIXT", vm((256, TOK), F32)),
        ("EWP", vm((256, 512), F32)),
        ("EWB", vm((256, 512), BF)),
        ("EWC", vm((256, 512), BF)),
        ("EWH", vm((2, 16, 512), F32)),
        ("EWR", vm((256, 512), BF)),
        ("PRP", vm((256, 384), F32)),
        ("PRB", vm((256, 384), BF)),
        ("PRC", vm((256, 384), BF)),
        ("PRH", vm((2, 16, 384), F32)),
        ("PRR", vm((256, 384), BF)),
        ("MT", vm((4, 256, TOK), BF)),
        ("PT", vm((4, NVAR, TOK), F32)),
        ("OAT", vm((256, TOK), F32)),
        ("OA", vm((TOK, 256), BF)),
        ("RSS", vm((5, TOK, D), BF)),
        ("RSR", vm((5, 3, SH, D), BF)),
        ("AG", vm((5, TOK, D), BF)),
        ("QKV", vm((3, TOK, 256), BF)),
        ("PB", vm((4, TOK, TOK), F32)),
        ("OB", vm((TOK, 256), BF)),
        ("OF", vm((SH, D), BF)),
        ("DOB", vm((TOK, 256), BF)),
        ("DOF", vm((SH, D), BF)),
        ("DMB", vm((TOK, 256), BF)),
        ("DMF", vm((SH, D), BF)),
        ("GEL", vm((TOK, 1024), BF)),
        ("GELP", vm((TOK, 1024), F32)),
        ("DU", vm((TOK, 1024), BF)),
        ("DQKV", vm((TOK, 768), BF)),
        ("LN", vm((2, SH, D), F32)),
        ("XS", vm((SH, D), F32)),
        ("RR", vm((2, SH, 128), F32)),
        ("H3", vm((SH, D), BF)),
        ("DP", vm((SH, 256), BF)),
        ("GVT", vm((DPN, 4, 8, 128), F32)),
        ("GVK", vm((256, 128), F32)),
        ("GVS", vm((128, 128), F32)),
        ("GVB", vm((128, 128), F32)),
        ("GVP", vm((128, D), F32)),
        ("GVN", vm((128, D), F32)),
        ("TG", vm((32, 256), F32)),
        ("TGR", vm((3, 32, 256), F32)),
        ("TGF", vm((32, 256), F32)),
        ("TMO", vm((32, 512), F32)),
        ("WT", vm((32, 256), F32)),
        ("VG", vm((32, 128), F32)),
        ("VGR", vm((3, 8, 128), F32)),
        ("HG", vm((MPN, 32, 128), F32)),
        ("HGR", vm((3, 32, 128), F32)),
        ("EG", vm((40, NVAR), F32)),
        ("NX", vm((8, 128), F32)),
        ("NXR", vm((3, 8, 128), F32)),
        ("NY", vm((8, 128), F32)),
        ("NYR", vm((256, 128), F32)),
    ]
    for name, width, kind in (
        ("A3", 256, BF),
        ("B", 768, BF),
        ("3", 256, BF),
        ("1", 1024, BF),
        ("2", 1024, BF),
        ("H", 256, BF),
    ):
        items.append(("G" + name, vm((D, width), kind)))
        items.append(("S" + name, vm((512, width), kind)))
        if name == "A3":
            items.append(("B" + name, vm((512, width), kind)))
        else:
            items.append(("FP" + name, vm((2, 3, 128, width // 2), kind)))
            items.append(("FQ" + name, vm((2, 3, 32, width // 2), kind)))
    for name in FETCH:
        items.append(("in_" + name, vm(*fetch_shape(name))))
    items += [
        ("fsem", dma((len(FETCH),))),
        ("ysend", dma((22,))),
        ("yrecv", dma((10,))),
        ("nrecv", dma((2, NQ))),
        ("rrecv", dma((5, NQ))),
        ("arecv", dma((5, NQ))),
        ("dsend", dma((19,))),
        ("drecv", dma((19,))),
        ("tsend", dma((12, 4))),
        ("trecv", dma((12, 4))),
        ("ssend", dma((19,))),
        ("srecv", dma((19,))),
    ]
    return items


SCRATCH = scratch_list()
NAMES = tuple(n + "_hbm" for n in FETCH) + OUTS + tuple(n for n, unused in SCRATCH)


def mega(*refs):
    r = dict(zip(NAMES, refs))
    step_kernel(type("Refs", (), r))


def step_kernel(R):
    d = lax.axis_index("dp")
    m = lax.axis_index("mp")
    c = lax.rem(d, 2)
    k = d // 2
    z = k // 4
    x = lax.rem(k, 4)
    sib = d + 1 - 2 * c
    rb = pl.multiple_of(c * 512 + k * 32, 32)
    half = pl.multiple_of(c * 512, 512)
    other = pl.multiple_of(512 - c * 512, 512)
    my_slot = pl.ds(pl.multiple_of(m * 128, 128), 128)
    my_eight = pl.ds(pl.multiple_of(m * 8, 8), 8)
    my_cols = pl.ds(pl.multiple_of(m * COLS, COLS), COLS)

    def rcopy(src, dst, ss, rs, dp, mp):
        return pltpu.make_async_remote_copy(
            src_ref=src,
            dst_ref=dst,
            send_sem=ss,
            recv_sem=rs,
            device_id={"dp": dp, "mp": mp},
            device_id_type=MESH,
        )

    def drain(ref, sem):
        pltpu.make_async_copy(ref, ref, sem).wait()

    def loop(first, last, fn):
        def step(i, carry):
            fn(i)
            return carry

        lax.fori_loop(first, last, step, 0)

    def to_peers(fn):
        for i in (2, 1, 3):
            fn(i, lax.rem(m + i, MPN))

    def to_chips(fn):
        for dz, dx in FAR_FIRST:
            kk = lax.rem(z + dz, 4) * 4 + lax.rem(x + dx, 4)
            fn(kk, kk * 2 + c)

    def fetch(name):
        i = FETCH.index(name)
        return pltpu.make_async_copy(
            getattr(R, name + "_hbm"), getattr(R, "in_" + name), R.fsem.at[i]
        )

    dsend, drecv, ssend, srecv = R.dsend, R.drecv, R.ssend, R.srecv
    ysend, yrecv = R.ysend, R.yrecv

    def gather_start(buf, g):
        block = buf.at[pl.ds(pl.multiple_of(c * 128 + k * 8, 8), 8)]
        to_chips(lambda kk, t: rcopy(block, block, dsend.at[g], drecv.at[g], t, m).start())

    def gather_cross(buf, g):
        drain(buf.at[pl.ds(0, 120)], drecv.at[g])
        part = buf.at[pl.ds(pl.multiple_of(c * 128, 128), 128)]
        rcopy(part, part, ssend.at[g], srecv.at[g], sib, m).start()

    def gather_wait(buf, g):
        drain(buf.at[pl.ds(0, buf.shape[0] // 2)], srecv.at[g])

    def gather_end(buf, g):
        drain(buf.at[pl.ds(0, 120)], dsend.at[g])
        drain(buf.at[pl.ds(0, 128)], ssend.at[g])

    def along(axis, i):
        if axis == "x":
            return (z * 4 + lax.rem(x + i, 4)) * 2 + c
        return (lax.rem(z + i, 4) * 4 + x) * 2 + c

    def sides(buf):
        n = buf.shape[1] // 2
        return pl.ds(0, n), pl.ds(n, n)

    def tcopy(src, dst, g, j, t):
        rcopy(src, dst, R.tsend.at[g, j], R.trecv.at[g, j], t, m).start()

    def two_first(buf, g):
        left, right = sides(buf)
        for i in (2, 1, 3):
            block = buf.at[pl.ds(rb, 32), left]
            tcopy(block, block, g, 0, along("x", i))
            block = buf.at[pl.ds(rb, 32), right]
            tcopy(block, block, g, 1, along("z", i))

    def two_second(buf, g):
        left, right = sides(buf)
        drain(buf.at[pl.ds(0, 96), left], R.trecv.at[g, 0])
        block = buf.at[pl.ds(pl.multiple_of(half + z * 128, 128), 128), left]
        for i in (2, 1, 3):
            tcopy(block, block, g, 2, along("z", i))
        drain(buf.at[pl.ds(0, 96), right], R.trecv.at[g, 1])

        def send(zz):
            block = buf.at[pl.ds(pl.multiple_of(half + zz * 128 + x * 32, 32), 32), right]
            for i in (2, 1, 3):
                tcopy(block, block, g, 3, along("x", i))

        loop(0, 4, send)

    def two_cross(buf, g):
        for side, j in zip(sides(buf), (2, 3)):
            drain(buf.at[pl.ds(0, 384), side], R.trecv.at[g, j])
        part = buf.at[pl.ds(half, 512)]
        g = {8: 5, 9: 16, 10: 17}.get(g, g)
        rcopy(part, part, ssend.at[g], srecv.at[g], sib, m).start()

    def two_end(buf, g):
        left, right = sides(buf)
        for j, rows in ((0, 96), (1, 96), (2, 384), (3, 384)):
            drain(buf.at[pl.ds(0, rows), left if j % 2 == 0 else right], R.tsend.at[g, j])
        drain(buf.at[pl.ds(0, 512)], ssend.at[{8: 5, 9: 16, 10: 17}.get(g, g)])

    def reduce_cross(name, g):
        buf, sbuf = getattr(R, "G" + name), getattr(R, "S" + name)
        rcopy(buf.at[pl.ds(other, 512)], sbuf, ssend.at[g], srecv.at[g], sib, m).start()

    def core_sum(name, g):
        buf, sbuf = getattr(R, "G" + name), getattr(R, "S" + name)
        drain(sbuf, srecv.at[g])

        def add(i):
            at = pl.multiple_of(i * 128, 128)
            sbuf[pl.ds(at, 128), :] = (
                sbuf[pl.ds(at, 128), :].astype(F32)
                + buf[pl.ds(pl.multiple_of(half + at, 128), 128), :].astype(F32)
            ).astype(sbuf.dtype)

        loop(0, 4, add)

    def reduce_spread(name, g):
        core_sum(name, g)
        sbuf, bbuf = getattr(R, "S" + name), getattr(R, "B" + name)
        land = bbuf.at[pl.ds(pl.multiple_of(k * 32, 32), 32)]

        def send(kk, t):
            src = sbuf.at[pl.ds(pl.multiple_of(kk * 32, 32), 32)]
            rcopy(src, land, dsend.at[g], drecv.at[g], t, m).start()

        to_chips(send)

    def row_block(zz, xx):
        return pl.ds(pl.multiple_of(zz * 128 + xx * 32, 32), 32)

    def fold_first(name, g):
        core_sum(name, g)
        sbuf, pbuf = getattr(R, "S" + name), getattr(R, "FP" + name)
        left, right = sides(sbuf)
        for i in (2, 1, 3):
            zz = lax.rem(z + i, 4)
            src = sbuf.at[pl.ds(pl.multiple_of(zz * 128, 128), 128), left]
            tcopy(src, pbuf.at[0, i - 1], g - 7, 0, along("z", i))

        def send(zz):
            for i in (2, 1, 3):
                src = sbuf.at[row_block(zz, lax.rem(x + i, 4)), right]
                land = pbuf.at[1, i - 1, pl.ds(pl.multiple_of(zz * 32, 32), 32)]
                tcopy(src, land, g - 7, 1, along("x", i))

        loop(0, 4, send)

    def fold_second(name, g):
        sbuf, pbuf, qbuf = getattr(R, "S" + name), getattr(R, "FP" + name), getattr(R, "FQ" + name)
        left, right = sides(sbuf)
        for side, j in ((left, 0), (right, 1)):
            drain(pbuf.at[j], R.trecv.at[g - 7, j])

            def add(i):
                at = row_block(z, i) if j == 0 else row_block(i, x)
                acc = sbuf[at, side].astype(F32)
                for n in range(3):
                    acc = acc + pbuf[j, n, pl.ds(pl.multiple_of(i * 32, 32), 32), :].astype(F32)
                sbuf[at, side] = acc.astype(sbuf.dtype)

            loop(0, 4, add)
            for i in (2, 1, 3):
                if j == 0:
                    src = sbuf.at[row_block(z, lax.rem(x + i, 4)), side]
                    tcopy(src, qbuf.at[0, i - 1], g - 7, 2, along("x", i))
                else:
                    src = sbuf.at[row_block(lax.rem(z + i, 4), x), side]
                    tcopy(src, qbuf.at[1, i - 1], g - 7, 3, along("z", i))

    def fold_end(name, g):
        sbuf, pbuf, qbuf = getattr(R, "S" + name), getattr(R, "FP" + name), getattr(R, "FQ" + name)
        parts = []
        for side, j in zip(sides(sbuf), (0, 1)):
            drain(qbuf.at[j], R.trecv.at[g - 7, 2 + j])
            acc = sbuf[row_block(z, x), side].astype(F32)
            for n in range(3):
                acc = acc + qbuf[j, n].astype(F32)
            parts.append(acc)
            drain(pbuf.at[j], R.tsend.at[g - 7, j])
            drain(qbuf.at[j], R.tsend.at[g - 7, 2 + j])
        drain(sbuf, ssend.at[g])
        return jnp.concatenate(parts, 1)

    def reduce_end(name, g):
        sbuf, bbuf = getattr(R, "S" + name), getattr(R, "B" + name)
        drain(bbuf.at[pl.ds(0, 480)], drecv.at[g])

        def add(i, acc):
            at = pl.multiple_of(lax.rem(k + i, CHIPS) * 32, 32)
            return acc + bbuf[pl.ds(at, 32), :].astype(F32)

        total = lax.fori_loop(
            1, CHIPS, add, sbuf[pl.ds(pl.multiple_of(k * 32, 32), 32), :].astype(F32)
        )
        drain(bbuf.at[pl.ds(0, 480)], dsend.at[g])
        drain(sbuf, ssend.at[g])
        return total

    def all_sum(src, cbuf, hbuf, res, g, hooks):
        at_k = pl.ds(pl.multiple_of(k * 16, 16), 16)

        def send(kk, t):
            block = src.at[pl.ds(pl.multiple_of(kk * 16, 16), 16)]
            rcopy(block, cbuf.at[at_k], dsend.at[g], drecv.at[g], t, m).start()

        to_chips(send)
        hooks[0]()
        drain(cbuf.at[pl.ds(0, 240)], drecv.at[g])
        total = src[at_k, :].astype(F32)
        for dz, dx in FAR_FIRST:
            kk = lax.rem(z + dz, 4) * 4 + lax.rem(x + dx, 4)
            total = total + cbuf[pl.ds(pl.multiple_of(kk * 16, 16), 16), :].astype(F32)
        hbuf[0] = total
        rcopy(hbuf.at[0], hbuf.at[1], ssend.at[g], srecv.at[g], sib, m).start()
        hooks[1]()
        drain(hbuf.at[1], srecv.at[g])
        res[at_k, :] = (hbuf[0] + hbuf[1]).astype(BF)
        part = res.at[at_k]
        to_chips(lambda kk, t: rcopy(part, part, dsend.at[g + 1], drecv.at[g + 1], t, m).start())
        hooks[2]()
        drain(res.at[pl.ds(0, 240)], drecv.at[g + 1])

    def all_sum_end(cbuf, hbuf, res, g):
        drain(hbuf.at[0], ssend.at[g])
        drain(cbuf.at[pl.ds(0, 240)], dsend.at[g])
        drain(res.at[pl.ds(0, 240)], dsend.at[g + 1])

    def rows_of(q):
        return pl.ds(pl.multiple_of(q * RQ, RQ), RQ)

    def own_of(q, t):
        return pl.ds(pl.multiple_of(q * RQ + t * CH, CH), CH)

    def local_of(q):
        return pl.ds(pl.multiple_of(q * CH, CH), CH)

    def branch_send(ix, q, left, weight, cols=None):
        for n in range(4):
            at = pl.ds(n * 256, 256)
            w = weight[at, :] if cols is None else weight[at, cols[0] : cols[1]]
            R.RSS[ix, rows_of(q), n * 256 : (n + 1) * 256] = nt(left, w).astype(BF)

        def send(i, t):
            rcopy(
                R.RSS.at[ix, own_of(q, t)],
                R.RSR.at[ix, i - 1, local_of(q)],
                ysend.at[ix],
                R.rrecv.at[ix, q],
                d,
                t,
            ).start()

        to_peers(send)

    def branch_sum(ix, q):
        drain(R.RSR.at[ix, :, pl.ds(0, CH)], R.rrecv.at[ix, q])
        acc = R.RSS[ix, own_of(q, m), :].astype(F32)
        for i in range(3):
            acc = acc + R.RSR[ix, i, local_of(q), :].astype(F32)
        return acc

    def share_send(ix, q, values):
        R.AG[ix, own_of(q, m), :] = values
        share_start(ix, q)

    def heads_out(src, dst, q, ss, rs):
        land = dst.at[local_of(q), my_cols]
        to_peers(lambda i, t: rcopy(src.at[own_of(q, t)], land, ss, rs, d, t).start())
        dst[local_of(q), my_cols] = src[own_of(q, m), :]

    def heads_back(src, dst, q, ss, rs):
        def send(i, t):
            block = src.at[local_of(q), pl.ds(pl.multiple_of(t * COLS, COLS), COLS)]
            rcopy(block, dst.at[own_of(q, m)], ss, rs, d, t).start()

        to_peers(send)
        dst[own_of(q, m), :] = src[local_of(q), my_cols]

    def share_start(ix, q):
        block = R.AG.at[ix, own_of(q, m)]
        to_peers(
            lambda i, t: rcopy(block, block, ysend.at[5 + ix], R.arecv.at[ix, q], d, t).start()
        )

    def share_wait(ix, q):
        drain(R.AG.at[ix, pl.ds(0, 3 * CH)], R.arecv.at[ix, q])

    bar = pltpu.get_barrier_semaphore()

    def greet(i):
        pl.semaphore_signal(
            bar, inc=1, device_id={"dp": lax.rem(d + i, DPN), "mp": m}, device_id_type=MESH
        )

    for i in range(1, MPN):
        pl.semaphore_signal(
            bar, inc=1, device_id={"dp": d, "mp": lax.rem(m + i, MPN)}, device_id_type=MESH
        )
    loop(1, DPN, greet)

    for name in FETCH:
        fetch(name).start()

    fetch("vid").wait()
    vhot = (iota((NVAR, NVAR), 0) == R.in_vid[...]).astype(F32)
    fetch("emb").wait()
    fetch("vec").wait()
    chosen = nn(R.in_emb[...], vhot, HIGH)
    R.TA[my_eight, :] = jnp.zeros((8, 384), F32)
    for p in range(5):
        R.TA[my_eight, p * 48 : (p + 1) * 48] = chosen[p * 8 : (p + 1) * 8, :]
    R.TA[my_eight, 256 : 256 + NVEC] = R.in_vec[...]
    fetch("aggw").wait()
    fetch("headw").wait()
    aw = [R.in_aggw[j].astype(BF) for j in range(3)]
    R.WA3[pl.ds(rb, 32), :] = R.in_aggw[3].astype(BF)
    R.HWT[...] = jnp.zeros_like(R.HWT)
    R.HWT[:, 0:NVAR] = R.in_headw[...]
    R.HWS[m] = R.HWT[...].astype(BF)
    fetch("mlpw").wait()
    R.W1[pl.ds(rb, 32), :] = R.in_mlpw[0].astype(BF)
    R.W2[pl.ds(rb, 32), :] = R.in_mlpw[1].astype(BF)
    fetch("attnw").wait()
    for j in range(3):
        R.WB[pl.ds(rb, 32), j * 256 : (j + 1) * 256] = R.in_attnw[j].astype(BF)
    R.WB3F[pl.ds(rb, 32), my_cols] = R.in_attnw[3].astype(BF)
    R.WA3F[pl.ds(rb, 32), my_cols] = R.in_aggw[3].astype(BF)
    fetch("targ").wait()
    R.TT[NVAR:, :] = jnp.zeros((128 - NVAR, TOK), F32)
    R.TT[0:NVAR, :] = R.in_targ[...]
    turned = R.TT[...].T
    for q in range(NQ):
        for t in range(MPN):
            at = q * RQ + t * CH
            R.TS[q, t] = turned[at : at + CH, :]
    R.TGT[m] = R.TS[:, m]
    R.GVP[...] = jnp.zeros_like(R.GVP)
    R.GVN[...] = jnp.zeros_like(R.GVN)
    R.NX[...] = jnp.zeros_like(R.NX)
    R.HG[...] = jnp.zeros_like(R.HG)
    R.VG[...] = jnp.zeros_like(R.VG)
    pl.semaphore_wait(bar, DPN + MPN - 2)

    def first_sends(i, t):
        part = R.TA.at[my_eight]
        rcopy(part, part, ysend.at[10], yrecv.at[0], d, t).start()
        block = R.WB3F.at[pl.ds(rb, 32), my_cols]
        rcopy(block, block, ysend.at[17], yrecv.at[7], d, t).start()

    def later_sends(i, t):
        slot = R.HWS.at[m]
        rcopy(slot, slot, ysend.at[11], yrecv.at[1], d, t).start()
        block = R.WA3F.at[pl.ds(rb, 32), my_cols]
        rcopy(block, block, ysend.at[18], yrecv.at[8], d, t).start()
        rcopy(R.TS.at[:, t], R.TGT.at[m], ysend.at[12], yrecv.at[2], d, t).start()

    to_peers(first_sends)
    two_first(R.WA3, 8)
    two_first(R.WB, 1)
    two_first(R.W1, 2)
    two_first(R.W2, 3)
    to_peers(later_sends)

    fetch("pix").wait()
    for name in SMALL:
        fetch(name).wait()
    rows = iota((256, 192), 0)
    cols = iota((256, 192), 1)
    pick = (rows < 192) & ((lax.rem(rows, NVAR) * P_SIZE + rows // NVAR) == cols)
    pixt = nn(pick.astype(BF), R.in_pix[...])
    row_at = iota((256, TOK), 0)
    R.PIXT[...] = jnp.where(row_at < 192, pixt, jnp.where(row_at < EROWS, 1.0, 0.0))

    drain(R.TA.at[pl.ds(0, 24)], yrecv.at[0])
    emb = R.TA[:, 0:256]
    high = emb.astype(BF)
    rest = (emb - high.astype(F32)).astype(BF)
    R.EWP[:, 0:256] = tn(high, aw[1]) + tn(rest, aw[1])
    R.EWP[:, 256:512] = tn(high, aw[2]) + tn(rest, aw[2])
    R.EWP[240:241, 0:256] = jnp.sum(R.TA[:, 256:257] * aw[0].astype(F32), 0, keepdims=True)
    R.EWB[...] = R.EWP[...].astype(BF)
    keep = R.in_mask[...].astype(F32)
    count = jnp.sum(jnp.sum(keep, 1, keepdims=True), 0, keepdims=True) * NVAR

    def per_patch():
        seg = R.in_seg[...]
        lead_row = jnp.zeros((1, TOK), F32)
        for s in range(SEGS):
            value = (R.in_leadi[:, s : s + 1] + 1).astype(F32) / LEADS
            lead_row = jnp.where(seg == s, value, lead_row)
        lat = R.in_lat[...]
        lat_row = jnp.zeros((1, TOK), F32)
        for j, value in enumerate(latitude_weights()):
            lat_row = jnp.where(lat == j, value, lat_row)
        R.ROWS[...] = jnp.zeros_like(R.ROWS)
        R.ROWS[0:1, :] = seg.astype(F32)
        R.ROWS[1:2, :] = lead_row
        R.ROWS[8:12, :] = keep * lat_row
        R.TCOL[...] = R.ROWS[...].T
        lane = iota((128, 128), 1)
        pick = (lane < NVAR) & (iota((128, 128), 0) == 8 + lax.rem(lane, P_SIZE))
        R.LW[...] = nn(R.TCOL[...], pick.astype(F32), HIGH)

    def own_vectors():
        at = pl.ds(pl.multiple_of(c * 128 + k * 8, 8), 8)
        for g in range(4):
            R.VPK[at, 32 * g : 32 * (g + 1)] = R.TA[8 * g : 8 * (g + 1), 256:288]
        R.VPK[at, 31:32] = jnp.broadcast_to(count, (8, 1))

    def embed_moments():
        for name in ("emb_f", "vec_f", "emb_s", "vec_s"):
            fetch(name).wait()
        R.TMO[my_eight, :] = jnp.zeros((8, 512), F32)
        for start, held, vecs in ((0, R.in_emb_f, R.in_vec_f), (256, R.in_emb_s, R.in_vec_s)):
            picked = nn(held[...], vhot, HIGH)
            for p in range(5):
                lane = start + p * 48
                R.TMO[my_eight, lane : lane + 48] = picked[p * 8 : (p + 1) * 8, :]
            R.TMO[my_eight, start + 240 : start + 241] = vecs[:, 0:1]
        part = R.TMO.at[my_eight]
        to_peers(lambda i, t: rcopy(part, part, ysend.at[21], yrecv.at[9], d, t).start())

    def first_bulk():
        own_vectors()
        two_second(R.WA3, 8)
        gather_start(R.VPK, 4)
        drain(R.WB3F.at[pl.ds(0, 32), pl.ds(0, 768)], yrecv.at[7])
        two_first(R.WB3F, 10)
        per_patch()
        embed_moments()

    def bulk():
        two_second(R.WB, 1)
        gather_cross(R.VPK, 4)
        two_cross(R.WA3, 8)

    all_sum(R.EWB, R.EWC, R.EWH, R.EWR, 6, (first_bulk, lambda: None, bulk))

    two_second(R.WB3F, 10)

    head_of = (iota((256, 128), 0) // HEAD_DIM == iota((256, 128), 1)).astype(F32)
    ewk = R.EWR[:, 0:256].astype(F32)
    qa = ewk[240:241, :]
    keyed = ewk * (qa * SCALE)
    high = keyed.astype(BF)
    rest = (keyed - high.astype(F32)).astype(BF)
    qe = nn(high, head_of.astype(BF)) + nn(rest, head_of.astype(BF))
    ewv = R.EWR[:, 256:512]
    for h in range(4):
        scores = R.PIXT[0:48, :] * qe[0:48, h : h + 1]
        for p in range(1, 5):
            at = slice(p * 48, (p + 1) * 48)
            scores = scores + R.PIXT[at, :] * qe[at, h : h + 1]
        e = jnp.exp(scores - jnp.max(scores, 0, keepdims=True))
        probs = e / jnp.sum(e, 0, keepdims=True)
        R.PT[h] = probs
        probs = probs.astype(BF).astype(F32)
        for p in range(5):
            at = slice(p * 48, (p + 1) * 48)
            R.MT[h, at, :] = (probs * R.PIXT[at, :]).astype(BF)
        R.MT[h, 240:256, :] = jnp.zeros((16, TOK), BF)
        R.OAT[h * 64 : (h + 1) * 64, :] = tn(ewv[:, h * 64 : (h + 1) * 64], R.MT[h])
    R.OA[...] = R.OAT[...].T.astype(BF)

    gather_wait(R.WA3, 5)
    loop(0, NQ, lambda q: branch_send(0, q, R.OA[rows_of(q), :], R.WA3))
    two_second(R.W1, 2)
    gather_wait(R.VPK, 4)
    packed = R.VPK[...].reshape(DPN, 8, 128)
    total_count = jnp.sum(packed, 0)[0:1, 31:32]
    for g in range(4):
        R.VEC[:, g, :, 0:32] = packed[:, :, 32 * g : 32 * (g + 1)]
    R.VR[...] = R.VEC[...].reshape(D, 128).T
    two_cross(R.WB, 1)

    def vrow(i):
        return R.VR[i : i + 1, :]

    def keep_norm(j, q, n, r):
        R.LN[j, local_of(q), :] = n
        R.RR[j, local_of(q), :] = jnp.broadcast_to(r, (CH, 128))

    def mixed_rows(q):
        lead = R.TCOL[own_of(q, m), 1:2]
        x0 = branch_sum(0, q) + vrow(1) + lead * vrow(2)
        n, r = ln_parts(x0)
        share_send(0, q, (n * vrow(3) + vrow(4)).astype(BF))
        R.XS[local_of(q), :] = x0
        keep_norm(0, q, n, r)

    loop(0, NQ // 2, mixed_rows)
    two_second(R.W2, 3)
    loop(NQ // 2, NQ, mixed_rows)

    def natural(i):
        block = R.VEC[lax.rem(i, 2) * 16 + i // 2]
        R.TMPV[pl.ds(pl.multiple_of(i * 32, 32), 32), :] = block.reshape(32, 128)

    loop(0, DPN, natural)
    R.VRN[...] = R.TMPV[...].T
    drain(R.HWS.at[pl.ds(0, 3)], yrecv.at[1])
    R.HW[pl.ds(rb, 32), :] = jnp.concatenate(
        [R.HWS[j].astype(F32)[:, 0:64] for j in range(MPN)], 1
    ).astype(BF)
    two_first(R.HW, 0)
    drain(R.WA3F.at[pl.ds(0, 32), pl.ds(0, 768)], yrecv.at[8])
    gather_wait(R.WB, 1)

    def project(q):
        share_wait(0, q)
        at = rows_of(q)
        h1 = R.AG[0, at, :]
        R.QKV[0, at, :] = (nn(h1, R.WB[:, 0:256]) + R.VRN[5:6, my_cols]).astype(BF)
        R.QKV[1, at, :] = nn(h1, R.WB[:, 256:512]).astype(BF)
        R.QKV[2, at, :] = (nn(h1, R.WB[:, 512:768]) + R.VRN[6:7, my_cols]).astype(BF)

    loop(0, NQ // 2, project)
    two_cross(R.WB3F, 10)
    loop(NQ // 2, NQ, project)
    seg_row = R.in_seg[...].astype(F32)

    same = R.TCOL[:, 0:1] == seg_row
    for h in range(4):
        at = slice(h * 64, (h + 1) * 64)
        scores = nt(R.QKV[0, :, at], R.QKV[1, :, at]) * SCALE
        scores = jnp.where(same, scores, -1e30)
        e = jnp.exp(scores - jnp.max(scores, 1, keepdims=True))
        probs = e / jnp.sum(e, 1, keepdims=True)
        R.PB[h] = probs
        R.OB[:, at] = nn(probs.astype(BF), R.QKV[2, :, at]).astype(BF)
    loop(0, NQ, lambda q: heads_out(R.OB, R.OF, q, ysend.at[1], R.rrecv.at[1, q]))
    two_cross(R.W1, 2)
    gather_wait(R.WB3F, 17)

    def second_rows(q):
        drain(R.OF.at[pl.ds(0, CH), pl.ds(0, 768)], R.rrecv.at[1, q])
        x1 = R.XS[local_of(q), :] + nt(R.OF[local_of(q), :], R.WB3F[...]) + vrow(7)
        n, r = ln_parts(x1)
        share_send(1, q, (n * vrow(8) + vrow(9)).astype(BF))
        R.XS[local_of(q), :] = x1
        keep_norm(1, q, n, r)

    loop(0, NQ // 2, second_rows)
    two_cross(R.W2, 3)
    loop(NQ // 2, NQ, second_rows)
    two_second(R.HW, 0)
    two_first(R.WA3F, 9)
    gather_wait(R.W1, 2)
    gather_wait(R.W2, 3)

    def feed(q):
        share_wait(1, q)
        rows = rows_of(q)
        for n in range(4):
            at = slice(n * 256, (n + 1) * 256)
            u = nn(R.AG[1, rows, :], R.W1[:, at]) + R.VRN[pl.ds(10 + m, 1), at]
            phi = 0.5 * (1.0 + lax.erf(u * (1.0 / math.sqrt(2.0))))
            R.GEL[rows, at] = (u * phi).astype(BF)
            R.GELP[rows, at] = phi + u * jnp.exp(-0.5 * u * u) * (1.0 / math.sqrt(2.0 * math.pi))
        branch_send(2, q, R.GEL[rows, :], R.W2)

    loop(0, NQ - 1, feed)
    two_cross(R.HW, 0)
    loop(NQ - 1, NQ, feed)
    two_second(R.WA3F, 9)
    gather_wait(R.HW, 0)
    drain(R.TGT.at[pl.ds(0, 3)], yrecv.at[2])

    def head_rows(q):
        here = local_of(q)
        x2 = R.XS[here, :] + branch_sum(2, q) + vrow(14)
        n, r = ln_parts(x2)
        h3 = (n * vrow(15) + vrow(16)).astype(BF)
        R.H3[here, :] = h3
        pred = nn(h3, R.HW[...])
        weight = R.LW[own_of(q, m), 0:64]
        for j in range(4):
            misfit = pred[:, j * 64 : (j + 1) * 64] - R.TGT[j, q, :, 0:64]
            weighted = weight * misfit
            R.NX[4 + j : 5 + j, 0:64] = R.NX[4 + j : 5 + j, 0:64] + jnp.sum(
                weighted * misfit, 0, keepdims=True
            )
            R.DP[here, j * 64 : (j + 1) * 64] = (2.0 * weighted / total_count).astype(BF)
        dh3 = nt(R.DP[here, :], R.HW[...])
        dx2, dgain, dbias = ln_back(n, r, vrow(15), dh3)
        share_send(2, q, dx2.astype(BF))
        R.XS[here, :] = dx2
        R.GVP[14:15, :] = R.GVP[14:15, :] + jnp.sum(dx2, 0, keepdims=True)
        R.GVP[15:16, :] = R.GVP[15:16, :] + dgain
        R.GVP[16:17, :] = R.GVP[16:17, :] + dbias

    loop(0, NQ, head_rows)

    def feed_back(q):
        share_wait(2, q)
        rows = rows_of(q)
        for n in range(4):
            at = slice(n * 256, (n + 1) * 256)
            du = (nn(R.AG[2, rows, :], R.W2[:, at]) * R.GELP[rows, at]).astype(BF)
            R.DU[rows, at] = du
            row = pl.ds(10 + m, 1)
            R.GVN[row, at] = R.GVN[row, at] + jnp.sum(du.astype(F32), 0, keepdims=True)
        branch_send(3, q, R.DU[rows, :], R.W1)

    loop(0, NQ, feed_back)
    two_cross(R.WA3F, 9)

    def pieces(q, fn):
        for j in range(4 // NQ):
            fn(pl.ds(pl.multiple_of((q * (4 // NQ) + j) * 256, 256), 256))

    def grad_two(at):
        R.G2[at, :] = tn(R.AG[2, :, at], R.GEL[...]).astype(BF)

    def grad_one(at):
        R.G1[at, :] = tn(R.AG[1, :, at], R.DU[...]).astype(BF)

    def back_rows(q):
        here = local_of(q)
        n = R.LN[1, here, :]
        dx1, dgain, dbias = ln_back(n, R.RR[1, here, 0:1], vrow(8), branch_sum(3, q))
        dx1 = dx1 + R.XS[here, :]
        dy = dx1.astype(BF)
        R.DOF[here, :] = nn(dy, R.WB3F[...]).astype(BF)
        heads_back(R.DOF, R.DOB, q, ysend.at[19], R.nrecv.at[0, q])
        R.AG[3, own_of(q, m), :] = dy
        R.XS[here, :] = dx1
        R.GVP[7:8, :] = R.GVP[7:8, :] + jnp.sum(dx1, 0, keepdims=True)
        R.GVP[8:9, :] = R.GVP[8:9, :] + dgain
        R.GVP[9:10, :] = R.GVP[9:10, :] + dbias

    for n in range(4):
        grad_two(pl.ds(n * 256, 256))
    reduce_cross("2", 13)
    for n in range(4):
        grad_one(pl.ds(n * 256, 256))
    reduce_cross("1", 12)
    loop(0, NQ // 2, back_rows)
    fold_first("2", 13)
    loop(NQ // 2, NQ, back_rows)
    loop(0, NQ, lambda q: share_start(3, q))
    fold_first("1", 12)
    R.GH[...] = tn(R.H3[...], R.DP[...]).astype(BF)
    reduce_cross("H", 14)
    gather_wait(R.WA3F, 16)
    fold_first("H", 14)

    loop(0, NQ, lambda q: drain(R.DOB.at[pl.ds(0, 3 * CH)], R.nrecv.at[0, q]))
    for h in range(4):
        at = slice(h * 64, (h + 1) * 64)
        probs = R.PB[h]
        dout = R.DOB[:, at]
        dv = tn(probs.astype(BF), dout).astype(BF)
        dprob = nt(dout, R.QKV[2, :, at])
        ds = (probs * (dprob - jnp.sum(probs * dprob, 1, keepdims=True))).astype(BF)
        dq = (nn(ds, R.QKV[1, :, at]) * SCALE).astype(BF)
        dk = (tn(ds, R.QKV[0, :, at]) * SCALE).astype(BF)
        R.DQKV[:, h * 64 : (h + 1) * 64] = dq
        R.DQKV[:, 256 + h * 64 : 256 + (h + 1) * 64] = dk
        R.DQKV[:, 512 + h * 64 : 512 + (h + 1) * 64] = dv
    loop(0, NQ, lambda q: branch_send(4, q, R.DQKV[rows_of(q), :], R.WB, (0, 768)))
    fold_second("2", 13)
    R.GVN[5:6, my_cols] = jnp.sum(R.DQKV[:, 0:256].astype(F32), 0, keepdims=True)
    R.GVN[6:7, my_cols] = jnp.sum(R.DQKV[:, 512:768].astype(F32), 0, keepdims=True)

    def grad_attn(at):
        R.GB[at, :] = tn(R.AG[0, :, at], R.DQKV[...]).astype(BF)

    def grad_out(n):
        at = pl.ds(pl.multiple_of(n * 256, 256), 256)
        R.G3[at, :] = tn(R.AG[3, :, at], R.OB[...]).astype(BF)

    def first_rows(q):
        here = local_of(q)
        n = R.LN[0, here, :]
        dx0, dgain, dbias = ln_back(n, R.RR[0, here, 0:1], vrow(3), branch_sum(4, q))
        dx0 = dx0 + R.XS[here, :]
        dya = dx0.astype(BF)
        R.DMF[here, :] = nn(dya, R.WA3F[...]).astype(BF)
        heads_back(R.DMF, R.DMB, q, ysend.at[20], R.nrecv.at[1, q])
        R.AG[4, own_of(q, m), :] = dya
        lead = R.TCOL[own_of(q, m), 1:2]
        R.GVP[1:2, :] = R.GVP[1:2, :] + jnp.sum(dx0, 0, keepdims=True)
        R.GVP[2:3, :] = R.GVP[2:3, :] + jnp.sum(lead * dx0, 0, keepdims=True)
        R.GVP[3:4, :] = R.GVP[3:4, :] + dgain
        R.GVP[4:5, :] = R.GVP[4:5, :] + dbias

    loop(0, NQ, lambda q: share_wait(3, q))
    loop(0, 4, grad_out)
    reduce_cross("3", 18)
    loop(0, 4, lambda n: grad_attn(pl.ds(pl.multiple_of(n * 256, 256), 256)))
    reduce_cross("B", 11)
    fold_first("3", 18)
    loop(0, NQ // 2, first_rows)
    fold_second("1", 12)
    fold_first("B", 11)
    loop(0, NQ // 2, lambda q: share_start(4, q))
    loop(NQ // 2, NQ, first_rows)
    loop(NQ // 2, NQ, lambda q: share_start(4, q))
    R.TMPV[...] = R.GVN[...].T
    R.GVT[...] = R.GVP[...].T.reshape(DPN, 4, 8, 128)

    def permuted(i):
        block = lax.rem(i, 2) * 16 + i // 2
        own = R.TMPV[pl.ds(pl.multiple_of(i * 32, 32), 32), :]
        R.GVT[block] = R.GVT[block] + own.reshape(4, 8, 128)

    loop(0, DPN, permuted)
    for g in range(4):
        R.GVK[:, 32 * g : 32 * (g + 1)] = R.GVT[:, g, :, 0:32].reshape(256, 32)
    core_rows = pl.ds(pl.multiple_of(c * 128, 128), 128)
    rcopy(
        R.GVK.at[pl.ds(pl.multiple_of(128 - c * 128, 128), 128)],
        R.GVS,
        ssend.at[15],
        srecv.at[15],
        sib,
        m,
    ).start()
    at_eight = pl.ds(pl.multiple_of(k * 8, 8), 8)

    def vectors_spread():
        drain(R.GVS, srecv.at[15])
        R.GVS[...] = R.GVS[...] + R.GVK[core_rows, :]

        def send(kk, t):
            src = R.GVS.at[pl.ds(pl.multiple_of(kk * 8, 8), 8)]
            rcopy(src, R.GVB.at[at_eight], dsend.at[15], drecv.at[15], t, m).start()

        to_chips(send)

    def vectors_end():
        drain(R.GVB.at[pl.ds(0, 120)], drecv.at[15])
        total = R.GVS[at_eight, :]
        for dz, dx in FAR_FIRST:
            kk = lax.rem(z + dz, 4) * 4 + lax.rem(x + dx, 4)
            total = total + R.GVB[pl.ds(pl.multiple_of(kk * 8, 8), 8), :]
        for g in range(4):
            R.VG[8 * g : 8 * (g + 1), 0:32] = total[:, 32 * g : 32 * (g + 1)]
        drain(R.GVB.at[pl.ds(0, 120)], dsend.at[15])
        drain(R.GVS, ssend.at[15])

    loop(0, NQ, lambda q: drain(R.DMB.at[pl.ds(0, 3 * CH)], R.nrecv.at[1, q]))
    vectors_spread()
    R.PRP[...] = jnp.zeros_like(R.PRP)
    for h in range(4):
        at = slice(h * 64, (h + 1) * 64)
        dout = R.DMB[:, at]
        through = nt(ewv[:, at], dout)
        dprob = R.PIXT[0:48, :] * through[0:48, :]
        for p in range(1, 5):
            row = slice(p * 48, (p + 1) * 48)
            dprob = dprob + R.PIXT[row, :] * through[row, :]
        probs = R.PT[h]
        ds = (probs * (dprob - jnp.sum(probs * dprob, 0, keepdims=True))).astype(BF).astype(F32)
        for p in range(5):
            row = slice(p * 48, (p + 1) * 48)
            R.PRP[row, 256 + h : 257 + h] = jnp.sum(ds * R.PIXT[row, :], 1, keepdims=True)
        R.PRP[:, at] = nn(R.MT[h], dout)
    R.PRB[...] = R.PRP[...].astype(BF)

    lanes = iota((1, 128), 1)
    sums = {"w": jnp.zeros((1, 128), F32), "u": jnp.zeros((1, 128), F32)}

    def square_sum(values):
        return jnp.sum(jnp.sum(values * values, 1, keepdims=True), 0, keepdims=True)

    def tensor(index, weight, gradient, first, second):
        unused, unused2, direction = adam_direction(weight, gradient, first, second)
        here = lanes == index
        sums["w"] = sums["w"] + jnp.where(here, square_sum(weight), 0.0)
        sums["u"] = sums["u"] + jnp.where(here, square_sum(direction), 0.0)

    def hook_first():
        fold_second("H", 14)
        fold_second("3", 18)
        loop(0, NQ, lambda q: share_wait(4, q))

        def piece(n):
            at = pl.ds(pl.multiple_of(n * 256, 256), 256)
            R.GA3[at, :] = tn(R.AG[4, :, at], R.OA[...]).astype(BF)

        loop(0, 4, piece)
        reduce_cross("A3", 10)
        for name in ("agg", "attn", "mlp", "head"):
            fetch(name + "_f").wait()
            fetch(name + "_s").wait()
        R.o_mlp[1] = fold_end("2", 13)
        R.o_mlp[0] = fold_end("1", 12)
        for j in range(2):
            tensor(8 + j, R.in_mlpw[j], R.o_mlp[j], R.in_mlp_f[j], R.in_mlp_s[j])
        reduce_spread("A3", 10)

    def hook_second():
        fold_second("B", 11)

    def hook_third():
        total = fold_end("H", 14)
        for j in range(MPN):
            R.HG[j, :, 0:64] = total[:, 64 * j : 64 * (j + 1)]
        vectors_end()

        def sends(i, t):
            rcopy(
                R.HG.at[t],
                R.HGR.at[i - 1],
                ysend.at[14],
                yrecv.at[4],
                d,
                t,
            ).start()
            rcopy(
                R.VG.at[pl.ds(pl.multiple_of(t * 8, 8), 8)],
                R.VGR.at[i - 1],
                ysend.at[15],
                yrecv.at[5],
                d,
                t,
            ).start()

        to_peers(sends)

    all_sum(R.PRB, R.PRC, R.PRH, R.PRR, 8, (hook_first, hook_second, hook_third))

    spread = nt(R.PRR[:, 256:384], head_of.astype(BF))
    dqa = jnp.sum(spread * ewk, 0, keepdims=True) * SCALE
    pk = spread * (qa * SCALE)
    pv = R.PRR[:, 0:256]
    emb = R.TA[:, 0:256]
    wa = [R.in_aggw[j].astype(BF).astype(F32) for j in range(3)]
    pk = pk.astype(BF)
    R.TG[...] = nt(wa[1].astype(BF), pk) + nt(wa[2].astype(BF), pv)
    R.TG[:, 240:241] = jnp.sum(wa[0] * dqa, 1, keepdims=True)

    to_peers(
        lambda i, t: rcopy(R.TG, R.TGR.at[i - 1], ysend.at[13], yrecv.at[3], d, t).start()
    )
    R.o_agg[0] = R.TA[:, 256:257] * dqa
    emb = emb.astype(BF)
    R.o_agg[1] = nn(emb, pk)
    R.o_agg[2] = nn(emb, pv)
    for j in range(3):
        tensor(j, R.in_aggw[j], R.o_agg[j], R.in_agg_f[j], R.in_agg_s[j])
    gsum = fold_end("B", 11)
    for j in range(3):
        R.o_attn[j] = gsum[:, j * 256 : (j + 1) * 256]
    R.o_attn[3] = fold_end("3", 18)
    for j in range(4):
        tensor(4 + j, R.in_attnw[j], R.o_attn[j], R.in_attn_f[j], R.in_attn_s[j])
    drain(R.HGR, yrecv.at[4])
    hgrad = R.HG[m] + R.HGR[0] + R.HGR[1] + R.HGR[2]
    R.o_head[...] = hgrad[:, 0:NVAR]
    tensor(10, R.in_headw[...], R.o_head[...], R.in_head_f[...], R.in_head_s[...])
    drain(R.VGR, yrecv.at[5])
    vgrad = R.VG[my_eight, :] + R.VGR[0] + R.VGR[1] + R.VGR[2]
    R.o_vec[...] = vgrad[:, 0:NVEC]
    unused, unused2, direction = adam_direction(
        R.in_vec[...], R.o_vec[...], R.in_vec_f[...], R.in_vec_s[...]
    )
    R.o_agg[3] = reduce_end("A3", 10)
    tensor(3, R.in_aggw[3], R.o_agg[3], R.in_agg_f[3], R.in_agg_s[3])
    R.NX[0:1, :] = sums["w"]
    R.NX[1:2, :] = sums["u"]
    vector_w = jnp.sum(R.in_vec[...] * R.in_vec[...], 0, keepdims=True)
    vector_u = jnp.sum(direction * direction, 0, keepdims=True)
    R.NX[0:1, 13 : 12 + NVEC] = vector_w[:, 1:]
    R.NX[1:2, 13 : 12 + NVEC] = vector_u[:, 1:]
    to_peers(lambda i, t: rcopy(R.NX, R.NXR.at[i - 1], ysend.at[16], yrecv.at[6], d, t).start())

    drain(R.TMO.at[pl.ds(0, 24)], yrecv.at[9])
    R.WT[...] = R.TA[:, 0:256]
    R.WT[:, 240:241] = R.TA[:, 256:257]
    R.o_vw[...] = R.in_vec[...]
    R.o_vf[...] = R.in_vec_f[...]
    R.o_vs[...] = R.in_vec_s[...]
    R.o_run[...] = R.in_run[...]
    R.o_ew[...] = R.in_emb[...]
    R.o_ef[...] = R.in_emb_f[...]
    R.o_es[...] = R.in_emb_s[...]
    R.o_hw[...] = R.in_headw[...]
    R.o_hf[...] = R.in_head_f[...]
    R.o_hs[...] = R.in_head_s[...]
    drain(R.TGR, yrecv.at[3])
    whole = R.TG[...] + R.TGR[0] + R.TGR[1] + R.TGR[2]
    R.TGF[...] = whole
    unused, unused2, direction = adam_direction(
        R.WT[...], whole, R.TMO[:, 0:256], R.TMO[:, 256:512]
    )
    lane = iota((1, 256), 1)

    def two_sums(values):
        columns = jnp.sum(values * values, 0, keepdims=True)
        embed = jnp.sum(jnp.where(lane < 240, columns, 0.0), 1, keepdims=True)
        first = jnp.sum(jnp.where(lane == 240, columns, 0.0), 1, keepdims=True)
        return jnp.where(lanes == 11, embed, 0.0) + jnp.where(lanes == 12, first, 0.0)

    embed_w, embed_u = two_sums(R.WT[...]), two_sums(direction)
    drain(R.NXR, yrecv.at[6])
    R.NY[...] = R.NX[...] + R.NXR[0] + R.NXR[1] + R.NXR[2]
    R.NY[0:1, :] = R.NY[0:1, :] + embed_w
    R.NY[1:2, :] = R.NY[1:2, :] + embed_u
    at_d = pl.ds(pl.multiple_of(d * 8, 8), 8)

    def norm_send(t):
        rcopy(R.NY, R.NYR.at[at_d], dsend.at[16], drecv.at[16], t, m).start()

    for dz, dx in FAR_FIRST:
        chip = lax.rem(z + dz, 4) * 4 + lax.rem(x + dx, 4)
        norm_send(chip * 2)
        norm_send(chip * 2 + 1)
    norm_send(sib)

    tgrad = R.TGF[my_eight, :]
    for p in range(5):
        R.EG[p * 8 : (p + 1) * 8, :] = tgrad[:, p * 48 : (p + 1) * 48]
    R.o_emb[...] = nt(R.EG[...], vhot, HIGH)
    R.o_vec[:, 0:1] = tgrad[:, 240:241]

    gather_end(R.VPK, 4)
    for buf, g in ((R.HW, 0), (R.WB, 1), (R.W1, 2), (R.W2, 3), (R.WA3, 8), (R.WA3F, 9), (R.WB3F, 10)):
        two_end(buf, g)
    all_sum_end(R.EWC, R.EWH, R.EWR, 6)
    all_sum_end(R.PRC, R.PRH, R.PRR, 8)
    for ix in range(5):
        if ix == 1:
            drain(R.OF.at[:, pl.ds(0, 768)], ysend.at[1])
        else:
            drain(R.RSR.at[ix], ysend.at[ix])
        drain(R.AG.at[ix, pl.ds(0, 192)], ysend.at[5 + ix])
    drain(R.TA.at[pl.ds(0, 24)], ysend.at[10])
    drain(R.HWS.at[pl.ds(0, 3)], ysend.at[11])
    drain(R.TGT.at[pl.ds(0, 3)], ysend.at[12])
    drain(R.TGR, ysend.at[13])
    drain(R.HGR, ysend.at[14])
    drain(R.VGR, ysend.at[15])
    drain(R.NXR, ysend.at[16])
    drain(R.TMO.at[pl.ds(0, 24)], ysend.at[21])
    drain(R.WB3F.at[pl.ds(0, 32), pl.ds(0, 768)], ysend.at[17])
    drain(R.WA3F.at[pl.ds(0, 32), pl.ds(0, 768)], ysend.at[18])
    drain(R.OF.at[:, pl.ds(0, 768)], ysend.at[19])
    drain(R.OF.at[:, pl.ds(0, 768)], ysend.at[20])

    drain(R.NYR.at[pl.ds(0, 248)], drecv.at[16])
    stats = R.NY[...]
    for i in range(1, DPN):
        at = pl.multiple_of(lax.rem(d + i, DPN) * 8, 8)
        stats = stats + R.NYR[pl.ds(at, 8), :]
    first_lane = (iota((8, 128), 0) == 0) & (iota((8, 128), 1) == 127)
    R.o_stats[...] = jnp.where(first_lane, total_count, stats)
    drain(R.NYR.at[pl.ds(0, 248)], dsend.at[16])


def mega_call(inputs):
    outs = [SHAPES[n] for n in ("emb", "vec", "agg", "attn", "mlp", "head")] + [((8, 128), F32)]
    outs += [SHAPES["vec"]] * 3 + [SHAPES["run"]] + [SHAPES["emb"]] * 3 + [SHAPES["head"]] * 3
    whole = pl.BlockSpec(memory_space=pltpu.VMEM)
    return pl.pallas_call(
        mega,
        out_shape=tuple(pltpu.VMEM(*item) for item in outs),
        in_specs=[pl.BlockSpec(memory_space=pl.ANY)] * len(inputs),
        out_specs=(whole,) * len(outs),
        scratch_shapes=[item for unused, item in SCRATCH],
        compiler_params=pltpu.CompilerParams(
            collective_id=0, has_side_effects=True, vmem_limit_bytes=56 * 2**20
        ),
        name="step",
    )(*inputs)


def finish(*refs):
    weights, firsts, seconds, grads = (refs[6 * i : 6 * i + 6] for i in range(4))
    stats, running = refs[24:26]
    o_loss, o_count, o_running, o_trust, o_norms = refs[26:31]
    outs = refs[31:49]
    norms = jnp.sqrt(stats[0:1, :])
    trust = norms / jnp.sqrt(stats[1:2, :])
    o_norms[...] = norms[:, 0:29]
    o_trust[...] = trust[:, 0:29]
    count = stats[0:1, 127:128]
    o_count[...] = count
    errors = jnp.zeros((1, NVAR), F32)
    for j in range(4):
        lane = iota((128, NVAR), 0)
        pick = (lane < NVAR) & (iota((128, NVAR), 1) == 12 * j + lane // P_SIZE)
        errors = errors + nn(stats[4 + j : 5 + j, :], pick.astype(F32), HIGH)
    o_loss[...] = jnp.sum(errors, 1, keepdims=True)
    o_running[...] = STATS_DECAY * running[...] + (1.0 - STATS_DECAY) * errors * (NVAR / count)

    def update(i, at, ratio):
        first, second, direction = adam_direction(
            weights[i][at], grads[i][at], firsts[i][at], seconds[i][at]
        )
        outs[i][at] = first
        outs[6 + i][at] = second
        outs[12 + i][at] = weights[i][at] - LEARN_RATE * ratio * direction

    for i, number, offset in ((0, 4, 0), (1, 4, 4), (2, 2, 8)):
        for j in range(number):
            update(i, j, trust[:, offset + j : offset + j + 1])
    update(3, Ellipsis, trust[:, 10:11])
    update(4, Ellipsis, trust[:, 11:12])
    update(5, Ellipsis, trust[:, 12 : 12 + NVEC])


def finish_call(weights, firsts, seconds, grads, stats, running):
    shapes = [(1, 1), (1, 1), (1, NVAR), (1, 29), (1, 29)] + 3 * [w.shape for w in weights]
    whole = pl.BlockSpec(memory_space=pltpu.VMEM)
    values = (*weights, *firsts, *seconds, *grads, stats, running)
    return pl.pallas_call(
        finish,
        out_shape=tuple(jax.ShapeDtypeStruct(s, F32) for s in shapes),
        in_specs=[whole] * 26,
        out_specs=(whole,) * 23,
        compiler_params=pltpu.CompilerParams(vmem_limit_bytes=32 * 2**20),
        name="finish",
    )(*values)


def on_device(
    pixels,
    targets,
    valid_mask,
    segments,
    lead_index,
    latitude,
    var_ids,
    running_error,
    *tensors,
):
    def turned(group):
        agg, attn, mlp, head, embed, vecs = group
        return (agg, attn, mlp, head, embed.transpose(1, 2, 0).reshape(40, NVAR), vecs.T)

    weights, firsts, seconds = (turned(tensors[6 * i : 6 * i + 6]) for i in range(3))
    agg, attn, mlp, head, embed, vecs = weights
    first = (embed, var_ids.reshape(1, NVAR), vecs, agg, head, mlp, attn, targets.T, pixels.T)
    second = (
        valid_mask.T,
        segments,
        lead_index,
        latitude.reshape(1, TOK),
        running_error.reshape(1, NVAR),
    )
    g_emb, g_vec, g_agg, g_attn, g_mlp, g_head, stats, *rest = mega_call(
        (*first, *second, *firsts, *seconds)
    )
    grads = (g_agg, g_attn, g_mlp, g_head, g_emb, g_vec)
    weights, firsts, seconds = (
        (*group[:3], head, embed, own)
        for group, own, embed, head in zip((weights, firsts, seconds), rest, rest[4:], rest[7:])
    )
    out = finish_call(weights, firsts, seconds, grads, stats, rest[3])

    def back(group):
        agg, attn, mlp, head, embed, vecs = group
        return (agg, attn, mlp, head, embed.reshape(5, 8, NVAR).transpose(2, 0, 1), vecs.T)

    return (
        out[0].reshape(()),
        out[1].reshape(()),
        out[2].reshape(NVAR),
        out[3].reshape(29),
        out[4].reshape(29),
        *back(out[5:11]),
        *back(out[11:17]),
        *back(out[17:23]),
    )


def solution(mesh):
    weights = (
        P(None, "dp", "mp"),
        P(None, "dp", "mp"),
        P(None, "dp", "mp"),
        P("dp", "mp"),
        P(None, None, ("dp", "mp")),
        P(None, ("dp", "mp")),
    )
    in_specs = (
        P("dp", None),
        P("dp", "mp"),
        P("dp", None),
        P("dp", None),
        P("dp", None),
        P("dp"),
        P(),
        P(),
        *weights,
        *weights,
        *weights,
    )
    out_specs = (P(), P(), P(), P(), P(), *weights, *weights, *weights)
    return jax.shard_map(
        on_device, mesh=mesh, in_specs=in_specs, out_specs=out_specs, check_vma=False
    )
```
